32 devices in a mesh: row: 8 (over y, x, core), col: 4 (over z).
Axes of the slice: x: 2, y: 2, z: 4, core: 2. Of those that a mesh axis runs over, the one named last changes fastest.
Arguments:
- inputs: bfloat16 [2048, 2048], P('row', 'col'), may hold values from -6 to 6
- cotangent: bfloat16 [2048, 2048], P('row', 'col'), may hold values from -6 to 6
- lengths: int32 [8], P('row'), may hold values from 128 to 256, as said below
- adapter_pick: int32 [8], P('row'), may hold values from 0 to 7
- attn_route: int32 [2048, 2], P('row'), may hold values from 0 to 7, all different within a row; in each aligned block of 256 rows (0 to 255, 256 to 511, ...) at most 80 rows name the same one
- ffn_route: int32 [2048, 2], P('row'), may hold values from 0 to 3, all different within a row; in each aligned block of 256 rows (0 to 255, 256 to 511, ...) at most 160 rows name the same one
- norm_one: float32 [2048], replicated, may hold values from 0.5 to 1.5
- norm_two: float32 [2048], replicated, may hold values from 0.5 to 1.5
- router_attn: bfloat16 [2048, 8], replicated, may hold values from -0.09375 to 0.09375
- router_ffn: bfloat16 [2048, 4], replicated, may hold values from -0.09375 to 0.09375
- kv_weight: bfloat16 [2, 2048, 2048], P(None, 'row', 'col'), may hold values from -0.125 to 0.125
- query_weight: bfloat16 [8, 2048, 2048], P(None, 'row', 'col'), may hold values from -0.125 to 0.125
- out_weight: bfloat16 [8, 2048, 2048], P(None, 'row', 'col'), may hold values from -0.5 to 0.5
- inner_weight: bfloat16 [4, 2048, 2, 5632], P(None, 'row', None, 'col'), may hold values from -0.125 to 0.125
- down_weight: bfloat16 [4, 2048, 5632], P(None, 'row', 'col'), may hold values from -0.078125 to 0.078125
- query_left: bfloat16 [8, 2048, 16], P(None, 'row'), may hold values from -0.125 to 0.125
- query_right: bfloat16 [8, 16, 2048], P(None, None, 'col'), may hold values from -1.5 to 1.5
- kv_left: bfloat16 [8, 2048, 16], P(None, 'row'), may hold values from -0.125 to 0.125
- kv_right: bfloat16 [8, 16, 2, 2048], P(None, None, None, 'col'), may hold values from -1.5 to 1.5
- out_left: bfloat16 [8, 2048, 16], P(None, 'row'), may hold values from -1.5 to 1.5
- out_right: bfloat16 [8, 16, 2048], P(None, None, 'col'), may hold values from -0.5 to 0.5
- inner_left: bfloat16 [8, 2048, 16], P(None, 'row'), may hold values from -0.125 to 0.125
- inner_right: bfloat16 [8, 16, 2, 5632], P(None, None, None, 'col'), may hold values from -1.5 to 1.5
- down_left: bfloat16 [8, 2048, 16], P(None, 'row'), may hold values from -1.5 to 1.5
- down_right: bfloat16 [8, 16, 5632], P(None, None, 'col'), may hold values from -0.078125 to 0.078125
Outputs:
- output: bfloat16 [2048, 2048], P('row', 'col')
- grad_inputs: float32 [2048, 2048], P('row', 'col')
- grad_query_left: float32 [8, 2048, 16], P(None, 'row')
- grad_query_right: float32 [8, 16, 2048], P(None, None, 'col')
- grad_kv_left: float32 [8, 2048, 16], P(None, 'row')
- grad_kv_right: float32 [8, 16, 2, 2048], P(None, None, None, 'col')
- grad_out_left: float32 [8, 2048, 16], P(None, 'row')
- grad_out_right: float32 [8, 16, 2048], P(None, None, 'col')
- grad_inner_left: float32 [8, 2048, 16], P(None, 'row')
- grad_inner_right: float32 [8, 16, 2, 5632], P(None, None, None, 'col')
- grad_down_left: float32 [8, 2048, 16], P(None, 'row')
- grad_down_right: float32 [8, 16, 5632], P(None, None, 'col')
The draws below stay inside these ranges and needn't reach their ends.
Inputs may be any that keep to these rules, and one draw needn't show every extreme that they name: `lengths`: every sequence has 128 to 256 tokens; some sequence has exactly 256. `attn_route`: within each aligned block of 256 rows (one row group) no attention expert is named more than 80 times; the two experts of a row differ. `ffn_route`: within each aligned block of 256 rows no feed-forward expert is named more than 160 times; the two experts of a row differ.
All inputs are finite; a program needn't handle non-finite values.
Results may differ from the reference program's by a relative error of at most 0.017.
Values may be sent and summed in bfloat16 or wider, within the bound.
A program may use at most 384 MiB of HBM per device.

```python
import math
import jax
import jax.numpy as jnp
import numpy as np
from jax import lax

D = 2048
KV_HEADS = 16
HEAD_DIM = 128
FF = 5632
EXP_ATT = 8
EXP_FF = 4
TOPK = 2
RANK = 16
ADAPT = 8
TOK = 256
CAP_ATT = 80
CAP_FF = 160
GROUPS = 8
TOKENS = 2048


def draw_lengths(key, part):
    drawn_lengths = jax.random.randint(jax.random.fold_in(key, 11), (GROUPS,), TOK // 2, TOK + 1)
    longest = jax.random.randint(jax.random.fold_in(key, 12), (), 0, GROUPS)
    return jnp.where(jnp.arange(GROUPS) == longest, TOK, drawn_lengths).astype(jnp.int32)


def with_ends(array, own_key, low, top_value):
    spot = [jax.random.randint(jax.random.fold_in(own_key, axis), (), 0, length) for axis, length in enumerate(array.shape)]
    widest = array.shape.index(max(array.shape))
    next_to = spot[:widest] + [(spot[widest] + 1) % array.shape[widest]] + spot[widest + 1:]
    return array.at[tuple(spot)].set(low).at[tuple(next_to)].set(top_value)


def steps_of(rng, dims, pieces, smallest, largest):
    def one(dim, blocks):
        heights = jax.random.uniform(jax.random.fold_in(jax.random.fold_in(rng, 6), dim), (blocks,), jnp.float32, smallest / len(pieces), largest / len(pieces))
        return jnp.repeat(jnp.exp(heights), dims[dim] // blocks).reshape((-1,) + (1,) * (len(dims) - dim - 1))

    level = one(*pieces[0])
    for cut in pieces[1:]:
        level = level * one(*cut)
    return level


def deal_out(rng, own, number, rows, number_of, top, most, skew):
    ranking = jax.random.permutation(rng, number_of)
    crowded, usual = load_shares(number_of, rows * top, most, skew, True), load_shares(number_of, rows * top, most, skew, False)
    places = jnp.arange(number_of)

    def named(sizes, turn):
        used = int((sizes > 0).sum())
        fixed = max(1, used // 4)
        moved = fixed + (places - fixed + turn * (used - fixed)) % max(1, number_of - fixed)
        return jnp.zeros((number_of,), jnp.int32).at[ranking[jnp.where(places < fixed, places, moved)]].set(jnp.asarray(sizes, jnp.int32))

    sizes = jnp.where(number % 4 == 0, named(crowded, number // 4), named(usual, number - number // 4 - 1))
    mixed = jax.random.permutation(jax.random.fold_in(own, 3), number_of)
    source_of, receiver = mixed[0:number_of // 2 * 2:2], mixed[1:number_of // 2 * 2:2]
    margin = jnp.minimum(sizes[source_of] - 1, most - sizes[receiver]) // 2
    margin = jnp.where((source_of == ranking[0]) | (receiver == ranking[0]) | (sizes[receiver] == 0), 0, jnp.maximum(margin, 0))
    moved = jax.random.randint(jax.random.fold_in(own, 4), (number_of // 2,), 0, 1 << 20) % (margin + 1)
    sizes = sizes.at[source_of].add(-moved).at[receiver].add(moved)
    members = jnp.searchsorted(jnp.cumsum(sizes), jnp.arange(rows * top), side="right").astype(jnp.int32)
    grid = members.reshape(top, rows).T
    grid = grid[jax.random.permutation(jax.random.fold_in(own, 1), rows)]
    turn = jax.random.randint(jax.random.fold_in(own, 2), (rows, 1), 0, top)
    return jnp.take_along_axis(grid, (jnp.arange(top)[None, :] + turn) % top, axis=1)


def load_shares(amount, total, bound, skew, full):
    weights = [(1 << 20) // math.isqrt(standing ** skew) + 1 for standing in range(1, amount + 1)]
    largest = bound if full else min(bound, max(-(-total // amount), total * weights[0] // sum(weights)))
    least = 1 if total - largest >= amount - 1 else 0
    holding, surplus = [largest] + [least] * (amount - 1), total - largest - least * (amount - 1)
    while surplus > 0:
        movable = [i for i in range(1, amount) if holding[i] < largest] or [i for i in range(1, amount) if holding[i] < bound]
        mass, left = sum([weights[i] for i in movable]), surplus
        for i in movable:
            more = min(bound - holding[i], max(1, left * weights[i] // mass), surplus)
            holding[i] = holding[i] + more
            surplus = surplus - more
    return np.array(holding)


def gaussian(stream_key, shape, spread, bound, cuts=(), kind=jnp.bfloat16):
    drawn = jax.random.normal(stream_key, shape, jnp.float32) * spread
    if len(cuts) > 0:
        drawn = steps_of(stream_key, shape, cuts, -0.22, 0.18) * drawn
    return jnp.clip(drawn, min=-bound, max=bound).astype(kind)


def setup_inputs(seed: int = 0) -> dict:
    key_list = jax.random.split(jax.random.key(seed), 26)
    inputs = gaussian(key_list[0], (TOKENS, D), 1.0, 6.0, ((0, 8), (1, 4)))
    cotangent = gaussian(key_list[1], (TOKENS, D), 1.0, 6.0, ((0, 8), (1, 4)))
    lengths = draw_lengths(jax.random.fold_in(key_list[25], 71), 0)
    adapter_pick = with_ends(jax.random.randint(key_list[3], (GROUPS,), 0, ADAPT), jax.random.fold_in(key_list[3], 1), 0, ADAPT - 1).astype(jnp.int32)
    attn_route_keys = jax.random.split(jax.random.fold_in(key_list[4], 1), TOKENS // TOK)
    attn_route_turns = jax.random.permutation(jax.random.fold_in(key_list[4], 3), TOKENS // TOK)
    attn_route = jax.vmap(lambda own, number: deal_out(jax.random.fold_in(key_list[4], 2), own, number, TOK, EXP_ATT, TOPK, CAP_ATT, 0))(attn_route_keys, attn_route_turns).reshape((TOKENS, TOPK))
    ffn_route_keys = jax.random.split(jax.random.fold_in(key_list[5], 1), TOKENS // TOK)
    ffn_route_turns = jax.random.permutation(jax.random.fold_in(key_list[5], 3), TOKENS // TOK)
    ffn_route = jax.vmap(lambda own, number: deal_out(jax.random.fold_in(key_list[5], 2), own, number, TOK, EXP_FF, TOPK, CAP_FF, 0))(ffn_route_keys, ffn_route_turns).reshape((TOKENS, TOPK))
    norm_one = jnp.clip(1.0 + 0.1 * jax.random.normal(key_list[6], (D,), jnp.float32), 0.5, 1.5)
    norm_two = jnp.clip(1.0 + 0.1 * jax.random.normal(key_list[7], (D,), jnp.float32), 0.5, 1.5)
    router_attn = gaussian(key_list[8], (D, EXP_ATT), (2 * D) ** -0.5, 0.09375)
    router_ffn = gaussian(key_list[9], (D, EXP_FF), (2 * D) ** -0.5, 0.09375)
    kv_weight = gaussian(key_list[10], (2, D, KV_HEADS * HEAD_DIM), D ** -0.5, 0.125, ((1, 8), (2, 4)))
    query_weight = gaussian(key_list[11], (EXP_ATT, D, KV_HEADS * HEAD_DIM), D ** -0.5, 0.125, ((1, 8), (2, 4)))
    out_weight = gaussian(key_list[12], (EXP_ATT, D, KV_HEADS * HEAD_DIM), (KV_HEADS * HEAD_DIM // 16) ** -0.5, 0.5, ((1, 8), (2, 4)))
    inner_weight = gaussian(key_list[13], (EXP_FF, D, 2, FF), D ** -0.5, 0.125, ((1, 8), (3, 4)))
    down_weight = gaussian(key_list[14], (EXP_FF, D, FF), FF ** -0.5, 0.078125, ((1, 8), (2, 4)))
    query_left = gaussian(key_list[15], (ADAPT, D, RANK), D ** -0.5, 0.125, ((1, 8),))
    query_right = gaussian(key_list[16], (ADAPT, RANK, KV_HEADS * HEAD_DIM), RANK ** -0.5, 1.5, ((2, 4),))
    kv_left = gaussian(key_list[17], (ADAPT, D, RANK), D ** -0.5, 0.125, ((1, 8),))
    kv_right = gaussian(key_list[18], (ADAPT, RANK, 2, KV_HEADS * HEAD_DIM), RANK ** -0.5, 1.5, ((3, 4),))
    out_left = gaussian(key_list[19], (ADAPT, D, RANK), RANK ** -0.5, 1.5, ((1, 8),))
    out_right = gaussian(key_list[20], (ADAPT, RANK, KV_HEADS * HEAD_DIM), (KV_HEADS * HEAD_DIM // 16) ** -0.5, 0.5, ((2, 4),))
    inner_left = gaussian(key_list[21], (ADAPT, D, RANK), D ** -0.5, 0.125, ((1, 8),))
    inner_right = gaussian(key_list[22], (ADAPT, RANK, 2, FF), RANK ** -0.5, 1.5, ((3, 4),))
    down_left = gaussian(key_list[23], (ADAPT, D, RANK), RANK ** -0.5, 1.5, ((1, 8),))
    down_right = gaussian(key_list[24], (ADAPT, RANK, FF), FF ** -0.5, 0.078125, ((2, 4),))
    return {"inputs": inputs, "cotangent": cotangent, "lengths": lengths, "adapter_pick": adapter_pick, "attn_route": attn_route, "ffn_route": ffn_route, "norm_one": norm_one, "norm_two": norm_two, "router_attn": router_attn, "router_ffn": router_ffn, "kv_weight": kv_weight, "query_weight": query_weight, "out_weight": out_weight, "inner_weight": inner_weight, "down_weight": down_weight, "query_left": query_left, "query_right": query_right, "kv_left": kv_left, "kv_right": kv_right, "out_left": out_left, "out_right": out_right, "inner_left": inner_left, "inner_right": inner_right, "down_left": down_left, "down_right": down_right}


EPSILON = 1e-06
ROPE_BASE = 10000.0
HIGHEST = lax.Precision.HIGHEST

@jax.custom_vjp
def low(v):
    return lax.optimization_barrier(v.astype(jnp.bfloat16)).astype(jnp.float32)

@jax.custom_vjp
def low_back(v):
    return v

def low_keep(v):
    return (low(v), None)

def low_pass(kept, grad):
    return (grad,)

def back_keep(v):
    return (v, None)

def back_low(kept, grad):
    return (low(grad),)
low.defvjp(low_keep, low_pass)
low_back.defvjp(back_keep, back_low)

def tables(count, head_width):
    position = jnp.arange(count).astype(jnp.float32)
    frequency = ROPE_BASE ** (-jnp.arange(head_width // 2).astype(jnp.float32) * 2.0 / head_width)
    angle = position[:, None] * frequency[None, :]
    return (jnp.cos(angle), jnp.sin(angle))

def rotate(values, cosine, sine):
    half_width = values.shape[-1] // 2
    shape = (values.shape[0],) + (1,) * (values.ndim - 2) + (half_width,)
    cos_part = cosine.reshape(shape)
    sin_part = sine.reshape(shape)
    first = values[..., :half_width]
    second = values[..., half_width:]
    return jnp.concatenate([first * cos_part - second * sin_part, second * cos_part + first * sin_part], axis=-1)

def dispatch(route, experts, capacity):
    slots = route.shape[0] * route.shape[1]
    flat_route = route.reshape(slots).astype(jnp.int32)
    onehot = (flat_route[:, None] == jnp.arange(experts, dtype=jnp.int32)[None, :]).astype(jnp.int32)
    earlier = jnp.cumsum(onehot, axis=0) - onehot
    position = lax.optimization_barrier(jnp.sum(earlier * onehot, axis=1)).astype(jnp.int32)
    target = (flat_route * capacity + position).astype(jnp.int32)
    source = jnp.full((experts * capacity,), slots, jnp.int32).at[target].set(jnp.arange(slots, dtype=jnp.int32))
    return (target, source)

def layer(x_rows, length, route_attn, route_ffn, weights, picked):
    norm_one, norm_two, router_attn, router_ffn, kv_weight, query_weight, out_weight, inner_weight, down_weight = weights
    left_query, right_query, left_kv, right_kv, left_out, right_out, left_inner, right_inner, left_down, right_down = picked
    count = x_rows.shape[0]
    width = x_rows.shape[1]
    cosine, sine = tables(count, HEAD_DIM)
    scale_one = lax.rsqrt(lax.optimization_barrier(jnp.mean(x_rows * x_rows, axis=1, keepdims=True)) + EPSILON)
    hidden_one = low(x_rows * scale_one * norm_one)
    chosen_attn = jnp.take_along_axis(jnp.dot(hidden_one, router_attn, precision=HIGHEST), route_attn, axis=1)
    gates_attn = jax.nn.softmax(chosen_attn, axis=1)
    target_attn, source_attn = dispatch(route_attn, EXP_ATT, CAP_ATT)
    rank_query = jnp.dot(hidden_one, left_query, precision=HIGHEST)
    rank_kv = jnp.dot(hidden_one, left_kv, precision=HIGHEST)
    kv_raw = jnp.einsum('td,sdw->stw', hidden_one, kv_weight, precision=HIGHEST) + jnp.einsum('tr,rsw->stw', rank_kv, right_kv, precision=HIGHEST)
    keys = low(rotate(low_back(kv_raw[0]).reshape(count, KV_HEADS, HEAD_DIM), cosine, sine))
    values = low(low_back(kv_raw[1])).reshape(count, KV_HEADS, HEAD_DIM)
    hidden_pad = jnp.concatenate([hidden_one, jnp.zeros((1, width), hidden_one.dtype)], axis=0)
    query_buf = jnp.einsum('ecd,edw->ecw', hidden_pad[source_attn // TOPK].reshape(EXP_ATT, CAP_ATT, width), query_weight, precision=HIGHEST)
    query_width = query_buf.shape[2]
    query_raw = query_buf.reshape(EXP_ATT * CAP_ATT, query_width)[target_attn] + jnp.repeat(jnp.dot(rank_query, right_query, precision=HIGHEST), TOPK, axis=0)
    queries = low(rotate(low_back(query_raw).reshape(count, TOPK, KV_HEADS, HEAD_DIM), cosine, sine))
    scores = low_back(jnp.einsum('tkhd,jhd->hktj', queries, keys, precision=HIGHEST) * HEAD_DIM ** (-0.5))
    place = jnp.arange(count)
    allowed = (place[None, :] <= place[:, None]) & (place[None, :] < length)
    probability = low(jax.nn.softmax(jnp.where(allowed, scores, -1e+30), axis=-1))
    attended = low(low_back(jnp.einsum('hktj,jhd->tkhd', probability, values, precision=HIGHEST))).reshape(count * TOPK, query_width)
    attended_pad = jnp.concatenate([attended, jnp.zeros((1, query_width), attended.dtype)], axis=0)
    out_buf = low_back(jnp.einsum('ecw,edw->ecd', attended_pad[source_attn].reshape(EXP_ATT, CAP_ATT, query_width), out_weight, precision=HIGHEST))
    out_slots = out_buf.reshape(EXP_ATT * CAP_ATT, width)[target_attn].reshape(count, TOPK, width)
    weighted = attended.reshape(count, TOPK, query_width) * gates_attn[:, :, None]
    low_out = jnp.einsum('tkw,rw->tr', weighted, right_out, precision=HIGHEST)
    middle = x_rows + lax.optimization_barrier(jnp.sum(out_slots * gates_attn[:, :, None], axis=1)) + jnp.dot(low_out, left_out.T, precision=HIGHEST)
    scale_two = lax.rsqrt(lax.optimization_barrier(jnp.mean(middle * middle, axis=1, keepdims=True)) + EPSILON)
    hidden_two = low(middle * scale_two * norm_two)
    chosen_ffn = jnp.take_along_axis(jnp.dot(hidden_two, router_ffn, precision=HIGHEST), route_ffn, axis=1)
    gates_ffn = jax.nn.softmax(chosen_ffn, axis=1)
    target_ffn, source_ffn = dispatch(route_ffn, EXP_FF, CAP_FF)
    rows_ffn = source_ffn // TOPK
    rank_inner = jnp.dot(hidden_two, left_inner, precision=HIGHEST)
    inner_adapt = jnp.einsum('tr,rsf->tsf', rank_inner, right_inner, precision=HIGHEST)
    inner_pad = jnp.concatenate([inner_adapt, jnp.zeros((1,) + inner_adapt.shape[1:], inner_adapt.dtype)], axis=0)
    two_pad = jnp.concatenate([hidden_two, jnp.zeros((1, width), hidden_two.dtype)], axis=0)
    gate_up = jnp.einsum('ecd,edsf->ecsf', two_pad[rows_ffn].reshape(EXP_FF, CAP_FF, width), inner_weight, precision=HIGHEST)
    gate_up = low_back(gate_up + inner_pad[rows_ffn].reshape(EXP_FF, CAP_FF, 2, FF))
    mixed = low(jax.nn.silu(gate_up[:, :, 0]) * gate_up[:, :, 1])
    down_buf = low_back(jnp.einsum('ecf,edf->ecd', mixed, down_weight, precision=HIGHEST))
    down_slots = down_buf.reshape(EXP_FF * CAP_FF, width)[target_ffn].reshape(count, TOPK, width)
    mixed_slots = mixed.reshape(EXP_FF * CAP_FF, FF)[target_ffn].reshape(count, TOPK, FF)
    low_down = jnp.einsum('tkf,rf->tr', mixed_slots * gates_ffn[:, :, None], right_down, precision=HIGHEST)
    branch_ffn = lax.optimization_barrier(jnp.sum(down_slots * gates_ffn[:, :, None], axis=1)) + jnp.dot(low_down, left_down.T, precision=HIGHEST)
    keep_rows = (place < length).astype(x_rows.dtype)
    return (middle + branch_ffn) * keep_rows[:, None]

def reference(inputs, cotangent, lengths, adapter_pick, attn_route, ffn_route, norm_one, norm_two, router_attn, router_ffn, kv_weight, query_weight, out_weight, inner_weight, down_weight, query_left, query_right, kv_left, kv_right, out_left, out_right, inner_left, inner_right, down_left, down_right):
    weights = (norm_one.astype(jnp.float32), norm_two.astype(jnp.float32), router_attn.astype(jnp.float32), router_ffn.astype(jnp.float32), kv_weight.astype(jnp.float32), query_weight.astype(jnp.float32), out_weight.astype(jnp.float32), inner_weight.astype(jnp.float32), down_weight.astype(jnp.float32))
    adapters = (query_left.astype(jnp.float32), query_right.astype(jnp.float32), kv_left.astype(jnp.float32), kv_right.astype(jnp.float32), out_left.astype(jnp.float32), out_right.astype(jnp.float32), inner_left.astype(jnp.float32), inner_right.astype(jnp.float32), down_left.astype(jnp.float32), down_right.astype(jnp.float32))
    groups = inputs.shape[0] // TOK
    width = inputs.shape[1]
    sequence_items = (inputs.reshape(groups, TOK, width), cotangent.reshape(groups, TOK, width), lengths, adapter_pick, attn_route.reshape(groups, TOK, TOPK), ffn_route.reshape(groups, TOK, TOPK))

    def one_group(totals, items):
        x_rows, cot_rows, length, pick, route_attn, route_ffn = items
        picked = tuple((table[pick] for table in adapters))

        def forward(x_in, chosen):
            return layer(x_in, length, route_attn, route_ffn, weights, chosen)
        result, pullback = jax.vjp(forward, x_rows.astype(jnp.float32), picked)
        grad_x, grad_picked = pullback(cot_rows.astype(jnp.float32))
        updated = tuple((total.at[pick].add(grad) for total, grad in zip(totals, grad_picked)))
        return (updated, (result.astype(jnp.bfloat16), grad_x))
    start_totals = tuple((jnp.zeros_like(table) for table in adapters))
    totals, (outputs, grad_rows) = lax.scan(one_group, start_totals, sequence_items)
    return (outputs.reshape(groups * TOK, width), grad_rows.reshape(groups * TOK, width), totals[0], totals[1], totals[2], totals[3], totals[4], totals[5], totals[6], totals[7], totals[8], totals[9])
```

```python
import jax
import jax.numpy as jnp
from jax import lax
from jax.sharding import PartitionSpec as P

HEAD_DIM = 128
EXP_ATT = 8
EXP_FF = 4
TOPK = 2
ADAPT = 8
RANK = 16
CAP_ATT = 80
CAP_FF = 160
EPSILON = 1e-06
ROPE_BASE = 10000.0
HIGHEST = lax.Precision.HIGHEST
F32 = jnp.float32
BF16 = jnp.bfloat16


def mm(spec, a, b):
    return jnp.einsum(spec, a, b, preferred_element_type=F32)


def exact(spec, a, b):
    return jnp.einsum(spec, a, b, precision=HIGHEST, preferred_element_type=F32)


def tables(count, head_width):
    position = jnp.arange(count).astype(F32)
    frequency = ROPE_BASE ** (-jnp.arange(head_width // 2).astype(F32) * 2.0 / head_width)
    angle = position[:, None] * frequency[None, :]
    return (jnp.cos(angle), jnp.sin(angle))


def rotate(values, cosine, sine):
    half = values.shape[-1] // 2
    first = values[..., :half]
    second = values[..., half:]
    return jnp.concatenate(
        [first * cosine - second * sine, second * cosine + first * sine], axis=-1
    )


def slot_rows(route, experts, capacity):
    count = route.shape[0]
    chosen = (route[:, :, None] == jnp.arange(experts, dtype=jnp.int32)).astype(BF16)
    per_token = jnp.sum(chosen, axis=1)
    place = jnp.arange(count)
    before = (place[None, :] < place[:, None]).astype(BF16)
    earlier = mm("tu,ue->te", before, per_token)
    inside = jnp.stack([jnp.zeros_like(chosen[:, 0]), chosen[:, 0]], axis=1).astype(F32)
    position = jnp.sum((earlier[:, None, :] + inside) * chosen.astype(F32), axis=2)
    return route * capacity + position.astype(jnp.int32)


def xor_chunks(array, axis, parts, index):
    shape = array.shape
    size = shape[axis] // parts
    step = 1
    while step < parts:
        view = array.reshape(
            shape[:axis] + (parts // (2 * step), 2, step * size) + shape[axis + 1 :]
        )
        first = lax.index_in_dim(view, 0, axis + 1, keepdims=True)
        second = lax.index_in_dim(view, 1, axis + 1, keepdims=True)
        flipped = jnp.concatenate([second, first], axis=axis + 1)
        array = jnp.where((index // step) % 2 == 1, flipped, view).reshape(shape)
        step *= 2
    return array


def chosen_of(logits, route, experts):
    onehot = (route[:, :, None] == jnp.arange(experts, dtype=jnp.int32)).astype(F32)
    return jnp.sum(onehot * logits[:, None, :], axis=2)


def router_back(gates, grad_gates, route, experts):
    centred = gates * (grad_gates - jnp.sum(gates * grad_gates, axis=1, keepdims=True))
    onehot = (route[:, :, None] == jnp.arange(experts, dtype=jnp.int32)).astype(F32)
    return jnp.sum(centred[:, :, None] * onehot, axis=1)


def on_device(
    inputs,
    cotangent,
    lengths,
    adapter_pick,
    attn_route,
    ffn_route,
    norm_one,
    norm_two,
    router_attn,
    router_ffn,
    kv_weight,
    query_weight,
    out_weight,
    inner_weight,
    down_weight,
    query_left,
    query_right,
    kv_left,
    kv_right,
    out_left,
    out_right,
    inner_left,
    inner_right,
    down_left,
    down_right,
):
    count, slice_width = inputs.shape
    width = router_attn.shape[0]
    rows_axis = lax.axis_size("row")
    replicas = rows_axis // EXP_FF
    row = lax.axis_index("row")
    col = lax.axis_index("col")
    expert = row // replicas
    depth = inner_weight.shape[1]
    units = inner_weight.shape[3]
    length = lengths[0]
    adapter = adapter_pick[0]
    position = jnp.arange(count)
    valid = (position < length).astype(F32)
    cosine, sine = tables(count, HEAD_DIM)
    scaling = HEAD_DIM ** (-0.5)

    def swap(value, offset):
        return lax.ppermute(value, "row", [(i, i ^ offset) for i in range(rows_axis)])

    def features(part):
        return lax.all_gather(part, "col", axis=1, tiled=True)

    def partials(part):
        return lax.psum_scatter(
            part.astype(BF16), "col", scatter_dimension=1, tiled=True
        ).astype(F32)

    def own_columns(table):
        return lax.dynamic_slice_in_dim(table, col * slice_width, slice_width, 0)

    kv_full = lax.all_gather(kv_weight, "row", axis=1, tiled=True)
    query_full = lax.all_gather(query_weight, "row", axis=1, tiled=True)
    out_full = lax.all_gather(out_weight, "row", axis=1, tiled=True)

    near = []
    for j in range(EXP_FF):
        which = expert ^ j
        inner_own = lax.dynamic_index_in_dim(inner_weight, which, 0, keepdims=False)
        down_own = lax.dynamic_index_in_dim(down_weight, which, 0, keepdims=False)
        piece = jnp.concatenate([inner_own[:, 0], inner_own[:, 1], down_own], axis=1)
        near.append(swap(piece, j * replicas) if j else piece)
    chunks = []
    for j in range(EXP_FF):
        for i in range(replicas):
            chunks.append(swap(near[j], i) if i else near[j])
    expert_block = jnp.concatenate(chunks, axis=0)
    gate_up_block = expert_block[:, : 2 * units]
    down_block = expert_block[:, 2 * units :]

    picks = lax.all_gather(adapter_pick, "row", axis=0, tiled=True)
    pick_onehot = (picks[:, None] == jnp.arange(ADAPT, dtype=jnp.int32)[None, :]).astype(BF16)
    lefts_own = jnp.stack(
        [query_left, kv_left, out_left, inner_left, down_left], axis=1
    ).swapaxes(2, 3)
    lefts_sent = mm(
        "ga,ax->gx", pick_onehot, lefts_own.reshape(ADAPT, 5 * RANK * depth)
    ).astype(BF16)
    lefts = lax.all_to_all(
        lefts_sent.reshape(rows_axis, 5 * RANK, depth), "row", 0, 0, tiled=False
    )
    lefts = lefts.swapaxes(0, 1).reshape(5, RANK, width)
    left_query, left_kv, left_out, left_inner, left_down = (lefts[i] for i in range(5))
    right_query = query_right[adapter].astype(F32)
    right_kv = kv_right[adapter].astype(F32)
    right_out = out_right[adapter].astype(F32)
    right_inner_all = inner_right.reshape(ADAPT * RANK, 2 * units)
    right_down_all = down_right.reshape(ADAPT * RANK, units)
    own_adapter = (jnp.arange(ADAPT, dtype=jnp.int32) == adapter).astype(F32)

    def spread(low):
        return (own_adapter[None, :, None] * low[:, None, :]).reshape(count, ADAPT * RANK)

    def unspread(high):
        return jnp.sum(
            own_adapter[None, :, None] * high.reshape(count, ADAPT, RANK), axis=1
        )

    slots_attn = slot_rows(attn_route, EXP_ATT, CAP_ATT)
    slots_ffn = slot_rows(ffn_route, EXP_FF, CAP_FF)
    rows_attn = jnp.arange(EXP_ATT * CAP_ATT, dtype=jnp.int32)
    pick_attn = [
        (rows_attn[:, None] == slots_attn[None, :, k]).astype(BF16) for k in range(TOPK)
    ]
    pick_attn_any = pick_attn[0] + pick_attn[1]
    pick_attn_both = jnp.concatenate(pick_attn, axis=1)
    order = (expert ^ jnp.arange(EXP_FF, dtype=jnp.int32))[:, None] * CAP_FF
    rows_ffn = (order + jnp.arange(CAP_FF, dtype=jnp.int32)[None, :]).reshape(EXP_FF * CAP_FF)
    pick_ffn = [(rows_ffn[:, None] == slots_ffn[None, :, k]).astype(BF16) for k in range(TOPK)]
    pick_ffn_any = pick_ffn[0] + pick_ffn[1]

    def trade(rows):
        blocks = rows.reshape(EXP_FF, CAP_FF, rows.shape[1])
        return jnp.concatenate(
            [blocks[j] if j == 0 else swap(blocks[j], j * replicas) for j in range(EXP_FF)]
        )

    masked_cot = cotangent * valid.astype(BF16)[:, None]
    cot_full = features(masked_cot)
    grad_low_down = mm("td,rd->tr", cot_full, left_down)
    cot_rows = trade(
        mm(
            "ct,td->cd",
            pick_ffn_any,
            jnp.concatenate([cot_full, spread(grad_low_down).astype(BF16)], axis=1),
        ).astype(BF16)
    )

    x_full = features(inputs)
    x_wide = x_full.astype(F32)
    scale_one = lax.rsqrt(jnp.mean(x_wide * x_wide, axis=1, keepdims=True) + EPSILON)
    hidden_one = (x_wide * scale_one * norm_one).astype(BF16)
    gates_attn = jax.nn.softmax(
        chosen_of(mm("td,de->te", hidden_one, router_attn), attn_route, EXP_ATT), axis=1
    )
    rank_query = mm("td,rd->tr", hidden_one, left_query)
    rank_kv = mm("td,rd->tr", hidden_one, left_kv)
    kv_raw = mm("td,sdw->stw", hidden_one, kv_full) + mm(
        "tr,rsw->stw", rank_kv.astype(BF16), right_kv.astype(BF16)
    )
    query_width = kv_raw.shape[2]
    heads = query_width // HEAD_DIM
    keys = rotate(
        kv_raw[0].reshape(count, heads, HEAD_DIM), cosine[:, None], sine[:, None]
    ).astype(BF16)
    values = kv_raw[1].reshape(count, heads, HEAD_DIM).astype(BF16)
    small = jnp.concatenate([rank_query, gates_attn, cosine, sine], axis=1)
    small_rows = exact("ct,tx->cx", pick_attn_any.astype(F32), small)
    rank_query_rows = small_rows[:, :RANK]
    gate_rows = exact("ct,tx->cx", pick_attn[0].astype(F32), gates_attn[:, :1]) + exact(
        "ct,tx->cx", pick_attn[1].astype(F32), gates_attn[:, 1:]
    )
    half = HEAD_DIM // 2
    cosine_rows = small_rows[:, RANK + TOPK : RANK + TOPK + half]
    sine_rows = small_rows[:, RANK + TOPK + half :]
    hidden_rows = mm("ct,td->cd", pick_attn_any, hidden_one).astype(BF16)
    query_rows = mm(
        "ecd,edw->ecw", hidden_rows.reshape(EXP_ATT, CAP_ATT, width), query_full
    ).reshape(EXP_ATT * CAP_ATT, query_width) + mm(
        "cr,rw->cw", rank_query_rows.astype(BF16), right_query.astype(BF16)
    )
    query_rows = (
        rotate(
            query_rows.reshape(EXP_ATT * CAP_ATT, heads, HEAD_DIM),
            cosine_rows[:, None],
            sine_rows[:, None],
        )
        .astype(BF16)
        .reshape(EXP_ATT * CAP_ATT, query_width)
    )
    queries = (
        mm("cx,cw->xw", pick_attn_both, query_rows)
        .astype(BF16)
        .reshape(TOPK, count, heads, HEAD_DIM)
    )
    allowed = (position[None, :] <= position[:, None]) & (position[None, :] < length)
    scores = mm("kbhd,jhd->hkbj", queries, keys) * scaling
    scores = jnp.where(allowed[None, None], scores, -1e30)
    exponent = jnp.exp(scores - jnp.max(scores, axis=-1, keepdims=True))
    probability = exponent / jnp.sum(exponent, axis=-1, keepdims=True)
    probs = probability.astype(BF16)
    attended = mm("hkbj,jhd->kbhd", probs, values).astype(BF16).reshape(TOPK * count, query_width)
    attended_rows = mm("cx,xw->cw", pick_attn_both, attended).astype(BF16)
    out_rows = mm(
        "ecw,edw->ecd", attended_rows.reshape(EXP_ATT, CAP_ATT, query_width), out_full
    ).reshape(EXP_ATT * CAP_ATT, width)
    low_rows = mm("cw,rw->cr", attended_rows, right_out.astype(BF16))
    out_ext = (jnp.concatenate([out_rows, low_rows], axis=1) * gate_rows).astype(BF16)
    combined = mm("ct,cd->td", pick_attn_any, out_ext)
    low_out_part = combined[:, width:]
    branch_attn = combined[:, :width] + mm("tr,rd->td", low_out_part.astype(BF16), left_out)
    x_local = inputs.astype(F32)
    middle = x_local + partials(branch_attn)
    square_sum, low_out_full = lax.psum((jnp.sum(middle * middle, axis=1), low_out_part), "col")
    scale_two = lax.rsqrt(square_sum[:, None] / width + EPSILON)
    hidden_two = features((middle * scale_two * own_columns(norm_two)).astype(BF16))

    gates_ffn = jax.nn.softmax(
        chosen_of(mm("td,de->te", hidden_two, router_ffn), ffn_route, EXP_FF), axis=1
    )
    rank_inner = mm("td,rd->tr", hidden_two, left_inner)
    hidden_ext = jnp.concatenate([hidden_two, spread(rank_inner).astype(BF16)], axis=1)
    hidden_out = mm("ct,td->cd", pick_ffn_any, hidden_ext).astype(BF16)
    gate_high = gates_ffn.astype(BF16)
    gate_low = (gates_ffn - gate_high.astype(F32)).astype(BF16)
    gate_out = sum(
        mm("ct,tx->cx", pick_ffn[k], jnp.stack([gate_high[:, k], gate_low[:, k]], axis=1))
        for k in range(TOPK)
    )
    gate_out = jnp.pad(gate_out, ((0, 0), (0, 126))).astype(BF16)
    hidden_in = trade(jnp.concatenate([hidden_out, gate_out], axis=1))
    gate_in = (
        hidden_in[:, width + 128].astype(F32) + hidden_in[:, width + 129].astype(F32)
    )[:, None]
    hidden_in_ext = hidden_in[:, width : width + 128]
    hidden_in = xor_chunks(hidden_in[:, :width], 1, rows_axis, row)
    cot_in_ext = cot_rows[:, width:]
    cot_in = xor_chunks(cot_rows[:, :width], 1, rows_axis, row)
    grad_mixed = mm("cd,df->cf", cot_in, down_block) + mm("cr,rf->cf", cot_in_ext, right_down_all)
    gate_up = mm("cd,df->cf", hidden_in, gate_up_block) + mm(
        "cr,rf->cf", hidden_in_ext, right_inner_all
    )
    gate_part = gate_up[:, :units]
    up_part = gate_up[:, units:]
    sig = jax.nn.sigmoid(gate_part)
    mixed = (gate_part * sig * up_part).astype(BF16)
    gate_grad_rows = jnp.sum(mixed.astype(F32) * grad_mixed, axis=1, keepdims=True)
    grad_mixed = grad_mixed * gate_in
    grad_gate_up = jnp.concatenate(
        [
            grad_mixed * up_part * sig * (1.0 + gate_part * (1.0 - sig)),
            grad_mixed * gate_part * sig,
        ],
        axis=1,
    ).astype(BF16)
    grad_rows = xor_chunks(
        mm("cf,df->cd", grad_gate_up, gate_up_block).astype(BF16), 1, rows_axis, row
    )
    grad_rank_rows = mm("cf,rf->cr", grad_gate_up, right_inner_all).astype(BF16)
    gg_high = gate_grad_rows.astype(BF16)
    gg_low = (gate_grad_rows - gg_high.astype(F32)).astype(BF16)
    grad_msg = jnp.concatenate(
        [grad_rows, grad_rank_rows, jnp.pad(jnp.concatenate([gg_high, gg_low], 1), ((0, 0), (0, 126)))],
        axis=1,
    )
    grad_back = trade(grad_msg)
    down_rows = xor_chunks(
        (mm("cf,df->cd", mixed, down_block) * gate_in).astype(BF16), 1, rows_axis, row
    )
    down_low_rows = (mm("cf,rf->cr", mixed, right_down_all) * gate_in).astype(BF16)
    down_back = trade(jnp.concatenate([down_rows, down_low_rows], axis=1))
    grad_right_inner = mm("cr,cf->rf", hidden_in_ext, grad_gate_up)
    grad_right_down = mm("cr,cf->rf", (cot_in_ext.astype(F32) * gate_in).astype(BF16), mixed)
    ffn_rights = lax.psum(
        jnp.concatenate([grad_right_inner, grad_right_down], axis=1).astype(BF16), "row"
    ).astype(F32)

    grad_comb = mm("ct,cd->td", pick_ffn_any, grad_back[:, : width + 128])
    gg_back = grad_back[:, width + 128 : width + 130]
    grad_gates_part = jnp.stack(
        [jnp.sum(mm("ct,cx->tx", pick_ffn[k], gg_back), axis=1) for k in range(TOPK)], axis=1
    )
    grad_rank_inner = unspread(grad_comb[:, width:])
    grad_two_part = grad_comb[:, :width] + mm(
        "tr,rd->td", grad_rank_inner.astype(BF16), left_inner
    )
    down_comb = mm("ct,cd->td", pick_ffn_any, down_back)
    low_down_part = unspread(down_comb[:, width:])
    branch_ffn = down_comb[:, :width] + mm("tr,rd->td", low_down_part.astype(BF16), left_down)
    (grad_gates_ffn,) = lax.psum((grad_gates_part,), "col")
    logits_ffn_grad = router_back(gates_ffn, grad_gates_ffn, ffn_route, EXP_FF)
    grad_two = partials(grad_two_part) + exact(
        "te,de->td", logits_ffn_grad, own_columns(router_ffn).astype(F32)
    )
    scaled_two = grad_two * own_columns(norm_two)
    inner_sum, rank_inner_grad_full, low_down_full = lax.psum(
        (jnp.sum(scaled_two * middle, axis=1), grad_rank_inner, low_down_part), "col"
    )
    grad_middle = (
        masked_cot.astype(F32)
        + scale_two * scaled_two
        - middle * scale_two**3 * inner_sum[:, None] / width
    )
    output = ((middle + partials(branch_ffn)) * valid[:, None]).astype(BF16)

    grad_full = features(grad_middle.astype(BF16))
    grad_low_out = mm("td,rd->tr", grad_full, left_out)
    grad_middle_rows = mm(
        "ct,td->cd",
        pick_attn_any,
        jnp.concatenate([grad_full, grad_low_out.astype(BF16)], axis=1),
    ).astype(BF16)
    grad_att_rows = mm(
        "ecd,edw->ecw",
        grad_middle_rows[:, :width].reshape(EXP_ATT, CAP_ATT, width),
        out_full,
    ).reshape(EXP_ATT * CAP_ATT, query_width) + mm(
        "cr,rw->cw", grad_middle_rows[:, width:], right_out.astype(BF16)
    )
    gg_attn_rows = jnp.sum(attended_rows.astype(F32) * grad_att_rows, axis=1, keepdims=True)
    grad_gates_attn_part = jnp.concatenate(
        [exact("ct,cx->tx", pick_attn[k].astype(F32), gg_attn_rows) for k in range(TOPK)], axis=1
    )
    grad_att_rows = (grad_att_rows * gate_rows).astype(BF16)
    grad_attended = (
        mm("cx,cw->xw", pick_attn_both, grad_att_rows)
        .astype(BF16)
        .reshape(TOPK, count, heads, HEAD_DIM)
    )
    gated_low = (gates_attn.T[:, :, None] * grad_low_out[None]).reshape(TOPK * count, RANK)
    grad_right_out = mm("xr,xw->rw", gated_low.astype(BF16), attended)
    grad_prob = mm("kbhd,jhd->hkbj", grad_attended, values)
    centre = jnp.sum(probability * grad_prob, axis=-1, keepdims=True)
    grad_scores = (probability * (grad_prob - centre)).astype(BF16)
    grad_queries = mm("hkbj,jhd->kbhd", grad_scores, keys) * scaling
    grad_keys = mm("hkbj,kbhd->jhd", grad_scores, queries) * scaling
    grad_values = mm("hkbj,kbhd->jhd", probs, grad_attended)
    grad_query_raw = (
        rotate(grad_queries, cosine[None, :, None], -sine[None, :, None])
        .astype(BF16)
        .reshape(TOPK * count, query_width)
    )
    grad_key_raw = rotate(grad_keys, cosine[:, None], -sine[:, None])
    grad_kv = jnp.stack([grad_key_raw, grad_values]).astype(BF16).reshape(2, count, query_width)
    grad_query_rows = mm("cx,xw->cw", pick_attn_both, grad_query_raw).astype(BF16)
    grad_one_rows = (
        mm("ecw,edw->ecd", grad_query_rows.reshape(EXP_ATT, CAP_ATT, query_width), query_full)
        .astype(BF16)
        .reshape(EXP_ATT * CAP_ATT, width)
    )
    grad_query_sum = jnp.sum(
        grad_query_raw.astype(F32).reshape(TOPK, count, query_width), axis=0
    )
    grad_query_sum_low = grad_query_sum.astype(BF16)
    grad_rank_query = mm("tw,rw->tr", grad_query_sum_low, right_query.astype(BF16))
    grad_rank_kv = mm("stw,rsw->tr", grad_kv, right_kv.astype(BF16))
    grad_one_part = (
        mm("ct,cd->td", pick_attn_any, grad_one_rows)
        + mm("stw,sdw->td", grad_kv, kv_full)
        + mm(
            "tr,rd->td",
            jnp.concatenate([grad_rank_query, grad_rank_kv], axis=1).astype(BF16),
            jnp.concatenate([left_query, left_kv], axis=0),
        )
    )
    grad_right_query = mm("tr,tw->rw", rank_query.astype(BF16), grad_query_sum_low)
    grad_right_kv = mm("tr,stw->rsw", rank_kv.astype(BF16), grad_kv)
    grad_gates_attn, rank_query_grad_full, rank_kv_grad_full = lax.psum(
        (grad_gates_attn_part, grad_rank_query, grad_rank_kv), "col"
    )
    logits_attn_grad = router_back(gates_attn, grad_gates_attn, attn_route, EXP_ATT)
    grad_one = partials(grad_one_part) + exact(
        "te,de->td", logits_attn_grad, own_columns(router_attn).astype(F32)
    )
    scaled_one = grad_one * own_columns(norm_one)
    outer_sum = lax.psum(jnp.sum(scaled_one * x_local, axis=1), "col")
    grad_inputs = (
        grad_middle
        + scale_one * scaled_one
        - x_local * scale_one**3 * outer_sum[:, None] / width
    )

    hiddens = (hidden_one, hidden_one, grad_full, hidden_two, cot_full)
    lows = (
        rank_query_grad_full,
        rank_kv_grad_full,
        low_out_full,
        rank_inner_grad_full,
        low_down_full,
    )
    left_parts = jnp.concatenate(
        [mm("tr,td->rd", low.astype(BF16), hidden) for low, hidden in zip(lows, hiddens)]
    ).astype(BF16)
    left_parts = lax.all_to_all(
        left_parts.reshape(5 * RANK, rows_axis, depth), "row", 1, 0, tiled=False
    )
    left_grads = mm("ga,gx->ax", pick_onehot, left_parts.reshape(rows_axis, 5 * RANK * depth))
    left_grads = left_grads.reshape(ADAPT, 5, RANK, depth).swapaxes(2, 3)
    right_parts = jnp.concatenate(
        [grad_right_query, grad_right_kv[:, 0], grad_right_kv[:, 1], grad_right_out], axis=1
    ).astype(BF16)
    right_all = lax.all_gather(right_parts, "row", axis=0)
    right_grads = mm(
        "ga,gx->ax", pick_onehot, right_all.reshape(rows_axis, RANK * 4 * query_width)
    ).reshape(ADAPT, RANK, 4, query_width)
    return (
        output,
        grad_inputs,
        left_grads[:, 0],
        right_grads[:, :, 0],
        left_grads[:, 1],
        right_grads[:, :, 1:3],
        left_grads[:, 2],
        right_grads[:, :, 3],
        left_grads[:, 3],
        ffn_rights[:, : 2 * units].reshape(ADAPT, RANK, 2, units),
        left_grads[:, 4],
        ffn_rights[:, 2 * units :].reshape(ADAPT, RANK, units),
    )


def solution(mesh):
    placed = (
        P("row", "col"),
        P("row", "col"),
        P("row"),
        P("row"),
        P("row", None),
        P("row", None),
        P(),
        P(),
        P(),
        P(),
        P(None, "row", "col"),
        P(None, "row", "col"),
        P(None, "row", "col"),
        P(None, "row", None, "col"),
        P(None, "row", "col"),
        P(None, "row", None),
        P(None, None, "col"),
        P(None, "row", None),
        P(None, None, None, "col"),
        P(None, "row", None),
        P(None, None, "col"),
        P(None, "row", None),
        P(None, None, None, "col"),
        P(None, "row", None),
        P(None, None, "col"),
    )
    return jax.shard_map(
        on_device,
        mesh=mesh,
        in_specs=placed,
        out_specs=(
            P("row", "col"),
            P("row", "col"),
            P(None, "row", None),
            P(None, None, "col"),
            P(None, "row", None),
            P(None, None, None, "col"),
            P(None, "row", None),
            P(None, None, "col"),
            P(None, "row", None),
            P(None, None, None, "col"),
            P(None, "row", None),
            P(None, None, "col"),
        ),
        check_vma=False,
    )
```

```python
import functools

import jax
import jax.numpy as jnp
from jax import lax
from jax.experimental import pallas as pl
from jax.experimental.pallas import tpu as pltpu
from jax.sharding import PartitionSpec as P

HEAD_DIM = 128
EXP_ATT = 8
EXP_FF = 4
TOPK = 2
ADAPT = 8
RANK = 16
CAP_ATT = 80
CAP_FF = 160
EPSILON = 1e-06
ROPE_BASE = 10000.0
HIGHEST = lax.Precision.HIGHEST
F32 = jnp.float32
BF16 = jnp.bfloat16
LANES = 128


def mm(spec, a, b):
    return jnp.einsum(spec, a, b, preferred_element_type=F32)


def exact(spec, a, b):
    return jnp.einsum(spec, a, b, precision=HIGHEST, preferred_element_type=F32)


def tables(count, head_width):
    position = jnp.arange(count).astype(F32)
    frequency = ROPE_BASE ** (-jnp.arange(head_width // 2).astype(F32) * 2.0 / head_width)
    angle = position[:, None] * frequency[None, :]
    return (jnp.cos(angle), jnp.sin(angle))


def rotate(values, cosine, sine):
    half = values.shape[-1] // 2
    first = values[..., :half]
    second = values[..., half:]
    return jnp.concatenate(
        [first * cosine - second * sine, second * cosine + first * sine], axis=-1
    )


def slot_rows(route, experts, capacity):
    count = route.shape[0]
    chosen = (route[:, :, None] == jnp.arange(experts, dtype=jnp.int32)).astype(BF16)
    per_token = jnp.sum(chosen, axis=1)
    place = jnp.arange(count)
    before = (place[None, :] < place[:, None]).astype(BF16)
    earlier = mm("tu,ue->te", before, per_token)
    inside = jnp.stack([jnp.zeros_like(chosen[:, 0]), chosen[:, 0]], axis=1).astype(F32)
    position = jnp.sum((earlier[:, None, :] + inside) * chosen.astype(F32), axis=2)
    return route * capacity + position.astype(jnp.int32)


def chosen_of(logits, route, experts):
    onehot = (route[:, :, None] == jnp.arange(experts, dtype=jnp.int32)).astype(F32)
    return jnp.sum(onehot * logits[:, None, :], axis=2)


def router_back(gates, grad_gates, route, experts):
    centred = gates * (grad_gates - jnp.sum(gates * grad_gates, axis=1, keepdims=True))
    onehot = (route[:, :, None] == jnp.arange(experts, dtype=jnp.int32)).astype(F32)
    return jnp.sum(centred[:, :, None] * onehot, axis=1)


def ffn_kernel(parts, depth, width, units, *refs):
    hids = refs[:EXP_FF]
    cots = refs[EXP_FF : 2 * EXP_FF]
    pieces = refs[2 * EXP_FF : 2 * EXP_FF + parts]
    rights = refs[2 * EXP_FF + parts]
    outs = refs[2 * EXP_FF + parts + 1 :]
    grads = outs[:EXP_FF]
    downs = outs[EXP_FF : 2 * EXP_FF]
    adapt = outs[2 * EXP_FF]
    hid, cot, block, act, product, sems = outs[2 * EXP_FF + 1 :]
    row = lax.axis_index("row")
    wide = width + LANES
    copies = []
    for j in range(EXP_FF):
        where = pl.ds(j * CAP_FF, CAP_FF)
        copies.append(pltpu.make_async_copy(hids[j], hid.at[where], sems.at[j]))
        copies.append(pltpu.make_async_copy(cots[j], cot.at[where], sems.at[EXP_FF + j]))
    copies.append(pltpu.make_async_copy(rights, block.at[pl.ds(width, LANES)], sems.at[2 * EXP_FF]))
    for m in range(parts):
        owner = jnp.bitwise_xor(row, m)
        where = pl.ds(pl.multiple_of(owner * depth, depth), depth)
        copies.append(pltpu.make_async_copy(pieces[m], block.at[where], sems.at[2 * EXP_FF + 1 + m]))
    for copy in copies:
        copy.start()
    for copy in copies:
        copy.wait()
    gate_scale = hid[:, wide : wide + 1].astype(F32) + hid[:, wide + 1 : wide + 2].astype(F32)
    product[...] = jnp.zeros_like(product)

    def forward(start, size):
        here = pl.ds(start, size)
        up_here = pl.ds(units + start, size)
        down_here = pl.ds(2 * units + start, size)
        gate = jnp.dot(hid[:, :wide], block[:, here], preferred_element_type=F32)
        up = jnp.dot(hid[:, :wide], block[:, up_here], preferred_element_type=F32)
        grad = jnp.dot(cot[...], block[:, down_here], preferred_element_type=F32)
        sig = 1.0 / (1.0 + jnp.exp(-gate))
        mixed = (gate * sig * up).astype(BF16)
        act[:, down_here] = mixed
        product[...] += jnp.sum(mixed.astype(F32) * grad, axis=1, keepdims=True)
        grad = grad * gate_scale
        act[:, here] = (grad * up * sig * (1.0 + gate * (1.0 - sig))).astype(BF16)
        act[:, up_here] = (grad * gate * sig).astype(BF16)

    step = 2 * LANES
    full = units // step

    @pl.loop(0, full)
    def _(i):
        forward(pl.multiple_of(i * step, step), step)

    if units % step:
        forward(full * step, units % step)

    def backward(start, size):
        here = pl.ds(start, size)
        result = lax.dot_general(
            act[:, : 2 * units], block[here, : 2 * units], (((1,), (1,)), ((), ())),
            preferred_element_type=F32,
        ).astype(BF16)
        for j in range(EXP_FF):
            grads[j][:, here] = result[j * CAP_FF : (j + 1) * CAP_FF]
        result = lax.dot_general(
            act[:, 2 * units :], block[here, 2 * units :], (((1,), (1,)), ((), ())),
            preferred_element_type=F32,
        )
        result = (result * gate_scale).astype(BF16)
        for j in range(EXP_FF):
            downs[j][:, here] = result[j * CAP_FF : (j + 1) * CAP_FF]

    full_rows = wide // step

    @pl.loop(0, full_rows)
    def _(i):
        backward(pl.multiple_of(i * step, step), step)

    if wide % step:
        backward(full_rows * step, wide % step)
    total = product[...]
    high = total.astype(BF16)
    low = (total - high.astype(F32)).astype(BF16)
    lane = lax.broadcasted_iota(jnp.int32, (EXP_FF * CAP_FF, LANES), 1)
    packed = jnp.where(lane == 0, high.astype(F32), jnp.where(lane == 1, low.astype(F32), 0.0)).astype(BF16)
    for j in range(EXP_FF):
        grads[j][:, wide:] = packed[j * CAP_FF : (j + 1) * CAP_FF]
    ext = hid[:, width:wide]
    low_ext = (cot[:, width:].astype(F32) * gate_scale).astype(BF16)
    adapt[:, : 2 * units] = lax.dot_general(
        ext, act[:, : 2 * units], (((0,), (0,)), ((), ())), preferred_element_type=F32
    ).astype(BF16)
    adapt[:, 2 * units :] = lax.dot_general(
        low_ext, act[:, 2 * units :], (((0,), (0,)), ((), ())), preferred_element_type=F32
    ).astype(BF16)

def feed_forward(hids, cots, pieces, rights):
    parts = len(pieces)
    depth, triple = pieces[0].shape
    units = triple // 3
    width = depth * parts
    rows = EXP_FF * CAP_FF
    hbm = pl.BlockSpec(memory_space=pl.ANY)
    vmem = pl.BlockSpec(memory_space=pltpu.VMEM)
    wide = width + LANES
    return pl.pallas_call(
        functools.partial(ffn_kernel, parts, depth, width, units),
        out_shape=[jax.ShapeDtypeStruct((CAP_FF, wide + LANES), BF16)] * EXP_FF
        + [jax.ShapeDtypeStruct((CAP_FF, wide), BF16)] * EXP_FF
        + [jax.ShapeDtypeStruct((LANES, triple), BF16)],
        in_specs=[hbm] * (2 * EXP_FF + parts + 1),
        out_specs=[vmem] * (2 * EXP_FF + 1),
        scratch_shapes=[
            pltpu.VMEM((rows, wide + LANES), BF16),
            pltpu.VMEM((rows, wide), BF16),
            pltpu.VMEM((wide, triple), BF16),
            pltpu.VMEM((rows, triple), BF16),
            pltpu.VMEM((rows, 1), F32),
            pltpu.SemaphoreType.DMA((2 * EXP_FF + 1 + parts,)),
        ],
        compiler_params=pltpu.CompilerParams(vmem_limit_bytes=56 * 2**20),
    )(*hids, *cots, *pieces, rights)


def on_device(
    inputs,
    cotangent,
    lengths,
    adapter_pick,
    attn_route,
    ffn_route,
    norm_one,
    norm_two,
    router_attn,
    router_ffn,
    kv_weight,
    query_weight,
    out_weight,
    inner_weight,
    down_weight,
    query_left,
    query_right,
    kv_left,
    kv_right,
    out_left,
    out_right,
    inner_left,
    inner_right,
    down_left,
    down_right,
):
    count, slice_width = inputs.shape
    width = router_attn.shape[0]
    rows_axis = lax.axis_size("row")
    replicas = rows_axis // EXP_FF
    row = lax.axis_index("row")
    col = lax.axis_index("col")
    expert = row // replicas
    depth = inner_weight.shape[1]
    units = inner_weight.shape[3]
    length = lengths[0]
    adapter = adapter_pick[0]
    position = jnp.arange(count)
    valid = (position < length).astype(F32)
    cosine, sine = tables(count, HEAD_DIM)
    scaling = HEAD_DIM ** (-0.5)

    def swap(value, offset):
        return lax.ppermute(value, "row", [(i, i ^ offset) for i in range(rows_axis)])

    def features(part):
        return lax.all_gather(part, "col", axis=1, tiled=True)

    def partials(part):
        return lax.psum_scatter(
            part.astype(BF16), "col", scatter_dimension=1, tiled=True
        ).astype(F32)

    def own_columns(table):
        return lax.dynamic_slice_in_dim(table, col * slice_width, slice_width, 0)

    kv_full = lax.all_gather(kv_weight, "row", axis=1, tiled=True)
    query_full = lax.all_gather(query_weight, "row", axis=1, tiled=True)
    out_full = lax.all_gather(out_weight, "row", axis=1, tiled=True)

    def later(value, *earlier):
        return lax.optimization_barrier((value, *earlier))[0]

    padding = -units % LANES

    def padded(value):
        return jnp.pad(value, ((0, 0), (0, padding))) if padding else value

    inner_later, down_later = later((inner_weight, down_weight), out_full)
    near = []
    for j in range(EXP_FF):
        which = expert ^ j
        inner_own = lax.dynamic_index_in_dim(inner_later, which, 0, keepdims=False)
        down_own = lax.dynamic_index_in_dim(down_later, which, 0, keepdims=False)
        piece = jnp.concatenate(
            [padded(inner_own[:, 0]), padded(inner_own[:, 1]), padded(down_own)], axis=1
        )
        near.append(swap(piece, j * replicas) if j else piece)
    chunks = []
    for j in range(EXP_FF):
        for i in range(replicas):
            chunks.append(swap(near[j], i) if i else near[j])

    picks = lax.all_gather(adapter_pick, "row", axis=0, tiled=True)
    pick_onehot = (picks[:, None] == jnp.arange(ADAPT, dtype=jnp.int32)[None, :]).astype(BF16)
    lefts_own = jnp.stack(
        [query_left, kv_left, out_left, inner_left, down_left], axis=1
    ).swapaxes(2, 3)
    lefts_sent = mm(
        "ga,ax->gx", pick_onehot, lefts_own.reshape(ADAPT, 5 * RANK * depth)
    ).astype(BF16)
    lefts = lax.all_to_all(
        lefts_sent.reshape(rows_axis, 5 * RANK, depth), "row", 0, 0, tiled=False
    )
    lefts = lefts.swapaxes(0, 1).reshape(5, RANK, width)
    left_query, left_kv, left_out, left_inner, left_down = (lefts[i] for i in range(5))
    right_query = query_right[adapter].astype(F32)
    right_kv = kv_right[adapter].astype(F32)
    right_out = out_right[adapter].astype(F32)
    right_inner_all = inner_right.reshape(ADAPT * RANK, 2, units)
    right_down_all = down_right.reshape(ADAPT * RANK, units)
    ffn_right = jnp.concatenate(
        [padded(right_inner_all[:, 0]), padded(right_inner_all[:, 1]), padded(right_down_all)],
        axis=1,
    )
    own_adapter = (jnp.arange(ADAPT, dtype=jnp.int32) == adapter).astype(F32)

    def spread(low):
        return (own_adapter[None, :, None] * low[:, None, :]).reshape(count, ADAPT * RANK)

    def unspread(high):
        return jnp.sum(
            own_adapter[None, :, None] * high.reshape(count, ADAPT, RANK), axis=1
        )

    slots_attn = slot_rows(attn_route, EXP_ATT, CAP_ATT)
    slots_ffn = slot_rows(ffn_route, EXP_FF, CAP_FF)
    rows_attn = jnp.arange(EXP_ATT * CAP_ATT, dtype=jnp.int32)
    pick_attn = [
        (rows_attn[:, None] == slots_attn[None, :, k]).astype(BF16) for k in range(TOPK)
    ]
    pick_attn_any = pick_attn[0] + pick_attn[1]
    pick_attn_both = jnp.concatenate(pick_attn, axis=1)
    order = (expert ^ jnp.arange(EXP_FF, dtype=jnp.int32))[:, None] * CAP_FF
    rows_ffn = (order + jnp.arange(CAP_FF, dtype=jnp.int32)[None, :]).reshape(EXP_FF * CAP_FF)
    pick_ffn = [(rows_ffn[:, None] == slots_ffn[None, :, k]).astype(BF16) for k in range(TOPK)]
    pick_ffn_any = pick_ffn[0] + pick_ffn[1]

    def blocks_of(rows):
        blocks = rows.reshape(EXP_FF, CAP_FF, rows.shape[1])
        return [blocks[j] for j in range(EXP_FF)]

    def trade(blocks):
        return [swap(block, j * replicas) if j else block for j, block in enumerate(blocks)]

    masked_cot = cotangent * valid.astype(BF16)[:, None]
    cot_full = features(masked_cot)
    grad_low_down = mm("td,rd->tr", cot_full, left_down)
    cot_ext = jnp.concatenate([cot_full, spread(grad_low_down).astype(BF16)], axis=1)
    cot_rows = trade(blocks_of(mm("ct,td->cd", pick_ffn_any, cot_ext).astype(BF16)))

    x_full = features(inputs)
    x_wide = x_full.astype(F32)
    scale_one = lax.rsqrt(jnp.mean(x_wide * x_wide, axis=1, keepdims=True) + EPSILON)
    hidden_one = (x_wide * scale_one * norm_one).astype(BF16)
    gates_attn = jax.nn.softmax(
        chosen_of(mm("td,de->te", hidden_one, router_attn), attn_route, EXP_ATT), axis=1
    )
    rank_query = mm("td,rd->tr", hidden_one, left_query)
    rank_kv = mm("td,rd->tr", hidden_one, left_kv)
    kv_raw = mm("td,sdw->stw", hidden_one, kv_full) + mm(
        "tr,rsw->stw", rank_kv.astype(BF16), right_kv.astype(BF16)
    )
    query_width = kv_raw.shape[2]
    heads = query_width // HEAD_DIM
    keys = rotate(
        kv_raw[0].reshape(count, heads, HEAD_DIM), cosine[:, None], sine[:, None]
    ).astype(BF16)
    values = kv_raw[1].reshape(count, heads, HEAD_DIM).astype(BF16)
    small = jnp.concatenate([rank_query, gates_attn, cosine, sine], axis=1)
    small_rows = exact("ct,tx->cx", pick_attn_any.astype(F32), small)
    rank_query_rows = small_rows[:, :RANK]
    gate_rows = exact("ct,tx->cx", pick_attn[0].astype(F32), gates_attn[:, :1]) + exact(
        "ct,tx->cx", pick_attn[1].astype(F32), gates_attn[:, 1:]
    )
    half = HEAD_DIM // 2
    cosine_rows = small_rows[:, RANK + TOPK : RANK + TOPK + half]
    sine_rows = small_rows[:, RANK + TOPK + half :]
    hidden_rows = mm("ct,td->cd", pick_attn_any, hidden_one).astype(BF16)
    query_rows = mm(
        "ecd,edw->ecw", hidden_rows.reshape(EXP_ATT, CAP_ATT, width), query_full
    ).reshape(EXP_ATT * CAP_ATT, query_width) + mm(
        "cr,rw->cw", rank_query_rows.astype(BF16), right_query.astype(BF16)
    )
    query_rows = (
        rotate(
            query_rows.reshape(EXP_ATT * CAP_ATT, heads, HEAD_DIM),
            cosine_rows[:, None],
            sine_rows[:, None],
        )
        .astype(BF16)
        .reshape(EXP_ATT * CAP_ATT, query_width)
    )
    queries = (
        mm("cx,cw->xw", pick_attn_both, query_rows)
        .astype(BF16)
        .reshape(TOPK, count, heads, HEAD_DIM)
    )
    allowed = (position[None, :] <= position[:, None]) & (position[None, :] < length)
    scores = mm("kbhd,jhd->hkbj", queries, keys) * scaling
    scores = jnp.where(allowed[None, None], scores, -1e30)
    exponent = jnp.exp(scores - jnp.max(scores, axis=-1, keepdims=True))
    probability = exponent / jnp.sum(exponent, axis=-1, keepdims=True)
    probs = probability.astype(BF16)
    attended = mm("hkbj,jhd->kbhd", probs, values).astype(BF16).reshape(TOPK * count, query_width)
    attended_rows = mm("cx,xw->cw", pick_attn_both, attended).astype(BF16)
    out_rows = mm(
        "ecw,edw->ecd", attended_rows.reshape(EXP_ATT, CAP_ATT, query_width), out_full
    ).reshape(EXP_ATT * CAP_ATT, width)
    low_rows = mm("cw,rw->cr", attended_rows, right_out.astype(BF16))
    out_ext = (jnp.concatenate([out_rows, low_rows], axis=1) * gate_rows).astype(BF16)
    combined = mm("ct,cd->td", pick_attn_any, out_ext)
    low_out_part = combined[:, width:]
    branch_attn = combined[:, :width] + mm("tr,rd->td", low_out_part.astype(BF16), left_out)
    x_local = inputs.astype(F32)
    middle = x_local + partials(branch_attn)
    square_sum, low_out_full = lax.psum((jnp.sum(middle * middle, axis=1), low_out_part), "col")
    scale_two = lax.rsqrt(square_sum[:, None] / width + EPSILON)
    hidden_two = features((middle * scale_two * own_columns(norm_two)).astype(BF16))

    gates_ffn = jax.nn.softmax(
        chosen_of(mm("td,de->te", hidden_two, router_ffn), ffn_route, EXP_FF), axis=1
    )
    rank_inner = mm("td,rd->tr", hidden_two, left_inner)
    hidden_ext = jnp.concatenate([hidden_two, spread(rank_inner).astype(BF16)], axis=1)
    hidden_out = mm("ct,td->cd", pick_ffn_any, hidden_ext).astype(BF16)
    gate_high = gates_ffn.astype(BF16)
    gate_low = (gates_ffn - gate_high.astype(F32)).astype(BF16)
    gate_out = sum(
        mm("ct,tx->cx", pick_ffn[k], jnp.stack([gate_high[:, k], gate_low[:, k]], axis=1))
        for k in range(TOPK)
    )
    gate_out = jnp.pad(gate_out, ((0, 0), (0, 126))).astype(BF16)
    hidden_in = trade(blocks_of(jnp.concatenate([hidden_out, gate_out], axis=1)))
    results = feed_forward(hidden_in, cot_rows, chunks, ffn_right)
    grad_back = jnp.concatenate(trade(results[:EXP_FF]))
    down_back = jnp.concatenate(trade(results[EXP_FF : 2 * EXP_FF]))
    ffn_rights = lax.optimization_barrier(lax.psum(results[2 * EXP_FF], "row")).astype(F32)
    ffn_rights = ffn_rights.reshape(ADAPT, RANK, 3, units + padding)[..., :units]

    grad_comb = mm("ct,cd->td", pick_ffn_any, grad_back[:, : width + 128])
    gg_back = grad_back[:, width + 128 : width + 130]
    grad_gates_part = jnp.stack(
        [jnp.sum(mm("ct,cx->tx", pick_ffn[k], gg_back), axis=1) for k in range(TOPK)], axis=1
    )
    grad_rank_inner = unspread(grad_comb[:, width:])
    grad_two_part = grad_comb[:, :width] + mm(
        "tr,rd->td", grad_rank_inner.astype(BF16), left_inner
    )
    down_comb = mm("ct,cd->td", pick_ffn_any, down_back)
    low_down_part = unspread(down_comb[:, width:])
    branch_ffn = down_comb[:, :width] + mm("tr,rd->td", low_down_part.astype(BF16), left_down)
    (grad_gates_ffn,) = lax.psum((grad_gates_part,), "col")
    logits_ffn_grad = router_back(gates_ffn, grad_gates_ffn, ffn_route, EXP_FF)
    grad_two = partials(grad_two_part) + exact(
        "te,de->td", logits_ffn_grad, own_columns(router_ffn).astype(F32)
    )
    scaled_two = grad_two * own_columns(norm_two)
    inner_sum, rank_inner_grad_full, low_down_full = lax.psum(
        (jnp.sum(scaled_two * middle, axis=1), grad_rank_inner, low_down_part), "col"
    )
    grad_middle = (
        masked_cot.astype(F32)
        + scale_two * scaled_two
        - middle * scale_two**3 * inner_sum[:, None] / width
    )
    output = ((middle + partials(branch_ffn)) * valid[:, None]).astype(BF16)

    grad_full = features(grad_middle.astype(BF16))
    grad_low_out = mm("td,rd->tr", grad_full, left_out)
    grad_middle_rows = mm(
        "ct,td->cd",
        pick_attn_any,
        jnp.concatenate([grad_full, grad_low_out.astype(BF16)], axis=1),
    ).astype(BF16)
    grad_att_rows = mm(
        "ecd,edw->ecw",
        grad_middle_rows[:, :width].reshape(EXP_ATT, CAP_ATT, width),
        out_full,
    ).reshape(EXP_ATT * CAP_ATT, query_width) + mm(
        "cr,rw->cw", grad_middle_rows[:, width:], right_out.astype(BF16)
    )
    gg_attn_rows = jnp.sum(attended_rows.astype(F32) * grad_att_rows, axis=1, keepdims=True)
    grad_gates_attn_part = jnp.concatenate(
        [exact("ct,cx->tx", pick_attn[k].astype(F32), gg_attn_rows) for k in range(TOPK)], axis=1
    )
    grad_att_rows = (grad_att_rows * gate_rows).astype(BF16)
    grad_attended = (
        mm("cx,cw->xw", pick_attn_both, grad_att_rows)
        .astype(BF16)
        .reshape(TOPK, count, heads, HEAD_DIM)
    )
    gated_low = (gates_attn.T[:, :, None] * grad_low_out[None]).reshape(TOPK * count, RANK)
    grad_right_out = mm("xr,xw->rw", gated_low.astype(BF16), attended)
    grad_prob = mm("kbhd,jhd->hkbj", grad_attended, values)
    centre = jnp.sum(probability * grad_prob, axis=-1, keepdims=True)
    grad_scores = (probability * (grad_prob - centre)).astype(BF16)
    grad_queries = mm("hkbj,jhd->kbhd", grad_scores, keys) * scaling
    grad_keys = mm("hkbj,kbhd->jhd", grad_scores, queries) * scaling
    grad_values = mm("hkbj,kbhd->jhd", probs, grad_attended)
    grad_query_raw = (
        rotate(grad_queries, cosine[None, :, None], -sine[None, :, None])
        .astype(BF16)
        .reshape(TOPK * count, query_width)
    )
    grad_key_raw = rotate(grad_keys, cosine[:, None], -sine[:, None])
    grad_kv = jnp.stack([grad_key_raw, grad_values]).astype(BF16).reshape(2, count, query_width)
    grad_query_rows = mm("cx,xw->cw", pick_attn_both, grad_query_raw).astype(BF16)
    grad_one_rows = (
        mm("ecw,edw->ecd", grad_query_rows.reshape(EXP_ATT, CAP_ATT, query_width), query_full)
        .astype(BF16)
        .reshape(EXP_ATT * CAP_ATT, width)
    )
    grad_query_sum = jnp.sum(
        grad_query_raw.astype(F32).reshape(TOPK, count, query_width), axis=0
    )
    grad_query_sum_low = grad_query_sum.astype(BF16)
    grad_rank_query = mm("tw,rw->tr", grad_query_sum_low, right_query.astype(BF16))
    grad_rank_kv = mm("stw,rsw->tr", grad_kv, right_kv.astype(BF16))
    grad_one_part = (
        mm("ct,cd->td", pick_attn_any, grad_one_rows)
        + mm("stw,sdw->td", grad_kv, kv_full)
        + mm(
            "tr,rd->td",
            jnp.concatenate([grad_rank_query, grad_rank_kv], axis=1).astype(BF16),
            jnp.concatenate([left_query, left_kv], axis=0),
        )
    )
    grad_right_query = mm("tr,tw->rw", rank_query.astype(BF16), grad_query_sum_low)
    grad_right_kv = mm("tr,stw->rsw", rank_kv.astype(BF16), grad_kv)
    grad_gates_attn, rank_query_grad_full, rank_kv_grad_full = lax.psum(
        (grad_gates_attn_part, grad_rank_query, grad_rank_kv), "col"
    )
    logits_attn_grad = router_back(gates_attn, grad_gates_attn, attn_route, EXP_ATT)
    grad_one = partials(grad_one_part) + exact(
        "te,de->td", logits_attn_grad, own_columns(router_attn).astype(F32)
    )
    scaled_one = grad_one * own_columns(norm_one)
    outer_sum = lax.psum(jnp.sum(scaled_one * x_local, axis=1), "col")
    grad_inputs = (
        grad_middle
        + scale_one * scaled_one
        - x_local * scale_one**3 * outer_sum[:, None] / width
    )

    hiddens = (hidden_one, hidden_one, grad_full, hidden_two, cot_full)
    lows = (
        rank_query_grad_full,
        rank_kv_grad_full,
        low_out_full,
        rank_inner_grad_full,
        low_down_full,
    )
    left_parts = jnp.concatenate(
        [mm("tr,td->rd", low.astype(BF16), hidden) for low, hidden in zip(lows, hiddens)]
    ).astype(BF16)
    left_parts = lax.all_to_all(
        left_parts.reshape(5 * RANK, rows_axis, depth), "row", 1, 0, tiled=False
    )
    left_grads = mm("ga,gx->ax", pick_onehot, left_parts.reshape(rows_axis, 5 * RANK * depth))
    left_grads = left_grads.reshape(ADAPT, 5, RANK, depth).swapaxes(2, 3)
    right_parts = jnp.concatenate(
        [grad_right_query, grad_right_kv[:, 0], grad_right_kv[:, 1], grad_right_out], axis=1
    ).astype(BF16)
    right_all = lax.all_gather(right_parts, "row", axis=0)
    right_grads = mm(
        "ga,gx->ax", pick_onehot, right_all.reshape(rows_axis, RANK * 4 * query_width)
    ).reshape(ADAPT, RANK, 4, query_width)
    return (
        output,
        grad_inputs,
        left_grads[:, 0],
        right_grads[:, :, 0],
        left_grads[:, 1],
        right_grads[:, :, 1:3],
        left_grads[:, 2],
        right_grads[:, :, 3],
        left_grads[:, 3],
        ffn_rights[:, :, :2],
        left_grads[:, 4],
        ffn_rights[:, :, 2],
    )


def solution(mesh):
    placed = (
        P("row", "col"),
        P("row", "col"),
        P("row"),
        P("row"),
        P("row", None),
        P("row", None),
        P(),
        P(),
        P(),
        P(),
        P(None, "row", "col"),
        P(None, "row", "col"),
        P(None, "row", "col"),
        P(None, "row", None, "col"),
        P(None, "row", "col"),
        P(None, "row", None),
        P(None, None, "col"),
        P(None, "row", None),
        P(None, None, None, "col"),
        P(None, "row", None),
        P(None, None, "col"),
        P(None, "row", None),
        P(None, None, None, "col"),
        P(None, "row", None),
        P(None, None, "col"),
    )
    return jax.shard_map(
        on_device,
        mesh=mesh,
        in_specs=placed,
        out_specs=(
            P("row", "col"),
            P("row", "col"),
            P(None, "row", None),
            P(None, None, "col"),
            P(None, "row", None),
            P(None, None, None, "col"),
            P(None, "row", None),
            P(None, None, "col"),
            P(None, "row", None),
            P(None, None, None, "col"),
            P(None, "row", None),
            P(None, None, "col"),
        ),
        check_vma=False,
    )
```

```python
import functools

import jax
import jax.numpy as jnp
from jax import lax
from jax.experimental import pallas as pl
from jax.experimental.pallas import tpu as pltpu
from jax.sharding import PartitionSpec as P

HEAD_DIM = 128
EXP_ATT = 8
EXP_FF = 4
TOPK = 2
ADAPT = 8
RANK = 16
CAP_ATT = 80
CAP_FF = 160
EPSILON = 1e-06
ROPE_BASE = 10000.0
HIGHEST = lax.Precision.HIGHEST
F32 = jnp.float32
BF16 = jnp.bfloat16
LANES = 128


def mm(spec, a, b):
    return jnp.einsum(spec, a, b, preferred_element_type=F32)


def exact(spec, a, b):
    return jnp.einsum(spec, a, b, precision=HIGHEST, preferred_element_type=F32)


def tables(count, head_width):
    position = jnp.arange(count).astype(F32)
    frequency = ROPE_BASE ** (-jnp.arange(head_width // 2).astype(F32) * 2.0 / head_width)
    angle = position[:, None] * frequency[None, :]
    return (jnp.cos(angle), jnp.sin(angle))


def rotate(values, cosine, sine):
    half = values.shape[-1] // 2
    first = values[..., :half]
    second = values[..., half:]
    return jnp.concatenate(
        [first * cosine - second * sine, second * cosine + first * sine], axis=-1
    )


def slot_rows(route, experts, capacity):
    count = route.shape[0]
    chosen = (route[:, :, None] == jnp.arange(experts, dtype=jnp.int32)).astype(BF16)
    per_token = jnp.sum(chosen, axis=1)
    place = jnp.arange(count)
    before = (place[None, :] < place[:, None]).astype(BF16)
    earlier = mm("tu,ue->te", before, per_token)
    inside = jnp.stack([jnp.zeros_like(chosen[:, 0]), chosen[:, 0]], axis=1).astype(F32)
    position = jnp.sum((earlier[:, None, :] + inside) * chosen.astype(F32), axis=2)
    return route * capacity + position.astype(jnp.int32)


def chosen_of(logits, route, experts):
    onehot = (route[:, :, None] == jnp.arange(experts, dtype=jnp.int32)).astype(F32)
    return jnp.sum(onehot * logits[:, None, :], axis=2)


def router_back(gates, grad_gates, route, experts):
    centred = gates * (grad_gates - jnp.sum(gates * grad_gates, axis=1, keepdims=True))
    onehot = (route[:, :, None] == jnp.arange(experts, dtype=jnp.int32)).astype(F32)
    return jnp.sum(centred[:, :, None] * onehot, axis=1)


def opposite(axis, offset):
    index = jnp.bitwise_xor(lax.axis_index(axis), offset)
    if axis == "row":
        return (index, lax.axis_index("col"))
    return (lax.axis_index("row"), index)


def greet(partners):
    barrier = pltpu.get_barrier_semaphore()
    for partner in partners:
        pl.semaphore_signal(
            barrier, inc=1, device_id=partner, device_id_type=pl.DeviceIdType.MESH
        )
    pl.semaphore_wait(barrier, len(partners))


def gather_kernel(parts, cols, counts, *refs):
    blocks = refs[: len(counts)]
    tokens = refs[len(counts) : len(counts) + 2]
    wholes = refs[len(counts) + 2 : 2 * len(counts) + 2]
    token_wholes = refs[2 * len(counts) + 2 : 2 * len(counts) + 4]
    send, recv, local = refs[2 * len(counts) + 4 :]
    row = lax.axis_index("row")
    col = lax.axis_index("col")
    depth = blocks[0].shape[1]
    wide = tokens[0].shape[1]
    partners = {offset: opposite("row", offset) for offset in (1, 2, 4)}
    greet(list(partners.values()) + [opposite("col", i) for i in range(1, cols)])
    chunks = [(a, i) for a, count in enumerate(counts) for i in range(count)]
    total = len(chunks)
    used = [0]
    started = []

    def place(chunk, offset):
        array, i = chunk
        owner = jnp.bitwise_xor(row, offset)
        return wholes[array].at[i, pl.ds(pl.multiple_of(owner * depth, depth), depth)]

    def push(source, chunk, target, offset):
        n = used[0]
        used[0] += 1
        copy = pltpu.make_async_remote_copy(
            src_ref=source,
            dst_ref=place(chunk, offset),
            send_sem=send.at[n],
            recv_sem=recv.at[n],
            device_id=partners[target],
            device_id_type=pl.DeviceIdType.MESH,
        )
        copy.start()
        started.append(copy)
        return copy

    copies = []
    for k in range(2):
        here = pl.ds(pl.multiple_of(col * wide, wide), wide)
        copy = pltpu.make_async_copy(tokens[k], token_wholes[k].at[:, here], local.at[k])
        copy.start()
        copies.append(copy)
        for i in range(1, cols):
            n = used[0]
            used[0] += 1
            copy = pltpu.make_async_remote_copy(
                src_ref=tokens[k],
                dst_ref=token_wholes[k].at[:, here],
                send_sem=send.at[n],
                recv_sem=recv.at[n],
                device_id=opposite("col", i),
                device_id_type=pl.DeviceIdType.MESH,
            )
            copy.start()
            started.append(copy)
    for a in range(len(counts)):
        where = pl.ds(pl.multiple_of(row * depth, depth), depth)
        copy = pltpu.make_async_copy(blocks[a], wholes[a].at[:, where], local.at[2 + a])
        copy.start()
        copies.append(copy)
    first = {}
    for number, chunk in enumerate(chunks):
        source = blocks[chunk[0]].at[chunk[1]]
        for target in (2, 4):
            first[number, target] = push(source, chunk, target, 0)
    for number, chunk in enumerate(chunks):
        push(blocks[chunk[0]].at[chunk[1]], chunk, 1, 0)
    relayed = {}
    for number, chunk in enumerate(chunks):
        first[number, 2].wait_recv()
        first[number, 4].wait_recv()
        if number % 2 == 0:
            relayed[number] = push(place(chunk, 2), chunk, 4, 2)
        else:
            relayed[number] = push(place(chunk, 4), chunk, 2, 4)
        for offset in (2, 4):
            push(place(chunk, offset), chunk, 1, offset)
    for number, chunk in enumerate(chunks):
        relayed[number].wait_recv()
        push(place(chunk, 6), chunk, 1, 6)
    waited = {id(copy) for copy in first.values()} | {id(copy) for copy in relayed.values()}
    for copy in started:
        if id(copy) not in waited:
            copy.wait_recv()
    for copy in started:
        copy.wait_send()
    for copy in copies:
        copy.wait()


def gather_all(blocks, tokens, parts, cols):
    counts = [block.shape[0] for block in blocks]
    hbm = pl.BlockSpec(memory_space=pl.ANY)
    remote = 7 * sum(counts) + 2 * (cols - 1)
    return pl.pallas_call(
        functools.partial(gather_kernel, parts, cols, counts),
        out_shape=[
            jax.ShapeDtypeStruct((b.shape[0], b.shape[1] * parts, b.shape[2]), b.dtype)
            for b in blocks
        ]
        + [jax.ShapeDtypeStruct((t.shape[0], t.shape[1] * cols), t.dtype) for t in tokens],
        in_specs=[hbm] * (len(blocks) + 2),
        out_specs=[hbm] * (len(blocks) + 2),
        scratch_shapes=[
            pltpu.SemaphoreType.DMA((remote,)),
            pltpu.SemaphoreType.DMA((remote,)),
            pltpu.SemaphoreType.DMA((2 + len(blocks),)),
        ],
        compiler_params=pltpu.CompilerParams(collective_id=1, has_side_effects=True),
    )(*blocks, *tokens)


def cot_kernel(cols, replicas, *refs):
    blocks, exts = refs[:EXP_FF], refs[EXP_FF : 2 * EXP_FF]
    wholes, ext_wholes = refs[2 * EXP_FF : 3 * EXP_FF], refs[3 * EXP_FF : 4 * EXP_FF]
    landed, send, recv, local = refs[4 * EXP_FF :]
    col = lax.axis_index("col")
    wide = blocks[0].shape[1]
    here = pl.ds(pl.multiple_of(col * wide, wide), wide)
    along = [opposite("col", i) for i in range(1, cols)]
    across = [opposite("row", j * replicas) for j in range(1, EXP_FF)]
    greet(along + across)
    copies = []

    def push(source, target, n, device):
        copy = pltpu.make_async_remote_copy(
            src_ref=source,
            dst_ref=target,
            send_sem=send.at[n],
            recv_sem=recv.at[n],
            device_id=device,
            device_id_type=pl.DeviceIdType.MESH,
        )
        copy.start()
        copies.append(copy)
        return copy

    def keep(source, target, n):
        copy = pltpu.make_async_copy(source, target, local.at[n])
        copy.start()
        return copy

    first = [
        push(blocks[j], landed.at[j - 1], j - 1, across[j - 1]) for j in range(1, EXP_FF)
    ]
    base = EXP_FF - 1
    for j in range(1, EXP_FF):
        push(exts[j], ext_wholes[j], base + j - 1, across[j - 1])
    base += EXP_FF - 1
    kept = [keep(exts[0], ext_wholes[0], 0)]
    for j in range(EXP_FF):
        if j:
            first[j - 1].wait_recv()
            source = landed.at[j - 1]
        else:
            source = blocks[0]
        kept.append(keep(source, wholes[j].at[:, here], 1 + j))
        for i in range(cols - 1):
            push(source, wholes[j].at[:, here], base + j * (cols - 1) + i, along[i])
    for copy in copies[EXP_FF - 1 :]:
        copy.wait_recv()
    for copy in copies:
        copy.wait_send()
    for copy in kept:
        copy.wait()


def spread_cot(blocks, exts, cols, replicas):
    hbm = pl.BlockSpec(memory_space=pl.ANY)
    wide = blocks[0].shape[1]
    remote = 2 * (EXP_FF - 1) + EXP_FF * (cols - 1)
    return pl.pallas_call(
        functools.partial(cot_kernel, cols, replicas),
        out_shape=[jax.ShapeDtypeStruct((CAP_FF, wide * cols), BF16)] * EXP_FF
        + [jax.ShapeDtypeStruct((CAP_FF, LANES), BF16)] * EXP_FF,
        in_specs=[hbm] * (2 * EXP_FF),
        out_specs=[hbm] * (2 * EXP_FF),
        scratch_shapes=[
            pltpu.VMEM((EXP_FF - 1, CAP_FF, wide), BF16),
            pltpu.SemaphoreType.DMA((remote,)),
            pltpu.SemaphoreType.DMA((remote,)),
            pltpu.SemaphoreType.DMA((1 + EXP_FF,)),
        ],
        compiler_params=pltpu.CompilerParams(collective_id=2, has_side_effects=True),
    )(*blocks, *exts)


def trade_kernel(replicas, *refs):
    count = EXP_FF - 1
    blocks, arrived = refs[:count], refs[count : 2 * count]
    send, recv = refs[2 * count :]
    across = [opposite("row", j * replicas) for j in range(1, EXP_FF)]
    greet(across)
    copies = []
    for j in (2, 1, 0):
        copy = pltpu.make_async_remote_copy(
            src_ref=blocks[j],
            dst_ref=arrived[j],
            send_sem=send.at[j],
            recv_sem=recv.at[j],
            device_id=across[j],
            device_id_type=pl.DeviceIdType.MESH,
        )
        copy.start()
        copies.append(copy)
    for copy in copies:
        copy.wait()


def trade_rows(blocks, replicas, number):
    hbm = pl.BlockSpec(memory_space=pl.ANY)
    count = EXP_FF - 1
    arrived = pl.pallas_call(
        functools.partial(trade_kernel, replicas),
        out_shape=[jax.ShapeDtypeStruct(b.shape, b.dtype) for b in blocks[1:]],
        in_specs=[hbm] * count,
        out_specs=[hbm] * count,
        scratch_shapes=[
            pltpu.SemaphoreType.DMA((count,)),
            pltpu.SemaphoreType.DMA((count,)),
        ],
        compiler_params=pltpu.CompilerParams(collective_id=number, has_side_effects=True),
    )(*blocks[1:])
    return [blocks[0], *arrived]


def ffn_kernel(parts, depth, width, units, *refs):
    hids = refs[:EXP_FF]
    cots = refs[EXP_FF : 2 * EXP_FF]
    cot_exts = refs[2 * EXP_FF : 3 * EXP_FF]
    pieces = refs[3 * EXP_FF : 3 * EXP_FF + parts]
    rights = refs[3 * EXP_FF + parts]
    outs = refs[3 * EXP_FF + parts + 1 :]
    grads = outs[:EXP_FF]
    downs = outs[EXP_FF : 2 * EXP_FF]
    adapt = outs[2 * EXP_FF]
    hid, cot, block, act, product, sems = outs[2 * EXP_FF + 1 :]
    row = lax.axis_index("row")
    wide = width + LANES
    copies = []
    for j in range(EXP_FF):
        where = pl.ds(j * CAP_FF, CAP_FF)
        copies.append(pltpu.make_async_copy(hids[j], hid.at[where], sems.at[j]))
        near = cot.at[where, pl.ds(0, width)]
        copies.append(pltpu.make_async_copy(cots[j], near, sems.at[EXP_FF + j]))
        near = cot.at[where, pl.ds(width, LANES)]
        copies.append(pltpu.make_async_copy(cot_exts[j], near, sems.at[2 * EXP_FF + j]))
    copies.append(pltpu.make_async_copy(rights, block.at[pl.ds(width, LANES)], sems.at[3 * EXP_FF]))
    for m in range(parts):
        owner = jnp.bitwise_xor(row, m)
        where = pl.ds(pl.multiple_of(owner * depth, depth), depth)
        copies.append(pltpu.make_async_copy(pieces[m], block.at[where], sems.at[3 * EXP_FF + 1 + m]))
    for copy in copies:
        copy.start()
    for copy in copies:
        copy.wait()
    gate_scale = hid[:, wide : wide + 1].astype(F32) + hid[:, wide + 1 : wide + 2].astype(F32)
    product[...] = jnp.zeros_like(product)

    def forward(start, size):
        here = pl.ds(start, size)
        up_here = pl.ds(units + start, size)
        down_here = pl.ds(2 * units + start, size)
        gate = jnp.dot(hid[:, :wide], block[:, here], preferred_element_type=F32)
        up = jnp.dot(hid[:, :wide], block[:, up_here], preferred_element_type=F32)
        grad = jnp.dot(cot[...], block[:, down_here], preferred_element_type=F32)
        sig = 1.0 / (1.0 + jnp.exp(-gate))
        mixed = (gate * sig * up).astype(BF16)
        act[:, down_here] = mixed
        product[...] += jnp.sum(mixed.astype(F32) * grad, axis=1, keepdims=True)
        grad = grad * gate_scale
        act[:, here] = (grad * up * sig * (1.0 + gate * (1.0 - sig))).astype(BF16)
        act[:, up_here] = (grad * gate * sig).astype(BF16)

    step = 2 * LANES
    full = units // step

    @pl.loop(0, full)
    def _(i):
        forward(pl.multiple_of(i * step, step), step)

    if units % step:
        forward(full * step, units % step)

    def backward(start, size):
        here = pl.ds(start, size)
        result = lax.dot_general(
            act[:, : 2 * units], block[here, : 2 * units], (((1,), (1,)), ((), ())),
            preferred_element_type=F32,
        ).astype(BF16)
        for j in range(EXP_FF):
            grads[j][:, here] = result[j * CAP_FF : (j + 1) * CAP_FF]
        result = lax.dot_general(
            act[:, 2 * units :], block[here, 2 * units :], (((1,), (1,)), ((), ())),
            preferred_element_type=F32,
        )
        result = (result * gate_scale).astype(BF16)
        for j in range(EXP_FF):
            downs[j][:, here] = result[j * CAP_FF : (j + 1) * CAP_FF]

    full_rows = wide // step

    @pl.loop(0, full_rows)
    def _(i):
        backward(pl.multiple_of(i * step, step), step)

    if wide % step:
        backward(full_rows * step, wide % step)
    total = product[...]
    high = total.astype(BF16)
    low = (total - high.astype(F32)).astype(BF16)
    lane = lax.broadcasted_iota(jnp.int32, (EXP_FF * CAP_FF, LANES), 1)
    packed = jnp.where(lane == 0, high.astype(F32), jnp.where(lane == 1, low.astype(F32), 0.0)).astype(BF16)
    for j in range(EXP_FF):
        grads[j][:, wide:] = packed[j * CAP_FF : (j + 1) * CAP_FF]
    ext = hid[:, width:wide]
    low_ext = (cot[:, width:].astype(F32) * gate_scale).astype(BF16)
    adapt[:, : 2 * units] = lax.dot_general(
        ext, act[:, : 2 * units], (((0,), (0,)), ((), ())), preferred_element_type=F32
    ).astype(BF16)
    adapt[:, 2 * units :] = lax.dot_general(
        low_ext, act[:, 2 * units :], (((0,), (0,)), ((), ())), preferred_element_type=F32
    ).astype(BF16)

def feed_forward(hids, cots, cot_exts, pieces, rights):
    parts = len(pieces)
    depth, triple = pieces[0].shape
    units = triple // 3
    width = depth * parts
    rows = EXP_FF * CAP_FF
    hbm = pl.BlockSpec(memory_space=pl.ANY)
    vmem = pl.BlockSpec(memory_space=pltpu.VMEM)
    wide = width + LANES
    return pl.pallas_call(
        functools.partial(ffn_kernel, parts, depth, width, units),
        out_shape=[jax.ShapeDtypeStruct((CAP_FF, wide + LANES), BF16)] * EXP_FF
        + [jax.ShapeDtypeStruct((CAP_FF, wide), BF16)] * EXP_FF
        + [jax.ShapeDtypeStruct((LANES, triple), BF16)],
        in_specs=[hbm] * (3 * EXP_FF + parts + 1),
        out_specs=[vmem] * (2 * EXP_FF + 1),
        scratch_shapes=[
            pltpu.VMEM((rows, wide + LANES), BF16),
            pltpu.VMEM((rows, wide), BF16),
            pltpu.VMEM((wide, triple), BF16),
            pltpu.VMEM((rows, triple), BF16),
            pltpu.VMEM((rows, 1), F32),
            pltpu.SemaphoreType.DMA((3 * EXP_FF + 1 + parts,)),
        ],
        compiler_params=pltpu.CompilerParams(vmem_limit_bytes=56 * 2**20),
    )(*hids, *cots, *cot_exts, *pieces, rights)


def on_device(
    inputs,
    cotangent,
    lengths,
    adapter_pick,
    attn_route,
    ffn_route,
    norm_one,
    norm_two,
    router_attn,
    router_ffn,
    kv_weight,
    query_weight,
    out_weight,
    inner_weight,
    down_weight,
    query_left,
    query_right,
    kv_left,
    kv_right,
    out_left,
    out_right,
    inner_left,
    inner_right,
    down_left,
    down_right,
):
    count, slice_width = inputs.shape
    width = router_attn.shape[0]
    rows_axis = lax.axis_size("row")
    replicas = rows_axis // EXP_FF
    row = lax.axis_index("row")
    col = lax.axis_index("col")
    expert = row // replicas
    depth = inner_weight.shape[1]
    units = inner_weight.shape[3]
    length = lengths[0]
    adapter = adapter_pick[0]
    position = jnp.arange(count)
    valid = (position < length).astype(F32)
    cosine, sine = tables(count, HEAD_DIM)
    scaling = HEAD_DIM ** (-0.5)

    def swap(value, offset):
        return lax.ppermute(value, "row", [(i, i ^ offset) for i in range(rows_axis)])

    def features(part):
        return lax.all_gather(part, "col", axis=1, tiled=True)

    def partials(part):
        return lax.psum_scatter(
            part.astype(BF16), "col", scatter_dimension=1, tiled=True
        ).astype(F32)

    def own_columns(table):
        return lax.dynamic_slice_in_dim(table, col * slice_width, slice_width, 0)

    def later(value, *earlier):
        return lax.optimization_barrier((value, *earlier))[0]

    cols = lax.axis_size("col")
    if rows_axis == 8:
        kv_full, query_full, x_full, cot_full = gather_all(
            [kv_weight, query_weight], [inputs, cotangent], rows_axis, cols
        )
    else:
        kv_full = lax.all_gather(kv_weight, "row", axis=1, tiled=True)
        query_full = lax.all_gather(query_weight, "row", axis=1, tiled=True)
        x_full = features(inputs)
        cot_full = features(cotangent)
    out_full = lax.all_gather(later(out_weight, query_full), "row", axis=1, tiled=True)

    padding = -units % LANES

    def padded(value):
        return jnp.pad(value, ((0, 0), (0, padding))) if padding else value

    near = []
    for j in range(EXP_FF):
        which = expert ^ j
        inner_own = lax.dynamic_index_in_dim(inner_weight, which, 0, keepdims=False)
        down_own = lax.dynamic_index_in_dim(down_weight, which, 0, keepdims=False)
        piece = jnp.concatenate(
            [padded(inner_own[:, 0]), padded(inner_own[:, 1]), padded(down_own)], axis=1
        )
        near.append(swap(later(piece, query_full), j * replicas) if j else piece)
    chunks = []
    for j in range(EXP_FF):
        for i in range(replicas):
            chunks.append(swap(near[j], i) if i else near[j])

    picks = lax.all_gather(adapter_pick, "row", axis=0, tiled=True)
    pick_onehot = (picks[:, None] == jnp.arange(ADAPT, dtype=jnp.int32)[None, :]).astype(BF16)
    lefts_own = jnp.stack(
        [query_left, kv_left, out_left, inner_left, down_left], axis=1
    ).swapaxes(2, 3)
    lefts_sent = mm(
        "ga,ax->gx", pick_onehot, lefts_own.reshape(ADAPT, 5 * RANK * depth)
    ).astype(BF16)
    lefts = lax.all_to_all(
        lefts_sent.reshape(rows_axis, 5 * RANK, depth), "row", 0, 0, tiled=False
    )
    lefts = lefts.swapaxes(0, 1).reshape(5, RANK, width)
    left_query, left_kv, left_out, left_inner, left_down = (lefts[i] for i in range(5))
    right_query = query_right[adapter].astype(F32)
    right_kv = kv_right[adapter].astype(F32)
    right_out = out_right[adapter].astype(F32)
    right_inner_all = inner_right.reshape(ADAPT * RANK, 2, units)
    right_down_all = down_right.reshape(ADAPT * RANK, units)
    ffn_right = jnp.concatenate(
        [padded(right_inner_all[:, 0]), padded(right_inner_all[:, 1]), padded(right_down_all)],
        axis=1,
    )
    own_adapter = (jnp.arange(ADAPT, dtype=jnp.int32) == adapter).astype(F32)

    def spread(low):
        return (own_adapter[None, :, None] * low[:, None, :]).reshape(count, ADAPT * RANK)

    def unspread(high):
        return jnp.sum(
            own_adapter[None, :, None] * high.reshape(count, ADAPT, RANK), axis=1
        )

    slots_attn = slot_rows(attn_route, EXP_ATT, CAP_ATT)
    slots_ffn = slot_rows(ffn_route, EXP_FF, CAP_FF)
    rows_attn = jnp.arange(EXP_ATT * CAP_ATT, dtype=jnp.int32)
    pick_attn = [
        (rows_attn[:, None] == slots_attn[None, :, k]).astype(BF16) for k in range(TOPK)
    ]
    pick_attn_any = pick_attn[0] + pick_attn[1]
    pick_attn_both = jnp.concatenate(pick_attn, axis=1)
    order = (expert ^ jnp.arange(EXP_FF, dtype=jnp.int32))[:, None] * CAP_FF
    rows_ffn = (order + jnp.arange(CAP_FF, dtype=jnp.int32)[None, :]).reshape(EXP_FF * CAP_FF)
    pick_ffn = [(rows_ffn[:, None] == slots_ffn[None, :, k]).astype(BF16) for k in range(TOPK)]
    pick_ffn_any = pick_ffn[0] + pick_ffn[1]

    def blocks_of(rows):
        blocks = rows.reshape(EXP_FF, CAP_FF, rows.shape[1])
        return [blocks[j] for j in range(EXP_FF)]

    def trade(blocks):
        return [swap(block, j * replicas) if j else block for j, block in enumerate(blocks)]

    masked_cot = cotangent * valid.astype(BF16)[:, None]
    cot_full = cot_full * valid.astype(BF16)[:, None]
    grad_low_down = mm("td,rd->tr", cot_full, left_down)
    cot_rows = spread_cot(
        blocks_of(mm("ct,td->cd", pick_ffn_any, masked_cot).astype(BF16)),
        blocks_of(mm("ct,td->cd", pick_ffn_any, spread(grad_low_down).astype(BF16)).astype(BF16)),
        cols,
        replicas,
    )

    x_wide = x_full.astype(F32)
    scale_one = lax.rsqrt(jnp.mean(x_wide * x_wide, axis=1, keepdims=True) + EPSILON)
    hidden_one = (x_wide * scale_one * norm_one).astype(BF16)
    gates_attn = jax.nn.softmax(
        chosen_of(mm("td,de->te", hidden_one, router_attn), attn_route, EXP_ATT), axis=1
    )
    rank_query = mm("td,rd->tr", hidden_one, left_query)
    rank_kv = mm("td,rd->tr", hidden_one, left_kv)
    kv_raw = mm("td,sdw->stw", hidden_one, kv_full) + mm(
        "tr,rsw->stw", rank_kv.astype(BF16), right_kv.astype(BF16)
    )
    query_width = kv_raw.shape[2]
    heads = query_width // HEAD_DIM
    keys = rotate(
        kv_raw[0].reshape(count, heads, HEAD_DIM), cosine[:, None], sine[:, None]
    ).astype(BF16)
    values = kv_raw[1].reshape(count, heads, HEAD_DIM).astype(BF16)
    small = jnp.concatenate([rank_query, gates_attn, cosine, sine], axis=1)
    small_rows = exact("ct,tx->cx", pick_attn_any.astype(F32), small)
    rank_query_rows = small_rows[:, :RANK]
    gate_rows = exact("ct,tx->cx", pick_attn[0].astype(F32), gates_attn[:, :1]) + exact(
        "ct,tx->cx", pick_attn[1].astype(F32), gates_attn[:, 1:]
    )
    half = HEAD_DIM // 2
    cosine_rows = small_rows[:, RANK + TOPK : RANK + TOPK + half]
    sine_rows = small_rows[:, RANK + TOPK + half :]
    hidden_rows = mm("ct,td->cd", pick_attn_any, hidden_one).astype(BF16)
    query_rows = mm(
        "ecd,edw->ecw", hidden_rows.reshape(EXP_ATT, CAP_ATT, width), query_full
    ).reshape(EXP_ATT * CAP_ATT, query_width) + mm(
        "cr,rw->cw", rank_query_rows.astype(BF16), right_query.astype(BF16)
    )
    query_rows = (
        rotate(
            query_rows.reshape(EXP_ATT * CAP_ATT, heads, HEAD_DIM),
            cosine_rows[:, None],
            sine_rows[:, None],
        )
        .astype(BF16)
        .reshape(EXP_ATT * CAP_ATT, query_width)
    )
    queries = (
        mm("cx,cw->xw", pick_attn_both, query_rows)
        .astype(BF16)
        .reshape(TOPK, count, heads, HEAD_DIM)
    )
    allowed = (position[None, :] <= position[:, None]) & (position[None, :] < length)
    scores = mm("kbhd,jhd->hkbj", queries, keys) * scaling
    scores = jnp.where(allowed[None, None], scores, -1e30)
    exponent = jnp.exp(scores - jnp.max(scores, axis=-1, keepdims=True))
    probability = exponent / jnp.sum(exponent, axis=-1, keepdims=True)
    probs = probability.astype(BF16)
    attended = mm("hkbj,jhd->kbhd", probs, values).astype(BF16).reshape(TOPK * count, query_width)
    attended_rows = mm("cx,xw->cw", pick_attn_both, attended).astype(BF16)
    out_rows = mm(
        "ecw,edw->ecd", attended_rows.reshape(EXP_ATT, CAP_ATT, query_width), out_full
    ).reshape(EXP_ATT * CAP_ATT, width)
    low_rows = mm("cw,rw->cr", attended_rows, right_out.astype(BF16))
    out_ext = (jnp.concatenate([out_rows, low_rows], axis=1) * gate_rows).astype(BF16)
    combined = mm("ct,cd->td", pick_attn_any, out_ext)
    low_out_part = combined[:, width:]
    branch_attn = combined[:, :width] + mm("tr,rd->td", low_out_part.astype(BF16), left_out)
    x_local = inputs.astype(F32)
    middle = x_local + partials(branch_attn)
    square_sum, low_out_full = lax.psum((jnp.sum(middle * middle, axis=1), low_out_part), "col")
    scale_two = lax.rsqrt(square_sum[:, None] / width + EPSILON)
    hidden_two = features((middle * scale_two * own_columns(norm_two)).astype(BF16))

    gates_ffn = jax.nn.softmax(
        chosen_of(mm("td,de->te", hidden_two, router_ffn), ffn_route, EXP_FF), axis=1
    )
    rank_inner = mm("td,rd->tr", hidden_two, left_inner)
    hidden_ext = jnp.concatenate([hidden_two, spread(rank_inner).astype(BF16)], axis=1)
    hidden_out = mm("ct,td->cd", pick_ffn_any, hidden_ext).astype(BF16)
    gate_high = gates_ffn.astype(BF16)
    gate_low = (gates_ffn - gate_high.astype(F32)).astype(BF16)
    gate_out = sum(
        mm("ct,tx->cx", pick_ffn[k], jnp.stack([gate_high[:, k], gate_low[:, k]], axis=1))
        for k in range(TOPK)
    )
    gate_out = jnp.pad(gate_out, ((0, 0), (0, 126))).astype(BF16)
    hidden_in = trade_rows(blocks_of(jnp.concatenate([hidden_out, gate_out], axis=1)), replicas, 3)
    results = feed_forward(hidden_in, cot_rows[:EXP_FF], cot_rows[EXP_FF:], chunks, ffn_right)
    grad_back = jnp.concatenate(trade_rows(results[:EXP_FF], replicas, 4))
    down_back = trade(list(later(tuple(results[EXP_FF : 2 * EXP_FF]), grad_back)))
    down_back = jnp.concatenate(down_back)
    ffn_rights = lax.optimization_barrier(lax.psum(results[2 * EXP_FF], "row")).astype(F32)
    ffn_rights = ffn_rights.reshape(ADAPT, RANK, 3, units + padding)[..., :units]

    grad_comb = mm("ct,cd->td", pick_ffn_any, grad_back[:, : width + 128])
    gg_back = grad_back[:, width + 128 : width + 130]
    grad_gates_part = jnp.stack(
        [jnp.sum(mm("ct,cx->tx", pick_ffn[k], gg_back), axis=1) for k in range(TOPK)], axis=1
    )
    grad_rank_inner = unspread(grad_comb[:, width:])
    grad_two_part = grad_comb[:, :width] + mm(
        "tr,rd->td", grad_rank_inner.astype(BF16), left_inner
    )
    down_comb = mm("ct,cd->td", pick_ffn_any, down_back)
    low_down_part = unspread(down_comb[:, width:])
    branch_ffn = down_comb[:, :width] + mm("tr,rd->td", low_down_part.astype(BF16), left_down)
    (grad_gates_ffn,) = lax.psum((grad_gates_part,), "col")
    logits_ffn_grad = router_back(gates_ffn, grad_gates_ffn, ffn_route, EXP_FF)
    grad_two = partials(grad_two_part) + exact(
        "te,de->td", logits_ffn_grad, own_columns(router_ffn).astype(F32)
    )
    scaled_two = grad_two * own_columns(norm_two)
    inner_sum, rank_inner_grad_full, low_down_full = lax.psum(
        (jnp.sum(scaled_two * middle, axis=1), grad_rank_inner, low_down_part), "col"
    )
    grad_middle = (
        masked_cot.astype(F32)
        + scale_two * scaled_two
        - middle * scale_two**3 * inner_sum[:, None] / width
    )
    output = ((middle + partials(branch_ffn)) * valid[:, None]).astype(BF16)

    grad_full = features(grad_middle.astype(BF16))
    grad_low_out = mm("td,rd->tr", grad_full, left_out)
    grad_middle_rows = mm(
        "ct,td->cd",
        pick_attn_any,
        jnp.concatenate([grad_full, grad_low_out.astype(BF16)], axis=1),
    ).astype(BF16)
    grad_att_rows = mm(
        "ecd,edw->ecw",
        grad_middle_rows[:, :width].reshape(EXP_ATT, CAP_ATT, width),
        out_full,
    ).reshape(EXP_ATT * CAP_ATT, query_width) + mm(
        "cr,rw->cw", grad_middle_rows[:, width:], right_out.astype(BF16)
    )
    gg_attn_rows = jnp.sum(attended_rows.astype(F32) * grad_att_rows, axis=1, keepdims=True)
    grad_gates_attn_part = jnp.concatenate(
        [exact("ct,cx->tx", pick_attn[k].astype(F32), gg_attn_rows) for k in range(TOPK)], axis=1
    )
    grad_att_rows = (grad_att_rows * gate_rows).astype(BF16)
    grad_attended = (
        mm("cx,cw->xw", pick_attn_both, grad_att_rows)
        .astype(BF16)
        .reshape(TOPK, count, heads, HEAD_DIM)
    )
    gated_low = (gates_attn.T[:, :, None] * grad_low_out[None]).reshape(TOPK * count, RANK)
    grad_right_out = mm("xr,xw->rw", gated_low.astype(BF16), attended)
    grad_prob = mm("kbhd,jhd->hkbj", grad_attended, values)
    centre = jnp.sum(probability * grad_prob, axis=-1, keepdims=True)
    grad_scores = (probability * (grad_prob - centre)).astype(BF16)
    grad_queries = mm("hkbj,jhd->kbhd", grad_scores, keys) * scaling
    grad_keys = mm("hkbj,kbhd->jhd", grad_scores, queries) * scaling
    grad_values = mm("hkbj,kbhd->jhd", probs, grad_attended)
    grad_query_raw = (
        rotate(grad_queries, cosine[None, :, None], -sine[None, :, None])
        .astype(BF16)
        .reshape(TOPK * count, query_width)
    )
    grad_key_raw = rotate(grad_keys, cosine[:, None], -sine[:, None])
    grad_kv = jnp.stack([grad_key_raw, grad_values]).astype(BF16).reshape(2, count, query_width)
    grad_query_rows = mm("cx,xw->cw", pick_attn_both, grad_query_raw).astype(BF16)
    grad_one_rows = (
        mm("ecw,edw->ecd", grad_query_rows.reshape(EXP_ATT, CAP_ATT, query_width), query_full)
        .astype(BF16)
        .reshape(EXP_ATT * CAP_ATT, width)
    )
    grad_query_sum = jnp.sum(
        grad_query_raw.astype(F32).reshape(TOPK, count, query_width), axis=0
    )
    grad_query_sum_low = grad_query_sum.astype(BF16)
    grad_rank_query = mm("tw,rw->tr", grad_query_sum_low, right_query.astype(BF16))
    grad_rank_kv = mm("stw,rsw->tr", grad_kv, right_kv.astype(BF16))
    grad_one_part = (
        mm("ct,cd->td", pick_attn_any, grad_one_rows)
        + mm("stw,sdw->td", grad_kv, kv_full)
        + mm(
            "tr,rd->td",
            jnp.concatenate([grad_rank_query, grad_rank_kv], axis=1).astype(BF16),
            jnp.concatenate([left_query, left_kv], axis=0),
        )
    )
    grad_right_query = mm("tr,tw->rw", rank_query.astype(BF16), grad_query_sum_low)
    grad_right_kv = mm("tr,stw->rsw", rank_kv.astype(BF16), grad_kv)
    grad_gates_attn, rank_query_grad_full, rank_kv_grad_full = lax.psum(
        (grad_gates_attn_part, grad_rank_query, grad_rank_kv), "col"
    )
    logits_attn_grad = router_back(gates_attn, grad_gates_attn, attn_route, EXP_ATT)
    grad_one = partials(grad_one_part) + exact(
        "te,de->td", logits_attn_grad, own_columns(router_attn).astype(F32)
    )
    scaled_one = grad_one * own_columns(norm_one)
    outer_sum = lax.psum(jnp.sum(scaled_one * x_local, axis=1), "col")
    grad_inputs = (
        grad_middle
        + scale_one * scaled_one
        - x_local * scale_one**3 * outer_sum[:, None] / width
    )

    hiddens = (hidden_one, hidden_one, grad_full, hidden_two, cot_full)
    lows = (
        rank_query_grad_full,
        rank_kv_grad_full,
        low_out_full,
        rank_inner_grad_full,
        low_down_full,
    )
    left_parts = jnp.concatenate(
        [mm("tr,td->rd", low.astype(BF16), hidden) for low, hidden in zip(lows, hiddens)]
    ).astype(BF16)
    left_parts = lax.all_to_all(
        left_parts.reshape(5 * RANK, rows_axis, depth), "row", 1, 0, tiled=False
    )
    left_grads = mm("ga,gx->ax", pick_onehot, left_parts.reshape(rows_axis, 5 * RANK * depth))
    left_grads = left_grads.reshape(ADAPT, 5, RANK, depth).swapaxes(2, 3)
    right_parts = jnp.concatenate(
        [grad_right_query, grad_right_kv[:, 0], grad_right_kv[:, 1], grad_right_out], axis=1
    ).astype(BF16)
    right_all = lax.all_gather(right_parts, "row", axis=0)
    right_grads = mm(
        "ga,gx->ax", pick_onehot, right_all.reshape(rows_axis, RANK * 4 * query_width)
    ).reshape(ADAPT, RANK, 4, query_width)
    return (
        output,
        grad_inputs,
        left_grads[:, 0],
        right_grads[:, :, 0],
        left_grads[:, 1],
        right_grads[:, :, 1:3],
        left_grads[:, 2],
        right_grads[:, :, 3],
        left_grads[:, 3],
        ffn_rights[:, :, :2],
        left_grads[:, 4],
        ffn_rights[:, :, 2],
    )


def solution(mesh):
    placed = (
        P("row", "col"),
        P("row", "col"),
        P("row"),
        P("row"),
        P("row", None),
        P("row", None),
        P(),
        P(),
        P(),
        P(),
        P(None, "row", "col"),
        P(None, "row", "col"),
        P(None, "row", "col"),
        P(None, "row", None, "col"),
        P(None, "row", "col"),
        P(None, "row", None),
        P(None, None, "col"),
        P(None, "row", None),
        P(None, None, None, "col"),
        P(None, "row", None),
        P(None, None, "col"),
        P(None, "row", None),
        P(None, None, None, "col"),
        P(None, "row", None),
        P(None, None, "col"),
    )
    return jax.shard_map(
        on_device,
        mesh=mesh,
        in_specs=placed,
        out_specs=(
            P("row", "col"),
            P("row", "col"),
            P(None, "row", None),
            P(None, None, "col"),
            P(None, "row", None),
            P(None, None, None, "col"),
            P(None, "row", None),
            P(None, None, "col"),
            P(None, "row", None),
            P(None, None, None, "col"),
            P(None, "row", None),
            P(None, None, "col"),
        ),
        check_vma=False,
    )
```

```python
import functools

import jax
import jax.numpy as jnp
from jax import lax
from jax.experimental import pallas as pl
from jax.experimental.pallas import tpu as pltpu
from jax.sharding import PartitionSpec as P

HEAD_DIM = 128
EXP_ATT = 8
EXP_FF = 4
TOPK = 2
ADAPT = 8
RANK = 16
CAP_ATT = 80
CAP_FF = 160
EPSILON = 1e-06
ROPE_BASE = 10000.0
HIGHEST = lax.Precision.HIGHEST
F32 = jnp.float32
BF16 = jnp.bfloat16
LANES = 128


def mm(spec, a, b):
    return jnp.einsum(spec, a, b, preferred_element_type=F32)


def exact(spec, a, b):
    return jnp.einsum(spec, a, b, precision=HIGHEST, preferred_element_type=F32)


def tables(count, head_width):
    position = jnp.arange(count).astype(F32)
    frequency = ROPE_BASE ** (-jnp.arange(head_width // 2).astype(F32) * 2.0 / head_width)
    angle = position[:, None] * frequency[None, :]
    return (jnp.cos(angle), jnp.sin(angle))


def rotate(values, cosine, sine):
    half = values.shape[-1] // 2
    first = values[..., :half]
    second = values[..., half:]
    return jnp.concatenate(
        [first * cosine - second * sine, second * cosine + first * sine], axis=-1
    )


def slot_rows(route, experts, capacity):
    count = route.shape[0]
    chosen = (route[:, :, None] == jnp.arange(experts, dtype=jnp.int32)).astype(BF16)
    per_token = jnp.sum(chosen, axis=1)
    place = jnp.arange(count)
    before = (place[None, :] < place[:, None]).astype(BF16)
    earlier = mm("tu,ue->te", before, per_token)
    inside = jnp.stack([jnp.zeros_like(chosen[:, 0]), chosen[:, 0]], axis=1).astype(F32)
    position = jnp.sum((earlier[:, None, :] + inside) * chosen.astype(F32), axis=2)
    return route * capacity + position.astype(jnp.int32)


def chosen_of(logits, route, experts):
    onehot = (route[:, :, None] == jnp.arange(experts, dtype=jnp.int32)).astype(F32)
    return jnp.sum(onehot * logits[:, None, :], axis=2)


def opposite(axis, offset):
    index = jnp.bitwise_xor(lax.axis_index(axis), offset)
    if axis == "row":
        return (index, lax.axis_index("col"))
    return (lax.axis_index("row"), index)


def greet(partners):
    barrier = pltpu.get_barrier_semaphore()
    for partner in partners:
        pl.semaphore_signal(
            barrier, inc=1, device_id=partner, device_id_type=pl.DeviceIdType.MESH
        )
    pl.semaphore_wait(barrier, len(partners))


def dispatch_matrix(route, flip, experts, capacity):
    count = route.shape[0]
    lane = lax.broadcasted_iota(jnp.int32, (count, LANES), 1)
    chosen = [(route[:, k : k + 1] == lane).astype(F32) for k in range(TOPK)]
    place = lax.broadcasted_iota(jnp.int32, (count, count), 0)
    other = lax.broadcasted_iota(jnp.int32, (count, count), 1)
    before = (other < place).astype(F32).astype(BF16)
    earlier = jnp.dot(
        before, (chosen[0] + chosen[1]).astype(BF16), preferred_element_type=F32
    )
    rows = lax.broadcasted_iota(jnp.int32, (count, experts * capacity), 1)
    result = None
    for k in range(TOPK):
        position = jnp.sum(earlier * chosen[k], axis=1, keepdims=True).astype(jnp.int32)
        mine = jnp.bitwise_xor(route[:, k : k + 1], flip) * capacity + position
        found = (rows == mine).astype(F32)
        result = found if result is None else result + found
    return result.astype(BF16)


def gather_kernel(parts, cols, replicas, counts, *refs):
    n_blocks = len(counts)
    lengths, route, tokens, cot = refs[:4]
    blocks = refs[4 : 4 + n_blocks]
    outs = refs[4 + n_blocks :]
    wholes = outs[:n_blocks]
    tokens_whole = outs[n_blocks]
    cot_wholes = outs[n_blocks + 1 : n_blocks + 1 + EXP_FF]
    own_rows, landed, send, recv, local = outs[n_blocks + 1 + EXP_FF :]
    row = lax.axis_index("row")
    col = lax.axis_index("col")
    depth = blocks[0].shape[1]
    count, wide = tokens.shape
    partners = {offset: opposite("row", offset) for offset in (1, 2, 4)}
    along = [opposite("col", i) for i in range(1, cols)]
    greet(list(partners.values()) + [opposite("row", 6)] + along)
    chunks = [(a, i) for a, number in enumerate(counts) for i in range(number)]
    used = [0]
    started = []
    received = set()
    kept = []
    here = pl.ds(pl.multiple_of(col * wide, wide), wide)

    def send_to(source, target, device):
        n = used[0]
        used[0] += 1
        copy = pltpu.make_async_remote_copy(
            src_ref=source,
            dst_ref=target,
            send_sem=send.at[n],
            recv_sem=recv.at[n],
            device_id=device,
            device_id_type=pl.DeviceIdType.MESH,
        )
        copy.start()
        started.append(copy)
        return copy

    def arrive(copy):
        copy.wait_recv()
        received.add(id(copy))

    def keep(source, target):
        copy = pltpu.make_async_copy(source, target, local.at[len(kept)])
        copy.start()
        kept.append(copy)

    def place(chunk, offset):
        array, i = chunk
        owner = jnp.bitwise_xor(row, offset)
        return wholes[array].at[i, pl.ds(pl.multiple_of(owner * depth, depth), depth)]

    def push(source, chunk, target, offset):
        return send_to(source, place(chunk, offset), partners[target])

    for device in along:
        send_to(tokens, tokens_whole.at[:, here], device)
    keep(tokens, tokens_whole.at[:, here])
    first = {}
    for number, chunk in enumerate(chunks):
        source = blocks[chunk[0]].at[chunk[1]]
        for target in (2, 4):
            first[number, target] = push(source, chunk, target, 0)
    for a in range(n_blocks):
        where = pl.ds(pl.multiple_of(row * depth, depth), depth)
        keep(blocks[a], wholes[a].at[:, where])
    for chunk in chunks:
        push(blocks[chunk[0]].at[chunk[1]], chunk, 1, 0)
    valid = lax.broadcasted_iota(jnp.int32, (count, 1), 0) < lengths[0]
    matrix = dispatch_matrix(route[...], row // replicas, EXP_FF, CAP_FF)
    masked = jnp.where(valid, cot[...].astype(F32), 0.0).astype(BF16)
    dispatched = lax.dot_general(
        matrix, masked, (((0,), (0,)), ((), ())), preferred_element_type=F32
    ).astype(BF16)
    for j in range(EXP_FF):
        own_rows[j] = dispatched[j * CAP_FF : (j + 1) * CAP_FF]
    traded = [
        send_to(own_rows.at[j], landed.at[j - 1], opposite("row", j * replicas))
        for j in range(1, EXP_FF)
    ]
    for j in range(EXP_FF):
        if j:
            arrive(traded[j - 1])
            source = landed.at[j - 1]
        else:
            source = own_rows.at[0]
        keep(source, cot_wholes[j].at[:, here])
        for device in along:
            send_to(source, cot_wholes[j].at[:, here], device)
    relayed = []
    for number, chunk in enumerate(chunks):
        arrive(first[number, 2])
        arrive(first[number, 4])
        if number % 2 == 0:
            relayed.append(push(place(chunk, 2), chunk, 4, 2))
        else:
            relayed.append(push(place(chunk, 4), chunk, 2, 4))
        for offset in (2, 4):
            push(place(chunk, offset), chunk, 1, offset)
    for number, chunk in enumerate(chunks):
        arrive(relayed[number])
        push(place(chunk, 6), chunk, 1, 6)
    for copy in started:
        if id(copy) not in received:
            copy.wait_recv()
    for copy in started:
        copy.wait_send()
    for copy in kept:
        copy.wait()


def gather_all(lengths, route, tokens, cot, blocks, parts, cols, replicas):
    counts = [block.shape[0] for block in blocks]
    hbm = pl.BlockSpec(memory_space=pl.ANY)
    vmem = pl.BlockSpec(memory_space=pltpu.VMEM)
    smem = pl.BlockSpec(memory_space=pltpu.SMEM)
    count, wide = tokens.shape
    remote = 7 * sum(counts) + (cols - 1) * (1 + EXP_FF) + EXP_FF - 1
    return pl.pallas_call(
        functools.partial(gather_kernel, parts, cols, replicas, counts),
        out_shape=[
            jax.ShapeDtypeStruct((b.shape[0], b.shape[1] * parts, b.shape[2]), b.dtype)
            for b in blocks
        ]
        + [jax.ShapeDtypeStruct((count, wide * cols), tokens.dtype)]
        + [jax.ShapeDtypeStruct((CAP_FF, wide * cols), BF16)] * EXP_FF,
        in_specs=[smem, vmem, hbm, vmem] + [hbm] * len(blocks),
        out_specs=[hbm] * (len(blocks) + 1 + EXP_FF),
        scratch_shapes=[
            pltpu.VMEM((EXP_FF, CAP_FF, wide), BF16),
            pltpu.VMEM((EXP_FF - 1, CAP_FF, wide), BF16),
            pltpu.SemaphoreType.DMA((remote,)),
            pltpu.SemaphoreType.DMA((remote,)),
            pltpu.SemaphoreType.DMA((1 + EXP_FF + len(blocks),)),
        ],
        compiler_params=pltpu.CompilerParams(collective_id=1, has_side_effects=True),
    )(lengths, route, tokens, cot, *blocks)


def cot_kernel(cols, replicas, *refs):
    blocks, wholes = refs[:EXP_FF], refs[EXP_FF : 2 * EXP_FF]
    landed, send, recv, local = refs[2 * EXP_FF :]
    col = lax.axis_index("col")
    wide = blocks[0].shape[1]
    here = pl.ds(pl.multiple_of(col * wide, wide), wide)
    along = [opposite("col", i) for i in range(1, cols)]
    across = [opposite("row", j * replicas) for j in range(1, EXP_FF)]
    greet(along + across)
    copies = []

    def push(source, target, n, device):
        copy = pltpu.make_async_remote_copy(
            src_ref=source,
            dst_ref=target,
            send_sem=send.at[n],
            recv_sem=recv.at[n],
            device_id=device,
            device_id_type=pl.DeviceIdType.MESH,
        )
        copy.start()
        copies.append(copy)
        return copy

    def keep(source, target, n):
        copy = pltpu.make_async_copy(source, target, local.at[n])
        copy.start()
        return copy

    first = [
        push(blocks[j], landed.at[j - 1], j - 1, across[j - 1]) for j in range(1, EXP_FF)
    ]
    base = EXP_FF - 1
    kept = []
    for j in range(EXP_FF):
        if j:
            first[j - 1].wait_recv()
            source = landed.at[j - 1]
        else:
            source = blocks[0]
        kept.append(keep(source, wholes[j].at[:, here], j))
        for i in range(cols - 1):
            push(source, wholes[j].at[:, here], base + j * (cols - 1) + i, along[i])
    for copy in copies[EXP_FF - 1 :]:
        copy.wait_recv()
    for copy in copies:
        copy.wait_send()
    for copy in kept:
        copy.wait()


def spread_cot(blocks, cols, replicas):
    hbm = pl.BlockSpec(memory_space=pl.ANY)
    wide = blocks[0].shape[1]
    remote = EXP_FF - 1 + EXP_FF * (cols - 1)
    return pl.pallas_call(
        functools.partial(cot_kernel, cols, replicas),
        out_shape=[jax.ShapeDtypeStruct((CAP_FF, wide * cols), BF16)] * EXP_FF,
        in_specs=[hbm] * EXP_FF,
        out_specs=[hbm] * EXP_FF,
        scratch_shapes=[
            pltpu.VMEM((EXP_FF - 1, CAP_FF, wide), BF16),
            pltpu.SemaphoreType.DMA((remote,)),
            pltpu.SemaphoreType.DMA((remote,)),
            pltpu.SemaphoreType.DMA((EXP_FF,)),
        ],
        compiler_params=pltpu.CompilerParams(collective_id=2, has_side_effects=True),
    )(*blocks)


def split(value):
    high = value.astype(BF16).astype(F32)
    return high, value - high


def pack(columns, lanes):
    lane = lax.broadcasted_iota(jnp.int32, (columns[0].shape[0], LANES), 1)
    result = jnp.zeros((columns[0].shape[0], LANES), F32)
    for column, n in zip(columns, lanes):
        result = jnp.where(lane == n, column, result)
    return result


def route_term(stat, grads, router, start, size):
    gates = [stat[:, k : k + 1] for k in range(TOPK)]
    mean = gates[0] * grads[0] + gates[1] * grads[1]
    product = 0.0
    term = 0.0
    weights = [gates[k] * (grads[k] - mean) for k in range(TOPK)]
    for k in range(TOPK):
        product += weights[k] * stat[:, 2 + k : 3 + k]
    for e in range(router.shape[0]):
        weight = 0.0
        for k in range(TOPK):
            weight += jnp.where(stat[:, 5 + k : 6 + k] == float(e), weights[k], 0.0)
        term += weight * router[e : e + 1, pl.ds(start, size)].astype(F32)
    return term, product


def fetch(sources, targets, sems):
    copies = []
    for n, (source, target) in enumerate(zip(sources, targets)):
        copies.append(pltpu.make_async_copy(source, target, sems.at[n]))
        copies[-1].start()
    return copies


def remote(source, target, send, recv, n, device):
    copy = pltpu.make_async_remote_copy(
        src_ref=source,
        dst_ref=target,
        send_sem=send.at[n],
        recv_sem=recv.at[n],
        device_id=device,
        device_id_type=pl.DeviceIdType.MESH,
    )
    copy.start()
    return copy


def middle_back_kernel(cols, replicas, *refs):
    blocks, downs = refs[:EXP_FF], refs[EXP_FF : 2 * EXP_FF]
    adapter, norm, router, stat = refs[2 * EXP_FF : 2 * EXP_FF + 4]
    sources = refs[2 * EXP_FF + 4 : 2 * EXP_FF + 10]
    grad_middle, grad_whole, totals, branch, low_down = refs[2 * EXP_FF + 10 : 2 * EXP_FF + 15]
    scratch = refs[2 * EXP_FF + 15 :]
    pick_0, pick_1, lefts, hidden, middle, cot = scratch[:6]
    rows, down_rows, exact_part, parts, extra, parts_in, extra_in, low, send, recv, local = (
        scratch[6:]
    )
    col = lax.axis_index("col")
    count, wide = middle.shape
    width = hidden.shape[1]
    across = [opposite("row", j * replicas) for j in range(1, EXP_FF)]
    along = [opposite("col", i) for i in range(1, cols)]
    greet(across + along)
    copies = [
        remote(
            blocks[j], rows.at[pl.ds(j * CAP_FF, CAP_FF)], send, recv, j - 1, across[j - 1]
        )
        for j in range(1, EXP_FF)
    ]
    near = fetch(
        [blocks[0], downs[0], *sources],
        [rows.at[pl.ds(0, CAP_FF)], down_rows.at[pl.ds(0, CAP_FF)], *scratch[:6]],
        local,
    )
    for copy in near:
        copy.wait()
    for copy in copies:
        copy.wait_recv()
    base = EXP_FF - 1
    down_copies = [
        remote(
            downs[j],
            down_rows.at[pl.ds(j * CAP_FF, CAP_FF)],
            send,
            recv,
            base + j - 1,
            across[j - 1],
        )
        for j in range(1, EXP_FF)
    ]
    picks = [pick_0[...], pick_1[...]]
    any_pick = picks[0] + picks[1]

    def back(pick, source, start, size):
        return lax.dot_general(
            pick,
            source[:, start : start + size],
            (((0,), (0,)), ((), ())),
            preferred_element_type=F32,
        )

    sub = lax.broadcasted_iota(jnp.int32, (LANES, LANES), 0)
    lane = lax.broadcasted_iota(jnp.int32, (LANES, LANES), 1)
    mine = lax.broadcasted_iota(jnp.int32, (count, LANES), 1) // RANK == adapter[0]
    place_rank = (lane == RANK + sub % RANK).astype(F32).astype(BF16)

    def own_rank(value):
        value = jnp.where(mine, value, 0.0).astype(BF16)
        return jnp.dot(value, place_rank, preferred_element_type=F32)

    gate_grads = []
    for k in range(TOPK):
        pair = back(picks[k], rows, width + LANES, LANES)
        gate_grads.append(pair[:, 0:1] + pair[:, 1:2])
    rank = own_rank(back(any_pick, rows, width, LANES))
    rank_low = rank[:, RANK : 2 * RANK].astype(BF16)
    product = jnp.zeros((count, 1), F32)
    for q in range(cols):
        here = slice(q * wide, (q + 1) * wide)
        part = back(any_pick, rows, q * wide, wide) + jnp.dot(
            rank_low, lefts[3 * RANK : 4 * RANK, here], preferred_element_type=F32
        )
        product += jnp.sum(part * hidden[:, here].astype(F32), axis=1, keepdims=True)
        exact_part[q] = part
        parts[q] = part.astype(BF16)
    columns = [*split(gate_grads[0]), *split(gate_grads[1]), *split(product)]
    small = pack(columns, range(6)) + rank
    extra[...] = small.astype(BF16)
    base += EXP_FF - 1
    arrivals = []
    for i in range(1, cols):
        target = jnp.bitwise_xor(col, i)
        n = base + 2 * (i - 1)
        arrivals.append(remote(extra, extra_in.at[i - 1], send, recv, n + 1, along[i - 1]))
        arrivals.append(
            remote(parts.at[target], parts_in.at[i - 1], send, recv, n, along[i - 1])
        )
    for copy in arrivals:
        copy.wait_recv()
    grad = exact_part[col]
    total = small
    for i in range(cols - 1):
        grad += parts_in[i].astype(F32)
        total += extra_in[i].astype(F32)
    totals[...] = total
    gate_grads = [total[:, 0:1] + total[:, 1:2], total[:, 2:3] + total[:, 3:4]]
    first = pl.multiple_of(col * wide, wide)
    term, more = route_term(stat, gate_grads, router, first, wide)
    inner = total[:, 4:5] + total[:, 5:6] + more
    scaled = (grad + term) * norm[:, pl.ds(first, wide)]
    factor = stat[:, 4:5]
    valid = stat[:, 7:8]
    result = (
        cot[...].astype(F32) * valid
        + factor * scaled
        - middle[...] * (factor * factor * inner * (1.0 / width))
    )
    grad_middle[...] = result
    low[...] = result.astype(BF16)
    here = pl.ds(first, wide)
    kept = pltpu.make_async_copy(low, grad_whole.at[:, here], local.at[8])
    kept.start()
    base += 2 * (cols - 1)
    last = [
        remote(low, grad_whole.at[:, here], send, recv, base + i, along[i])
        for i in range(cols - 1)
    ]
    for copy in down_copies:
        copy.wait_recv()
    rank = own_rank(back(any_pick, down_rows, width, LANES))
    rank_low = rank[:, RANK : 2 * RANK].astype(BF16)
    low_down[...] = rank
    for q in range(cols):
        here = slice(q * wide, (q + 1) * wide)
        part = back(any_pick, down_rows, q * wide, wide) + jnp.dot(
            rank_low, lefts[4 * RANK : 5 * RANK, here], preferred_element_type=F32
        )
        branch[:, here] = part.astype(BF16)
    for copy in last:
        copy.wait_recv()
    for copy in copies + down_copies + arrivals + last:
        copy.wait_send()
    kept.wait()


def middle_back(blocks, downs, adapter, norm, router, stat, sources, cols, replicas):
    hbm = pl.BlockSpec(memory_space=pl.ANY)
    vmem = pl.BlockSpec(memory_space=pltpu.VMEM)
    smem = pl.BlockSpec(memory_space=pltpu.SMEM)
    count, wide = sources[-1].shape
    total = 2 * (EXP_FF - 1) + 3 * (cols - 1)
    rows = EXP_FF * CAP_FF
    return pl.pallas_call(
        functools.partial(middle_back_kernel, cols, replicas),
        out_shape=[
            jax.ShapeDtypeStruct((count, wide), F32),
            jax.ShapeDtypeStruct((count, wide * cols), BF16),
            jax.ShapeDtypeStruct((count, LANES), F32),
            jax.ShapeDtypeStruct((count, wide * cols), BF16),
            jax.ShapeDtypeStruct((count, LANES), F32),
        ],
        in_specs=[hbm] * (2 * EXP_FF) + [smem, vmem, vmem, vmem] + [hbm] * 6,
        out_specs=[vmem, hbm, vmem, vmem, vmem],
        scratch_shapes=[pltpu.VMEM(source.shape, source.dtype) for source in sources]
        + [
            pltpu.VMEM((rows, blocks[0].shape[1]), BF16),
            pltpu.VMEM((rows, downs[0].shape[1]), BF16),
            pltpu.VMEM((cols, count, wide), F32),
            pltpu.VMEM((cols, count, wide), BF16),
            pltpu.VMEM((count, LANES), BF16),
            pltpu.VMEM((cols - 1, count, wide), BF16),
            pltpu.VMEM((cols - 1, count, LANES), BF16),
            pltpu.VMEM((count, wide), BF16),
            pltpu.SemaphoreType.DMA((total,)),
            pltpu.SemaphoreType.DMA((total,)),
            pltpu.SemaphoreType.DMA((9,)),
        ],
        compiler_params=pltpu.CompilerParams(
            collective_id=4, has_side_effects=True, vmem_limit_bytes=48 * 2**20
        ),
    )(*blocks, *downs, adapter, norm, router, stat, *sources)


def input_back_kernel(parts_axis, cols, *refs):
    adapters, part, small_in, norm, router, stat, lows, rights = refs[:8]
    sources = refs[8:14]
    grad_inputs = refs[14]
    left_outs = refs[15:20]
    right_outs = refs[20:24]
    hidden_one, grad_whole, hidden_two, cot_whole, tokens, grad_middle = refs[24:30]
    parts, extra, parts_in, extra_in, lefts, lefts_in, rights_in, send, recv, local = refs[30:]
    row = lax.axis_index("row")
    col = lax.axis_index("col")
    count, wide = tokens.shape
    width = hidden_one.shape[1]
    depth = width // parts_axis
    right_width = rights.shape[1] // 4
    along = [opposite("col", i) for i in range(1, cols)]
    across = [opposite("row", m) for m in range(1, parts_axis)]
    greet(across + along)
    near = fetch(sources, refs[24:30], local)
    near[0].wait()
    product = jnp.zeros((count, 1), F32)
    for q in range(cols):
        value = part[:, q * wide : (q + 1) * wide]
        product += jnp.sum(
            value * hidden_one[:, q * wide : (q + 1) * wide].astype(F32), axis=1, keepdims=True
        )
        parts[q] = value.astype(BF16)
    lane = lax.broadcasted_iota(jnp.int32, (count, LANES), 1)
    columns = [*split(small_in[:, 0:1]), *split(small_in[:, 2:3]), *split(product)]
    small = jnp.where(lane < RANK, 0.0, small_in[...]) + pack(columns, range(6))
    extra[...] = small.astype(BF16)
    arrivals = []
    for i in range(1, cols):
        target = jnp.bitwise_xor(col, i)
        n = 2 * (i - 1)
        arrivals.append(remote(extra, extra_in.at[i - 1], send, recv, n + 1, along[i - 1]))
        arrivals.append(
            remote(parts.at[target], parts_in.at[i - 1], send, recv, n, along[i - 1])
        )
    base = 2 * (cols - 1)
    right_copies = [
        remote(rights, rights_in.at[m], send, recv, base + m, across[m])
        for m in range(parts_axis - 1)
    ]
    base += parts_axis - 1
    total = small
    for i in range(cols - 1):
        arrivals[2 * i].wait_recv()
        total += extra_in[i].astype(F32)
    ranks = total.astype(BF16)

    def outer(left, right):
        return lax.dot_general(
            left, right, (((0,), (0,)), ((), ())), preferred_element_type=F32
        ).astype(BF16)

    for copy in near[1:]:
        copy.wait()
    whole = outer(ranks, hidden_one[...])
    for m in range(parts_axis):
        lefts[m, : 2 * RANK] = whole[RANK : 3 * RANK, m * depth : (m + 1) * depth]
    whole = outer(lows[...], grad_whole[...])
    for m in range(parts_axis):
        lefts[m, 2 * RANK : 3 * RANK] = whole[:RANK, m * depth : (m + 1) * depth]
    whole = outer(lows[...], hidden_two[...])
    for m in range(parts_axis):
        lefts[m, 3 * RANK : 4 * RANK] = whole[RANK : 2 * RANK, m * depth : (m + 1) * depth]
    whole = outer(ranks, cot_whole[...])
    for m in range(parts_axis):
        lefts[m, 4 * RANK :] = whole[3 * RANK : 4 * RANK, m * depth : (m + 1) * depth]
    left_copies = [
        remote(
            lefts.at[jnp.bitwise_xor(row, m)],
            lefts_in.at[m - 1],
            send,
            recv,
            base + m - 1,
            across[m - 1],
        )
        for m in range(1, parts_axis)
    ]
    first = pl.multiple_of(col * wide, wide)
    grad = part[:, pl.ds(first, wide)]
    for i in range(cols - 1):
        arrivals[2 * i + 1].wait_recv()
        grad += parts_in[i].astype(F32)
    gate_grads = [total[:, 0:1] + total[:, 1:2], total[:, 2:3] + total[:, 3:4]]
    term, more = route_term(stat, gate_grads, router, first, wide)
    inner = total[:, 4:5] + total[:, 5:6] + more
    factor = stat[:, 4:5]
    grad_inputs[...] = (
        grad_middle[...]
        + factor * ((grad + term) * norm[:, pl.ds(first, wide)])
        - tokens[...].astype(F32) * (factor * factor * inner * (1.0 / width))
    )
    chosen_by = [
        [
            jnp.where(adapters[jnp.bitwise_xor(row, m)] == a, 1.0, 0.0).astype(F32)
            for a in range(ADAPT)
        ]
        for m in range(parts_axis)
    ]
    for copy in right_copies:
        copy.wait_recv()
    for p in range(4):
        here = slice(p * right_width, (p + 1) * right_width)
        values = [rights[:, here].astype(F32)] + [
            rights_in[m, :, here].astype(F32) for m in range(parts_axis - 1)
        ]
        for a in range(ADAPT):
            result = chosen_by[0][a] * values[0]
            for m in range(1, parts_axis):
                result += chosen_by[m][a] * values[m]
            right_outs[p][a] = result
    for copy in left_copies:
        copy.wait_recv()
    for p in range(5):
        here = slice(p * RANK, (p + 1) * RANK)
        values = [lefts[row, here].astype(F32)] + [
            lefts_in[m, here].astype(F32) for m in range(parts_axis - 1)
        ]
        for a in range(ADAPT):
            result = chosen_by[0][a] * values[0]
            for m in range(1, parts_axis):
                result += chosen_by[m][a] * values[m]
            left_outs[p][a] = result
    for copy in arrivals + right_copies + left_copies:
        copy.wait_send()


def input_back(adapters, part, small, norm, router, stat, lows, rights, sources, parts_axis, cols):
    hbm = pl.BlockSpec(memory_space=pl.ANY)
    vmem = pl.BlockSpec(memory_space=pltpu.VMEM)
    smem = pl.BlockSpec(memory_space=pltpu.SMEM)
    count, width = part.shape
    wide = width // cols
    depth = width // parts_axis
    right_width = rights.shape[1] // 4
    total = 2 * (cols - 1) + 2 * (parts_axis - 1)
    return pl.pallas_call(
        functools.partial(input_back_kernel, parts_axis, cols),
        out_shape=[jax.ShapeDtypeStruct((count, wide), F32)]
        + [jax.ShapeDtypeStruct((ADAPT, RANK, depth), F32)] * 5
        + [jax.ShapeDtypeStruct((ADAPT, RANK, right_width), F32)] * 4,
        in_specs=[smem] + [vmem] * 7 + [hbm] * 6,
        out_specs=[vmem] * 10,
        scratch_shapes=[pltpu.VMEM(source.shape, source.dtype) for source in sources]
        + [
            pltpu.VMEM((cols, count, wide), BF16),
            pltpu.VMEM((count, LANES), BF16),
            pltpu.VMEM((cols - 1, count, wide), BF16),
            pltpu.VMEM((cols - 1, count, LANES), BF16),
            pltpu.VMEM((parts_axis, 5 * RANK, depth), BF16),
            pltpu.VMEM((parts_axis - 1, 5 * RANK, depth), BF16),
            pltpu.VMEM((parts_axis - 1, RANK, 4 * right_width), BF16),
            pltpu.SemaphoreType.DMA((total,)),
            pltpu.SemaphoreType.DMA((total,)),
            pltpu.SemaphoreType.DMA((6,)),
        ],
        compiler_params=pltpu.CompilerParams(
            collective_id=5, has_side_effects=True, vmem_limit_bytes=48 * 2**20
        ),
    )(adapters, part, small, norm, router, stat, lows, rights, *sources)


def trade_kernel(replicas, *refs):
    count = EXP_FF - 1
    blocks, arrived = refs[:count], refs[count : 2 * count]
    send, recv = refs[2 * count :]
    across = [opposite("row", j * replicas) for j in range(1, EXP_FF)]
    greet(across)
    copies = []
    for j in (2, 1, 0):
        copy = pltpu.make_async_remote_copy(
            src_ref=blocks[j],
            dst_ref=arrived[j],
            send_sem=send.at[j],
            recv_sem=recv.at[j],
            device_id=across[j],
            device_id_type=pl.DeviceIdType.MESH,
        )
        copy.start()
        copies.append(copy)
    for copy in copies:
        copy.wait()


def trade_rows(blocks, replicas, number):
    hbm = pl.BlockSpec(memory_space=pl.ANY)
    count = EXP_FF - 1
    arrived = pl.pallas_call(
        functools.partial(trade_kernel, replicas),
        out_shape=[jax.ShapeDtypeStruct(b.shape, b.dtype) for b in blocks[1:]],
        in_specs=[hbm] * count,
        out_specs=[hbm] * count,
        scratch_shapes=[
            pltpu.SemaphoreType.DMA((count,)),
            pltpu.SemaphoreType.DMA((count,)),
        ],
        compiler_params=pltpu.CompilerParams(collective_id=number, has_side_effects=True),
    )(*blocks[1:])
    return [blocks[0], *arrived]


def ffn_kernel(parts, depth, width, units, *refs):
    hids = refs[:EXP_FF]
    cots = refs[EXP_FF : 2 * EXP_FF]
    pieces = refs[2 * EXP_FF : 2 * EXP_FF + parts]
    rights = refs[2 * EXP_FF + parts]
    outs = refs[2 * EXP_FF + parts + 1 :]
    grads = outs[:EXP_FF]
    downs = outs[EXP_FF : 2 * EXP_FF]
    adapt = outs[2 * EXP_FF : 2 * EXP_FF + 3]
    hid, cot, block, act, product, sems = outs[2 * EXP_FF + 3 :]
    row = lax.axis_index("row")
    wide = width + LANES
    copies = []
    for j in range(EXP_FF):
        where = pl.ds(j * CAP_FF, CAP_FF)
        near = hids[j].at[:, pl.ds(0, wide + LANES)]
        copies.append(pltpu.make_async_copy(near, hid.at[where], sems.at[j]))
        near = cot.at[where, pl.ds(0, width)]
        copies.append(pltpu.make_async_copy(cots[j], near, sems.at[EXP_FF + j]))
        near = cot.at[where, pl.ds(width, LANES)]
        low = hids[j].at[:, pl.ds(wide + LANES, LANES)]
        copies.append(pltpu.make_async_copy(low, near, sems.at[2 * EXP_FF + j]))
    copies.append(pltpu.make_async_copy(rights, block.at[pl.ds(width, LANES)], sems.at[3 * EXP_FF]))
    for m in range(parts):
        owner = jnp.bitwise_xor(row, m)
        where = pl.ds(pl.multiple_of(owner * depth, depth), depth)
        copies.append(pltpu.make_async_copy(pieces[m], block.at[where], sems.at[3 * EXP_FF + 1 + m]))
    for copy in copies:
        copy.start()
    for copy in copies:
        copy.wait()
    gate_scale = hid[:, wide : wide + 1].astype(F32) + hid[:, wide + 1 : wide + 2].astype(F32)
    product[...] = jnp.zeros_like(product)

    def forward(start, size):
        here = pl.ds(start, size)
        up_here = pl.ds(units + start, size)
        down_here = pl.ds(2 * units + start, size)
        gate = jnp.dot(hid[:, :wide], block[:, here], preferred_element_type=F32)
        up = jnp.dot(hid[:, :wide], block[:, up_here], preferred_element_type=F32)
        grad = jnp.dot(cot[...], block[:, down_here], preferred_element_type=F32)
        sig = 1.0 / (1.0 + jnp.exp(-gate))
        mixed = (gate * sig * up).astype(BF16)
        act[:, down_here] = mixed
        product[...] += jnp.sum(mixed.astype(F32) * grad, axis=1, keepdims=True)
        grad = grad * gate_scale
        act[:, here] = (grad * up * sig * (1.0 + gate * (1.0 - sig))).astype(BF16)
        act[:, up_here] = (grad * gate * sig).astype(BF16)

    step = 2 * LANES
    full = units // step

    @pl.loop(0, full)
    def _(i):
        forward(pl.multiple_of(i * step, step), step)

    if units % step:
        forward(full * step, units % step)

    def backward(start, size):
        here = pl.ds(start, size)
        result = lax.dot_general(
            act[:, : 2 * units], block[here, : 2 * units], (((1,), (1,)), ((), ())),
            preferred_element_type=F32,
        ).astype(BF16)
        for j in range(EXP_FF):
            grads[j][:, here] = result[j * CAP_FF : (j + 1) * CAP_FF]
        result = lax.dot_general(
            act[:, 2 * units :], block[here, 2 * units :], (((1,), (1,)), ((), ())),
            preferred_element_type=F32,
        )
        result = (result * gate_scale).astype(BF16)
        for j in range(EXP_FF):
            downs[j][:, here] = result[j * CAP_FF : (j + 1) * CAP_FF]

    full_rows = wide // step

    @pl.loop(0, full_rows)
    def _(i):
        backward(pl.multiple_of(i * step, step), step)

    if wide % step:
        backward(full_rows * step, wide % step)
    total = product[...]
    high = total.astype(BF16)
    low = (total - high.astype(F32)).astype(BF16)
    lane = lax.broadcasted_iota(jnp.int32, (EXP_FF * CAP_FF, LANES), 1)
    packed = jnp.where(lane == 0, high.astype(F32), jnp.where(lane == 1, low.astype(F32), 0.0)).astype(BF16)
    for j in range(EXP_FF):
        grads[j][:, wide:] = packed[j * CAP_FF : (j + 1) * CAP_FF]
    ext = hid[:, width:wide]
    low_ext = (cot[:, width:].astype(F32) * gate_scale).astype(BF16)
    for n, low_rows in enumerate((ext, ext, low_ext)):
        adapt[n][...] = lax.dot_general(
            low_rows,
            act[:, n * units : (n + 1) * units],
            (((0,), (0,)), ((), ())),
            preferred_element_type=F32,
        ).astype(BF16)


def feed_forward(hids, cots, pieces, rights):
    parts = len(pieces)
    depth, triple = pieces[0].shape
    units = triple // 3
    width = depth * parts
    rows = EXP_FF * CAP_FF
    hbm = pl.BlockSpec(memory_space=pl.ANY)
    vmem = pl.BlockSpec(memory_space=pltpu.VMEM)
    wide = width + LANES
    return pl.pallas_call(
        functools.partial(ffn_kernel, parts, depth, width, units),
        out_shape=[jax.ShapeDtypeStruct((CAP_FF, wide + LANES), BF16)] * EXP_FF
        + [jax.ShapeDtypeStruct((CAP_FF, wide), BF16)] * EXP_FF
        + [jax.ShapeDtypeStruct((LANES, units), BF16)] * 3,
        in_specs=[hbm] * (2 * EXP_FF + parts + 1),
        out_specs=[vmem] * (2 * EXP_FF + 3),
        scratch_shapes=[
            pltpu.VMEM((rows, wide + LANES), BF16),
            pltpu.VMEM((rows, wide), BF16),
            pltpu.VMEM((wide, triple), BF16),
            pltpu.VMEM((rows, triple), BF16),
            pltpu.VMEM((rows, 1), F32),
            pltpu.SemaphoreType.DMA((3 * EXP_FF + 1 + parts,)),
        ],
        compiler_params=pltpu.CompilerParams(vmem_limit_bytes=56 * 2**20),
    )(*hids, *cots, *pieces, rights)


def on_device(
    inputs,
    cotangent,
    lengths,
    adapter_pick,
    attn_route,
    ffn_route,
    norm_one,
    norm_two,
    router_attn,
    router_ffn,
    kv_weight,
    query_weight,
    out_weight,
    inner_weight,
    down_weight,
    query_left,
    query_right,
    kv_left,
    kv_right,
    out_left,
    out_right,
    inner_left,
    inner_right,
    down_left,
    down_right,
):
    count, slice_width = inputs.shape
    width = router_attn.shape[0]
    rows_axis = lax.axis_size("row")
    replicas = rows_axis // EXP_FF
    row = lax.axis_index("row")
    col = lax.axis_index("col")
    expert = row // replicas
    depth = inner_weight.shape[1]
    units = inner_weight.shape[3]
    length = lengths[0]
    adapter = adapter_pick[0]
    position = jnp.arange(count)
    valid = (position < length).astype(F32)
    cosine, sine = tables(count, HEAD_DIM)
    scaling = HEAD_DIM ** (-0.5)

    def swap(value, offset):
        return lax.ppermute(value, "row", [(i, i ^ offset) for i in range(rows_axis)])

    def features(part):
        return lax.all_gather(part, "col", axis=1, tiled=True)

    def partials(part):
        return lax.psum_scatter(
            part.astype(BF16), "col", scatter_dimension=1, tiled=True
        ).astype(F32)

    def own_columns(table):
        return lax.dynamic_slice_in_dim(table, col * slice_width, slice_width, 0)

    def later(value, *earlier):
        return lax.optimization_barrier((value, *earlier))[0]

    lanes = lax.broadcasted_iota(jnp.int32, (count, LANES), 1)

    def table_of(*columns):
        result = jnp.zeros((count, LANES), F32)
        for n, column in enumerate(columns):
            if column is not None:
                result = jnp.where(lanes == n, column, result)
        return result

    cols = lax.axis_size("col")
    if rows_axis == 8:
        kv_full, query_full, x_full, *cot_rows = gather_all(
            lengths, ffn_route, inputs, cotangent, [kv_weight, query_weight], rows_axis, cols, replicas
        )
    else:
        kv_full = lax.all_gather(kv_weight, "row", axis=1, tiled=True)
        query_full = lax.all_gather(query_weight, "row", axis=1, tiled=True)
        x_full = features(inputs)
        cot_rows = None
    out_full = lax.all_gather(later(out_weight, query_full), "row", axis=1, tiled=True)

    padding = -units % LANES

    def padded(value):
        return jnp.pad(value, ((0, 0), (0, padding))) if padding else value

    near = []
    for j in range(EXP_FF):
        which = expert ^ j
        inner_own = lax.dynamic_index_in_dim(inner_weight, which, 0, keepdims=False)
        down_own = lax.dynamic_index_in_dim(down_weight, which, 0, keepdims=False)
        piece = jnp.concatenate(
            [padded(inner_own[:, 0]), padded(inner_own[:, 1]), padded(down_own)], axis=1
        )
        near.append(swap(later(piece, out_full), j * replicas) if j else piece)
    chunks = []
    for j in range(EXP_FF):
        for i in range(replicas):
            chunks.append(swap(near[j], i) if i else near[j])

    picks = lax.all_gather(adapter_pick, "row", axis=0, tiled=True)
    pick_onehot = (picks[:, None] == jnp.arange(ADAPT, dtype=jnp.int32)[None, :]).astype(BF16)
    lefts_own = jnp.stack(
        [query_left, kv_left, out_left, inner_left, down_left], axis=1
    ).swapaxes(2, 3)
    lefts_sent = mm(
        "ga,ax->gx", pick_onehot, lefts_own.reshape(ADAPT, 5 * RANK * depth)
    ).astype(BF16)
    lefts = lax.all_to_all(
        lefts_sent.reshape(rows_axis, 5 * RANK, depth), "row", 0, 0, tiled=False
    )
    lefts = lefts.swapaxes(0, 1).reshape(5, RANK, width)
    left_query, left_kv, left_out, left_inner, left_down = (lefts[i] for i in range(5))
    right_query = query_right[adapter].astype(F32)
    right_kv = kv_right[adapter].astype(F32)
    right_out = out_right[adapter].astype(F32)
    right_inner_all = inner_right.reshape(ADAPT * RANK, 2, units)
    right_down_all = down_right.reshape(ADAPT * RANK, units)
    ffn_right = jnp.concatenate(
        [padded(right_inner_all[:, 0]), padded(right_inner_all[:, 1]), padded(right_down_all)],
        axis=1,
    )
    own_adapter = (jnp.arange(ADAPT, dtype=jnp.int32) == adapter).astype(F32)

    def spread(low):
        return (own_adapter[None, :, None] * low[:, None, :]).reshape(count, ADAPT * RANK)

    def unspread(high):
        return jnp.sum(
            own_adapter[None, :, None] * high.reshape(count, ADAPT, RANK), axis=1
        )

    slots_attn = slot_rows(attn_route, EXP_ATT, CAP_ATT)
    slots_ffn = slot_rows(ffn_route, EXP_FF, CAP_FF)
    rows_attn = jnp.arange(EXP_ATT * CAP_ATT, dtype=jnp.int32)
    pick_attn = [
        (rows_attn[:, None] == slots_attn[None, :, k]).astype(BF16) for k in range(TOPK)
    ]
    pick_attn_any = pick_attn[0] + pick_attn[1]
    pick_attn_both = jnp.concatenate(pick_attn, axis=1)
    order = (expert ^ jnp.arange(EXP_FF, dtype=jnp.int32))[:, None] * CAP_FF
    rows_ffn = (order + jnp.arange(CAP_FF, dtype=jnp.int32)[None, :]).reshape(EXP_FF * CAP_FF)
    pick_ffn = [(rows_ffn[:, None] == slots_ffn[None, :, k]).astype(BF16) for k in range(TOPK)]
    pick_ffn_any = pick_ffn[0] + pick_ffn[1]

    def blocks_of(rows):
        blocks = rows.reshape(EXP_FF, CAP_FF, rows.shape[1])
        return [blocks[j] for j in range(EXP_FF)]

    masked_cot = cotangent * valid.astype(BF16)[:, None]
    left_down_own = lax.dynamic_slice_in_dim(left_down, col * slice_width, slice_width, 1)
    grad_low_down_part = mm("td,rd->tr", masked_cot, left_down_own)
    if cot_rows is None:
        cot_rows = spread_cot(
            blocks_of(mm("ct,td->cd", pick_ffn_any, masked_cot).astype(BF16)), cols, replicas
        )

    x_wide = x_full.astype(F32)
    scale_one = lax.rsqrt(jnp.mean(x_wide * x_wide, axis=1, keepdims=True) + EPSILON)
    hidden_one = (x_wide * scale_one * norm_one).astype(BF16)
    chosen_attn = chosen_of(mm("td,de->te", hidden_one, router_attn), attn_route, EXP_ATT)
    gates_attn = jax.nn.softmax(chosen_attn, axis=1)
    rank_query = mm("td,rd->tr", hidden_one, left_query)
    rank_kv = mm("td,rd->tr", hidden_one, left_kv)
    kv_raw = mm("td,sdw->stw", hidden_one, kv_full) + mm(
        "tr,rsw->stw", rank_kv.astype(BF16), right_kv.astype(BF16)
    )
    query_width = kv_raw.shape[2]
    heads = query_width // HEAD_DIM
    keys = rotate(
        kv_raw[0].reshape(count, heads, HEAD_DIM), cosine[:, None], sine[:, None]
    ).astype(BF16)
    values = kv_raw[1].reshape(count, heads, HEAD_DIM).astype(BF16)
    small = jnp.concatenate([rank_query, gates_attn, cosine, sine], axis=1)
    small_rows = exact("ct,tx->cx", pick_attn_any.astype(F32), small)
    rank_query_rows = small_rows[:, :RANK]
    gate_rows = exact("ct,tx->cx", pick_attn[0].astype(F32), gates_attn[:, :1]) + exact(
        "ct,tx->cx", pick_attn[1].astype(F32), gates_attn[:, 1:]
    )
    half = HEAD_DIM // 2
    cosine_rows = small_rows[:, RANK + TOPK : RANK + TOPK + half]
    sine_rows = small_rows[:, RANK + TOPK + half :]
    hidden_rows = mm("ct,td->cd", pick_attn_any, hidden_one).astype(BF16)
    query_rows = mm(
        "ecd,edw->ecw", hidden_rows.reshape(EXP_ATT, CAP_ATT, width), query_full
    ).reshape(EXP_ATT * CAP_ATT, query_width) + mm(
        "cr,rw->cw", rank_query_rows.astype(BF16), right_query.astype(BF16)
    )
    query_rows = (
        rotate(
            query_rows.reshape(EXP_ATT * CAP_ATT, heads, HEAD_DIM),
            cosine_rows[:, None],
            sine_rows[:, None],
        )
        .astype(BF16)
        .reshape(EXP_ATT * CAP_ATT, query_width)
    )
    queries = (
        mm("cx,cw->xw", pick_attn_both, query_rows)
        .astype(BF16)
        .reshape(TOPK, count, heads, HEAD_DIM)
    )
    allowed = (position[None, :] <= position[:, None]) & (position[None, :] < length)
    scores = mm("kbhd,jhd->hkbj", queries, keys) * scaling
    scores = jnp.where(allowed[None, None], scores, -1e30)
    exponent = jnp.exp(scores - jnp.max(scores, axis=-1, keepdims=True))
    probability = exponent / jnp.sum(exponent, axis=-1, keepdims=True)
    probs = probability.astype(BF16)
    attended = mm("hkbj,jhd->kbhd", probs, values).astype(BF16).reshape(TOPK * count, query_width)
    attended_rows = mm("cx,xw->cw", pick_attn_both, attended).astype(BF16)
    out_rows = mm(
        "ecw,edw->ecd", attended_rows.reshape(EXP_ATT, CAP_ATT, query_width), out_full
    ).reshape(EXP_ATT * CAP_ATT, width)
    low_rows = mm("cw,rw->cr", attended_rows, right_out.astype(BF16))
    out_ext = (jnp.concatenate([out_rows, low_rows], axis=1) * gate_rows).astype(BF16)
    combined = mm("ct,cd->td", pick_attn_any, out_ext)
    low_out_part = combined[:, width:]
    branch_attn = combined[:, :width] + mm("tr,rd->td", low_out_part.astype(BF16), left_out)
    x_local = inputs.astype(F32)
    middle = x_local + partials(branch_attn)
    square_sum, low_out_full, grad_low_down = lax.psum(
        (jnp.sum(middle * middle, axis=1), low_out_part, grad_low_down_part), "col"
    )
    scale_two = lax.rsqrt(square_sum[:, None] / width + EPSILON)
    hidden_two = features((middle * scale_two * own_columns(norm_two)).astype(BF16))

    chosen_ffn = chosen_of(mm("td,de->te", hidden_two, router_ffn), ffn_route, EXP_FF)
    gates_ffn = jax.nn.softmax(chosen_ffn, axis=1)
    rank_inner = mm("td,rd->tr", hidden_two, left_inner)
    hidden_ext = jnp.concatenate([hidden_two, spread(rank_inner).astype(BF16)], axis=1)
    hidden_out = mm("ct,td->cd", pick_ffn_any, hidden_ext).astype(BF16)
    gate_high = lax.reduce_precision(gates_ffn, 8, 7)
    gate_low = (gates_ffn - gate_high).astype(BF16)
    gate_high = gate_high.astype(BF16)
    gate_out = sum(
        mm("ct,tx->cx", pick_ffn[k], jnp.stack([gate_high[:, k], gate_low[:, k]], axis=1))
        for k in range(TOPK)
    )
    gate_out = jnp.pad(gate_out, ((0, 0), (0, 126))).astype(BF16)
    cot_ext = mm("ct,td->cd", pick_ffn_any, spread(grad_low_down).astype(BF16)).astype(BF16)
    hidden_in = trade_rows(
        blocks_of(jnp.concatenate([hidden_out, gate_out, cot_ext], axis=1)), replicas, 3
    )
    results = feed_forward(hidden_in, cot_rows, chunks, ffn_right)
    grad_middle, grad_full, totals, branch_ffn, low_down_part = middle_back(
        results[:EXP_FF],
        results[EXP_FF : 2 * EXP_FF],
        adapter_pick,
        norm_two[None, :],
        router_ffn.T,
        table_of(
            gates_ffn[:, 0:1],
            gates_ffn[:, 1:2],
            chosen_ffn[:, 0:1],
            chosen_ffn[:, 1:2],
            scale_two,
            ffn_route[:, 0:1].astype(F32),
            ffn_route[:, 1:2].astype(F32),
            valid[:, None],
        ),
        [pick_ffn[0], pick_ffn[1], lefts.reshape(5 * RANK, width), hidden_two, middle, cotangent],
        cols,
        replicas,
    )
    rights_ffn = lax.optimization_barrier(lax.psum(tuple(results[2 * EXP_FF :]), "row"))
    rights_ffn = [
        value[:, :units].reshape(ADAPT, RANK, units).astype(F32) for value in rights_ffn
    ]

    output = ((middle + partials(branch_ffn)) * valid[:, None]).astype(BF16)

    grad_low_out = mm("td,rd->tr", grad_full, left_out)
    grad_middle_rows = mm("ct,td->cd", pick_attn_any, grad_full).astype(BF16)
    grad_low_rows = mm("ct,tr->cr", pick_attn_any, grad_low_out.astype(BF16)).astype(BF16)
    grad_att_rows = mm(
        "ecd,edw->ecw", grad_middle_rows.reshape(EXP_ATT, CAP_ATT, width), out_full
    ).reshape(EXP_ATT * CAP_ATT, query_width) + mm(
        "cr,rw->cw", grad_low_rows, right_out.astype(BF16)
    )
    gg_attn_rows = jnp.sum(attended_rows.astype(F32) * grad_att_rows, axis=1, keepdims=True)
    grad_gates_attn_part = jnp.concatenate(
        [exact("ct,cx->tx", pick_attn[k].astype(F32), gg_attn_rows) for k in range(TOPK)], axis=1
    )
    grad_att_rows = (grad_att_rows * gate_rows).astype(BF16)
    grad_attended = (
        mm("cx,cw->xw", pick_attn_both, grad_att_rows)
        .astype(BF16)
        .reshape(TOPK, count, heads, HEAD_DIM)
    )
    gated_low = (gates_attn.T[:, :, None] * grad_low_out[None]).reshape(TOPK * count, RANK)
    grad_right_out = mm("xr,xw->rw", gated_low.astype(BF16), attended)
    grad_prob = mm("kbhd,jhd->hkbj", grad_attended, values)
    centre = jnp.sum(probability * grad_prob, axis=-1, keepdims=True)
    grad_scores = (probability * (grad_prob - centre)).astype(BF16)
    grad_queries = mm("hkbj,jhd->kbhd", grad_scores, keys) * scaling
    grad_keys = mm("hkbj,kbhd->jhd", grad_scores, queries) * scaling
    grad_values = mm("hkbj,kbhd->jhd", probs, grad_attended)
    grad_query_raw = (
        rotate(grad_queries, cosine[None, :, None], -sine[None, :, None])
        .astype(BF16)
        .reshape(TOPK * count, query_width)
    )
    grad_key_raw = rotate(grad_keys, cosine[:, None], -sine[:, None])
    grad_kv = jnp.stack([grad_key_raw, grad_values]).astype(BF16).reshape(2, count, query_width)
    grad_query_rows = mm("cx,xw->cw", pick_attn_both, grad_query_raw).astype(BF16)
    grad_one_rows = (
        mm("ecw,edw->ecd", grad_query_rows.reshape(EXP_ATT, CAP_ATT, query_width), query_full)
        .astype(BF16)
        .reshape(EXP_ATT * CAP_ATT, width)
    )
    grad_query_sum = jnp.sum(
        grad_query_raw.astype(F32).reshape(TOPK, count, query_width), axis=0
    )
    grad_query_sum_low = grad_query_sum.astype(BF16)
    grad_rank_query = mm("tw,rw->tr", grad_query_sum_low, right_query.astype(BF16))
    grad_rank_kv = mm("stw,rsw->tr", grad_kv, right_kv.astype(BF16))
    grad_one_part = (
        mm("ct,cd->td", pick_attn_any, grad_one_rows)
        + mm("stw,sdw->td", grad_kv, kv_full)
        + mm(
            "tr,rd->td",
            jnp.concatenate([grad_rank_query, grad_rank_kv], axis=1).astype(BF16),
            jnp.concatenate([left_query, left_kv], axis=0),
        )
    )
    grad_right_query = mm("tr,tw->rw", rank_query.astype(BF16), grad_query_sum_low)
    grad_right_kv = mm("tr,stw->rsw", rank_kv.astype(BF16), grad_kv)
    cot_full = features(masked_cot)
    small = table_of(grad_gates_attn_part[:, 0:1], None, grad_gates_attn_part[:, 1:2])
    small += jnp.pad(
        jnp.concatenate([grad_rank_query, grad_rank_kv, low_down_part[:, RANK : 2 * RANK]], axis=1),
        ((0, 0), (RANK, LANES - 4 * RANK)),
    )
    lows = (jnp.pad(low_out_full, ((0, 0), (0, LANES - RANK))) + jnp.where(
        (lanes >= RANK) & (lanes < 2 * RANK), totals, 0.0
    )).astype(BF16)
    right_parts = jnp.concatenate(
        [grad_right_query, grad_right_kv[:, 0], grad_right_kv[:, 1], grad_right_out], axis=1
    ).astype(BF16)
    grad_inputs, *grads = input_back(
        picks,
        grad_one_part,
        small,
        norm_one[None, :],
        router_attn.T,
        table_of(
            gates_attn[:, 0:1],
            gates_attn[:, 1:2],
            chosen_attn[:, 0:1],
            chosen_attn[:, 1:2],
            scale_one,
            attn_route[:, 0:1].astype(F32),
            attn_route[:, 1:2].astype(F32),
        ),
        lows,
        right_parts,
        [hidden_one, grad_full, hidden_two, cot_full, inputs, grad_middle],
        rows_axis,
        cols,
    )
    lefts_back = [grad.swapaxes(1, 2) for grad in grads[:5]]
    rights_back = grads[5:]
    return (
        output,
        grad_inputs,
        lefts_back[0],
        rights_back[0],
        lefts_back[1],
        jnp.stack(rights_back[1:3], axis=2),
        lefts_back[2],
        rights_back[3],
        lefts_back[3],
        jnp.stack(rights_ffn[:2], axis=2),
        lefts_back[4],
        rights_ffn[2],
    )


def solution(mesh):
    placed = (
        P("row", "col"),
        P("row", "col"),
        P("row"),
        P("row"),
        P("row", None),
        P("row", None),
        P(),
        P(),
        P(),
        P(),
        P(None, "row", "col"),
        P(None, "row", "col"),
        P(None, "row", "col"),
        P(None, "row", None, "col"),
        P(None, "row", "col"),
        P(None, "row", None),
        P(None, None, "col"),
        P(None, "row", None),
        P(None, None, None, "col"),
        P(None, "row", None),
        P(None, None, "col"),
        P(None, "row", None),
        P(None, None, None, "col"),
        P(None, "row", None),
        P(None, None, "col"),
    )
    return jax.shard_map(
        on_device,
        mesh=mesh,
        in_specs=placed,
        out_specs=(
            P("row", "col"),
            P("row", "col"),
            P(None, "row", None),
            P(None, None, "col"),
            P(None, "row", None),
            P(None, None, None, "col"),
            P(None, "row", None),
            P(None, None, "col"),
            P(None, "row", None),
            P(None, None, None, "col"),
            P(None, "row", None),
            P(None, None, "col"),
        ),
        check_vma=False,
    )
```

```python
import functools

import jax
import jax.numpy as jnp
from jax import lax
from jax.experimental import pallas as pl
from jax.experimental.pallas import tpu as pltpu
from jax.sharding import PartitionSpec as P

HEAD_DIM = 128
EXP_ATT = 8
EXP_FF = 4
TOPK = 2
ADAPT = 8
RANK = 16
CAP_ATT = 80
CAP_FF = 160
EPSILON = 1e-06
ROPE_BASE = 10000.0
HIGHEST = lax.Precision.HIGHEST
F32 = jnp.float32
BF16 = jnp.bfloat16
LANES = 128


def mm(spec, a, b):
    return jnp.einsum(spec, a, b, preferred_element_type=F32)


def exact(spec, a, b):
    return jnp.einsum(spec, a, b, precision=HIGHEST, preferred_element_type=F32)


def tables(count, head_width):
    position = jnp.arange(count).astype(F32)
    frequency = ROPE_BASE ** (-jnp.arange(head_width // 2).astype(F32) * 2.0 / head_width)
    angle = position[:, None] * frequency[None, :]
    return (jnp.cos(angle), jnp.sin(angle))


def rotate(values, cosine, sine):
    half = values.shape[-1] // 2
    first = values[..., :half]
    second = values[..., half:]
    return jnp.concatenate(
        [first * cosine - second * sine, second * cosine + first * sine], axis=-1
    )


def slot_rows(route, experts, capacity):
    count = route.shape[0]
    chosen = (route[:, :, None] == jnp.arange(experts, dtype=jnp.int32)).astype(BF16)
    per_token = jnp.sum(chosen, axis=1)
    place = jnp.arange(count)
    before = (place[None, :] < place[:, None]).astype(BF16)
    earlier = mm("tu,ue->te", before, per_token)
    inside = jnp.stack([jnp.zeros_like(chosen[:, 0]), chosen[:, 0]], axis=1).astype(F32)
    position = jnp.sum((earlier[:, None, :] + inside) * chosen.astype(F32), axis=2)
    return route * capacity + position.astype(jnp.int32)


def chosen_of(logits, route, experts):
    onehot = (route[:, :, None] == jnp.arange(experts, dtype=jnp.int32)).astype(F32)
    return jnp.sum(onehot * logits[:, None, :], axis=2)


def opposite(axis, offset):
    index = jnp.bitwise_xor(lax.axis_index(axis), offset)
    if axis == "row":
        return (index, lax.axis_index("col"))
    return (lax.axis_index("row"), index)


def greet(partners):
    barrier = pltpu.get_barrier_semaphore()
    for partner in partners:
        pl.semaphore_signal(
            barrier, inc=1, device_id=partner, device_id_type=pl.DeviceIdType.MESH
        )
    pl.semaphore_wait(barrier, len(partners))


def dispatch_matrix(route, flip, experts, capacity):
    count = route.shape[0]
    lane = lax.broadcasted_iota(jnp.int32, (count, LANES), 1)
    chosen = [(route[:, k : k + 1] == lane).astype(F32) for k in range(TOPK)]
    place = lax.broadcasted_iota(jnp.int32, (count, count), 0)
    other = lax.broadcasted_iota(jnp.int32, (count, count), 1)
    before = (other < place).astype(F32).astype(BF16)
    earlier = jnp.dot(
        before, (chosen[0] + chosen[1]).astype(BF16), preferred_element_type=F32
    )
    rows = lax.broadcasted_iota(jnp.int32, (count, experts * capacity), 1)
    result = None
    for k in range(TOPK):
        position = jnp.sum(earlier * chosen[k], axis=1, keepdims=True).astype(jnp.int32)
        mine = jnp.bitwise_xor(route[:, k : k + 1], flip) * capacity + position
        found = (rows == mine).astype(F32)
        result = found if result is None else result + found
    return result.astype(BF16)


def gather_kernel(parts, cols, replicas, counts, *refs):
    n_blocks = len(counts)
    lengths, route, tokens, cot = refs[:4]
    blocks = refs[4 : 4 + n_blocks]
    outs = refs[4 + n_blocks :]
    wholes = outs[:n_blocks]
    tokens_whole = outs[n_blocks]
    cot_wholes = outs[n_blocks + 1 : n_blocks + 1 + EXP_FF]
    own_rows, landed, send, recv, local = outs[n_blocks + 1 + EXP_FF :]
    row = lax.axis_index("row")
    col = lax.axis_index("col")
    depth = blocks[0].shape[1]
    count, wide = tokens.shape
    partners = {offset: opposite("row", offset) for offset in (1, 2, 4)}
    along = [opposite("col", i) for i in range(1, cols)]
    greet(list(partners.values()) + [opposite("row", 6)] + along)
    chunks = [(a, i) for a, number in enumerate(counts) for i in range(number)]
    used = [0]
    started = []
    received = set()
    kept = []
    here = pl.ds(pl.multiple_of(col * wide, wide), wide)

    def send_to(source, target, device):
        n = used[0]
        used[0] += 1
        copy = pltpu.make_async_remote_copy(
            src_ref=source,
            dst_ref=target,
            send_sem=send.at[n],
            recv_sem=recv.at[n],
            device_id=device,
            device_id_type=pl.DeviceIdType.MESH,
        )
        copy.start()
        started.append(copy)
        return copy

    def arrive(copy):
        copy.wait_recv()
        received.add(id(copy))

    def keep(source, target):
        copy = pltpu.make_async_copy(source, target, local.at[len(kept)])
        copy.start()
        kept.append(copy)

    def place(chunk, offset):
        array, i = chunk
        owner = jnp.bitwise_xor(row, offset)
        return wholes[array].at[i, pl.ds(pl.multiple_of(owner * depth, depth), depth)]

    def push(source, chunk, target, offset):
        return send_to(source, place(chunk, offset), partners[target])

    for device in along:
        send_to(tokens, tokens_whole.at[:, here], device)
    keep(tokens, tokens_whole.at[:, here])
    first = {}
    for number, chunk in enumerate(chunks):
        source = blocks[chunk[0]].at[chunk[1]]
        for target in (2, 4):
            first[number, target] = push(source, chunk, target, 0)
    for a in range(n_blocks):
        where = pl.ds(pl.multiple_of(row * depth, depth), depth)
        keep(blocks[a], wholes[a].at[:, where])
    for chunk in chunks:
        push(blocks[chunk[0]].at[chunk[1]], chunk, 1, 0)
    valid = lax.broadcasted_iota(jnp.int32, (count, 1), 0) < lengths[0]
    matrix = dispatch_matrix(route[...], row // replicas, EXP_FF, CAP_FF)
    masked = jnp.where(valid, cot[...].astype(F32), 0.0).astype(BF16)
    dispatched = lax.dot_general(
        matrix, masked, (((0,), (0,)), ((), ())), preferred_element_type=F32
    ).astype(BF16)
    for j in range(EXP_FF):
        own_rows[j] = dispatched[j * CAP_FF : (j + 1) * CAP_FF]
    traded = [
        send_to(own_rows.at[j], landed.at[j - 1], opposite("row", j * replicas))
        for j in range(1, EXP_FF)
    ]
    for j in range(EXP_FF):
        if j:
            arrive(traded[j - 1])
            source = landed.at[j - 1]
        else:
            source = own_rows.at[0]
        keep(source, cot_wholes[j].at[:, here])
        for device in along:
            send_to(source, cot_wholes[j].at[:, here], device)
    relayed = []
    for number, chunk in enumerate(chunks):
        arrive(first[number, 2])
        arrive(first[number, 4])
        if number % 2 == 0:
            relayed.append(push(place(chunk, 2), chunk, 4, 2))
        else:
            relayed.append(push(place(chunk, 4), chunk, 2, 4))
        for offset in (2, 4):
            push(place(chunk, offset), chunk, 1, offset)
    for number, chunk in enumerate(chunks):
        arrive(relayed[number])
        push(place(chunk, 6), chunk, 1, 6)
    for copy in started:
        if id(copy) not in received:
            copy.wait_recv()
    for copy in started:
        copy.wait_send()
    for copy in kept:
        copy.wait()


def gather_all(lengths, route, tokens, cot, blocks, parts, cols, replicas):
    counts = [block.shape[0] for block in blocks]
    hbm = pl.BlockSpec(memory_space=pl.ANY)
    vmem = pl.BlockSpec(memory_space=pltpu.VMEM)
    smem = pl.BlockSpec(memory_space=pltpu.SMEM)
    count, wide = tokens.shape
    remote = 7 * sum(counts) + (cols - 1) * (1 + EXP_FF) + EXP_FF - 1
    return pl.pallas_call(
        functools.partial(gather_kernel, parts, cols, replicas, counts),
        out_shape=[
            jax.ShapeDtypeStruct((b.shape[0], b.shape[1] * parts, b.shape[2]), b.dtype)
            for b in blocks
        ]
        + [jax.ShapeDtypeStruct((count, wide * cols), tokens.dtype)]
        + [jax.ShapeDtypeStruct((CAP_FF, wide * cols), BF16)] * EXP_FF,
        in_specs=[smem, vmem, hbm, vmem] + [hbm] * len(blocks),
        out_specs=[hbm] * (len(blocks) + 1 + EXP_FF),
        scratch_shapes=[
            pltpu.VMEM((EXP_FF, CAP_FF, wide), BF16),
            pltpu.VMEM((EXP_FF - 1, CAP_FF, wide), BF16),
            pltpu.SemaphoreType.DMA((remote,)),
            pltpu.SemaphoreType.DMA((remote,)),
            pltpu.SemaphoreType.DMA((1 + EXP_FF + len(blocks),)),
        ],
        compiler_params=pltpu.CompilerParams(collective_id=1, has_side_effects=True),
    )(lengths, route, tokens, cot, *blocks)


def cot_kernel(cols, replicas, *refs):
    blocks, wholes = refs[:EXP_FF], refs[EXP_FF : 2 * EXP_FF]
    landed, send, recv, local = refs[2 * EXP_FF :]
    col = lax.axis_index("col")
    wide = blocks[0].shape[1]
    here = pl.ds(pl.multiple_of(col * wide, wide), wide)
    along = [opposite("col", i) for i in range(1, cols)]
    across = [opposite("row", j * replicas) for j in range(1, EXP_FF)]
    greet(along + across)
    copies = []

    def push(source, target, n, device):
        copy = pltpu.make_async_remote_copy(
            src_ref=source,
            dst_ref=target,
            send_sem=send.at[n],
            recv_sem=recv.at[n],
            device_id=device,
            device_id_type=pl.DeviceIdType.MESH,
        )
        copy.start()
        copies.append(copy)
        return copy

    def keep(source, target, n):
        copy = pltpu.make_async_copy(source, target, local.at[n])
        copy.start()
        return copy

    first = [
        push(blocks[j], landed.at[j - 1], j - 1, across[j - 1]) for j in range(1, EXP_FF)
    ]
    base = EXP_FF - 1
    kept = []
    for j in range(EXP_FF):
        if j:
            first[j - 1].wait_recv()
            source = landed.at[j - 1]
        else:
            source = blocks[0]
        kept.append(keep(source, wholes[j].at[:, here], j))
        for i in range(cols - 1):
            push(source, wholes[j].at[:, here], base + j * (cols - 1) + i, along[i])
    for copy in copies[EXP_FF - 1 :]:
        copy.wait_recv()
    for copy in copies:
        copy.wait_send()
    for copy in kept:
        copy.wait()


def spread_cot(blocks, cols, replicas):
    hbm = pl.BlockSpec(memory_space=pl.ANY)
    wide = blocks[0].shape[1]
    remote = EXP_FF - 1 + EXP_FF * (cols - 1)
    return pl.pallas_call(
        functools.partial(cot_kernel, cols, replicas),
        out_shape=[jax.ShapeDtypeStruct((CAP_FF, wide * cols), BF16)] * EXP_FF,
        in_specs=[hbm] * EXP_FF,
        out_specs=[hbm] * EXP_FF,
        scratch_shapes=[
            pltpu.VMEM((EXP_FF - 1, CAP_FF, wide), BF16),
            pltpu.SemaphoreType.DMA((remote,)),
            pltpu.SemaphoreType.DMA((remote,)),
            pltpu.SemaphoreType.DMA((EXP_FF,)),
        ],
        compiler_params=pltpu.CompilerParams(collective_id=2, has_side_effects=True),
    )(*blocks)


def split(value):
    high = value.astype(BF16).astype(F32)
    return high, value - high


def pack(columns, lanes):
    lane = lax.broadcasted_iota(jnp.int32, (columns[0].shape[0], LANES), 1)
    result = jnp.zeros((columns[0].shape[0], LANES), F32)
    for column, n in zip(columns, lanes):
        result = jnp.where(lane == n, column, result)
    return result


def route_term(stat, grads, router, start, size):
    gates = [stat[:, k : k + 1] for k in range(TOPK)]
    mean = gates[0] * grads[0] + gates[1] * grads[1]
    product = 0.0
    term = 0.0
    weights = [gates[k] * (grads[k] - mean) for k in range(TOPK)]
    for k in range(TOPK):
        product += weights[k] * stat[:, 2 + k : 3 + k]
    for e in range(router.shape[0]):
        weight = 0.0
        for k in range(TOPK):
            weight += jnp.where(stat[:, 5 + k : 6 + k] == float(e), weights[k], 0.0)
        term += weight * router[e : e + 1, pl.ds(start, size)].astype(F32)
    return term, product


def fetch(sources, targets, sems):
    copies = []
    for n, (source, target) in enumerate(zip(sources, targets)):
        copies.append(pltpu.make_async_copy(source, target, sems.at[n]))
        copies[-1].start()
    return copies


def remote(source, target, send, recv, n, device):
    copy = pltpu.make_async_remote_copy(
        src_ref=source,
        dst_ref=target,
        send_sem=send.at[n],
        recv_sem=recv.at[n],
        device_id=device,
        device_id_type=pl.DeviceIdType.MESH,
    )
    copy.start()
    return copy


def middle_back_kernel(cols, replicas, *refs):
    blocks, downs = refs[:EXP_FF], refs[EXP_FF : 2 * EXP_FF]
    adapter, norm, router, stat = refs[2 * EXP_FF : 2 * EXP_FF + 4]
    sources = refs[2 * EXP_FF + 4 : 2 * EXP_FF + 10]
    grad_middle, grad_whole, totals, branch, low_down = refs[2 * EXP_FF + 10 : 2 * EXP_FF + 15]
    scratch = refs[2 * EXP_FF + 15 :]
    pick_0, pick_1, lefts, hidden, middle, cot = scratch[:6]
    rows, down_rows, exact_part, parts, extra, parts_in, extra_in, low, send, recv, local = (
        scratch[6:]
    )
    col = lax.axis_index("col")
    count, wide = middle.shape
    width = hidden.shape[1]
    across = [opposite("row", j * replicas) for j in range(1, EXP_FF)]
    along = [opposite("col", i) for i in range(1, cols)]
    greet(across + along)
    copies = [
        remote(
            blocks[j], rows.at[pl.ds(j * CAP_FF, CAP_FF)], send, recv, j - 1, across[j - 1]
        )
        for j in range(1, EXP_FF)
    ]
    near = fetch(
        [blocks[0], downs[0], *sources],
        [rows.at[pl.ds(0, CAP_FF)], down_rows.at[pl.ds(0, CAP_FF)], *scratch[:6]],
        local,
    )
    for copy in near:
        copy.wait()
    for copy in copies:
        copy.wait_recv()
    base = EXP_FF - 1
    down_copies = [
        remote(
            downs[j],
            down_rows.at[pl.ds(j * CAP_FF, CAP_FF)],
            send,
            recv,
            base + j - 1,
            across[j - 1],
        )
        for j in range(1, EXP_FF)
    ]
    picks = [pick_0[...], pick_1[...]]
    any_pick = picks[0] + picks[1]

    def back(pick, source, start, size):
        return lax.dot_general(
            pick,
            source[:, start : start + size],
            (((0,), (0,)), ((), ())),
            preferred_element_type=F32,
        )

    sub = lax.broadcasted_iota(jnp.int32, (LANES, LANES), 0)
    lane = lax.broadcasted_iota(jnp.int32, (LANES, LANES), 1)
    mine = lax.broadcasted_iota(jnp.int32, (count, LANES), 1) // RANK == adapter[0]
    place_rank = (lane == RANK + sub % RANK).astype(F32).astype(BF16)

    def own_rank(value):
        value = jnp.where(mine, value, 0.0).astype(BF16)
        return jnp.dot(value, place_rank, preferred_element_type=F32)

    gate_grads = []
    for k in range(TOPK):
        pair = back(picks[k], rows, width + LANES, LANES)
        gate_grads.append(pair[:, 0:1] + pair[:, 1:2])
    rank = own_rank(back(any_pick, rows, width, LANES))
    rank_low = rank[:, RANK : 2 * RANK].astype(BF16)
    product = jnp.zeros((count, 1), F32)
    for q in range(cols):
        here = slice(q * wide, (q + 1) * wide)
        part = back(any_pick, rows, q * wide, wide) + jnp.dot(
            rank_low, lefts[3 * RANK : 4 * RANK, here], preferred_element_type=F32
        )
        product += jnp.sum(part * hidden[:, here].astype(F32), axis=1, keepdims=True)
        exact_part[q] = part
        parts[q] = part.astype(BF16)
    columns = [*split(gate_grads[0]), *split(gate_grads[1]), *split(product)]
    small = pack(columns, range(6)) + rank
    extra[...] = small.astype(BF16)
    base += EXP_FF - 1
    arrivals = []
    for i in range(1, cols):
        target = jnp.bitwise_xor(col, i)
        n = base + 2 * (i - 1)
        arrivals.append(remote(extra, extra_in.at[i - 1], send, recv, n + 1, along[i - 1]))
        arrivals.append(
            remote(parts.at[target], parts_in.at[i - 1], send, recv, n, along[i - 1])
        )
    for copy in arrivals:
        copy.wait_recv()
    grad = exact_part[col]
    total = small
    for i in range(cols - 1):
        grad += parts_in[i].astype(F32)
        total += extra_in[i].astype(F32)
    totals[...] = total
    gate_grads = [total[:, 0:1] + total[:, 1:2], total[:, 2:3] + total[:, 3:4]]
    first = pl.multiple_of(col * wide, wide)
    term, more = route_term(stat, gate_grads, router, first, wide)
    inner = total[:, 4:5] + total[:, 5:6] + more
    scaled = (grad + term) * norm[:, pl.ds(first, wide)]
    factor = stat[:, 4:5]
    valid = stat[:, 7:8]
    result = (
        cot[...].astype(F32) * valid
        + factor * scaled
        - middle[...] * (factor * factor * inner * (1.0 / width))
    )
    grad_middle[...] = result
    low[...] = result.astype(BF16)
    here = pl.ds(first, wide)
    kept = pltpu.make_async_copy(low, grad_whole.at[:, here], local.at[8])
    kept.start()
    base += 2 * (cols - 1)
    last = [
        remote(low, grad_whole.at[:, here], send, recv, base + i, along[i])
        for i in range(cols - 1)
    ]
    for copy in down_copies:
        copy.wait_recv()
    rank = own_rank(back(any_pick, down_rows, width, LANES))
    rank_low = rank[:, RANK : 2 * RANK].astype(BF16)
    low_down[...] = rank
    for q in range(cols):
        here = slice(q * wide, (q + 1) * wide)
        part = back(any_pick, down_rows, q * wide, wide) + jnp.dot(
            rank_low, lefts[4 * RANK : 5 * RANK, here], preferred_element_type=F32
        )
        branch[:, here] = part.astype(BF16)
    for copy in last:
        copy.wait_recv()
    for copy in copies + down_copies + arrivals + last:
        copy.wait_send()
    kept.wait()


def middle_back(blocks, downs, adapter, norm, router, stat, sources, cols, replicas):
    hbm = pl.BlockSpec(memory_space=pl.ANY)
    vmem = pl.BlockSpec(memory_space=pltpu.VMEM)
    smem = pl.BlockSpec(memory_space=pltpu.SMEM)
    count, wide = sources[-1].shape
    total = 2 * (EXP_FF - 1) + 3 * (cols - 1)
    rows = EXP_FF * CAP_FF
    return pl.pallas_call(
        functools.partial(middle_back_kernel, cols, replicas),
        out_shape=[
            jax.ShapeDtypeStruct((count, wide), F32),
            jax.ShapeDtypeStruct((count, wide * cols), BF16),
            jax.ShapeDtypeStruct((count, LANES), F32),
            jax.ShapeDtypeStruct((count, wide * cols), BF16),
            jax.ShapeDtypeStruct((count, LANES), F32),
        ],
        in_specs=[hbm] * (2 * EXP_FF) + [smem, vmem, vmem, vmem] + [hbm] * 6,
        out_specs=[vmem, hbm, vmem, vmem, vmem],
        scratch_shapes=[pltpu.VMEM(source.shape, source.dtype) for source in sources]
        + [
            pltpu.VMEM((rows, blocks[0].shape[1]), BF16),
            pltpu.VMEM((rows, downs[0].shape[1]), BF16),
            pltpu.VMEM((cols, count, wide), F32),
            pltpu.VMEM((cols, count, wide), BF16),
            pltpu.VMEM((count, LANES), BF16),
            pltpu.VMEM((cols - 1, count, wide), BF16),
            pltpu.VMEM((cols - 1, count, LANES), BF16),
            pltpu.VMEM((count, wide), BF16),
            pltpu.SemaphoreType.DMA((total,)),
            pltpu.SemaphoreType.DMA((total,)),
            pltpu.SemaphoreType.DMA((9,)),
        ],
        compiler_params=pltpu.CompilerParams(
            collective_id=4, has_side_effects=True, vmem_limit_bytes=48 * 2**20
        ),
    )(*blocks, *downs, adapter, norm, router, stat, *sources)


def input_back_kernel(parts_axis, cols, *refs):
    adapters, part, small_in, norm, router, stat, lows, rights = refs[:8]
    sources = refs[8:14]
    grad_inputs = refs[14]
    left_outs = refs[15:20]
    right_outs = refs[20:24]
    hidden_one, grad_whole, hidden_two, cot_whole, tokens, grad_middle = refs[24:30]
    parts, extra, parts_in, extra_in, lefts, lefts_in, rights_in, send, recv, local = refs[30:]
    row = lax.axis_index("row")
    col = lax.axis_index("col")
    count, wide = tokens.shape
    width = hidden_one.shape[1]
    depth = width // parts_axis
    right_width = rights.shape[1] // 4
    along = [opposite("col", i) for i in range(1, cols)]
    across = [opposite("row", m) for m in range(1, parts_axis)]
    greet(across + along)
    near = fetch(sources, refs[24:30], local)
    near[0].wait()
    product = jnp.zeros((count, 1), F32)
    for q in range(cols):
        value = part[:, q * wide : (q + 1) * wide]
        product += jnp.sum(
            value * hidden_one[:, q * wide : (q + 1) * wide].astype(F32), axis=1, keepdims=True
        )
        parts[q] = value.astype(BF16)
    lane = lax.broadcasted_iota(jnp.int32, (count, LANES), 1)
    columns = [*split(small_in[:, 0:1]), *split(small_in[:, 2:3]), *split(product)]
    small = jnp.where(lane < RANK, 0.0, small_in[...]) + pack(columns, range(6))
    extra[...] = small.astype(BF16)
    arrivals = []
    for i in range(1, cols):
        target = jnp.bitwise_xor(col, i)
        n = 2 * (i - 1)
        arrivals.append(remote(extra, extra_in.at[i - 1], send, recv, n + 1, along[i - 1]))
        arrivals.append(
            remote(parts.at[target], parts_in.at[i - 1], send, recv, n, along[i - 1])
        )
    base = 2 * (cols - 1)
    right_copies = [
        remote(rights, rights_in.at[m], send, recv, base + m, across[m])
        for m in range(parts_axis - 1)
    ]
    base += parts_axis - 1
    total = small
    for i in range(cols - 1):
        arrivals[2 * i].wait_recv()
        total += extra_in[i].astype(F32)
    ranks = total.astype(BF16)

    def outer(left, right):
        return lax.dot_general(
            left, right, (((0,), (0,)), ((), ())), preferred_element_type=F32
        ).astype(BF16)

    for copy in near[1:]:
        copy.wait()
    whole = outer(ranks, hidden_one[...])
    for m in range(parts_axis):
        lefts[m, : 2 * RANK] = whole[RANK : 3 * RANK, m * depth : (m + 1) * depth]
    whole = outer(lows[...], grad_whole[...])
    for m in range(parts_axis):
        lefts[m, 2 * RANK : 3 * RANK] = whole[:RANK, m * depth : (m + 1) * depth]
    whole = outer(lows[...], hidden_two[...])
    for m in range(parts_axis):
        lefts[m, 3 * RANK : 4 * RANK] = whole[RANK : 2 * RANK, m * depth : (m + 1) * depth]
    whole = outer(ranks, cot_whole[...])
    for m in range(parts_axis):
        lefts[m, 4 * RANK :] = whole[3 * RANK : 4 * RANK, m * depth : (m + 1) * depth]
    left_copies = [
        remote(
            lefts.at[jnp.bitwise_xor(row, m)],
            lefts_in.at[m - 1],
            send,
            recv,
            base + m - 1,
            across[m - 1],
        )
        for m in range(1, parts_axis)
    ]
    first = pl.multiple_of(col * wide, wide)
    grad = part[:, pl.ds(first, wide)]
    for i in range(cols - 1):
        arrivals[2 * i + 1].wait_recv()
        grad += parts_in[i].astype(F32)
    gate_grads = [total[:, 0:1] + total[:, 1:2], total[:, 2:3] + total[:, 3:4]]
    term, more = route_term(stat, gate_grads, router, first, wide)
    inner = total[:, 4:5] + total[:, 5:6] + more
    factor = stat[:, 4:5]
    grad_inputs[...] = (
        grad_middle[...]
        + factor * ((grad + term) * norm[:, pl.ds(first, wide)])
        - tokens[...].astype(F32) * (factor * factor * inner * (1.0 / width))
    )
    chosen_by = [
        [
            jnp.where(adapters[jnp.bitwise_xor(row, m)] == a, 1.0, 0.0).astype(F32)
            for a in range(ADAPT)
        ]
        for m in range(parts_axis)
    ]
    for copy in right_copies:
        copy.wait_recv()
    for p in range(4):
        here = slice(p * right_width, (p + 1) * right_width)
        values = [rights[:, here].astype(F32)] + [
            rights_in[m, :, here].astype(F32) for m in range(parts_axis - 1)
        ]
        for a in range(ADAPT):
            result = chosen_by[0][a] * values[0]
            for m in range(1, parts_axis):
                result += chosen_by[m][a] * values[m]
            right_outs[p][a] = result
    for copy in left_copies:
        copy.wait_recv()
    for p in range(5):
        here = slice(p * RANK, (p + 1) * RANK)
        values = [lefts[row, here].astype(F32)] + [
            lefts_in[m, here].astype(F32) for m in range(parts_axis - 1)
        ]
        for a in range(ADAPT):
            result = chosen_by[0][a] * values[0]
            for m in range(1, parts_axis):
                result += chosen_by[m][a] * values[m]
            left_outs[p][a] = result
    for copy in arrivals + right_copies + left_copies:
        copy.wait_send()


def input_back(adapters, part, small, norm, router, stat, lows, rights, sources, parts_axis, cols):
    hbm = pl.BlockSpec(memory_space=pl.ANY)
    vmem = pl.BlockSpec(memory_space=pltpu.VMEM)
    smem = pl.BlockSpec(memory_space=pltpu.SMEM)
    count, width = part.shape
    wide = width // cols
    depth = width // parts_axis
    right_width = rights.shape[1] // 4
    total = 2 * (cols - 1) + 2 * (parts_axis - 1)
    return pl.pallas_call(
        functools.partial(input_back_kernel, parts_axis, cols),
        out_shape=[jax.ShapeDtypeStruct((count, wide), F32)]
        + [jax.ShapeDtypeStruct((ADAPT, RANK, depth), F32)] * 5
        + [jax.ShapeDtypeStruct((ADAPT, RANK, right_width), F32)] * 4,
        in_specs=[smem] + [vmem] * 7 + [hbm] * 6,
        out_specs=[vmem] * 10,
        scratch_shapes=[pltpu.VMEM(source.shape, source.dtype) for source in sources]
        + [
            pltpu.VMEM((cols, count, wide), BF16),
            pltpu.VMEM((count, LANES), BF16),
            pltpu.VMEM((cols - 1, count, wide), BF16),
            pltpu.VMEM((cols - 1, count, LANES), BF16),
            pltpu.VMEM((parts_axis, 5 * RANK, depth), BF16),
            pltpu.VMEM((parts_axis - 1, 5 * RANK, depth), BF16),
            pltpu.VMEM((parts_axis - 1, RANK, 4 * right_width), BF16),
            pltpu.SemaphoreType.DMA((total,)),
            pltpu.SemaphoreType.DMA((total,)),
            pltpu.SemaphoreType.DMA((6,)),
        ],
        compiler_params=pltpu.CompilerParams(
            collective_id=5, has_side_effects=True, vmem_limit_bytes=48 * 2**20
        ),
    )(adapters, part, small, norm, router, stat, lows, rights, *sources)


def middle_kernel(parts_axis, cols, replicas, *refs):
    adapter, norm, router, route, low_rows, low_in = refs[:6]
    sources = refs[6:12]
    weights = refs[12:14]
    outs = refs[14:]
    extra_chunks = parts_axis - 1
    chunks = [(None,) + tuple(outs[n * extra_chunks : (n + 1) * extra_chunks]) for n in (0, 1)]
    outs = outs[2 * extra_chunks :]
    hids = outs[:EXP_FF]
    hidden_out, middle, stat, totals = outs[EXP_FF : EXP_FF + 4]
    scratch = outs[EXP_FF + 4 :]
    out_rows, pick_attn, pick_0, pick_1, lefts, tokens = scratch[:6]
    (
        exact_part,
        parts,
        extra,
        parts_in,
        extra_in,
        square,
        square_in,
        low,
        hidden,
        message,
        send,
        recv,
        local,
    ) = scratch[6:]
    col = lax.axis_index("col")
    count, wide = tokens.shape
    width = hidden.shape[1]
    across = [opposite("row", j * replicas) for j in range(1, EXP_FF)]
    beside = [opposite("row", i) for i in range(1, replicas)]
    along = [opposite("col", i) for i in range(1, cols)]
    greet(across + beside + along)
    near = fetch(sources, scratch[:6], local)
    used = [0]
    started = []

    def send_to(source, target, device):
        copy = remote(source, target, send, recv, used[0], device)
        used[0] += 1
        started.append(copy)
        return copy

    expert = lax.axis_index("row") // replicas
    piece_copies = [
        [
            send_to(weights[n].at[jnp.bitwise_xor(expert, j)], chunks[n][j * replicas], across[j - 1])
            for n in (0, 1)
        ]
        for j in range(1, EXP_FF)
    ]
    sibling_copies = [
        send_to(weights[n].at[expert], chunks[n][i], beside[i - 1])
        for i in range(1, replicas)
        for n in (0, 1)
    ]
    for copy in near:
        copy.wait()

    def back(source):
        return lax.dot_general(
            pick_attn[...], source, (((0,), (0,)), ((), ())), preferred_element_type=F32
        )

    sub = lax.broadcasted_iota(jnp.int32, (LANES, LANES), 0)
    lane = lax.broadcasted_iota(jnp.int32, (LANES, LANES), 1)
    lanes = lax.broadcasted_iota(jnp.int32, (count, LANES), 1)
    low_out = back(low_rows[...])
    small = low_in[...] + low_out
    low_out = low_out[:, RANK : 2 * RANK].astype(BF16)
    for q in range(cols):
        here = slice(q * wide, (q + 1) * wide)
        part = back(out_rows[:, here]) + jnp.dot(
            low_out, lefts[2 * RANK : 3 * RANK, here], preferred_element_type=F32
        )
        exact_part[q] = part
        parts[q] = part.astype(BF16)
    extra[...] = small.astype(BF16)
    part_copies = []
    extra_copies = []
    for i in range(1, cols):
        target = jnp.bitwise_xor(col, i)
        part_copies.append(send_to(parts.at[target], parts_in.at[i - 1], along[i - 1]))
        extra_copies.append(send_to(extra, extra_in.at[i - 1], along[i - 1]))
    value = tokens[...].astype(F32) + exact_part[col]
    total = small
    for i in range(cols - 1):
        part_copies[i].wait_recv()
        value += parts_in[i].astype(F32)
    middle[...] = value
    square[...] = lax.dot_general(
        jnp.ones((8, wide), F32),
        value * value,
        (((1,), (1,)), ((), ())),
        precision=HIGHEST,
        preferred_element_type=F32,
    )
    square_copies = [
        send_to(square, square_in.at[i], along[i]) for i in range(cols - 1)
    ]
    for i in range(cols - 1):
        extra_copies[i].wait_recv()
        total += extra_in[i].astype(F32)
    totals[...] = total
    squares = square[...]
    for i in range(cols - 1):
        square_copies[i].wait_recv()
        squares += square_in[i]
    squares = lax.dot_general(
        squares,
        jnp.full((8, LANES), 0.125, F32),
        (((0,), (0,)), ((), ())),
        precision=HIGHEST,
        preferred_element_type=F32,
    )
    scale = lax.rsqrt(squares[:, 0:1] * (1.0 / width) + EPSILON)
    first = pl.multiple_of(col * wide, wide)
    here = pl.ds(first, wide)
    low[...] = (value * scale * norm[:, here]).astype(BF16)
    hidden[:, here] = low[...]
    hidden_copies = [send_to(low, hidden.at[:, here], along[i]) for i in range(cols - 1)]
    mine = lanes // RANK == adapter[0]

    def own_adapter(value, start):
        spread = (sub - start == lane % RANK).astype(F32).astype(BF16)
        value = jnp.dot(value.astype(BF16), spread, preferred_element_type=F32)
        return jnp.where(mine, value, 0.0).astype(BF16)

    picks = [pick_0[...], pick_1[...]]
    any_pick = picks[0] + picks[1]
    message[:, width + 2 * LANES :] = jnp.dot(
        any_pick, own_adapter(total, 2 * RANK), preferred_element_type=F32
    ).astype(BF16)
    for copy in hidden_copies:
        copy.wait_recv()
    kept = pltpu.make_async_copy(hidden, hidden_out, local.at[6])
    kept.start()

    def times(right):
        return lax.dot_general(
            hidden[...], right, (((1,), (1,)), ((), ())), preferred_element_type=F32
        )

    logits = times(router[...])
    routes = [route[:, k : k + 1] for k in range(TOPK)]
    chosen = []
    for k in range(TOPK):
        score = 0.0
        for e in range(EXP_FF):
            score += jnp.where(routes[k] == float(e), logits[:, e : e + 1], 0.0)
        chosen.append(score)
    top = jnp.maximum(chosen[0], chosen[1])
    powers = [jnp.exp(score - top) for score in chosen]
    gates = [power / (powers[0] + powers[1]) for power in powers]
    stat[...] = pack(
        [*gates, *chosen, scale, *routes, route[:, 2:3]], range(8)
    )
    gate_rows = 0.0
    for k in range(TOPK):
        columns = pack([*split(gates[k])], range(2)).astype(BF16)
        gate_rows += jnp.dot(picks[k], columns, preferred_element_type=F32)
    message[:, width + LANES : width + 2 * LANES] = gate_rows.astype(BF16)
    rank = times(lefts[3 * RANK : 4 * RANK])
    rank = jnp.concatenate([rank, jnp.zeros((count, LANES - RANK), F32)], axis=1)
    message[:, width : width + LANES] = jnp.dot(
        any_pick, own_adapter(rank, 0), preferred_element_type=F32
    ).astype(BF16)
    traded = []
    for j in range(EXP_FF - 1, -1, -1):
        rows = slice(j * CAP_FF, (j + 1) * CAP_FF)
        message[rows, :width] = jnp.dot(
            any_pick[rows], hidden[...], preferred_element_type=F32
        ).astype(BF16)
        if j:
            traded.append(send_to(message.at[pl.ds(j * CAP_FF, CAP_FF)], hids[j], across[j - 1]))
    own = pltpu.make_async_copy(message.at[pl.ds(0, CAP_FF)], hids[0], local.at[7])
    own.start()
    for j in range(1, EXP_FF):
        for n in (0, 1):
            piece_copies[j - 1][n].wait_recv()
            for i in range(1, replicas):
                m = j * replicas
                sibling_copies.append(send_to(chunks[n][m], chunks[n][m + i], beside[i - 1]))
    for copy in traded + sibling_copies:
        copy.wait_recv()
    for copy in started:
        copy.wait_send()
    kept.wait()
    own.wait()


def middle_forward(adapter, norm, router, route, low_rows, low_in, sources, weights, parts_axis, cols, replicas):
    hbm = pl.BlockSpec(memory_space=pl.ANY)
    vmem = pl.BlockSpec(memory_space=pltpu.VMEM)
    smem = pl.BlockSpec(memory_space=pltpu.SMEM)
    count, wide = sources[-1].shape
    width = wide * cols
    rows = EXP_FF * CAP_FF
    full = width + 3 * LANES
    total = 2 * (parts_axis - 1) + 4 * (cols - 1) + EXP_FF - 1
    return pl.pallas_call(
        functools.partial(middle_kernel, parts_axis, cols, replicas),
        out_shape=[jax.ShapeDtypeStruct(weights[0].shape[1:], BF16)] * (parts_axis - 1)
        + [jax.ShapeDtypeStruct(weights[1].shape[1:], BF16)] * (parts_axis - 1)
        + [jax.ShapeDtypeStruct((CAP_FF, full), BF16)] * EXP_FF
        + [
            jax.ShapeDtypeStruct((count, width), BF16),
            jax.ShapeDtypeStruct((count, wide), F32),
            jax.ShapeDtypeStruct((count, LANES), F32),
            jax.ShapeDtypeStruct((count, LANES), F32),
        ],
        in_specs=[smem] + [vmem] * 5 + [hbm] * 8,
        out_specs=[hbm] * (2 * parts_axis - 1 + EXP_FF) + [vmem] * 3,
        scratch_shapes=[pltpu.VMEM(source.shape, source.dtype) for source in sources]
        + [
            pltpu.VMEM((cols, count, wide), F32),
            pltpu.VMEM((cols, count, wide), BF16),
            pltpu.VMEM((count, LANES), BF16),
            pltpu.VMEM((cols - 1, count, wide), BF16),
            pltpu.VMEM((cols - 1, count, LANES), BF16),
            pltpu.VMEM((8, count), F32),
            pltpu.VMEM((cols - 1, 8, count), F32),
            pltpu.VMEM((count, wide), BF16),
            pltpu.VMEM((count, width), BF16),
            pltpu.VMEM((rows, full), BF16),
            pltpu.SemaphoreType.DMA((total,)),
            pltpu.SemaphoreType.DMA((total,)),
            pltpu.SemaphoreType.DMA((8,)),
        ],
        compiler_params=pltpu.CompilerParams(
            collective_id=3, has_side_effects=True, vmem_limit_bytes=48 * 2**20
        ),
    )(adapter, norm, router, route, low_rows, low_in, *sources, *weights)


def ffn_kernel(parts, depth, width, units, *refs):
    hids = refs[:EXP_FF]
    cots = refs[EXP_FF : 2 * EXP_FF]
    inners = refs[2 * EXP_FF : 2 * EXP_FF + parts]
    lasts = refs[2 * EXP_FF + parts : 2 * EXP_FF + 2 * parts]
    rights = refs[2 * EXP_FF + 2 * parts]
    outs = refs[2 * EXP_FF + 2 * parts + 1 :]
    grads = outs[:EXP_FF]
    downs = outs[EXP_FF : 2 * EXP_FF]
    adapt = outs[2 * EXP_FF : 2 * EXP_FF + 3]
    hid, cot, block, act, product, sems = outs[2 * EXP_FF + 3 :]
    row = lax.axis_index("row")
    wide = width + LANES
    copies = []
    for j in range(EXP_FF):
        where = pl.ds(j * CAP_FF, CAP_FF)
        near = hids[j].at[:, pl.ds(0, wide + LANES)]
        copies.append(pltpu.make_async_copy(near, hid.at[where], sems.at[j]))
        near = cot.at[where, pl.ds(0, width)]
        copies.append(pltpu.make_async_copy(cots[j], near, sems.at[EXP_FF + j]))
        near = cot.at[where, pl.ds(width, LANES)]
        low = hids[j].at[:, pl.ds(wide + LANES, LANES)]
        copies.append(pltpu.make_async_copy(low, near, sems.at[2 * EXP_FF + j]))
    copies.append(pltpu.make_async_copy(rights, block.at[pl.ds(width, LANES)], sems.at[3 * EXP_FF]))
    expert = row // (parts // EXP_FF)
    for m in range(parts):
        owner = jnp.bitwise_xor(row, m)
        where = pl.ds(pl.multiple_of(owner * depth, depth), depth)
        inner = inners[m] if m else inners[0].at[expert]
        last = lasts[m] if m else lasts[0].at[expert]
        near = block.at[where, pl.ds(0, 2 * units)]
        copies.append(pltpu.make_async_copy(inner, near, sems.at[3 * EXP_FF + 1 + m]))
        near = block.at[where, pl.ds(2 * units, units)]
        copies.append(pltpu.make_async_copy(last, near, sems.at[3 * EXP_FF + 1 + parts + m]))
    for copy in copies:
        copy.start()
    for copy in copies:
        copy.wait()
    gate_scale = hid[:, wide : wide + 1].astype(F32) + hid[:, wide + 1 : wide + 2].astype(F32)
    product[...] = jnp.zeros_like(product)

    def forward(start, size):
        here = pl.ds(start, size)
        up_here = pl.ds(units + start, size)
        down_here = pl.ds(2 * units + start, size)
        gate = jnp.dot(hid[:, :wide], block[:, here], preferred_element_type=F32)
        up = jnp.dot(hid[:, :wide], block[:, up_here], preferred_element_type=F32)
        grad = jnp.dot(cot[...], block[:, down_here], preferred_element_type=F32)
        sig = 1.0 / (1.0 + jnp.exp(-gate))
        mixed = (gate * sig * up).astype(BF16)
        act[:, down_here] = mixed
        product[...] += jnp.sum(mixed.astype(F32) * grad, axis=1, keepdims=True)
        grad = grad * gate_scale
        act[:, here] = (grad * up * sig * (1.0 + gate * (1.0 - sig))).astype(BF16)
        act[:, up_here] = (grad * gate * sig).astype(BF16)

    step = 2 * LANES
    full = units // step

    @pl.loop(0, full)
    def _(i):
        forward(pl.multiple_of(i * step, step), step)

    if units % step:
        forward(full * step, units % step)

    def backward(start, size):
        here = pl.ds(start, size)
        result = lax.dot_general(
            act[:, : 2 * units], block[here, : 2 * units], (((1,), (1,)), ((), ())),
            preferred_element_type=F32,
        ).astype(BF16)
        for j in range(EXP_FF):
            grads[j][:, here] = result[j * CAP_FF : (j + 1) * CAP_FF]
        result = lax.dot_general(
            act[:, 2 * units :], block[here, 2 * units :], (((1,), (1,)), ((), ())),
            preferred_element_type=F32,
        )
        result = (result * gate_scale).astype(BF16)
        for j in range(EXP_FF):
            downs[j][:, here] = result[j * CAP_FF : (j + 1) * CAP_FF]

    full_rows = wide // step

    @pl.loop(0, full_rows)
    def _(i):
        backward(pl.multiple_of(i * step, step), step)

    if wide % step:
        backward(full_rows * step, wide % step)
    total = product[...]
    high = total.astype(BF16)
    low = (total - high.astype(F32)).astype(BF16)
    lane = lax.broadcasted_iota(jnp.int32, (EXP_FF * CAP_FF, LANES), 1)
    packed = jnp.where(lane == 0, high.astype(F32), jnp.where(lane == 1, low.astype(F32), 0.0)).astype(BF16)
    for j in range(EXP_FF):
        grads[j][:, wide:] = packed[j * CAP_FF : (j + 1) * CAP_FF]
    ext = hid[:, width:wide]
    low_ext = (cot[:, width:].astype(F32) * gate_scale).astype(BF16)
    for n, low_rows in enumerate((ext, ext, low_ext)):
        adapt[n][...] = lax.dot_general(
            low_rows,
            act[:, n * units : (n + 1) * units],
            (((0,), (0,)), ((), ())),
            preferred_element_type=F32,
        ).astype(BF16)


def feed_forward(hids, cots, inners, lasts, rights):
    parts = len(inners)
    depth, units = lasts[1].shape
    triple = 3 * units
    width = depth * parts
    rows = EXP_FF * CAP_FF
    hbm = pl.BlockSpec(memory_space=pl.ANY)
    vmem = pl.BlockSpec(memory_space=pltpu.VMEM)
    wide = width + LANES
    return pl.pallas_call(
        functools.partial(ffn_kernel, parts, depth, width, units),
        out_shape=[jax.ShapeDtypeStruct((CAP_FF, wide + LANES), BF16)] * EXP_FF
        + [jax.ShapeDtypeStruct((CAP_FF, wide), BF16)] * EXP_FF
        + [jax.ShapeDtypeStruct((LANES, units), BF16)] * 3,
        in_specs=[hbm] * (2 * EXP_FF + 2 * parts + 1),
        out_specs=[vmem] * (2 * EXP_FF + 3),
        scratch_shapes=[
            pltpu.VMEM((rows, wide + LANES), BF16),
            pltpu.VMEM((rows, wide), BF16),
            pltpu.VMEM((wide, triple), BF16),
            pltpu.VMEM((rows, triple), BF16),
            pltpu.VMEM((rows, 1), F32),
            pltpu.SemaphoreType.DMA((3 * EXP_FF + 1 + 2 * parts,)),
        ],
        compiler_params=pltpu.CompilerParams(vmem_limit_bytes=56 * 2**20),
    )(*hids, *cots, *inners, *lasts, rights)


def on_device(
    inputs,
    cotangent,
    lengths,
    adapter_pick,
    attn_route,
    ffn_route,
    norm_one,
    norm_two,
    router_attn,
    router_ffn,
    kv_weight,
    query_weight,
    out_weight,
    inner_weight,
    down_weight,
    query_left,
    query_right,
    kv_left,
    kv_right,
    out_left,
    out_right,
    inner_left,
    inner_right,
    down_left,
    down_right,
):
    count, slice_width = inputs.shape
    width = router_attn.shape[0]
    rows_axis = lax.axis_size("row")
    replicas = rows_axis // EXP_FF
    row = lax.axis_index("row")
    col = lax.axis_index("col")
    expert = row // replicas
    depth = inner_weight.shape[1]
    units = inner_weight.shape[3]
    length = lengths[0]
    adapter = adapter_pick[0]
    position = jnp.arange(count)
    valid = (position < length).astype(F32)
    cosine, sine = tables(count, HEAD_DIM)
    scaling = HEAD_DIM ** (-0.5)

    def features(part):
        return lax.all_gather(part, "col", axis=1, tiled=True)

    def partials(part):
        return lax.psum_scatter(
            part.astype(BF16), "col", scatter_dimension=1, tiled=True
        ).astype(F32)

    def own_columns(table):
        return lax.dynamic_slice_in_dim(table, col * slice_width, slice_width, 0)

    def later(value, *earlier):
        return lax.optimization_barrier((value, *earlier))[0]

    lanes = lax.broadcasted_iota(jnp.int32, (count, LANES), 1)

    def table_of(*columns):
        result = jnp.zeros((count, LANES), F32)
        for n, column in enumerate(columns):
            if column is not None:
                result = jnp.where(lanes == n, column, result)
        return result

    cols = lax.axis_size("col")
    if rows_axis == 8:
        kv_full, query_full, x_full, *cot_rows = gather_all(
            lengths, ffn_route, inputs, cotangent, [kv_weight, query_weight], rows_axis, cols, replicas
        )
    else:
        kv_full = lax.all_gather(kv_weight, "row", axis=1, tiled=True)
        query_full = lax.all_gather(query_weight, "row", axis=1, tiled=True)
        x_full = features(inputs)
        cot_rows = None
    out_full = lax.all_gather(later(out_weight, query_full), "row", axis=1, tiled=True)

    padding = -units % LANES

    def padded(value):
        if not padding:
            return value
        return jnp.pad(value, [(0, 0)] * (value.ndim - 1) + [(0, padding)])

    inner_flat = padded(inner_weight).reshape(EXP_FF, depth, 2 * (units + padding))
    down_flat = padded(down_weight)

    picks = lax.all_gather(adapter_pick, "row", axis=0, tiled=True)
    pick_onehot = (picks[:, None] == jnp.arange(ADAPT, dtype=jnp.int32)[None, :]).astype(BF16)
    lefts_own = jnp.stack(
        [query_left, kv_left, out_left, inner_left, down_left], axis=1
    ).swapaxes(2, 3)
    lefts_sent = mm(
        "ga,ax->gx", pick_onehot, lefts_own.reshape(ADAPT, 5 * RANK * depth)
    ).astype(BF16)
    lefts = lax.all_to_all(
        lefts_sent.reshape(rows_axis, 5 * RANK, depth), "row", 0, 0, tiled=False
    )
    lefts = lefts.swapaxes(0, 1).reshape(5, RANK, width)
    left_query, left_kv, left_out, left_inner, left_down = (lefts[i] for i in range(5))
    right_query = query_right[adapter].astype(F32)
    right_kv = kv_right[adapter].astype(F32)
    right_out = out_right[adapter].astype(F32)
    right_inner_all = inner_right.reshape(ADAPT * RANK, 2, units)
    right_down_all = down_right.reshape(ADAPT * RANK, units)
    ffn_right = jnp.concatenate(
        [padded(right_inner_all[:, 0]), padded(right_inner_all[:, 1]), padded(right_down_all)],
        axis=1,
    )

    slots_attn = slot_rows(attn_route, EXP_ATT, CAP_ATT)
    slots_ffn = slot_rows(ffn_route, EXP_FF, CAP_FF)
    rows_attn = jnp.arange(EXP_ATT * CAP_ATT, dtype=jnp.int32)
    pick_attn = [
        (rows_attn[:, None] == slots_attn[None, :, k]).astype(BF16) for k in range(TOPK)
    ]
    pick_attn_any = pick_attn[0] + pick_attn[1]
    pick_attn_both = jnp.concatenate(pick_attn, axis=1)
    order = (expert ^ jnp.arange(EXP_FF, dtype=jnp.int32))[:, None] * CAP_FF
    rows_ffn = (order + jnp.arange(CAP_FF, dtype=jnp.int32)[None, :]).reshape(EXP_FF * CAP_FF)
    pick_ffn = [(rows_ffn[:, None] == slots_ffn[None, :, k]).astype(BF16) for k in range(TOPK)]
    pick_ffn_any = pick_ffn[0] + pick_ffn[1]

    def blocks_of(rows):
        blocks = rows.reshape(EXP_FF, CAP_FF, rows.shape[1])
        return [blocks[j] for j in range(EXP_FF)]

    masked_cot = cotangent * valid.astype(BF16)[:, None]
    left_down_own = lax.dynamic_slice_in_dim(left_down, col * slice_width, slice_width, 1)
    grad_low_down_part = mm("td,rd->tr", masked_cot, left_down_own)
    if cot_rows is None:
        cot_rows = spread_cot(
            blocks_of(mm("ct,td->cd", pick_ffn_any, masked_cot).astype(BF16)), cols, replicas
        )

    x_wide = x_full.astype(F32)
    scale_one = lax.rsqrt(jnp.mean(x_wide * x_wide, axis=1, keepdims=True) + EPSILON)
    hidden_one = (x_wide * scale_one * norm_one).astype(BF16)
    chosen_attn = chosen_of(mm("td,de->te", hidden_one, router_attn), attn_route, EXP_ATT)
    gates_attn = jax.nn.softmax(chosen_attn, axis=1)
    rank_query = mm("td,rd->tr", hidden_one, left_query)
    rank_kv = mm("td,rd->tr", hidden_one, left_kv)
    kv_raw = mm("td,sdw->stw", hidden_one, kv_full) + mm(
        "tr,rsw->stw", rank_kv.astype(BF16), right_kv.astype(BF16)
    )
    query_width = kv_raw.shape[2]
    heads = query_width // HEAD_DIM
    keys = rotate(
        kv_raw[0].reshape(count, heads, HEAD_DIM), cosine[:, None], sine[:, None]
    ).astype(BF16)
    values = kv_raw[1].reshape(count, heads, HEAD_DIM).astype(BF16)
    small = jnp.concatenate([rank_query, gates_attn, cosine, sine], axis=1)
    small_rows = exact("ct,tx->cx", pick_attn_any.astype(F32), small)
    rank_query_rows = small_rows[:, :RANK]
    gate_rows = exact("ct,tx->cx", pick_attn[0].astype(F32), gates_attn[:, :1]) + exact(
        "ct,tx->cx", pick_attn[1].astype(F32), gates_attn[:, 1:]
    )
    half = HEAD_DIM // 2
    cosine_rows = small_rows[:, RANK + TOPK : RANK + TOPK + half]
    sine_rows = small_rows[:, RANK + TOPK + half :]
    hidden_rows = mm("ct,td->cd", pick_attn_any, hidden_one).astype(BF16)
    query_rows = mm(
        "ecd,edw->ecw", hidden_rows.reshape(EXP_ATT, CAP_ATT, width), query_full
    ).reshape(EXP_ATT * CAP_ATT, query_width) + mm(
        "cr,rw->cw", rank_query_rows.astype(BF16), right_query.astype(BF16)
    )
    query_rows = (
        rotate(
            query_rows.reshape(EXP_ATT * CAP_ATT, heads, HEAD_DIM),
            cosine_rows[:, None],
            sine_rows[:, None],
        )
        .astype(BF16)
        .reshape(EXP_ATT * CAP_ATT, query_width)
    )
    queries = (
        mm("cx,cw->xw", pick_attn_both, query_rows)
        .astype(BF16)
        .reshape(TOPK, count, heads, HEAD_DIM)
    )
    allowed = (position[None, :] <= position[:, None]) & (position[None, :] < length)
    scores = mm("kbhd,jhd->hkbj", queries, keys) * scaling
    scores = jnp.where(allowed[None, None], scores, -1e30)
    exponent = jnp.exp(scores - jnp.max(scores, axis=-1, keepdims=True))
    probability = exponent / jnp.sum(exponent, axis=-1, keepdims=True)
    probs = probability.astype(BF16)
    attended = mm("hkbj,jhd->kbhd", probs, values).astype(BF16).reshape(TOPK * count, query_width)
    attended_rows = mm("cx,xw->cw", pick_attn_both, attended).astype(BF16)
    attended_rows = later(attended_rows, inner_flat)
    out_rows = mm(
        "ecw,edw->ecd", attended_rows.reshape(EXP_ATT, CAP_ATT, query_width), out_full
    ).reshape(EXP_ATT * CAP_ATT, width)
    out_rows = (out_rows * gate_rows).astype(BF16)
    low_rows = mm("cw,rw->cr", attended_rows, right_out.astype(BF16)) * gate_rows
    low_rows = jnp.pad(low_rows.astype(BF16), ((0, 0), (RANK, LANES - 2 * RANK)))
    lefts_flat = lefts.reshape(5 * RANK, width)

    *outs, hidden_two, middle, stat_ffn, totals_attn = middle_forward(
        adapter_pick,
        norm_two[None, :],
        router_ffn.T,
        table_of(ffn_route[:, 0:1].astype(F32), ffn_route[:, 1:2].astype(F32), valid[:, None]),
        low_rows,
        jnp.pad(grad_low_down_part, ((0, 0), (2 * RANK, LANES - 3 * RANK))),
        [out_rows, pick_attn_any, pick_ffn[0], pick_ffn[1], lefts_flat, inputs],
        [inner_flat, down_flat],
        rows_axis,
        cols,
        replicas,
    )
    inners = [inner_flat, *outs[: rows_axis - 1]]
    lasts = [down_flat, *outs[rows_axis - 1 : 2 * rows_axis - 2]]
    hidden_in = outs[2 * rows_axis - 2 :]
    results = feed_forward(hidden_in, cot_rows, inners, lasts, ffn_right)
    grad_middle, grad_full, totals, branch_ffn, low_down_part = middle_back(
        results[:EXP_FF],
        results[EXP_FF : 2 * EXP_FF],
        adapter_pick,
        norm_two[None, :],
        router_ffn.T,
        stat_ffn,
        [pick_ffn[0], pick_ffn[1], lefts_flat, hidden_two, middle, cotangent],
        cols,
        replicas,
    )
    rights_ffn = lax.optimization_barrier(lax.psum(tuple(results[2 * EXP_FF :]), "row"))
    rights_ffn = [
        value[:, :units].reshape(ADAPT, RANK, units).astype(F32) for value in rights_ffn
    ]

    branch_own = partials(branch_ffn)
    output = ((middle + branch_own) * valid[:, None]).astype(BF16)

    grad_low_out = mm("td,rd->tr", grad_full, left_out)
    grad_middle_rows = mm("ct,td->cd", pick_attn_any, grad_full).astype(BF16)
    grad_low_rows = mm("ct,tr->cr", pick_attn_any, grad_low_out.astype(BF16)).astype(BF16)
    grad_att_rows = mm(
        "ecd,edw->ecw", grad_middle_rows.reshape(EXP_ATT, CAP_ATT, width), out_full
    ).reshape(EXP_ATT * CAP_ATT, query_width) + mm(
        "cr,rw->cw", grad_low_rows, right_out.astype(BF16)
    )
    gg_attn_rows = jnp.sum(attended_rows.astype(F32) * grad_att_rows, axis=1, keepdims=True)
    grad_gates_attn_part = jnp.concatenate(
        [exact("ct,cx->tx", pick_attn[k].astype(F32), gg_attn_rows) for k in range(TOPK)], axis=1
    )
    grad_att_rows = (grad_att_rows * gate_rows).astype(BF16)
    grad_attended = (
        mm("cx,cw->xw", pick_attn_both, grad_att_rows)
        .astype(BF16)
        .reshape(TOPK, count, heads, HEAD_DIM)
    )
    gated_low = (gates_attn.T[:, :, None] * grad_low_out[None]).reshape(TOPK * count, RANK)
    grad_right_out = mm("xr,xw->rw", gated_low.astype(BF16), attended)
    grad_prob = mm("kbhd,jhd->hkbj", grad_attended, values)
    centre = jnp.sum(probability * grad_prob, axis=-1, keepdims=True)
    grad_scores = (probability * (grad_prob - centre)).astype(BF16)
    grad_queries = mm("hkbj,jhd->kbhd", grad_scores, keys) * scaling
    grad_keys = mm("hkbj,kbhd->jhd", grad_scores, queries) * scaling
    grad_values = mm("hkbj,kbhd->jhd", probs, grad_attended)
    grad_query_raw = (
        rotate(grad_queries, cosine[None, :, None], -sine[None, :, None])
        .astype(BF16)
        .reshape(TOPK * count, query_width)
    )
    grad_key_raw = rotate(grad_keys, cosine[:, None], -sine[:, None])
    grad_kv = jnp.stack([grad_key_raw, grad_values]).astype(BF16).reshape(2, count, query_width)
    grad_query_rows = mm("cx,xw->cw", pick_attn_both, grad_query_raw).astype(BF16)
    grad_one_rows = (
        mm("ecw,edw->ecd", grad_query_rows.reshape(EXP_ATT, CAP_ATT, query_width), query_full)
        .astype(BF16)
        .reshape(EXP_ATT * CAP_ATT, width)
    )
    grad_query_sum = jnp.sum(
        grad_query_raw.astype(F32).reshape(TOPK, count, query_width), axis=0
    )
    grad_query_sum_low = grad_query_sum.astype(BF16)
    grad_rank_query = mm("tw,rw->tr", grad_query_sum_low, right_query.astype(BF16))
    grad_rank_kv = mm("stw,rsw->tr", grad_kv, right_kv.astype(BF16))
    grad_one_part = (
        mm("ct,cd->td", pick_attn_any, grad_one_rows)
        + mm("stw,sdw->td", grad_kv, kv_full)
        + mm(
            "tr,rd->td",
            jnp.concatenate([grad_rank_query, grad_rank_kv], axis=1).astype(BF16),
            jnp.concatenate([left_query, left_kv], axis=0),
        )
    )
    grad_right_query = mm("tr,tw->rw", rank_query.astype(BF16), grad_query_sum_low)
    grad_right_kv = mm("tr,stw->rsw", rank_kv.astype(BF16), grad_kv)
    cot_full = features(masked_cot)
    small = table_of(grad_gates_attn_part[:, 0:1], None, grad_gates_attn_part[:, 1:2])
    small += jnp.pad(
        jnp.concatenate([grad_rank_query, grad_rank_kv, low_down_part[:, RANK : 2 * RANK]], axis=1),
        ((0, 0), (RANK, LANES - 4 * RANK)),
    )
    lows = jnp.where(lanes < RANK, jnp.roll(totals_attn, -RANK, axis=1), 0.0) + jnp.where(
        (lanes >= RANK) & (lanes < 2 * RANK), totals, 0.0
    )
    lows = lows.astype(BF16)
    right_parts = jnp.concatenate(
        [grad_right_query, grad_right_kv[:, 0], grad_right_kv[:, 1], grad_right_out], axis=1
    ).astype(BF16)
    grad_inputs, *grads = input_back(
        picks,
        later(grad_one_part, output, *rights_ffn),
        small,
        norm_one[None, :],
        router_attn.T,
        table_of(
            gates_attn[:, 0:1],
            gates_attn[:, 1:2],
            chosen_attn[:, 0:1],
            chosen_attn[:, 1:2],
            scale_one,
            attn_route[:, 0:1].astype(F32),
            attn_route[:, 1:2].astype(F32),
        ),
        lows,
        right_parts,
        [hidden_one, grad_full, hidden_two, cot_full, inputs, grad_middle],
        rows_axis,
        cols,
    )
    lefts_back = [grad.swapaxes(1, 2) for grad in grads[:5]]
    rights_back = grads[5:]
    return (
        output,
        grad_inputs,
        lefts_back[0],
        rights_back[0],
        lefts_back[1],
        jnp.stack(rights_back[1:3], axis=2),
        lefts_back[2],
        rights_back[3],
        lefts_back[3],
        jnp.stack(rights_ffn[:2], axis=2),
        lefts_back[4],
        rights_ffn[2],
    )


def solution(mesh):
    placed = (
        P("row", "col"),
        P("row", "col"),
        P("row"),
        P("row"),
        P("row", None),
        P("row", None),
        P(),
        P(),
        P(),
        P(),
        P(None, "row", "col"),
        P(None, "row", "col"),
        P(None, "row", "col"),
        P(None, "row", None, "col"),
        P(None, "row", "col"),
        P(None, "row", None),
        P(None, None, "col"),
        P(None, "row", None),
        P(None, None, None, "col"),
        P(None, "row", None),
        P(None, None, "col"),
        P(None, "row", None),
        P(None, None, None, "col"),
        P(None, "row", None),
        P(None, None, "col"),
    )
    return jax.shard_map(
        on_device,
        mesh=mesh,
        in_specs=placed,
        out_specs=(
            P("row", "col"),
            P("row", "col"),
            P(None, "row", None),
            P(None, None, "col"),
            P(None, "row", None),
            P(None, None, None, "col"),
            P(None, "row", None),
            P(None, None, "col"),
            P(None, "row", None),
            P(None, None, None, "col"),
            P(None, "row", None),
            P(None, None, "col"),
        ),
        check_vma=False,
    )
```

```python
import functools

import jax
import jax.numpy as jnp
from jax import lax
from jax.experimental import pallas as pl
from jax.experimental.pallas import tpu as pltpu
from jax.sharding import PartitionSpec as P

HEAD_DIM = 128
EXP_ATT = 8
EXP_FF = 4
TOPK = 2
ADAPT = 8
RANK = 16
CAP_ATT = 80
CAP_FF = 160
EPSILON = 1e-06
ROPE_BASE = 10000.0
HIGHEST = lax.Precision.HIGHEST
F32 = jnp.float32
BF16 = jnp.bfloat16
LANES = 128


def mm(spec, a, b):
    return jnp.einsum(spec, a, b, preferred_element_type=F32)


def exact(spec, a, b):
    return jnp.einsum(spec, a, b, precision=HIGHEST, preferred_element_type=F32)


def tables(count, head_width):
    position = jnp.arange(count).astype(F32)
    frequency = ROPE_BASE ** (-jnp.arange(head_width // 2).astype(F32) * 2.0 / head_width)
    angle = position[:, None] * frequency[None, :]
    return (jnp.cos(angle), jnp.sin(angle))


def rotate(values, cosine, sine):
    half = values.shape[-1] // 2
    first = values[..., :half]
    second = values[..., half:]
    return jnp.concatenate(
        [first * cosine - second * sine, second * cosine + first * sine], axis=-1
    )


def opposite(axis, offset):
    index = jnp.bitwise_xor(lax.axis_index(axis), offset)
    if axis == "row":
        return (index, lax.axis_index("col"))
    return (lax.axis_index("row"), index)


def greet(partners):
    barrier = pltpu.get_barrier_semaphore()
    for partner in partners:
        pl.semaphore_signal(
            barrier, inc=1, device_id=partner, device_id_type=pl.DeviceIdType.MESH
        )
    pl.semaphore_wait(barrier, len(partners))


def split(value):
    high = value.astype(BF16).astype(F32)
    return high, value - high


def pack(columns, lanes):
    lane = lax.broadcasted_iota(jnp.int32, (columns[0].shape[0], LANES), 1)
    result = jnp.zeros((columns[0].shape[0], LANES), F32)
    for column, n in zip(columns, lanes):
        result = jnp.where(lane == n, column, result)
    return result


def route_term(stat, grads, router, start, size):
    gates = [stat[:, k : k + 1] for k in range(TOPK)]
    mean = gates[0] * grads[0] + gates[1] * grads[1]
    product = 0.0
    term = 0.0
    weights = [gates[k] * (grads[k] - mean) for k in range(TOPK)]
    for k in range(TOPK):
        product += weights[k] * stat[:, 2 + k : 3 + k]
    for e in range(router.shape[0]):
        weight = 0.0
        for k in range(TOPK):
            weight += jnp.where(stat[:, 5 + k : 6 + k] == float(e), weights[k], 0.0)
        term += weight * router[e : e + 1, pl.ds(start, size)].astype(F32)
    return term, product


def fetch(sources, targets, sems):
    copies = []
    for n, (source, target) in enumerate(zip(sources, targets)):
        copies.append(pltpu.make_async_copy(source, target, sems.at[n]))
        copies[-1].start()
    return copies


def remote(source, target, send, recv, n, device):
    copy = pltpu.make_async_remote_copy(
        src_ref=source,
        dst_ref=target,
        send_sem=send.at[n],
        recv_sem=recv.at[n],
        device_id=device,
        device_id_type=pl.DeviceIdType.MESH,
    )
    copy.start()
    return copy


def dispatch_matrices(route, flip, experts, capacity):
    count = route.shape[0]
    lane = lax.broadcasted_iota(jnp.int32, (count, LANES), 1)
    chosen = [(route[:, k : k + 1] == lane).astype(F32) for k in range(TOPK)]
    place = lax.broadcasted_iota(jnp.int32, (count, count), 0)
    other = lax.broadcasted_iota(jnp.int32, (count, count), 1)
    before = (other < place).astype(F32).astype(BF16)
    earlier = jnp.dot(
        before, (chosen[0] + chosen[1]).astype(BF16), preferred_element_type=F32
    )
    rows = lax.broadcasted_iota(jnp.int32, (count, experts * capacity), 1)
    results = []
    for k in range(TOPK):
        position = jnp.sum(earlier * chosen[k], axis=1, keepdims=True).astype(jnp.int32)
        mine = jnp.bitwise_xor(route[:, k : k + 1], flip) * capacity + position
        results.append((rows == mine).astype(F32).astype(BF16))
    return results


def turn(value, cosine, sine):
    half = HEAD_DIM // 2
    heads = []
    for h in range(value.shape[1] // HEAD_DIM):
        head = value[:, h * HEAD_DIM : (h + 1) * HEAD_DIM]
        heads.append(head * cosine + pltpu.roll(head, half, axis=1) * sine)
    return jnp.concatenate(heads, axis=1)


def scores_of(stat_route, logits, experts):
    chosen = []
    for k in range(TOPK):
        score = 0.0
        for e in range(experts):
            score += jnp.where(stat_route[k] == float(e), logits[:, e : e + 1], 0.0)
        chosen.append(score)
    top = jnp.maximum(chosen[0], chosen[1])
    powers = [jnp.exp(score - top) for score in chosen]
    return chosen, [power / (powers[0] + powers[1]) for power in powers]


def front_kernel(parts, cols, replicas, *refs):
    lengths, pick, route_attn, route_ffn, cot, norm, router, cosine, sine, rights = refs[:10]
    left_refs = refs[10:15]
    tokens = refs[15]
    blocks = refs[16:19]
    pairs = refs[19]
    outs = refs[20:]
    flat = outs[0]
    outs = outs[1:]
    wholes = outs[:3]
    cot_wholes = outs[3 : 3 + EXP_FF]
    (
        hidden,
        lefts,
        stat,
        low_in,
        keys,
        values,
        queries,
        attended,
        probability,
        att_rows,
        low_rows,
        out_rows,
        picks_attn,
        picks_ffn,
        ranks,
        gate_rows,
        picks,
    ) = outs[3 + EXP_FF : 20 + EXP_FF]
    (
        x_all,
        own_rows,
        landed,
        hidden_rows,
        buffer,
        query_rows,
        pick_out,
        lefts_out,
        pair_in,
        pair_out,
        send,
        recv,
        local,
        load,
    ) = outs[20 + EXP_FF :]
    row = lax.axis_index("row")
    col = lax.axis_index("col")
    depth = blocks[0].shape[1]
    count, wide = tokens.shape
    width = hidden.shape[1]
    head_width = keys.shape[1]
    heads = head_width // HEAD_DIM
    across = [None] + [opposite("row", m) for m in range(1, parts)]
    along = [opposite("col", i) for i in range(1, cols)]
    greet(across[1:] + along)
    started, kept = [], []
    received = set()
    here = pl.ds(pl.multiple_of(col * wide, wide), wide)
    own = pl.ds(pl.multiple_of(row * depth, depth), depth)

    def send_to(source, target, device):
        copy = remote(source, target, send, recv, len(started), device)
        started.append(copy)
        return copy

    def arrive(copy):
        copy.wait_recv()
        received.add(id(copy))

    def keep(source, target):
        copy = pltpu.make_async_copy(source, target, local.at[len(kept)])
        copy.start()
        kept.append(copy)
        return copy

    pair = 2
    chunks = [
        (a, start) for a in range(3) for start in range(0, blocks[a].shape[0], pair)
    ]

    def place(n, offset, item=None):
        array, start = chunks[n]
        owner = jnp.bitwise_xor(row, offset)
        owner_rows = pl.ds(pl.multiple_of(owner * depth, depth), depth)
        if item is None:
            return wholes[array].at[pl.ds(start, pair), owner_rows]
        return wholes[array].at[start + item, owner_rows]

    first, direct, relayed, beside = {}, {}, {}, {}

    def push_own(n):
        if n >= len(chunks):
            return
        array, start = chunks[n]
        source = blocks[array].at[pl.ds(start, pair)]
        if parts == 8:
            first[n] = [send_to(source, place(n, 0), across[m]) for m in (2, 4)]
            beside[n] = [send_to(source, place(n, 0), across[1])]
        else:
            direct[n] = [send_to(source, place(n, 0), across[m]) for m in range(1, parts)]

    def relay(n):
        if parts == 8:
            for copy in first[n]:
                arrive(copy)
            relayed[n] = [
                send_to(place(n, 2, 0), place(n, 2, 0), across[4]),
                send_to(place(n, 4, 1), place(n, 4, 1), across[2]),
            ]
            for offset in (2, 4):
                beside[n].append(send_to(place(n, offset), place(n, offset), across[1]))

    def finish(n):
        if parts == 8:
            for copy in relayed[n]:
                arrive(copy)
            beside[n].append(send_to(place(n, 6), place(n, 6), across[1]))
            for copy in beside[n]:
                arrive(copy)
        else:
            for copy in direct[n]:
                arrive(copy)

    token_copies = [send_to(tokens, x_all.at[:, here], device) for device in along]
    token_kept = keep(tokens, x_all.at[:, here])
    block_kept = [keep(blocks[a], wholes[a].at[:, own]) for a in range(3)]
    pick_out[...] = jnp.full(pick_out.shape, 1.0, F32) * pick[0].astype(F32)
    picks[0] = pick_out[...]
    pick_copies = [
        send_to(pick_out, picks.at[m], across[m]) for m in range(1, parts)
    ]
    window, behind = 9, 5
    for n in range(window):
        push_own(n)

    position = lax.broadcasted_iota(jnp.int32, (count, 1), 0)
    valid = position < lengths[0]
    matrices = dispatch_matrices(route_ffn[...], row // replicas, EXP_FF, CAP_FF)
    for k in range(TOPK):
        picks_ffn[k] = matrices[k]
    masked = jnp.where(valid, cot[...].astype(F32), 0.0).astype(BF16)

    def rows_of(matrix, value):
        return lax.dot_general(
            matrix, value, (((0,), (0,)), ((), ())), preferred_element_type=F32
        )

    def times(left, right):
        return lax.dot_general(
            left, right, (((1,), (1,)), ((), ())), preferred_element_type=F32
        )

    dispatched = rows_of(matrices[0] + matrices[1], masked).astype(BF16)
    for j in range(EXP_FF):
        own_rows[j] = dispatched[j * CAP_FF : (j + 1) * CAP_FF]
    traded = [
        send_to(own_rows.at[j], landed.at[j - 1], across[j * replicas])
        for j in range(1, EXP_FF)
    ]
    attn = dispatch_matrices(route_attn[...], 0, EXP_ATT, CAP_ATT)
    for k in range(TOPK):
        picks_attn[k] = attn[k]
    attn_any = attn[0] + attn[1]
    picks_attn[TOPK] = attn_any

    left_copies = []
    for m in range(parts):
        if m:
            arrive(pick_copies[m - 1])
        theirs = picks[m, 0:1, 0:1]
        for p in range(5):
            value = jnp.zeros((RANK, depth), F32)
            for a in range(ADAPT):
                value += jnp.where(theirs == float(a), left_refs[p][a].astype(F32), 0.0)
            lefts_out[m, p * RANK : (p + 1) * RANK] = value.astype(BF16)
        if m:
            left_copies.append(send_to(lefts_out.at[m], lefts.at[:, own], across[m]))
        else:
            lefts[:, own] = lefts_out[0]
    for j in range(EXP_FF):
        if j:
            arrive(traded[j - 1])
            source = landed.at[j - 1]
        else:
            source = own_rows.at[0]
        keep(source, cot_wholes[j].at[:, here])
        for device in along:
            send_to(source, cot_wholes[j].at[:, here], device)
    relay(0)
    push_own(window)

    for copy in token_copies:
        arrive(copy)
    token_kept.wait()
    square = jnp.zeros((count, 1), F32)
    for q in range(cols):
        value = x_all[:, q * wide : (q + 1) * wide].astype(F32)
        square += jnp.sum(value * value, axis=1, keepdims=True)
    scale = lax.rsqrt(square * (1.0 / width) + EPSILON)
    for q in range(cols):
        span = slice(q * wide, (q + 1) * wide)
        value = x_all[:, span].astype(F32)
        hidden[:, span] = (value * scale * norm[:, span]).astype(BF16)
    for copy in left_copies:
        arrive(copy)
    relay(1)
    push_own(window + 1)
    logits = times(hidden[...], router[...])
    routes = [route_attn[:, k : k + 1].astype(F32) for k in range(TOPK)]
    chosen, gates = scores_of(routes, logits, EXP_ATT)
    extras = [valid.astype(F32), *(route_ffn[:, k : k + 1].astype(F32) for k in range(TOPK))]
    stat[...] = pack([*gates, *chosen, scale, *routes, *extras], range(10))
    rank_both = times(hidden[...], lefts[: 2 * RANK])
    ranks[...] = rank_both
    rank_query = rank_both[:, :RANK].astype(BF16)
    rank_kv = rank_both[:, RANK:].astype(BF16)
    low_down = times(masked, lefts[4 * RANK : 5 * RANK, here])
    low_in[...] = jnp.concatenate(
        [
            jnp.zeros((count, 2 * RANK), F32),
            low_down,
            jnp.zeros((count, LANES - 3 * RANK), F32),
        ],
        axis=1,
    )
    gate_wide = 0.0
    for k in range(TOPK):
        columns = pack([*split(gates[k])], range(2)).astype(BF16)
        gate_wide += rows_of(attn[k], columns)
    gate_row = gate_wide[:, 0:1] + gate_wide[:, 1:2]
    gate_rows[...] = gate_row
    rank_rows = rows_of(attn_any, rank_query).astype(BF16)
    for q in range(cols):
        span = slice(q * wide, (q + 1) * wide)
        hidden_rows[:, span] = rows_of(attn_any, hidden[:, span]).astype(BF16)

    def attend():
        value = query_rows[...]
        high = value.astype(BF16)
        low = (value - high.astype(F32)).astype(BF16)
        for k in range(TOPK):
            query = jnp.dot(attn[k], high, preferred_element_type=F32) + jnp.dot(
                attn[k], low, preferred_element_type=F32
            )
            queries[k] = turn(query, cosine[...], sine[...]).astype(BF16)
        other = lax.broadcasted_iota(jnp.int32, (count, count), 1)
        place_row = lax.broadcasted_iota(jnp.int32, (count, count), 0)
        allowed = (other <= place_row) & (other < lengths[0])
        for h in range(heads):
            span = slice(h * HEAD_DIM, (h + 1) * HEAD_DIM)
            for k in range(TOPK):
                scores = times(queries[k, :, span], keys[:, span]) * HEAD_DIM ** (-0.5)
                scores = jnp.where(allowed, scores, -1e30)
                power = jnp.exp(scores - jnp.max(scores, axis=1, keepdims=True))
                probs = power / jnp.sum(power, axis=1, keepdims=True)
                probability[h, k] = probs
                attended[k, :, span] = jnp.dot(
                    probs.astype(BF16), values[:, span], preferred_element_type=F32
                ).astype(BF16)
        rows = rows_of(attn[0], attended[0]) + rows_of(attn[1], attended[1])
        att_rows[...] = rows.astype(BF16)
        low = times(att_rows[...], rights[3 * RANK :]) * gate_row
        low_rows[...] = jnp.concatenate(
            [
                jnp.zeros((low.shape[0], RANK), F32),
                low,
                jnp.zeros((low.shape[0], LANES - 2 * RANK), F32),
            ],
            axis=1,
        ).astype(BF16)

    def compute(n):
        array, start = chunks[n]
        weight = buffer.at[n % 2]
        if array == 0:
            key = jnp.dot(hidden[...], weight[0], preferred_element_type=F32) + jnp.dot(
                rank_kv, rights[RANK : 2 * RANK], preferred_element_type=F32
            )
            keys[...] = turn(key, cosine[...], sine[...]).astype(BF16)
            value = jnp.dot(hidden[...], weight[1], preferred_element_type=F32) + jnp.dot(
                rank_kv, rights[2 * RANK : 3 * RANK], preferred_element_type=F32
            )
            values[...] = value.astype(BF16)
            return
        for item in range(pair):
            e = start + item
            span = slice(e * CAP_ATT, (e + 1) * CAP_ATT)
            if array == 1:
                query_rows[span] = jnp.dot(
                    hidden_rows[span], weight[item], preferred_element_type=F32
                ) + jnp.dot(rank_rows[span], rights[:RANK], preferred_element_type=F32)
            else:
                out_rows[span] = (times(att_rows[span], weight[item]) * gate_row[span]).astype(
                    BF16
                )
        if array == 1 and start + pair == EXP_ATT:
            attend()

    def flatten(e):
        copy = pltpu.make_async_copy(pairs.at[e], pair_in, load.at[2])
        copy.start()
        copy.wait()
        step = 64

        @pl.loop(0, pair_in.shape[0] // step)
        def _(i):
            span = pl.ds(pl.multiple_of(i * step, step), step)
            pair_out[span] = pair_in[span].reshape(step, pair_out.shape[1])

        copy = pltpu.make_async_copy(pair_out, flat.at[e], load.at[3])
        copy.start()
        copy.wait()

    loads = {}
    total = len(chunks)
    for n in range(2, total + behind + 1):
        if n < total:
            relay(n)
            push_own(n + window)
        if n - 2 < EXP_FF:
            flatten(n - 2)
        for m in range(n - behind + 1) if n == 2 else [n - behind]:
            if 0 <= m < total:
                if m == 0:
                    for copy in block_kept:
                        copy.wait()
                finish(m)
                loads[m] = pltpu.make_async_copy(
                    place_whole(wholes, chunks[m], pair), buffer.at[m % 2], load.at[m % 2]
                )
                loads[m].start()
            if 0 <= m - 1 < total:
                loads[m - 1].wait()
                compute(m - 1)
    for copy in started:
        if id(copy) not in received:
            copy.wait_recv()
    for copy in started:
        copy.wait_send()
    for copy in kept[1 + len(block_kept) :]:
        copy.wait()


def place_whole(wholes, chunk, pair):
    array, start = chunk
    return wholes[array].at[pl.ds(start, pair)]


def front(smalls, lefts, tokens, blocks, pairs, parts, cols, replicas):
    hbm = pl.BlockSpec(memory_space=pl.ANY)
    vmem = pl.BlockSpec(memory_space=pltpu.VMEM)
    smem = pl.BlockSpec(memory_space=pltpu.SMEM)
    count, wide = tokens.shape
    width = wide * cols
    depth, head_width = blocks[0].shape[1:]
    heads = head_width // HEAD_DIM
    rows = EXP_ATT * CAP_ATT
    rows_ffn = EXP_FF * CAP_FF
    shape = jax.ShapeDtypeStruct
    flat = (pairs.shape[0], pairs.shape[1], 2 * pairs.shape[3])
    n_chunks = sum(block.shape[0] for block in blocks) // 2
    per_chunk = 8 if parts == 8 else parts - 1
    remotes = (
        n_chunks * per_chunk + (cols - 1) * (1 + EXP_FF) + EXP_FF - 1 + 2 * (parts - 1)
    )
    return pl.pallas_call(
        functools.partial(front_kernel, parts, cols, replicas),
        out_shape=[shape(flat, BF16)]
        + [shape((b.shape[0], width, head_width), BF16) for b in blocks]
        + [shape((CAP_FF, width), BF16)] * EXP_FF
        + [
            shape((count, width), BF16),
            shape((5 * RANK, width), BF16),
            shape((count, LANES), F32),
            shape((count, LANES), F32),
            shape((count, head_width), BF16),
            shape((count, head_width), BF16),
            shape((TOPK, count, head_width), BF16),
            shape((TOPK, count, head_width), BF16),
            shape((heads, TOPK, count, count), F32),
            shape((rows, head_width), BF16),
            shape((rows, LANES), BF16),
            shape((rows, width), BF16),
            shape((TOPK + 1, count, rows), BF16),
            shape((TOPK, count, rows_ffn), BF16),
            shape((count, 2 * RANK), F32),
            shape((rows, 1), F32),
            shape((parts, 8, LANES), F32),
        ],
        in_specs=[smem] * 2 + [vmem] * 13 + [hbm] * 5,
        out_specs=[hbm] * (4 + EXP_FF) + [vmem] * 17,
        scratch_shapes=[
            pltpu.VMEM((count, width), BF16),
            pltpu.VMEM((EXP_FF, CAP_FF, wide), BF16),
            pltpu.VMEM((EXP_FF - 1, CAP_FF, wide), BF16),
            pltpu.VMEM((rows, width), BF16),
            pltpu.VMEM((2, 2, width, head_width), BF16),
            pltpu.VMEM((rows, head_width), F32),
            pltpu.VMEM((8, LANES), F32),
            pltpu.VMEM((parts, 5 * RANK, depth), BF16),
            pltpu.VMEM(pairs.shape[1:], BF16),
            pltpu.VMEM(flat[1:], BF16),
            pltpu.SemaphoreType.DMA((remotes,)),
            pltpu.SemaphoreType.DMA((remotes,)),
            pltpu.SemaphoreType.DMA((4 + EXP_FF,)),
            pltpu.SemaphoreType.DMA((4,)),
        ],
        compiler_params=pltpu.CompilerParams(
            collective_id=1, has_side_effects=True, vmem_limit_bytes=56 * 2**20
        ),
    )(*smalls, *lefts, tokens, *blocks, pairs)


def middle_back_kernel(cols, replicas, *refs):
    blocks, downs = refs[:EXP_FF], refs[EXP_FF : 2 * EXP_FF]
    adapter, norm, router, stat = refs[2 * EXP_FF : 2 * EXP_FF + 4]
    sources = refs[2 * EXP_FF + 4 : 2 * EXP_FF + 9]
    grad_middle, grad_whole, totals, branch, low_down = refs[2 * EXP_FF + 9 : 2 * EXP_FF + 14]
    scratch = refs[2 * EXP_FF + 14 :]
    picks_ffn, lefts, hidden, middle, cot = scratch[:5]
    rows, down_rows, exact_part, parts, extra, parts_in, extra_in, low, send, recv, local = (
        scratch[5:]
    )
    col = lax.axis_index("col")
    count, wide = middle.shape
    width = hidden.shape[1]
    across = [opposite("row", j * replicas) for j in range(1, EXP_FF)]
    along = [opposite("col", i) for i in range(1, cols)]
    greet(across + along)
    copies = [
        remote(
            blocks[j], rows.at[pl.ds(j * CAP_FF, CAP_FF)], send, recv, j - 1, across[j - 1]
        )
        for j in range(1, EXP_FF)
    ]
    near = fetch(
        [blocks[0], downs[0], *sources],
        [rows.at[pl.ds(0, CAP_FF)], down_rows.at[pl.ds(0, CAP_FF)], *scratch[:5]],
        local,
    )
    for copy in near:
        copy.wait()
    for copy in copies:
        copy.wait_recv()
    base = EXP_FF - 1
    down_copies = [
        remote(
            downs[j],
            down_rows.at[pl.ds(j * CAP_FF, CAP_FF)],
            send,
            recv,
            base + j - 1,
            across[j - 1],
        )
        for j in range(1, EXP_FF)
    ]
    picks = [picks_ffn[0], picks_ffn[1]]
    any_pick = picks[0] + picks[1]

    def back(pick, source, start, size):
        return jnp.dot(pick, source[:, start : start + size], preferred_element_type=F32)

    sub = lax.broadcasted_iota(jnp.int32, (LANES, LANES), 0)
    lane = lax.broadcasted_iota(jnp.int32, (LANES, LANES), 1)
    mine = lax.broadcasted_iota(jnp.int32, (count, LANES), 1) // RANK == adapter[0]
    place_rank = (lane == RANK + sub % RANK).astype(F32).astype(BF16)

    def own_rank(value):
        value = jnp.where(mine, value, 0.0).astype(BF16)
        return jnp.dot(value, place_rank, preferred_element_type=F32)

    gate_grads = []
    for k in range(TOPK):
        pair = back(picks[k], rows, width + LANES, LANES)
        gate_grads.append(pair[:, 0:1] + pair[:, 1:2])
    rank = own_rank(back(any_pick, rows, width, LANES))
    rank_low = rank[:, RANK : 2 * RANK].astype(BF16)
    product = jnp.zeros((count, 1), F32)
    for q in range(cols):
        here = slice(q * wide, (q + 1) * wide)
        part = back(any_pick, rows, q * wide, wide) + jnp.dot(
            rank_low, lefts[3 * RANK : 4 * RANK, here], preferred_element_type=F32
        )
        product += jnp.sum(part * hidden[:, here].astype(F32), axis=1, keepdims=True)
        exact_part[q] = part
        parts[q] = part.astype(BF16)
    columns = [*split(gate_grads[0]), *split(gate_grads[1]), *split(product)]
    small = pack(columns, range(6)) + rank
    extra[...] = small.astype(BF16)
    base += EXP_FF - 1
    arrivals = []
    for i in range(1, cols):
        target = jnp.bitwise_xor(col, i)
        n = base + 2 * (i - 1)
        arrivals.append(remote(extra, extra_in.at[i - 1], send, recv, n + 1, along[i - 1]))
        arrivals.append(
            remote(parts.at[target], parts_in.at[i - 1], send, recv, n, along[i - 1])
        )
    for copy in arrivals:
        copy.wait_recv()
    grad = exact_part[col]
    total = small
    for i in range(cols - 1):
        grad += parts_in[i].astype(F32)
        total += extra_in[i].astype(F32)
    totals[...] = total
    gate_grads = [total[:, 0:1] + total[:, 1:2], total[:, 2:3] + total[:, 3:4]]
    first = pl.multiple_of(col * wide, wide)
    term, more = route_term(stat, gate_grads, router, first, wide)
    inner = total[:, 4:5] + total[:, 5:6] + more
    scaled = (grad + term) * norm[:, pl.ds(first, wide)]
    factor = stat[:, 4:5]
    valid = stat[:, 7:8]
    result = (
        cot[...].astype(F32) * valid
        + factor * scaled
        - middle[...] * (factor * factor * inner * (1.0 / width))
    )
    grad_middle[...] = result
    low[...] = result.astype(BF16)
    here = pl.ds(first, wide)
    kept = pltpu.make_async_copy(low, grad_whole.at[:, here], local.at[8])
    kept.start()
    base += 2 * (cols - 1)
    last = [
        remote(low, grad_whole.at[:, here], send, recv, base + i, along[i])
        for i in range(cols - 1)
    ]
    for copy in down_copies:
        copy.wait_recv()
    rank = own_rank(back(any_pick, down_rows, width, LANES))
    rank_low = rank[:, RANK : 2 * RANK].astype(BF16)
    low_down[...] = rank
    for q in range(cols):
        here = slice(q * wide, (q + 1) * wide)
        part = back(any_pick, down_rows, q * wide, wide) + jnp.dot(
            rank_low, lefts[4 * RANK : 5 * RANK, here], preferred_element_type=F32
        )
        branch[:, here] = part.astype(BF16)
    for copy in last:
        copy.wait_recv()
    for copy in copies + down_copies + arrivals + last:
        copy.wait_send()
    kept.wait()


def middle_back(blocks, downs, adapter, norm, router, stat, sources, cols, replicas):
    hbm = pl.BlockSpec(memory_space=pl.ANY)
    vmem = pl.BlockSpec(memory_space=pltpu.VMEM)
    smem = pl.BlockSpec(memory_space=pltpu.SMEM)
    count, wide = sources[-1].shape
    total = 2 * (EXP_FF - 1) + 3 * (cols - 1)
    rows = EXP_FF * CAP_FF
    return pl.pallas_call(
        functools.partial(middle_back_kernel, cols, replicas),
        out_shape=[
            jax.ShapeDtypeStruct((count, wide), F32),
            jax.ShapeDtypeStruct((count, wide * cols), BF16),
            jax.ShapeDtypeStruct((count, LANES), F32),
            jax.ShapeDtypeStruct((count, wide * cols), BF16),
            jax.ShapeDtypeStruct((count, LANES), F32),
        ],
        in_specs=[hbm] * (2 * EXP_FF) + [smem, vmem, vmem, vmem] + [hbm] * 5,
        out_specs=[vmem, hbm, vmem, vmem, vmem],
        scratch_shapes=[pltpu.VMEM(source.shape, source.dtype) for source in sources]
        + [
            pltpu.VMEM((rows, blocks[0].shape[1]), BF16),
            pltpu.VMEM((rows, downs[0].shape[1]), BF16),
            pltpu.VMEM((cols, count, wide), F32),
            pltpu.VMEM((cols, count, wide), BF16),
            pltpu.VMEM((count, LANES), BF16),
            pltpu.VMEM((cols - 1, count, wide), BF16),
            pltpu.VMEM((cols - 1, count, LANES), BF16),
            pltpu.VMEM((count, wide), BF16),
            pltpu.SemaphoreType.DMA((total,)),
            pltpu.SemaphoreType.DMA((total,)),
            pltpu.SemaphoreType.DMA((9,)),
        ],
        compiler_params=pltpu.CompilerParams(
            collective_id=4, has_side_effects=True, vmem_limit_bytes=48 * 2**20
        ),
    )(*blocks, *downs, adapter, norm, router, stat, *sources)


def input_back_kernel(parts_axis, cols, *refs):
    adapters, part, small_in, norm, router, stat, lows, rights = refs[:8]
    sources = refs[8:14]
    grad_inputs = refs[14]
    left_outs = refs[15:20]
    right_outs = refs[20:24]
    hidden_one, grad_whole, hidden_two, cot_whole, tokens, grad_middle = refs[24:30]
    parts, extra, parts_in, extra_in, lefts, lefts_in, rights_in, send, recv, local = refs[30:]
    row = lax.axis_index("row")
    col = lax.axis_index("col")
    count, wide = tokens.shape
    width = hidden_one.shape[1]
    depth = width // parts_axis
    right_width = rights.shape[1] // 4
    along = [opposite("col", i) for i in range(1, cols)]
    across = [opposite("row", m) for m in range(1, parts_axis)]
    greet(across + along)
    near = fetch(sources, refs[24:30], local)
    near[0].wait()
    product = jnp.zeros((count, 1), F32)
    for q in range(cols):
        value = part[:, q * wide : (q + 1) * wide]
        product += jnp.sum(
            value * hidden_one[:, q * wide : (q + 1) * wide].astype(F32), axis=1, keepdims=True
        )
        parts[q] = value.astype(BF16)
    lane = lax.broadcasted_iota(jnp.int32, (count, LANES), 1)
    columns = [*split(small_in[:, 0:1]), *split(small_in[:, 2:3]), *split(product)]
    small = jnp.where(lane < RANK, 0.0, small_in[...]) + pack(columns, range(6))
    extra[...] = small.astype(BF16)
    arrivals = []
    for i in range(1, cols):
        target = jnp.bitwise_xor(col, i)
        n = 2 * (i - 1)
        arrivals.append(remote(extra, extra_in.at[i - 1], send, recv, n + 1, along[i - 1]))
        arrivals.append(
            remote(parts.at[target], parts_in.at[i - 1], send, recv, n, along[i - 1])
        )
    base = 2 * (cols - 1)
    right_copies = [
        remote(rights, rights_in.at[m], send, recv, base + m, across[m])
        for m in range(parts_axis - 1)
    ]
    base += parts_axis - 1
    total = small
    for i in range(cols - 1):
        arrivals[2 * i].wait_recv()
        total += extra_in[i].astype(F32)
    ranks = total.astype(BF16)

    def outer(left, right):
        return lax.dot_general(
            left, right, (((0,), (0,)), ((), ())), preferred_element_type=F32
        ).astype(BF16)

    for copy in near[1:]:
        copy.wait()
    whole = outer(ranks, hidden_one[...])
    for m in range(parts_axis):
        lefts[m, : 2 * RANK] = whole[RANK : 3 * RANK, m * depth : (m + 1) * depth]
    whole = outer(lows[...], grad_whole[...])
    for m in range(parts_axis):
        lefts[m, 2 * RANK : 3 * RANK] = whole[:RANK, m * depth : (m + 1) * depth]
    whole = outer(lows[...], hidden_two[...])
    for m in range(parts_axis):
        lefts[m, 3 * RANK : 4 * RANK] = whole[RANK : 2 * RANK, m * depth : (m + 1) * depth]
    whole = outer(ranks, cot_whole[...])
    for m in range(parts_axis):
        lefts[m, 4 * RANK :] = whole[3 * RANK : 4 * RANK, m * depth : (m + 1) * depth]
    left_copies = [
        remote(
            lefts.at[jnp.bitwise_xor(row, m)],
            lefts_in.at[m - 1],
            send,
            recv,
            base + m - 1,
            across[m - 1],
        )
        for m in range(1, parts_axis)
    ]
    first = pl.multiple_of(col * wide, wide)
    grad = part[:, pl.ds(first, wide)]
    for i in range(cols - 1):
        arrivals[2 * i + 1].wait_recv()
        grad += parts_in[i].astype(F32)
    gate_grads = [total[:, 0:1] + total[:, 1:2], total[:, 2:3] + total[:, 3:4]]
    term, more = route_term(stat, gate_grads, router, first, wide)
    inner = total[:, 4:5] + total[:, 5:6] + more
    factor = stat[:, 4:5]
    grad_inputs[...] = (
        grad_middle[...]
        + factor * ((grad + term) * norm[:, pl.ds(first, wide)])
        - tokens[...].astype(F32) * (factor * factor * inner * (1.0 / width))
    )
    chosen_by = [
        [
            jnp.where(adapters[m] == a, 1.0, 0.0).astype(F32)
            for a in range(ADAPT)
        ]
        for m in range(parts_axis)
    ]
    for copy in right_copies:
        copy.wait_recv()
    for p in range(4):
        here = slice(p * right_width, (p + 1) * right_width)
        values = [rights[:, here].astype(F32)] + [
            rights_in[m, :, here].astype(F32) for m in range(parts_axis - 1)
        ]
        for a in range(ADAPT):
            result = chosen_by[0][a] * values[0]
            for m in range(1, parts_axis):
                result += chosen_by[m][a] * values[m]
            right_outs[p][a] = result
    for copy in left_copies:
        copy.wait_recv()
    for p in range(5):
        here = slice(p * RANK, (p + 1) * RANK)
        values = [lefts[row, here].astype(F32)] + [
            lefts_in[m, here].astype(F32) for m in range(parts_axis - 1)
        ]
        for a in range(ADAPT):
            result = chosen_by[0][a] * values[0]
            for m in range(1, parts_axis):
                result += chosen_by[m][a] * values[m]
            left_outs[p][a] = result
    for copy in arrivals + right_copies + left_copies:
        copy.wait_send()


def input_back(adapters, part, small, norm, router, stat, lows, rights, sources, parts_axis, cols):
    hbm = pl.BlockSpec(memory_space=pl.ANY)
    vmem = pl.BlockSpec(memory_space=pltpu.VMEM)
    smem = pl.BlockSpec(memory_space=pltpu.SMEM)
    count, width = part.shape
    wide = width // cols
    depth = width // parts_axis
    right_width = rights.shape[1] // 4
    total = 2 * (cols - 1) + 2 * (parts_axis - 1)
    return pl.pallas_call(
        functools.partial(input_back_kernel, parts_axis, cols),
        out_shape=[jax.ShapeDtypeStruct((count, wide), F32)]
        + [jax.ShapeDtypeStruct((ADAPT, RANK, depth), F32)] * 5
        + [jax.ShapeDtypeStruct((ADAPT, RANK, right_width), F32)] * 4,
        in_specs=[smem] + [vmem] * 7 + [hbm] * 6,
        out_specs=[vmem] * 10,
        scratch_shapes=[pltpu.VMEM(source.shape, source.dtype) for source in sources]
        + [
            pltpu.VMEM((cols, count, wide), BF16),
            pltpu.VMEM((count, LANES), BF16),
            pltpu.VMEM((cols - 1, count, wide), BF16),
            pltpu.VMEM((cols - 1, count, LANES), BF16),
            pltpu.VMEM((parts_axis, 5 * RANK, depth), BF16),
            pltpu.VMEM((parts_axis - 1, 5 * RANK, depth), BF16),
            pltpu.VMEM((parts_axis - 1, RANK, 4 * right_width), BF16),
            pltpu.SemaphoreType.DMA((total,)),
            pltpu.SemaphoreType.DMA((total,)),
            pltpu.SemaphoreType.DMA((6,)),
        ],
        compiler_params=pltpu.CompilerParams(
            collective_id=5, has_side_effects=True, vmem_limit_bytes=48 * 2**20
        ),
    )(adapters, part, small, norm, router, stat, lows, rights, *sources)


def middle_kernel(parts_axis, cols, replicas, *refs):
    adapter, norm, router, route, low_rows, low_in = refs[:6]
    sources = refs[6:11]
    weights = refs[11:13]
    outs = refs[13:]
    extra_chunks = parts_axis - 1
    chunks = [(None,) + tuple(outs[n * extra_chunks : (n + 1) * extra_chunks]) for n in (0, 1)]
    outs = outs[2 * extra_chunks :]
    hids = outs[:EXP_FF]
    hidden_out, middle, stat, totals = outs[EXP_FF : EXP_FF + 4]
    scratch = outs[EXP_FF + 4 :]
    out_rows, picks_attn, picks_ffn, lefts, tokens = scratch[:5]
    (
        exact_part,
        parts,
        extra,
        parts_in,
        extra_in,
        square,
        square_in,
        low,
        hidden,
        message,
        send,
        recv,
        local,
    ) = scratch[5:]
    col = lax.axis_index("col")
    count, wide = tokens.shape
    width = hidden.shape[1]
    across = [opposite("row", j * replicas) for j in range(1, EXP_FF)]
    beside = [opposite("row", i) for i in range(1, replicas)]
    along = [opposite("col", i) for i in range(1, cols)]
    greet(across + beside + along)
    near = fetch(sources, scratch[:5], local)
    used = [0]
    started = []

    def send_to(source, target, device):
        copy = remote(source, target, send, recv, used[0], device)
        used[0] += 1
        started.append(copy)
        return copy

    expert = lax.axis_index("row") // replicas
    piece_copies = [
        [
            send_to(weights[n].at[jnp.bitwise_xor(expert, j)], chunks[n][j * replicas], across[j - 1])
            for n in (0, 1)
        ]
        for j in range(1, EXP_FF)
    ]
    sibling_copies = [
        send_to(weights[n].at[expert], chunks[n][i], beside[i - 1])
        for i in range(1, replicas)
        for n in (0, 1)
    ]
    for copy in near:
        copy.wait()

    def back(source):
        return jnp.dot(picks_attn[TOPK], source, preferred_element_type=F32)

    def rows_of(matrix, value):
        return lax.dot_general(
            matrix, value, (((0,), (0,)), ((), ())), preferred_element_type=F32
        )

    sub = lax.broadcasted_iota(jnp.int32, (LANES, LANES), 0)
    lane = lax.broadcasted_iota(jnp.int32, (LANES, LANES), 1)
    lanes = lax.broadcasted_iota(jnp.int32, (count, LANES), 1)
    low_out = back(low_rows[...])
    small = low_in[...] + low_out
    low_out = low_out[:, RANK : 2 * RANK].astype(BF16)
    for q in range(cols):
        here = slice(q * wide, (q + 1) * wide)
        part = back(out_rows[:, here]) + jnp.dot(
            low_out, lefts[2 * RANK : 3 * RANK, here], preferred_element_type=F32
        )
        exact_part[q] = part
        parts[q] = part.astype(BF16)
    extra[...] = small.astype(BF16)
    part_copies = []
    extra_copies = []
    for i in range(1, cols):
        target = jnp.bitwise_xor(col, i)
        part_copies.append(send_to(parts.at[target], parts_in.at[i - 1], along[i - 1]))
        extra_copies.append(send_to(extra, extra_in.at[i - 1], along[i - 1]))
    value = tokens[...].astype(F32) + exact_part[col]
    total = small
    for i in range(cols - 1):
        part_copies[i].wait_recv()
        value += parts_in[i].astype(F32)
    middle[...] = value
    square[...] = lax.dot_general(
        jnp.ones((8, wide), F32),
        value * value,
        (((1,), (1,)), ((), ())),
        precision=HIGHEST,
        preferred_element_type=F32,
    )
    square_copies = [
        send_to(square, square_in.at[i], along[i]) for i in range(cols - 1)
    ]
    for i in range(cols - 1):
        extra_copies[i].wait_recv()
        total += extra_in[i].astype(F32)
    totals[...] = total
    squares = square[...]
    for i in range(cols - 1):
        square_copies[i].wait_recv()
        squares += square_in[i]
    squares = lax.dot_general(
        squares,
        jnp.full((8, LANES), 0.125, F32),
        (((0,), (0,)), ((), ())),
        precision=HIGHEST,
        preferred_element_type=F32,
    )
    scale = lax.rsqrt(squares[:, 0:1] * (1.0 / width) + EPSILON)
    first = pl.multiple_of(col * wide, wide)
    here = pl.ds(first, wide)
    low[...] = (value * scale * norm[:, here]).astype(BF16)
    hidden[:, here] = low[...]
    hidden_copies = [send_to(low, hidden.at[:, here], along[i]) for i in range(cols - 1)]
    mine = lanes // RANK == adapter[0]

    def own_adapter(value, start):
        spread = (sub - start == lane % RANK).astype(F32).astype(BF16)
        value = jnp.dot(value.astype(BF16), spread, preferred_element_type=F32)
        return jnp.where(mine, value, 0.0).astype(BF16)

    picks = [picks_ffn[0], picks_ffn[1]]
    any_pick = picks[0] + picks[1]
    message[:, width + 2 * LANES :] = rows_of(any_pick, own_adapter(total, 2 * RANK)).astype(BF16)
    for copy in hidden_copies:
        copy.wait_recv()
    kept = pltpu.make_async_copy(hidden, hidden_out, local.at[6])
    kept.start()

    def times(right):
        return lax.dot_general(
            hidden[...], right, (((1,), (1,)), ((), ())), preferred_element_type=F32
        )

    logits = times(router[...])
    routes = [route[:, 8 + k : 9 + k] for k in range(TOPK)]
    chosen, gates = scores_of(routes, logits, EXP_FF)
    stat[...] = pack(
        [*gates, *chosen, scale, *routes, route[:, 7:8]], range(8)
    )
    gate_rows = 0.0
    for k in range(TOPK):
        columns = pack([*split(gates[k])], range(2)).astype(BF16)
        gate_rows += rows_of(picks[k], columns)
    message[:, width + LANES : width + 2 * LANES] = gate_rows.astype(BF16)
    rank = times(lefts[3 * RANK : 4 * RANK])
    rank = jnp.concatenate([rank, jnp.zeros((count, LANES - RANK), F32)], axis=1)
    message[:, width : width + LANES] = rows_of(any_pick, own_adapter(rank, 0)).astype(BF16)
    for q in range(cols):
        span = slice(q * wide, (q + 1) * wide)
        message[:, span] = rows_of(any_pick, hidden[:, span]).astype(BF16)
    traded = [
        send_to(message.at[pl.ds(j * CAP_FF, CAP_FF)], hids[j], across[j - 1])
        for j in range(EXP_FF - 1, 0, -1)
    ]
    own = pltpu.make_async_copy(message.at[pl.ds(0, CAP_FF)], hids[0], local.at[7])
    own.start()
    for j in range(1, EXP_FF):
        for n in (0, 1):
            piece_copies[j - 1][n].wait_recv()
            for i in range(1, replicas):
                m = j * replicas
                sibling_copies.append(send_to(chunks[n][m], chunks[n][m + i], beside[i - 1]))
    for copy in traded + sibling_copies:
        copy.wait_recv()
    for copy in started:
        copy.wait_send()
    kept.wait()
    own.wait()


def middle_forward(adapter, norm, router, route, low_rows, low_in, sources, weights, parts_axis, cols, replicas):
    hbm = pl.BlockSpec(memory_space=pl.ANY)
    vmem = pl.BlockSpec(memory_space=pltpu.VMEM)
    smem = pl.BlockSpec(memory_space=pltpu.SMEM)
    count, wide = sources[-1].shape
    width = wide * cols
    rows = EXP_FF * CAP_FF
    full = width + 3 * LANES
    total = 2 * (parts_axis - 1) + 4 * (cols - 1) + EXP_FF - 1
    return pl.pallas_call(
        functools.partial(middle_kernel, parts_axis, cols, replicas),
        out_shape=[jax.ShapeDtypeStruct(weights[0].shape[1:], BF16)] * (parts_axis - 1)
        + [jax.ShapeDtypeStruct(weights[1].shape[1:], BF16)] * (parts_axis - 1)
        + [jax.ShapeDtypeStruct((CAP_FF, full), BF16)] * EXP_FF
        + [
            jax.ShapeDtypeStruct((count, width), BF16),
            jax.ShapeDtypeStruct((count, wide), F32),
            jax.ShapeDtypeStruct((count, LANES), F32),
            jax.ShapeDtypeStruct((count, LANES), F32),
        ],
        in_specs=[smem] + [vmem] * 5 + [hbm] * 7,
        out_specs=[hbm] * (2 * parts_axis - 1 + EXP_FF) + [vmem] * 3,
        scratch_shapes=[pltpu.VMEM(source.shape, source.dtype) for source in sources]
        + [
            pltpu.VMEM((cols, count, wide), F32),
            pltpu.VMEM((cols, count, wide), BF16),
            pltpu.VMEM((count, LANES), BF16),
            pltpu.VMEM((cols - 1, count, wide), BF16),
            pltpu.VMEM((cols - 1, count, LANES), BF16),
            pltpu.VMEM((8, count), F32),
            pltpu.VMEM((cols - 1, 8, count), F32),
            pltpu.VMEM((count, wide), BF16),
            pltpu.VMEM((count, width), BF16),
            pltpu.VMEM((rows, full), BF16),
            pltpu.SemaphoreType.DMA((total,)),
            pltpu.SemaphoreType.DMA((total,)),
            pltpu.SemaphoreType.DMA((8,)),
        ],
        compiler_params=pltpu.CompilerParams(
            collective_id=3, has_side_effects=True, vmem_limit_bytes=48 * 2**20
        ),
    )(adapter, norm, router, route, low_rows, low_in, *sources, *weights)


def ffn_kernel(parts, depth, width, units, *refs):
    hids = refs[:EXP_FF]
    cots = refs[EXP_FF : 2 * EXP_FF]
    inners = refs[2 * EXP_FF : 2 * EXP_FF + parts]
    lasts = refs[2 * EXP_FF + parts : 2 * EXP_FF + 2 * parts]
    rights = refs[2 * EXP_FF + 2 * parts]
    outs = refs[2 * EXP_FF + 2 * parts + 1 :]
    grads = outs[:EXP_FF]
    downs = outs[EXP_FF : 2 * EXP_FF]
    adapt = outs[2 * EXP_FF : 2 * EXP_FF + 3]
    hid, cot, block, act, product, sems = outs[2 * EXP_FF + 3 :]
    row = lax.axis_index("row")
    wide = width + LANES
    copies = []
    for j in range(EXP_FF):
        where = pl.ds(j * CAP_FF, CAP_FF)
        near = hids[j].at[:, pl.ds(0, wide + LANES)]
        copies.append(pltpu.make_async_copy(near, hid.at[where], sems.at[j]))
        near = cot.at[where, pl.ds(0, width)]
        copies.append(pltpu.make_async_copy(cots[j], near, sems.at[EXP_FF + j]))
        near = cot.at[where, pl.ds(width, LANES)]
        low = hids[j].at[:, pl.ds(wide + LANES, LANES)]
        copies.append(pltpu.make_async_copy(low, near, sems.at[2 * EXP_FF + j]))
    copies.append(pltpu.make_async_copy(rights, block.at[pl.ds(width, LANES)], sems.at[3 * EXP_FF]))
    expert = row // (parts // EXP_FF)
    for m in range(parts):
        owner = jnp.bitwise_xor(row, m)
        where = pl.ds(pl.multiple_of(owner * depth, depth), depth)
        inner = inners[m] if m else inners[0].at[expert]
        last = lasts[m] if m else lasts[0].at[expert]
        near = block.at[where, pl.ds(0, 2 * units)]
        copies.append(pltpu.make_async_copy(inner, near, sems.at[3 * EXP_FF + 1 + m]))
        near = block.at[where, pl.ds(2 * units, units)]
        copies.append(pltpu.make_async_copy(last, near, sems.at[3 * EXP_FF + 1 + parts + m]))
    for copy in copies:
        copy.start()
    for copy in copies:
        copy.wait()
    gate_scale = hid[:, wide : wide + 1].astype(F32) + hid[:, wide + 1 : wide + 2].astype(F32)
    product[...] = jnp.zeros_like(product)

    def forward(start, size):
        here = pl.ds(start, size)
        up_here = pl.ds(units + start, size)
        down_here = pl.ds(2 * units + start, size)
        gate = jnp.dot(hid[:, :wide], block[:, here], preferred_element_type=F32)
        up = jnp.dot(hid[:, :wide], block[:, up_here], preferred_element_type=F32)
        grad = jnp.dot(cot[...], block[:, down_here], preferred_element_type=F32)
        sig = 1.0 / (1.0 + jnp.exp(-gate))
        mixed = (gate * sig * up).astype(BF16)
        act[:, down_here] = mixed
        product[...] += jnp.sum(mixed.astype(F32) * grad, axis=1, keepdims=True)
        grad = grad * gate_scale
        act[:, here] = (grad * up * sig * (1.0 + gate * (1.0 - sig))).astype(BF16)
        act[:, up_here] = (grad * gate * sig).astype(BF16)

    step = 2 * LANES
    full = units // step

    @pl.loop(0, full)
    def _(i):
        forward(pl.multiple_of(i * step, step), step)

    if units % step:
        forward(full * step, units % step)

    def backward(start, size):
        here = pl.ds(start, size)
        result = lax.dot_general(
            act[:, : 2 * units], block[here, : 2 * units], (((1,), (1,)), ((), ())),
            preferred_element_type=F32,
        ).astype(BF16)
        for j in range(EXP_FF):
            grads[j][:, here] = result[j * CAP_FF : (j + 1) * CAP_FF]
        result = lax.dot_general(
            act[:, 2 * units :], block[here, 2 * units :], (((1,), (1,)), ((), ())),
            preferred_element_type=F32,
        )
        result = (result * gate_scale).astype(BF16)
        for j in range(EXP_FF):
            downs[j][:, here] = result[j * CAP_FF : (j + 1) * CAP_FF]

    full_rows = wide // step

    @pl.loop(0, full_rows)
    def _(i):
        backward(pl.multiple_of(i * step, step), step)

    if wide % step:
        backward(full_rows * step, wide % step)
    total = product[...]
    high = total.astype(BF16)
    low = (total - high.astype(F32)).astype(BF16)
    lane = lax.broadcasted_iota(jnp.int32, (EXP_FF * CAP_FF, LANES), 1)
    packed = jnp.where(lane == 0, high.astype(F32), jnp.where(lane == 1, low.astype(F32), 0.0)).astype(BF16)
    for j in range(EXP_FF):
        grads[j][:, wide:] = packed[j * CAP_FF : (j + 1) * CAP_FF]
    ext = hid[:, width:wide]
    low_ext = (cot[:, width:].astype(F32) * gate_scale).astype(BF16)
    for n, low_rows in enumerate((ext, ext, low_ext)):
        adapt[n][...] = lax.dot_general(
            low_rows,
            act[:, n * units : (n + 1) * units],
            (((0,), (0,)), ((), ())),
            preferred_element_type=F32,
        ).astype(BF16)


def feed_forward(hids, cots, inners, lasts, rights):
    parts = len(inners)
    depth, units = lasts[1].shape
    triple = 3 * units
    width = depth * parts
    rows = EXP_FF * CAP_FF
    hbm = pl.BlockSpec(memory_space=pl.ANY)
    vmem = pl.BlockSpec(memory_space=pltpu.VMEM)
    wide = width + LANES
    return pl.pallas_call(
        functools.partial(ffn_kernel, parts, depth, width, units),
        out_shape=[jax.ShapeDtypeStruct((CAP_FF, wide + LANES), BF16)] * EXP_FF
        + [jax.ShapeDtypeStruct((CAP_FF, wide), BF16)] * EXP_FF
        + [jax.ShapeDtypeStruct((LANES, units), BF16)] * 3,
        in_specs=[hbm] * (2 * EXP_FF + 2 * parts + 1),
        out_specs=[vmem] * (2 * EXP_FF + 3),
        scratch_shapes=[
            pltpu.VMEM((rows, wide + LANES), BF16),
            pltpu.VMEM((rows, wide), BF16),
            pltpu.VMEM((wide, triple), BF16),
            pltpu.VMEM((rows, triple), BF16),
            pltpu.VMEM((rows, 1), F32),
            pltpu.SemaphoreType.DMA((3 * EXP_FF + 1 + 2 * parts,)),
        ],
        compiler_params=pltpu.CompilerParams(vmem_limit_bytes=56 * 2**20),
    )(*hids, *cots, *inners, *lasts, rights)


def on_device(
    inputs,
    cotangent,
    lengths,
    adapter_pick,
    attn_route,
    ffn_route,
    norm_one,
    norm_two,
    router_attn,
    router_ffn,
    kv_weight,
    query_weight,
    out_weight,
    inner_weight,
    down_weight,
    query_left,
    query_right,
    kv_left,
    kv_right,
    out_left,
    out_right,
    inner_left,
    inner_right,
    down_left,
    down_right,
):
    count, slice_width = inputs.shape
    width = router_attn.shape[0]
    rows_axis = lax.axis_size("row")
    replicas = rows_axis // EXP_FF
    row = lax.axis_index("row")
    col = lax.axis_index("col")
    expert = row // replicas
    depth = inner_weight.shape[1]
    units = inner_weight.shape[3]
    length = lengths[0]
    adapter = adapter_pick[0]
    position = jnp.arange(count)
    valid = (position < length).astype(F32)
    cosine, sine = tables(count, HEAD_DIM)
    scaling = HEAD_DIM ** (-0.5)

    def features(part):
        return lax.all_gather(part, "col", axis=1, tiled=True)

    def partials(part):
        return lax.psum_scatter(
            part.astype(BF16), "col", scatter_dimension=1, tiled=True
        ).astype(F32)

    def own_columns(table):
        return lax.dynamic_slice_in_dim(table, col * slice_width, slice_width, 0)

    def later(value, *earlier):
        return lax.optimization_barrier((value, *earlier))[0]

    lanes = lax.broadcasted_iota(jnp.int32, (count, LANES), 1)

    def table_of(*columns):
        result = jnp.zeros((count, LANES), F32)
        for n, column in enumerate(columns):
            if column is not None:
                result = jnp.where(lanes == n, column, result)
        return result

    cols = lax.axis_size("col")
    padding = -units % LANES

    def padded(value):
        if not padding:
            return value
        return jnp.pad(value, [(0, 0)] * (value.ndim - 1) + [(0, padding)])

    down_flat = padded(down_weight)

    rights = jnp.concatenate(
        [
            query_right[adapter],
            kv_right[adapter][:, 0],
            kv_right[adapter][:, 1],
            out_right[adapter],
        ]
    )
    lefts_own = [
        value.swapaxes(1, 2)
        for value in (query_left, kv_left, out_left, inner_left, down_left)
    ]
    (
        inner_flat,
        kv_full,
        query_full,
        out_full,
        *cot_rows,
        hidden_one,
        lefts,
        stat_attn,
        low_in,
        keys,
        values,
        queries,
        attended,
        probability,
        attended_rows,
        low_rows,
        out_rows,
        picks_attn,
        picks_ffn,
        ranks,
        gate_rows,
        picks,
    ) = front(
        [
            lengths,
            adapter_pick,
            attn_route,
            ffn_route,
            cotangent,
            norm_one[None, :],
            router_attn.T,
            jnp.concatenate([cosine, cosine], axis=1),
            jnp.concatenate([-sine, sine], axis=1),
            rights,
        ],
        lefts_own,
        inputs,
        [kv_weight, query_weight, out_weight],
        padded(inner_weight),
        rows_axis,
        cols,
        replicas,
    )
    picks = picks[:, 0, 0].astype(jnp.int32)
    gates_attn = stat_attn[:, :TOPK]
    query_width = keys.shape[1]
    heads = query_width // HEAD_DIM
    keys = keys.reshape(count, heads, HEAD_DIM)
    values = values.reshape(count, heads, HEAD_DIM)
    queries = queries.reshape(TOPK, count, heads, HEAD_DIM)
    attended = attended.reshape(TOPK * count, query_width)
    pick_attn_any = picks_attn[TOPK]
    pick_attn_both = picks_attn[:TOPK]
    rank_query = ranks[:, :RANK]
    rank_kv = ranks[:, RANK:]
    right_query = rights[:RANK]
    right_kv = rights[RANK : 3 * RANK].reshape(2, RANK, query_width)
    right_out = rights[3 * RANK :]
    right_inner_all = inner_right.reshape(ADAPT * RANK, 2, units)
    right_down_all = down_right.reshape(ADAPT * RANK, units)
    ffn_right = jnp.concatenate(
        [padded(right_inner_all[:, 0]), padded(right_inner_all[:, 1]), padded(right_down_all)],
        axis=1,
    )

    *outs, hidden_two, middle, stat_ffn, totals_attn = middle_forward(
        adapter_pick,
        norm_two[None, :],
        router_ffn.T,
        stat_attn,
        low_rows,
        low_in,
        [out_rows, picks_attn, picks_ffn, lefts, inputs],
        [inner_flat, down_flat],
        rows_axis,
        cols,
        replicas,
    )
    inners = [inner_flat, *outs[: rows_axis - 1]]
    lasts = [down_flat, *outs[rows_axis - 1 : 2 * rows_axis - 2]]
    hidden_in = outs[2 * rows_axis - 2 :]
    results = feed_forward(hidden_in, cot_rows, inners, lasts, ffn_right)
    grad_middle, grad_full, totals, branch_ffn, low_down_part = middle_back(
        results[:EXP_FF],
        results[EXP_FF : 2 * EXP_FF],
        adapter_pick,
        norm_two[None, :],
        router_ffn.T,
        stat_ffn,
        [picks_ffn, lefts, hidden_two, middle, cotangent],
        cols,
        replicas,
    )
    rights_ffn = lax.optimization_barrier(lax.psum(tuple(results[2 * EXP_FF :]), "row"))
    rights_ffn = [
        value[:, :units].reshape(ADAPT, RANK, units).astype(F32) for value in rights_ffn
    ]

    branch_own = partials(branch_ffn)
    output = ((middle + branch_own) * valid[:, None]).astype(BF16)

    grad_low_out = mm("td,rd->tr", grad_full, lefts[2 * RANK : 3 * RANK])
    grad_middle_rows = mm("tc,td->cd", pick_attn_any, grad_full).astype(BF16)
    grad_low_rows = mm("tc,tr->cr", pick_attn_any, grad_low_out.astype(BF16)).astype(BF16)
    grad_att_rows = mm(
        "ecd,edw->ecw", grad_middle_rows.reshape(EXP_ATT, CAP_ATT, width), out_full
    ).reshape(EXP_ATT * CAP_ATT, query_width) + mm("cr,rw->cw", grad_low_rows, right_out)
    gg_attn_rows = jnp.sum(attended_rows.astype(F32) * grad_att_rows, axis=1, keepdims=True)
    grad_gates_attn_part = exact("ktc,cx->ktx", pick_attn_both.astype(F32), gg_attn_rows)
    grad_att_rows = (grad_att_rows * gate_rows).astype(BF16)
    grad_attended = (
        mm("ktc,cw->ktw", pick_attn_both, grad_att_rows)
        .astype(BF16)
        .reshape(TOPK, count, heads, HEAD_DIM)
    )
    gated_low = (gates_attn.T[:, :, None] * grad_low_out[None]).reshape(TOPK * count, RANK)
    grad_right_out = mm("xr,xw->rw", gated_low.astype(BF16), attended)
    grad_prob = mm("kbhd,jhd->hkbj", grad_attended, values)
    centre = jnp.sum(probability * grad_prob, axis=-1, keepdims=True)
    grad_scores = (probability * (grad_prob - centre)).astype(BF16)
    grad_queries = mm("hkbj,jhd->kbhd", grad_scores, keys) * scaling
    grad_keys = mm("hkbj,kbhd->jhd", grad_scores, queries) * scaling
    grad_values = mm("hkbj,kbhd->jhd", probability.astype(BF16), grad_attended)
    grad_query_raw = (
        rotate(grad_queries, cosine[None, :, None], -sine[None, :, None])
        .astype(BF16)
        .reshape(TOPK * count, query_width)
    )
    grad_key_raw = rotate(grad_keys, cosine[:, None], -sine[:, None])
    grad_kv = jnp.stack([grad_key_raw, grad_values]).astype(BF16).reshape(2, count, query_width)
    grad_query_rows = mm(
        "ktc,ktw->cw", pick_attn_both, grad_query_raw.reshape(TOPK, count, query_width)
    ).astype(BF16)
    grad_one_rows = (
        mm("ecw,edw->ecd", grad_query_rows.reshape(EXP_ATT, CAP_ATT, query_width), query_full)
        .astype(BF16)
        .reshape(EXP_ATT * CAP_ATT, width)
    )
    grad_query_sum = jnp.sum(
        grad_query_raw.astype(F32).reshape(TOPK, count, query_width), axis=0
    )
    grad_query_sum_low = grad_query_sum.astype(BF16)
    grad_rank_query = mm("tw,rw->tr", grad_query_sum_low, right_query)
    grad_rank_kv = mm("stw,srw->tr", grad_kv, right_kv)
    grad_one_part = (
        mm("tc,cd->td", pick_attn_any, grad_one_rows)
        + mm("stw,sdw->td", grad_kv, kv_full)
        + mm(
            "tr,rd->td",
            jnp.concatenate([grad_rank_query, grad_rank_kv], axis=1).astype(BF16),
            lefts[: 2 * RANK],
        )
    )
    grad_right_query = mm("tr,tw->rw", rank_query.astype(BF16), grad_query_sum_low)
    grad_right_kv = mm("tr,stw->rsw", rank_kv.astype(BF16), grad_kv)
    cot_full = features(cotangent * valid.astype(BF16)[:, None])
    small = table_of(grad_gates_attn_part[0], None, grad_gates_attn_part[1])
    small += jnp.pad(
        jnp.concatenate([grad_rank_query, grad_rank_kv, low_down_part[:, RANK : 2 * RANK]], axis=1),
        ((0, 0), (RANK, LANES - 4 * RANK)),
    )
    lows = jnp.where(lanes < RANK, jnp.roll(totals_attn, -RANK, axis=1), 0.0) + jnp.where(
        (lanes >= RANK) & (lanes < 2 * RANK), totals, 0.0
    )
    lows = lows.astype(BF16)
    right_parts = jnp.concatenate(
        [grad_right_query, grad_right_kv[:, 0], grad_right_kv[:, 1], grad_right_out], axis=1
    ).astype(BF16)
    grad_inputs, *grads = input_back(
        picks,
        later(grad_one_part, output, *rights_ffn),
        small,
        norm_one[None, :],
        router_attn.T,
        stat_attn,
        lows,
        right_parts,
        [hidden_one, grad_full, hidden_two, cot_full, inputs, grad_middle],
        rows_axis,
        cols,
    )
    lefts_back = [grad.swapaxes(1, 2) for grad in grads[:5]]
    rights_back = grads[5:]
    return (
        output,
        grad_inputs,
        lefts_back[0],
        rights_back[0],
        lefts_back[1],
        jnp.stack(rights_back[1:3], axis=2),
        lefts_back[2],
        rights_back[3],
        lefts_back[3],
        jnp.stack(rights_ffn[:2], axis=2),
        lefts_back[4],
        rights_ffn[2],
    )


def solution(mesh):
    placed = (
        P("row", "col"),
        P("row", "col"),
        P("row"),
        P("row"),
        P("row", None),
        P("row", None),
        P(),
        P(),
        P(),
        P(),
        P(None, "row", "col"),
        P(None, "row", "col"),
        P(None, "row", "col"),
        P(None, "row", None, "col"),
        P(None, "row", "col"),
        P(None, "row", None),
        P(None, None, "col"),
        P(None, "row", None),
        P(None, None, None, "col"),
        P(None, "row", None),
        P(None, None, "col"),
        P(None, "row", None),
        P(None, None, None, "col"),
        P(None, "row", None),
        P(None, None, "col"),
    )
    return jax.shard_map(
        on_device,
        mesh=mesh,
        in_specs=placed,
        out_specs=(
            P("row", "col"),
            P("row", "col"),
            P(None, "row", None),
            P(None, None, "col"),
            P(None, "row", None),
            P(None, None, None, "col"),
            P(None, "row", None),
            P(None, None, "col"),
            P(None, "row", None),
            P(None, None, None, "col"),
            P(None, "row", None),
            P(None, None, "col"),
        ),
        check_vma=False,
    )
```

```python
import functools

import jax
import jax.numpy as jnp
from jax import lax
from jax.experimental import pallas as pl
from jax.experimental.pallas import tpu as pltpu
from jax.sharding import PartitionSpec as P

HEAD_DIM = 128
EXP_ATT = 8
EXP_FF = 4
TOPK = 2
ADAPT = 8
RANK = 16
CAP_ATT = 80
CAP_FF = 160
EPSILON = 1e-06
ROPE_BASE = 10000.0
HIGHEST = lax.Precision.HIGHEST
F32 = jnp.float32
BF16 = jnp.bfloat16
LANES = 128


def tables(count, head_width):
    position = jnp.arange(count).astype(F32)
    frequency = ROPE_BASE ** (-jnp.arange(head_width // 2).astype(F32) * 2.0 / head_width)
    angle = position[:, None] * frequency[None, :]
    return (jnp.cos(angle), jnp.sin(angle))


def opposite(axis, offset):
    index = jnp.bitwise_xor(lax.axis_index(axis), offset)
    if axis == "row":
        return (index, lax.axis_index("col"))
    return (lax.axis_index("row"), index)


def greet(partners):
    barrier = pltpu.get_barrier_semaphore()
    for partner in partners:
        pl.semaphore_signal(
            barrier, inc=1, device_id=partner, device_id_type=pl.DeviceIdType.MESH
        )
    pl.semaphore_wait(barrier, len(partners))


def split(value):
    high = value.astype(BF16).astype(F32)
    return high, value - high


def pack(columns, lanes):
    lane = lax.broadcasted_iota(jnp.int32, (columns[0].shape[0], LANES), 1)
    result = jnp.zeros((columns[0].shape[0], LANES), F32)
    for column, n in zip(columns, lanes):
        result = jnp.where(lane == n, column, result)
    return result


def route_term(stat, grads, router, start, size):
    gates = [stat[:, k : k + 1] for k in range(TOPK)]
    mean = gates[0] * grads[0] + gates[1] * grads[1]
    product = 0.0
    term = 0.0
    weights = [gates[k] * (grads[k] - mean) for k in range(TOPK)]
    for k in range(TOPK):
        product += weights[k] * stat[:, 2 + k : 3 + k]
    for e in range(router.shape[0]):
        weight = 0.0
        for k in range(TOPK):
            weight += jnp.where(stat[:, 5 + k : 6 + k] == float(e), weights[k], 0.0)
        term += weight * router[e : e + 1, pl.ds(start, size)].astype(F32)
    return term, product


def fetch(sources, targets, sems):
    copies = []
    for n, (source, target) in enumerate(zip(sources, targets)):
        copies.append(pltpu.make_async_copy(source, target, sems.at[n]))
        copies[-1].start()
    return copies


def remote(source, target, send, recv, n, device):
    copy = pltpu.make_async_remote_copy(
        src_ref=source,
        dst_ref=target,
        send_sem=send.at[n],
        recv_sem=recv.at[n],
        device_id=device,
        device_id_type=pl.DeviceIdType.MESH,
    )
    copy.start()
    return copy


def dispatch_matrices(route, flip, experts, capacity):
    count = route.shape[0]
    lane = lax.broadcasted_iota(jnp.int32, (count, LANES), 1)
    chosen = [(route[:, k : k + 1] == lane).astype(F32) for k in range(TOPK)]
    place = lax.broadcasted_iota(jnp.int32, (count, count), 0)
    other = lax.broadcasted_iota(jnp.int32, (count, count), 1)
    before = (other < place).astype(F32).astype(BF16)
    earlier = jnp.dot(
        before, (chosen[0] + chosen[1]).astype(BF16), preferred_element_type=F32
    )
    rows = lax.broadcasted_iota(jnp.int32, (count, experts * capacity), 1)
    results = []
    for k in range(TOPK):
        position = jnp.sum(earlier * chosen[k], axis=1, keepdims=True).astype(jnp.int32)
        mine = jnp.bitwise_xor(route[:, k : k + 1], flip) * capacity + position
        results.append((rows == mine).astype(F32).astype(BF16))
    return results


def turn(value, cosine, sine):
    half = HEAD_DIM // 2
    heads = []
    for h in range(value.shape[1] // HEAD_DIM):
        head = value[:, h * HEAD_DIM : (h + 1) * HEAD_DIM]
        heads.append(head * cosine + pltpu.roll(head, half, axis=1) * sine)
    return jnp.concatenate(heads, axis=1)


def scores_of(stat_route, logits, experts):
    chosen = []
    for k in range(TOPK):
        score = 0.0
        for e in range(experts):
            score += jnp.where(stat_route[k] == float(e), logits[:, e : e + 1], 0.0)
        chosen.append(score)
    top = jnp.maximum(chosen[0], chosen[1])
    powers = [jnp.exp(score - top) for score in chosen]
    return chosen, [power / (powers[0] + powers[1]) for power in powers]


def front_kernel(parts, cols, replicas, *refs):
    lengths, pick, route_attn, route_ffn, cot, norm, router, cosine, sine, rights = refs[:10]
    left_refs = refs[10:15]
    tokens = refs[15]
    blocks = refs[16:19]
    pairs = refs[19]
    outs = refs[20:]
    flat = outs[0]
    outs = outs[1:]
    wholes = outs[:3]
    cot_wholes = outs[3 : 3 + EXP_FF]
    (
        hidden,
        lefts,
        stat,
        low_in,
        keys,
        values,
        queries,
        attended,
        probability,
        att_rows,
        low_rows,
        out_rows,
        picks_attn,
        picks_ffn,
        ranks,
        gate_rows,
        picks,
    ) = outs[3 + EXP_FF : 20 + EXP_FF]
    (
        x_all,
        own_rows,
        landed,
        hidden_rows,
        buffer,
        query_rows,
        pick_out,
        lefts_out,
        pair_in,
        pair_out,
        send,
        recv,
        local,
        load,
    ) = outs[20 + EXP_FF :]
    row = lax.axis_index("row")
    col = lax.axis_index("col")
    depth = blocks[0].shape[1]
    count, wide = tokens.shape
    width = hidden.shape[1]
    head_width = keys.shape[1]
    heads = head_width // HEAD_DIM
    across = [None] + [opposite("row", m) for m in range(1, parts)]
    along = [opposite("col", i) for i in range(1, cols)]
    greet(across[1:] + along)
    started, kept = [], []
    received = set()
    here = pl.ds(pl.multiple_of(col * wide, wide), wide)
    own = pl.ds(pl.multiple_of(row * depth, depth), depth)

    def send_to(source, target, device):
        copy = remote(source, target, send, recv, len(started), device)
        started.append(copy)
        return copy

    def arrive(copy):
        copy.wait_recv()
        received.add(id(copy))

    def keep(source, target):
        copy = pltpu.make_async_copy(source, target, local.at[len(kept)])
        copy.start()
        kept.append(copy)
        return copy

    pair = 2
    chunks = [
        (a, start) for a in range(3) for start in range(0, blocks[a].shape[0], pair)
    ]

    def place(n, offset, item=None):
        array, start = chunks[n]
        owner = jnp.bitwise_xor(row, offset)
        owner_rows = pl.ds(pl.multiple_of(owner * depth, depth), depth)
        if item is None:
            return wholes[array].at[pl.ds(start, pair), owner_rows]
        return wholes[array].at[start + item, owner_rows]

    first, direct, relayed, beside = {}, {}, {}, {}

    def push_own(n):
        if n >= len(chunks):
            return
        array, start = chunks[n]
        source = blocks[array].at[pl.ds(start, pair)]
        if parts == 8:
            first[n] = [send_to(source, place(n, 0), across[m]) for m in (2, 4)]
            beside[n] = [send_to(source, place(n, 0), across[1])]
        else:
            direct[n] = [send_to(source, place(n, 0), across[m]) for m in range(1, parts)]

    def relay(n):
        if parts == 8:
            for copy in first[n]:
                arrive(copy)
            relayed[n] = [
                send_to(place(n, 2, 0), place(n, 2, 0), across[4]),
                send_to(place(n, 4, 1), place(n, 4, 1), across[2]),
            ]
            for offset in (2, 4):
                beside[n].append(send_to(place(n, offset), place(n, offset), across[1]))

    def finish(n):
        if parts == 8:
            for copy in relayed[n]:
                arrive(copy)
            beside[n].append(send_to(place(n, 6), place(n, 6), across[1]))
            for copy in beside[n]:
                arrive(copy)
        else:
            for copy in direct[n]:
                arrive(copy)

    token_copies = [send_to(tokens, x_all.at[:, here], device) for device in along]
    token_kept = keep(tokens, x_all.at[:, here])
    block_kept = [keep(blocks[a], wholes[a].at[:, own]) for a in range(3)]
    pick_out[...] = jnp.full(pick_out.shape, 1.0, F32) * pick[0].astype(F32)
    picks[0] = pick_out[...]
    pick_copies = [
        send_to(pick_out, picks.at[m], across[m]) for m in range(1, parts)
    ]
    window, behind = 9, 5
    for n in range(window):
        push_own(n)

    position = lax.broadcasted_iota(jnp.int32, (count, 1), 0)
    valid = position < lengths[0]
    matrices = dispatch_matrices(route_ffn[...], row // replicas, EXP_FF, CAP_FF)
    for k in range(TOPK):
        picks_ffn[k] = matrices[k]
    masked = jnp.where(valid, cot[...].astype(F32), 0.0).astype(BF16)

    def rows_of(matrix, value):
        return lax.dot_general(
            matrix, value, (((0,), (0,)), ((), ())), preferred_element_type=F32
        )

    def times(left, right):
        return lax.dot_general(
            left, right, (((1,), (1,)), ((), ())), preferred_element_type=F32
        )

    dispatched = rows_of(matrices[0] + matrices[1], masked).astype(BF16)
    for j in range(EXP_FF):
        own_rows[j] = dispatched[j * CAP_FF : (j + 1) * CAP_FF]
    traded = [
        send_to(own_rows.at[j], landed.at[j - 1], across[j * replicas])
        for j in range(1, EXP_FF)
    ]
    attn = dispatch_matrices(route_attn[...], 0, EXP_ATT, CAP_ATT)
    for k in range(TOPK):
        picks_attn[k] = attn[k]
    attn_any = attn[0] + attn[1]
    picks_attn[TOPK] = attn_any

    left_copies = []
    for m in range(parts):
        if m:
            arrive(pick_copies[m - 1])
        theirs = picks[m, 0:1, 0:1]
        for p in range(5):
            value = jnp.zeros((RANK, depth), F32)
            for a in range(ADAPT):
                value += jnp.where(theirs == float(a), left_refs[p][a].astype(F32), 0.0)
            lefts_out[m, p * RANK : (p + 1) * RANK] = value.astype(BF16)
        if m:
            left_copies.append(send_to(lefts_out.at[m], lefts.at[:, own], across[m]))
        else:
            lefts[:, own] = lefts_out[0]
    for j in range(EXP_FF):
        if j:
            arrive(traded[j - 1])
            source = landed.at[j - 1]
        else:
            source = own_rows.at[0]
        keep(source, cot_wholes[j].at[:, here])
        for device in along:
            send_to(source, cot_wholes[j].at[:, here], device)
    relay(0)
    push_own(window)

    for copy in token_copies:
        arrive(copy)
    token_kept.wait()
    square = jnp.zeros((count, 1), F32)
    for q in range(cols):
        value = x_all[:, q * wide : (q + 1) * wide].astype(F32)
        square += jnp.sum(value * value, axis=1, keepdims=True)
    scale = lax.rsqrt(square * (1.0 / width) + EPSILON)
    for q in range(cols):
        span = slice(q * wide, (q + 1) * wide)
        value = x_all[:, span].astype(F32)
        hidden[:, span] = (value * scale * norm[:, span]).astype(BF16)
    for copy in left_copies:
        arrive(copy)
    relay(1)
    push_own(window + 1)
    logits = times(hidden[...], router[...])
    routes = [route_attn[:, k : k + 1].astype(F32) for k in range(TOPK)]
    chosen, gates = scores_of(routes, logits, EXP_ATT)
    extras = [valid.astype(F32), *(route_ffn[:, k : k + 1].astype(F32) for k in range(TOPK))]
    stat[...] = pack([*gates, *chosen, scale, *routes, *extras], range(10))
    rank_both = times(hidden[...], lefts[: 2 * RANK])
    ranks[...] = rank_both
    rank_query = rank_both[:, :RANK].astype(BF16)
    rank_kv = rank_both[:, RANK:].astype(BF16)
    low_down = times(masked, lefts[4 * RANK : 5 * RANK, here])
    low_in[...] = jnp.concatenate(
        [
            jnp.zeros((count, 2 * RANK), F32),
            low_down,
            jnp.zeros((count, LANES - 3 * RANK), F32),
        ],
        axis=1,
    )
    gate_wide = 0.0
    for k in range(TOPK):
        columns = pack([*split(gates[k])], range(2)).astype(BF16)
        gate_wide += rows_of(attn[k], columns)
    gate_row = gate_wide[:, 0:1] + gate_wide[:, 1:2]
    gate_rows[...] = gate_row
    rank_rows = rows_of(attn_any, rank_query).astype(BF16)
    for q in range(cols):
        span = slice(q * wide, (q + 1) * wide)
        hidden_rows[:, span] = rows_of(attn_any, hidden[:, span]).astype(BF16)

    def attend():
        value = query_rows[...]
        high = value.astype(BF16)
        low = (value - high.astype(F32)).astype(BF16)
        for k in range(TOPK):
            query = jnp.dot(attn[k], high, preferred_element_type=F32) + jnp.dot(
                attn[k], low, preferred_element_type=F32
            )
            queries[k] = turn(query, cosine[...], sine[...]).astype(BF16)
        other = lax.broadcasted_iota(jnp.int32, (count, count), 1)
        place_row = lax.broadcasted_iota(jnp.int32, (count, count), 0)
        allowed = (other <= place_row) & (other < lengths[0])
        for h in range(heads):
            span = slice(h * HEAD_DIM, (h + 1) * HEAD_DIM)
            for k in range(TOPK):
                scores = times(queries[k, :, span], keys[:, span]) * HEAD_DIM ** (-0.5)
                scores = jnp.where(allowed, scores, -1e30)
                power = jnp.exp(scores - jnp.max(scores, axis=1, keepdims=True))
                probs = power / jnp.sum(power, axis=1, keepdims=True)
                probability[h, k] = probs
                attended[k, :, span] = jnp.dot(
                    probs.astype(BF16), values[:, span], preferred_element_type=F32
                ).astype(BF16)
        rows = rows_of(attn[0], attended[0]) + rows_of(attn[1], attended[1])
        att_rows[...] = rows.astype(BF16)
        low = times(att_rows[...], rights[3 * RANK :]) * gate_row
        low_rows[...] = jnp.concatenate(
            [
                jnp.zeros((low.shape[0], RANK), F32),
                low,
                jnp.zeros((low.shape[0], LANES - 2 * RANK), F32),
            ],
            axis=1,
        ).astype(BF16)

    def compute(n):
        array, start = chunks[n]
        weight = buffer.at[n % 2]
        if array == 0:
            key = jnp.dot(hidden[...], weight[0], preferred_element_type=F32) + jnp.dot(
                rank_kv, rights[RANK : 2 * RANK], preferred_element_type=F32
            )
            keys[...] = turn(key, cosine[...], sine[...]).astype(BF16)
            value = jnp.dot(hidden[...], weight[1], preferred_element_type=F32) + jnp.dot(
                rank_kv, rights[2 * RANK : 3 * RANK], preferred_element_type=F32
            )
            values[...] = value.astype(BF16)
            return
        for item in range(pair):
            e = start + item
            span = slice(e * CAP_ATT, (e + 1) * CAP_ATT)
            if array == 1:
                query_rows[span] = jnp.dot(
                    hidden_rows[span], weight[item], preferred_element_type=F32
                ) + jnp.dot(rank_rows[span], rights[:RANK], preferred_element_type=F32)
            else:
                out_rows[span] = (times(att_rows[span], weight[item]) * gate_row[span]).astype(
                    BF16
                )
        if array == 1 and start + pair == EXP_ATT:
            attend()

    def flatten(e):
        copy = pltpu.make_async_copy(pairs.at[e], pair_in, load.at[2])
        copy.start()
        copy.wait()
        step = 64

        @pl.loop(0, pair_in.shape[0] // step)
        def _(i):
            span = pl.ds(pl.multiple_of(i * step, step), step)
            pair_out[span] = pair_in[span].reshape(step, pair_out.shape[1])

        copy = pltpu.make_async_copy(pair_out, flat.at[e], load.at[3])
        copy.start()
        copy.wait()

    loads = {}
    total = len(chunks)
    for n in range(2, total + behind + 1):
        if n < total:
            relay(n)
            push_own(n + window)
        if n - 2 < EXP_FF:
            flatten(n - 2)
        for m in range(n - behind + 1) if n == 2 else [n - behind]:
            if 0 <= m < total:
                if m == 0:
                    for copy in block_kept:
                        copy.wait()
                finish(m)
                loads[m] = pltpu.make_async_copy(
                    place_whole(wholes, chunks[m], pair), buffer.at[m % 2], load.at[m % 2]
                )
                loads[m].start()
            if 0 <= m - 1 < total:
                loads[m - 1].wait()
                compute(m - 1)
    for copy in started:
        if id(copy) not in received:
            copy.wait_recv()
    for copy in started:
        copy.wait_send()
    for copy in kept[1 + len(block_kept) :]:
        copy.wait()


def place_whole(wholes, chunk, pair):
    array, start = chunk
    return wholes[array].at[pl.ds(start, pair)]


def front(smalls, lefts, tokens, blocks, pairs, parts, cols, replicas):
    hbm = pl.BlockSpec(memory_space=pl.ANY)
    vmem = pl.BlockSpec(memory_space=pltpu.VMEM)
    smem = pl.BlockSpec(memory_space=pltpu.SMEM)
    count, wide = tokens.shape
    width = wide * cols
    depth, head_width = blocks[0].shape[1:]
    heads = head_width // HEAD_DIM
    rows = EXP_ATT * CAP_ATT
    rows_ffn = EXP_FF * CAP_FF
    shape = jax.ShapeDtypeStruct
    flat = (pairs.shape[0], pairs.shape[1], 2 * pairs.shape[3])
    n_chunks = sum(block.shape[0] for block in blocks) // 2
    per_chunk = 8 if parts == 8 else parts - 1
    remotes = (
        n_chunks * per_chunk + (cols - 1) * (1 + EXP_FF) + EXP_FF - 1 + 2 * (parts - 1)
    )
    return pl.pallas_call(
        functools.partial(front_kernel, parts, cols, replicas),
        out_shape=[shape(flat, BF16)]
        + [shape((b.shape[0], width, head_width), BF16) for b in blocks]
        + [shape((CAP_FF, width), BF16)] * EXP_FF
        + [
            shape((count, width), BF16),
            shape((5 * RANK, width), BF16),
            shape((count, LANES), F32),
            shape((count, LANES), F32),
            shape((count, head_width), BF16),
            shape((count, head_width), BF16),
            shape((TOPK, count, head_width), BF16),
            shape((TOPK, count, head_width), BF16),
            shape((heads, TOPK, count, count), F32),
            shape((rows, head_width), BF16),
            shape((rows, LANES), BF16),
            shape((rows, width), BF16),
            shape((TOPK + 1, count, rows), BF16),
            shape((TOPK, count, rows_ffn), BF16),
            shape((count, 2 * RANK), F32),
            shape((rows, 1), F32),
            shape((parts, 8, LANES), F32),
        ],
        in_specs=[smem] * 2 + [vmem] * 13 + [hbm] * 5,
        out_specs=[hbm] * (4 + EXP_FF) + [vmem] * 17,
        scratch_shapes=[
            pltpu.VMEM((count, width), BF16),
            pltpu.VMEM((EXP_FF, CAP_FF, wide), BF16),
            pltpu.VMEM((EXP_FF - 1, CAP_FF, wide), BF16),
            pltpu.VMEM((rows, width), BF16),
            pltpu.VMEM((2, 2, width, head_width), BF16),
            pltpu.VMEM((rows, head_width), F32),
            pltpu.VMEM((8, LANES), F32),
            pltpu.VMEM((parts, 5 * RANK, depth), BF16),
            pltpu.VMEM(pairs.shape[1:], BF16),
            pltpu.VMEM(flat[1:], BF16),
            pltpu.SemaphoreType.DMA((remotes,)),
            pltpu.SemaphoreType.DMA((remotes,)),
            pltpu.SemaphoreType.DMA((4 + EXP_FF,)),
            pltpu.SemaphoreType.DMA((4,)),
        ],
        compiler_params=pltpu.CompilerParams(
            collective_id=1, has_side_effects=True, vmem_limit_bytes=62 * 2**20
        ),
    )(*smalls, *lefts, tokens, *blocks, pairs)


def middle_back_kernel(cols, replicas, *refs):
    blocks, downs = refs[:EXP_FF], refs[EXP_FF : 2 * EXP_FF]
    adapter, norm, router, stat = refs[2 * EXP_FF : 2 * EXP_FF + 4]
    sources = refs[2 * EXP_FF + 4 : 2 * EXP_FF + 9]
    grad_middle, grad_whole, totals, branch, low_down = refs[2 * EXP_FF + 9 : 2 * EXP_FF + 14]
    scratch = refs[2 * EXP_FF + 14 :]
    picks_ffn, lefts, hidden, middle, cot = scratch[:5]
    rows, down_rows, exact_part, parts, extra, parts_in, extra_in, low, send, recv, local = (
        scratch[5:]
    )
    col = lax.axis_index("col")
    count, wide = middle.shape
    width = hidden.shape[1]
    across = [opposite("row", j * replicas) for j in range(1, EXP_FF)]
    along = [opposite("col", i) for i in range(1, cols)]
    greet(across + along)
    copies = [
        remote(
            blocks[j], rows.at[pl.ds(j * CAP_FF, CAP_FF)], send, recv, j - 1, across[j - 1]
        )
        for j in range(1, EXP_FF)
    ]
    near = fetch(
        [blocks[0], downs[0], *sources],
        [rows.at[pl.ds(0, CAP_FF)], down_rows.at[pl.ds(0, CAP_FF)], *scratch[:5]],
        local,
    )
    for copy in near:
        copy.wait()
    for copy in copies:
        copy.wait_recv()
    base = EXP_FF - 1
    down_copies = [
        remote(
            downs[j],
            down_rows.at[pl.ds(j * CAP_FF, CAP_FF)],
            send,
            recv,
            base + j - 1,
            across[j - 1],
        )
        for j in range(1, EXP_FF)
    ]
    picks = [picks_ffn[0], picks_ffn[1]]
    any_pick = picks[0] + picks[1]

    def back(pick, source, start, size):
        return jnp.dot(pick, source[:, start : start + size], preferred_element_type=F32)

    sub = lax.broadcasted_iota(jnp.int32, (LANES, LANES), 0)
    lane = lax.broadcasted_iota(jnp.int32, (LANES, LANES), 1)
    mine = lax.broadcasted_iota(jnp.int32, (count, LANES), 1) // RANK == adapter[0]
    place_rank = (lane == RANK + sub % RANK).astype(F32).astype(BF16)

    def own_rank(value):
        value = jnp.where(mine, value, 0.0).astype(BF16)
        return jnp.dot(value, place_rank, preferred_element_type=F32)

    gate_grads = []
    for k in range(TOPK):
        pair = back(picks[k], rows, width + LANES, LANES)
        gate_grads.append(pair[:, 0:1] + pair[:, 1:2])
    rank = own_rank(back(any_pick, rows, width, LANES))
    rank_low = rank[:, RANK : 2 * RANK].astype(BF16)
    product = jnp.zeros((count, 1), F32)
    for q in range(cols):
        here = slice(q * wide, (q + 1) * wide)
        part = back(any_pick, rows, q * wide, wide) + jnp.dot(
            rank_low, lefts[3 * RANK : 4 * RANK, here], preferred_element_type=F32
        )
        product += jnp.sum(part * hidden[:, here].astype(F32), axis=1, keepdims=True)
        exact_part[q] = part
        parts[q] = part.astype(BF16)
    columns = [*split(gate_grads[0]), *split(gate_grads[1]), *split(product)]
    small = pack(columns, range(6)) + rank
    extra[...] = small.astype(BF16)
    base += EXP_FF - 1
    arrivals = []
    for i in range(1, cols):
        target = jnp.bitwise_xor(col, i)
        n = base + 2 * (i - 1)
        arrivals.append(remote(extra, extra_in.at[i - 1], send, recv, n + 1, along[i - 1]))
        arrivals.append(
            remote(parts.at[target], parts_in.at[i - 1], send, recv, n, along[i - 1])
        )
    for copy in arrivals:
        copy.wait_recv()
    grad = exact_part[col]
    total = small
    for i in range(cols - 1):
        grad += parts_in[i].astype(F32)
        total += extra_in[i].astype(F32)
    totals[...] = total
    gate_grads = [total[:, 0:1] + total[:, 1:2], total[:, 2:3] + total[:, 3:4]]
    first = pl.multiple_of(col * wide, wide)
    term, more = route_term(stat, gate_grads, router, first, wide)
    inner = total[:, 4:5] + total[:, 5:6] + more
    scaled = (grad + term) * norm[:, pl.ds(first, wide)]
    factor = stat[:, 4:5]
    valid = stat[:, 7:8]
    result = (
        cot[...].astype(F32) * valid
        + factor * scaled
        - middle[...] * (factor * factor * inner * (1.0 / width))
    )
    grad_middle[...] = result
    low[...] = result.astype(BF16)
    here = pl.ds(first, wide)
    kept = pltpu.make_async_copy(low, grad_whole.at[:, here], local.at[8])
    kept.start()
    base += 2 * (cols - 1)
    last = [
        remote(low, grad_whole.at[:, here], send, recv, base + i, along[i])
        for i in range(cols - 1)
    ]
    for copy in down_copies:
        copy.wait_recv()
    rank = own_rank(back(any_pick, down_rows, width, LANES))
    rank_low = rank[:, RANK : 2 * RANK].astype(BF16)
    low_down[...] = rank
    for q in range(cols):
        here = slice(q * wide, (q + 1) * wide)
        part = back(any_pick, down_rows, q * wide, wide) + jnp.dot(
            rank_low, lefts[4 * RANK : 5 * RANK, here], preferred_element_type=F32
        )
        branch[:, here] = part.astype(BF16)
    for copy in last:
        copy.wait_recv()
    for copy in copies + down_copies + arrivals + last:
        copy.wait_send()
    kept.wait()


def middle_back(blocks, downs, adapter, norm, router, stat, sources, cols, replicas):
    hbm = pl.BlockSpec(memory_space=pl.ANY)
    vmem = pl.BlockSpec(memory_space=pltpu.VMEM)
    smem = pl.BlockSpec(memory_space=pltpu.SMEM)
    count, wide = sources[-1].shape
    total = 2 * (EXP_FF - 1) + 3 * (cols - 1)
    rows = EXP_FF * CAP_FF
    return pl.pallas_call(
        functools.partial(middle_back_kernel, cols, replicas),
        out_shape=[
            jax.ShapeDtypeStruct((count, wide), F32),
            jax.ShapeDtypeStruct((count, wide * cols), BF16),
            jax.ShapeDtypeStruct((count, LANES), F32),
            jax.ShapeDtypeStruct((count, wide * cols), BF16),
            jax.ShapeDtypeStruct((count, LANES), F32),
        ],
        in_specs=[hbm] * (2 * EXP_FF) + [smem, vmem, vmem, vmem] + [hbm] * 5,
        out_specs=[vmem, hbm, vmem, vmem, vmem],
        scratch_shapes=[pltpu.VMEM(source.shape, source.dtype) for source in sources]
        + [
            pltpu.VMEM((rows, blocks[0].shape[1]), BF16),
            pltpu.VMEM((rows, downs[0].shape[1]), BF16),
            pltpu.VMEM((cols, count, wide), F32),
            pltpu.VMEM((cols, count, wide), BF16),
            pltpu.VMEM((count, LANES), BF16),
            pltpu.VMEM((cols - 1, count, wide), BF16),
            pltpu.VMEM((cols - 1, count, LANES), BF16),
            pltpu.VMEM((count, wide), BF16),
            pltpu.SemaphoreType.DMA((total,)),
            pltpu.SemaphoreType.DMA((total,)),
            pltpu.SemaphoreType.DMA((9,)),
        ],
        compiler_params=pltpu.CompilerParams(
            collective_id=4, has_side_effects=True, vmem_limit_bytes=62 * 2**20
        ),
    )(*blocks, *downs, adapter, norm, router, stat, *sources)


def tail_kernel(parts_axis, cols, *refs):
    (
        adapters,
        norm,
        router,
        stat,
        cosine,
        sine,
        rights,
        ranks,
        gate_rows,
        totals_attn,
        totals_ffn,
        low_down,
    ) = refs[:12]
    sources = refs[12:27]
    branch, out_whole, query_whole, kv_whole = refs[27:31]
    output, grad_inputs = refs[31:33]
    left_outs = refs[33:38]
    right_outs = refs[38:42]
    (
        grad_whole,
        picks,
        att_rows,
        queries,
        keys,
        values,
        probability,
        attended,
        lefts_whole,
        hidden_one,
        hidden_two,
        grad_middle,
        middle,
        cot,
        tokens,
    ) = refs[42:57]
    (
        cot_own,
        cot_whole,
        branch_in,
        rows,
        grads,
        buffer,
        query_grads,
        key_grad,
        value_grad,
        part,
        parts,
        extra,
        parts_in,
        extra_in,
        right_parts,
        rights_in,
        lefts,
        lefts_in,
        send,
        recv,
        local,
        load,
    ) = refs[57:]
    row = lax.axis_index("row")
    col = lax.axis_index("col")
    count, wide = tokens.shape
    width = hidden_one.shape[1]
    depth = width // parts_axis
    head_width = keys.shape[1]
    heads = head_width // HEAD_DIM
    along = [opposite("col", i) for i in range(1, cols)]
    across = [opposite("row", m) for m in range(1, parts_axis)]
    greet(across + along)
    started = []

    def send_to(source, target, device):
        copy = remote(source, target, send, recv, len(started), device)
        started.append(copy)
        return copy

    pair = 2
    chunks = [
        (whole, start)
        for whole in (out_whole, query_whole, kv_whole)
        for start in range(0, whole.shape[0], pair)
    ]
    loads = []
    for n, (whole, start) in enumerate(chunks):
        loads.append(
            pltpu.make_async_copy(whole.at[pl.ds(start, pair)], buffer.at[n % 2], load.at[n % 2])
        )
    near = fetch(sources, refs[42:57], local)
    loads[0].start()
    loads[1].start()
    first = pl.multiple_of(col * wide, wide)
    here = pl.ds(first, wide)
    valid = stat[:, 7:8]
    branch_copies = []
    for i in range(1, cols):
        target = jnp.bitwise_xor(col, i)
        theirs = pl.ds(pl.multiple_of(target * wide, wide), wide)
        branch_copies.append(send_to(branch.at[:, theirs], branch_in.at[i - 1], along[i - 1]))
    mine = pltpu.make_async_copy(branch.at[:, here], branch_in.at[cols - 1], local.at[15])
    mine.start()
    for copy in near:
        copy.wait()
    cot_own[...] = (cot[...].astype(F32) * valid).astype(BF16)
    cot_whole[:, here] = cot_own[...]
    cot_copies = [send_to(cot_own, cot_whole.at[:, here], device) for device in along]

    def rows_of(matrix, value):
        return lax.dot_general(
            matrix, value, (((0,), (0,)), ((), ())), preferred_element_type=F32
        )

    def times(left, right):
        return lax.dot_general(
            left, right, (((1,), (1,)), ((), ())), preferred_element_type=F32
        )

    def dot(left, right):
        return jnp.dot(left, right, preferred_element_type=F32)

    any_pick = picks[TOPK]
    low_grad = times(grad_whole[...], lefts_whole[2 * RANK : 3 * RANK])
    low_rows = rows_of(any_pick, low_grad.astype(BF16)).astype(BF16)
    for q in range(cols):
        span = slice(q * wide, (q + 1) * wide)
        rows[:, span] = rows_of(any_pick, grad_whole[:, span]).astype(BF16)
    number = 0

    def next_weights():
        nonlocal number
        loads[number].wait()
        return buffer.at[number % 2]

    def done_weights():
        nonlocal number
        if number + 2 < len(chunks):
            loads[number + 2].start()
        number += 1

    for start in range(0, EXP_ATT, pair):
        weight = next_weights()
        for item in range(pair):
            span = slice((start + item) * CAP_ATT, (start + item + 1) * CAP_ATT)
            grads[span] = dot(rows[span], weight[item]) + dot(low_rows[span], rights[3 * RANK :])
        done_weights()
    value = grads[...]
    gate_grad = jnp.sum(att_rows[...].astype(F32) * value, axis=1, keepdims=True)
    gate_pack = pack([*split(gate_grad)], range(2)).astype(BF16)
    gate_grads = []
    gated = (value * gate_rows[...]).astype(BF16)
    right_out = jnp.zeros((RANK, head_width), F32)
    for k in range(TOPK):
        both = dot(picks[k], gate_pack)
        gate_grads.append(both[:, 0:1] + both[:, 1:2])
        query_grads[k] = dot(picks[k], gated).astype(BF16)
        right_out += rows_of((stat[:, k : k + 1] * low_grad).astype(BF16), attended[k])
    scaling = HEAD_DIM ** (-0.5)
    query_sum = []
    for h in range(heads):
        span = slice(h * HEAD_DIM, (h + 1) * HEAD_DIM)
        key_total, value_total, sum_head = 0.0, 0.0, 0.0
        for k in range(TOPK):
            grad_att = query_grads[k, :, span]
            probs = probability[h, k]
            grad_prob = times(grad_att, values[:, span])
            centre = jnp.sum(probs * grad_prob, axis=1, keepdims=True)
            grad_score = (probs * (grad_prob - centre)).astype(BF16)
            value_total += rows_of(probs.astype(BF16), grad_att)
            key_total += rows_of(grad_score, queries[k, :, span])
            grad_query = dot(grad_score, keys[:, span]) * scaling
            turned = turn(grad_query, cosine[...], -sine[...]).astype(BF16)
            query_grads[k, :, span] = turned
            sum_head += turned.astype(F32)
        key_grad[:, span] = turn(key_total * scaling, cosine[...], -sine[...]).astype(BF16)
        value_grad[:, span] = value_total.astype(BF16)
        query_sum.append(sum_head.astype(BF16))
    query_sum = jnp.concatenate(query_sum, axis=1)
    rank_query = ranks[:, :RANK].astype(BF16)
    rank_kv = ranks[:, RANK:].astype(BF16)
    right_values = [
        rows_of(rank_query, query_sum),
        rows_of(rank_kv, key_grad[...]),
        rows_of(rank_kv, value_grad[...]),
        right_out,
    ]
    for p in range(4):
        right_parts[:, p * head_width : (p + 1) * head_width] = right_values[p].astype(BF16)
    right_copies = [
        send_to(right_parts, rights_in.at[m], across[m]) for m in range(parts_axis - 1)
    ]
    grad_rank_query = times(query_sum, rights[:RANK])
    grad_rank_kv = times(key_grad[...], rights[RANK : 2 * RANK]) + times(
        value_grad[...], rights[2 * RANK : 3 * RANK]
    )
    query_rows = (rows_of(picks[0], query_grads[0]) + rows_of(picks[1], query_grads[1])).astype(
        BF16
    )
    for start in range(0, EXP_ATT, pair):
        weight = next_weights()
        for item in range(pair):
            span = slice((start + item) * CAP_ATT, (start + item + 1) * CAP_ATT)
            rows[span] = times(query_rows[span], weight[item]).astype(BF16)
        done_weights()
    weight = next_weights()
    low = jnp.concatenate([grad_rank_query, grad_rank_kv], axis=1).astype(BF16)
    product = jnp.zeros((count, 1), F32)
    for q in range(cols):
        span = slice(q * wide, (q + 1) * wide)
        value = (
            dot(any_pick, rows[:, span])
            + times(key_grad[...], weight[0, span])
            + times(value_grad[...], weight[1, span])
            + dot(low, lefts_whole[: 2 * RANK, span])
        )
        product += jnp.sum(value * hidden_one[:, span].astype(F32), axis=1, keepdims=True)
        part[q] = value
        parts[q] = value.astype(BF16)
    columns = [*split(gate_grads[0]), *split(gate_grads[1]), *split(product)]
    small = pack(columns, range(6)) + jnp.concatenate(
        [
            jnp.zeros((count, RANK), F32),
            grad_rank_query,
            grad_rank_kv,
            low_down[:, RANK : 2 * RANK],
            jnp.zeros((count, LANES - 4 * RANK), F32),
        ],
        axis=1,
    )
    extra[...] = small.astype(BF16)
    extra_copies, part_copies = [], []
    for i in range(1, cols):
        target = jnp.bitwise_xor(col, i)
        extra_copies.append(send_to(extra, extra_in.at[i - 1], along[i - 1]))
        part_copies.append(send_to(parts.at[target], parts_in.at[i - 1], along[i - 1]))
    mine.wait()
    for copy in branch_copies:
        copy.wait_recv()
    result = middle[...]
    for i in range(cols):
        result += branch_in[i].astype(F32)
    output[...] = (result * valid).astype(BF16)
    for copy in cot_copies:
        copy.wait_recv()

    def outer(left, right):
        return rows_of(left, right).astype(BF16)

    whole = outer(totals_attn[...].astype(BF16), grad_whole[...])
    for m in range(parts_axis):
        lefts[m, 2 * RANK : 3 * RANK] = whole[RANK : 2 * RANK, m * depth : (m + 1) * depth]
    whole = outer(totals_ffn[...].astype(BF16), hidden_two[...])
    for m in range(parts_axis):
        lefts[m, 3 * RANK : 4 * RANK] = whole[RANK : 2 * RANK, m * depth : (m + 1) * depth]
    chosen_by = [
        [jnp.where(adapters[m] == a, 1.0, 0.0).astype(F32) for a in range(ADAPT)]
        for m in range(parts_axis)
    ]

    def share(values, target):
        for a in range(ADAPT):
            result = chosen_by[0][a] * values[0]
            for m in range(1, parts_axis):
                result += chosen_by[m][a] * values[m]
            target[a] = result

    for copy in right_copies:
        copy.wait_recv()
    for p in range(4):
        span = slice(p * head_width, (p + 1) * head_width)
        share(
            [right_parts[:, span].astype(F32)]
            + [rights_in[m, :, span].astype(F32) for m in range(parts_axis - 1)],
            right_outs[p],
        )
    total = small
    for i in range(cols - 1):
        extra_copies[i].wait_recv()
        total += extra_in[i].astype(F32)
    low_totals = total.astype(BF16)
    whole = outer(low_totals, hidden_one[...])
    for m in range(parts_axis):
        lefts[m, : 2 * RANK] = whole[RANK : 3 * RANK, m * depth : (m + 1) * depth]
    whole = outer(low_totals, cot_whole[...])
    for m in range(parts_axis):
        lefts[m, 4 * RANK :] = whole[3 * RANK : 4 * RANK, m * depth : (m + 1) * depth]
    left_copies = [
        send_to(lefts.at[jnp.bitwise_xor(row, m)], lefts_in.at[m - 1], across[m - 1])
        for m in range(1, parts_axis)
    ]
    gate_totals = [total[:, 0:1] + total[:, 1:2], total[:, 2:3] + total[:, 3:4]]
    term, more = route_term(stat, gate_totals, router, first, wide)
    inner = total[:, 4:5] + total[:, 5:6] + more
    grad = part[col] + term
    for i in range(cols - 1):
        part_copies[i].wait_recv()
        grad += parts_in[i].astype(F32)
    factor = stat[:, 4:5]
    grad_inputs[...] = (
        grad_middle[...]
        + factor * (grad * norm[:, here])
        - tokens[...].astype(F32) * (factor * factor * inner * (1.0 / width))
    )
    for copy in left_copies:
        copy.wait_recv()
    for p in range(5):
        span = slice(p * RANK, (p + 1) * RANK)
        share(
            [lefts[row, span].astype(F32)]
            + [lefts_in[m, span].astype(F32) for m in range(parts_axis - 1)],
            left_outs[p],
        )
    for copy in started:
        copy.wait_send()


def tail(smalls, sources, branch, wholes, parts_axis, cols):
    hbm = pl.BlockSpec(memory_space=pl.ANY)
    vmem = pl.BlockSpec(memory_space=pltpu.VMEM)
    smem = pl.BlockSpec(memory_space=pltpu.SMEM)
    count, wide = sources[-1].shape
    width = wide * cols
    depth = width // parts_axis
    head_width = wholes[0].shape[2]
    rows = EXP_ATT * CAP_ATT
    shape = jax.ShapeDtypeStruct
    total = 4 * (cols - 1) + 2 * (parts_axis - 1)
    return pl.pallas_call(
        functools.partial(tail_kernel, parts_axis, cols),
        out_shape=[shape((count, wide), BF16), shape((count, wide), F32)]
        + [shape((ADAPT, RANK, depth), F32)] * 5
        + [shape((ADAPT, RANK, head_width), F32)] * 4,
        in_specs=[smem] + [vmem] * 11 + [hbm] * 19,
        out_specs=[vmem] * 11,
        scratch_shapes=[pltpu.VMEM(source.shape, source.dtype) for source in sources]
        + [
            pltpu.VMEM((count, wide), BF16),
            pltpu.VMEM((count, width), BF16),
            pltpu.VMEM((cols, count, wide), BF16),
            pltpu.VMEM((rows, width), BF16),
            pltpu.VMEM((rows, head_width), F32),
            pltpu.VMEM((2, 2, width, head_width), BF16),
            pltpu.VMEM((TOPK, count, head_width), BF16),
            pltpu.VMEM((count, head_width), BF16),
            pltpu.VMEM((count, head_width), BF16),
            pltpu.VMEM((cols, count, wide), F32),
            pltpu.VMEM((cols, count, wide), BF16),
            pltpu.VMEM((count, LANES), BF16),
            pltpu.VMEM((cols - 1, count, wide), BF16),
            pltpu.VMEM((cols - 1, count, LANES), BF16),
            pltpu.VMEM((RANK, 4 * head_width), BF16),
            pltpu.VMEM((parts_axis - 1, RANK, 4 * head_width), BF16),
            pltpu.VMEM((parts_axis, 5 * RANK, depth), BF16),
            pltpu.VMEM((parts_axis - 1, 5 * RANK, depth), BF16),
            pltpu.SemaphoreType.DMA((total,)),
            pltpu.SemaphoreType.DMA((total,)),
            pltpu.SemaphoreType.DMA((16,)),
            pltpu.SemaphoreType.DMA((2,)),
        ],
        compiler_params=pltpu.CompilerParams(
            collective_id=5, has_side_effects=True, vmem_limit_bytes=62 * 2**20
        ),
    )(*smalls, *sources, branch, *wholes)


def middle_kernel(parts_axis, cols, replicas, *refs):
    adapter, norm, router, route, low_rows, low_in = refs[:6]
    sources = refs[6:11]
    weights = refs[11:13]
    outs = refs[13:]
    extra_chunks = parts_axis - 1
    chunks = [(None,) + tuple(outs[n * extra_chunks : (n + 1) * extra_chunks]) for n in (0, 1)]
    outs = outs[2 * extra_chunks :]
    hids = outs[:EXP_FF]
    hidden_out, middle, stat, totals = outs[EXP_FF : EXP_FF + 4]
    scratch = outs[EXP_FF + 4 :]
    out_rows, picks_attn, picks_ffn, lefts, tokens = scratch[:5]
    (
        exact_part,
        parts,
        extra,
        parts_in,
        extra_in,
        square,
        square_in,
        low,
        hidden,
        message,
        send,
        recv,
        local,
    ) = scratch[5:]
    col = lax.axis_index("col")
    count, wide = tokens.shape
    width = hidden.shape[1]
    across = [opposite("row", j * replicas) for j in range(1, EXP_FF)]
    beside = [opposite("row", i) for i in range(1, replicas)]
    along = [opposite("col", i) for i in range(1, cols)]
    greet(across + beside + along)
    near = fetch(sources, scratch[:5], local)
    used = [0]
    started = []

    def send_to(source, target, device):
        copy = remote(source, target, send, recv, used[0], device)
        used[0] += 1
        started.append(copy)
        return copy

    expert = lax.axis_index("row") // replicas
    piece_copies = [
        [
            send_to(weights[n].at[jnp.bitwise_xor(expert, j)], chunks[n][j * replicas], across[j - 1])
            for n in (0, 1)
        ]
        for j in range(1, EXP_FF)
    ]
    sibling_copies = [
        send_to(weights[n].at[expert], chunks[n][i], beside[i - 1])
        for i in range(1, replicas)
        for n in (0, 1)
    ]
    for copy in near:
        copy.wait()

    def back(source):
        return jnp.dot(picks_attn[TOPK], source, preferred_element_type=F32)

    def rows_of(matrix, value):
        return lax.dot_general(
            matrix, value, (((0,), (0,)), ((), ())), preferred_element_type=F32
        )

    sub = lax.broadcasted_iota(jnp.int32, (LANES, LANES), 0)
    lane = lax.broadcasted_iota(jnp.int32, (LANES, LANES), 1)
    lanes = lax.broadcasted_iota(jnp.int32, (count, LANES), 1)
    low_out = back(low_rows[...])
    small = low_in[...] + low_out
    low_out = low_out[:, RANK : 2 * RANK].astype(BF16)
    for q in range(cols):
        here = slice(q * wide, (q + 1) * wide)
        part = back(out_rows[:, here]) + jnp.dot(
            low_out, lefts[2 * RANK : 3 * RANK, here], preferred_element_type=F32
        )
        exact_part[q] = part
        parts[q] = part.astype(BF16)
    extra[...] = small.astype(BF16)
    part_copies = []
    extra_copies = []
    for i in range(1, cols):
        target = jnp.bitwise_xor(col, i)
        part_copies.append(send_to(parts.at[target], parts_in.at[i - 1], along[i - 1]))
        extra_copies.append(send_to(extra, extra_in.at[i - 1], along[i - 1]))
    value = tokens[...].astype(F32) + exact_part[col]
    total = small
    for i in range(cols - 1):
        part_copies[i].wait_recv()
        value += parts_in[i].astype(F32)
    middle[...] = value
    square[...] = lax.dot_general(
        jnp.ones((8, wide), F32),
        value * value,
        (((1,), (1,)), ((), ())),
        precision=HIGHEST,
        preferred_element_type=F32,
    )
    square_copies = [
        send_to(square, square_in.at[i], along[i]) for i in range(cols - 1)
    ]
    for i in range(cols - 1):
        extra_copies[i].wait_recv()
        total += extra_in[i].astype(F32)
    totals[...] = total
    squares = square[...]
    for i in range(cols - 1):
        square_copies[i].wait_recv()
        squares += square_in[i]
    squares = lax.dot_general(
        squares,
        jnp.full((8, LANES), 0.125, F32),
        (((0,), (0,)), ((), ())),
        precision=HIGHEST,
        preferred_element_type=F32,
    )
    scale = lax.rsqrt(squares[:, 0:1] * (1.0 / width) + EPSILON)
    first = pl.multiple_of(col * wide, wide)
    here = pl.ds(first, wide)
    low[...] = (value * scale * norm[:, here]).astype(BF16)
    hidden[:, here] = low[...]
    hidden_copies = [send_to(low, hidden.at[:, here], along[i]) for i in range(cols - 1)]
    mine = lanes // RANK == adapter[0]

    def own_adapter(value, start):
        spread = (sub - start == lane % RANK).astype(F32).astype(BF16)
        value = jnp.dot(value.astype(BF16), spread, preferred_element_type=F32)
        return jnp.where(mine, value, 0.0).astype(BF16)

    picks = [picks_ffn[0], picks_ffn[1]]
    any_pick = picks[0] + picks[1]
    message[:, width + 2 * LANES :] = rows_of(any_pick, own_adapter(total, 2 * RANK)).astype(BF16)
    for copy in hidden_copies:
        copy.wait_recv()
    kept = pltpu.make_async_copy(hidden, hidden_out, local.at[6])
    kept.start()

    def times(right):
        return lax.dot_general(
            hidden[...], right, (((1,), (1,)), ((), ())), preferred_element_type=F32
        )

    logits = times(router[...])
    routes = [route[:, 8 + k : 9 + k] for k in range(TOPK)]
    chosen, gates = scores_of(routes, logits, EXP_FF)
    stat[...] = pack(
        [*gates, *chosen, scale, *routes, route[:, 7:8]], range(8)
    )
    gate_rows = 0.0
    for k in range(TOPK):
        columns = pack([*split(gates[k])], range(2)).astype(BF16)
        gate_rows += rows_of(picks[k], columns)
    message[:, width + LANES : width + 2 * LANES] = gate_rows.astype(BF16)
    rank = times(lefts[3 * RANK : 4 * RANK])
    rank = jnp.concatenate([rank, jnp.zeros((count, LANES - RANK), F32)], axis=1)
    message[:, width : width + LANES] = rows_of(any_pick, own_adapter(rank, 0)).astype(BF16)
    for q in range(cols):
        span = slice(q * wide, (q + 1) * wide)
        message[:, span] = rows_of(any_pick, hidden[:, span]).astype(BF16)
    traded = [
        send_to(message.at[pl.ds(j * CAP_FF, CAP_FF)], hids[j], across[j - 1])
        for j in range(EXP_FF - 1, 0, -1)
    ]
    own = pltpu.make_async_copy(message.at[pl.ds(0, CAP_FF)], hids[0], local.at[7])
    own.start()
    for j in range(1, EXP_FF):
        for n in (0, 1):
            piece_copies[j - 1][n].wait_recv()
            for i in range(1, replicas):
                m = j * replicas
                sibling_copies.append(send_to(chunks[n][m], chunks[n][m + i], beside[i - 1]))
    for copy in traded + sibling_copies:
        copy.wait_recv()
    for copy in started:
        copy.wait_send()
    kept.wait()
    own.wait()


def middle_forward(adapter, norm, router, route, low_rows, low_in, sources, weights, parts_axis, cols, replicas):
    hbm = pl.BlockSpec(memory_space=pl.ANY)
    vmem = pl.BlockSpec(memory_space=pltpu.VMEM)
    smem = pl.BlockSpec(memory_space=pltpu.SMEM)
    count, wide = sources[-1].shape
    width = wide * cols
    rows = EXP_FF * CAP_FF
    full = width + 3 * LANES
    total = 2 * (parts_axis - 1) + 4 * (cols - 1) + EXP_FF - 1
    return pl.pallas_call(
        functools.partial(middle_kernel, parts_axis, cols, replicas),
        out_shape=[jax.ShapeDtypeStruct(weights[0].shape[1:], BF16)] * (parts_axis - 1)
        + [jax.ShapeDtypeStruct(weights[1].shape[1:], BF16)] * (parts_axis - 1)
        + [jax.ShapeDtypeStruct((CAP_FF, full), BF16)] * EXP_FF
        + [
            jax.ShapeDtypeStruct((count, width), BF16),
            jax.ShapeDtypeStruct((count, wide), F32),
            jax.ShapeDtypeStruct((count, LANES), F32),
            jax.ShapeDtypeStruct((count, LANES), F32),
        ],
        in_specs=[smem] + [vmem] * 5 + [hbm] * 7,
        out_specs=[hbm] * (2 * parts_axis - 1 + EXP_FF) + [vmem] * 3,
        scratch_shapes=[pltpu.VMEM(source.shape, source.dtype) for source in sources]
        + [
            pltpu.VMEM((cols, count, wide), F32),
            pltpu.VMEM((cols, count, wide), BF16),
            pltpu.VMEM((count, LANES), BF16),
            pltpu.VMEM((cols - 1, count, wide), BF16),
            pltpu.VMEM((cols - 1, count, LANES), BF16),
            pltpu.VMEM((8, count), F32),
            pltpu.VMEM((cols - 1, 8, count), F32),
            pltpu.VMEM((count, wide), BF16),
            pltpu.VMEM((count, width), BF16),
            pltpu.VMEM((rows, full), BF16),
            pltpu.SemaphoreType.DMA((total,)),
            pltpu.SemaphoreType.DMA((total,)),
            pltpu.SemaphoreType.DMA((8,)),
        ],
        compiler_params=pltpu.CompilerParams(
            collective_id=3, has_side_effects=True, vmem_limit_bytes=62 * 2**20
        ),
    )(adapter, norm, router, route, low_rows, low_in, *sources, *weights)


def ffn_kernel(parts, depth, width, units, *refs):
    hids = refs[:EXP_FF]
    cots = refs[EXP_FF : 2 * EXP_FF]
    inners = refs[2 * EXP_FF : 2 * EXP_FF + parts]
    lasts = refs[2 * EXP_FF + parts : 2 * EXP_FF + 2 * parts]
    rights = refs[2 * EXP_FF + 2 * parts]
    outs = refs[2 * EXP_FF + 2 * parts + 1 :]
    grads = outs[:EXP_FF]
    downs = outs[EXP_FF : 2 * EXP_FF]
    adapt = outs[2 * EXP_FF : 2 * EXP_FF + 3]
    hid, cot, block, act, product, sems = outs[2 * EXP_FF + 3 :]
    row = lax.axis_index("row")
    wide = width + LANES
    copies = []
    for j in range(EXP_FF):
        where = pl.ds(j * CAP_FF, CAP_FF)
        near = hids[j].at[:, pl.ds(0, wide + LANES)]
        copies.append(pltpu.make_async_copy(near, hid.at[where], sems.at[j]))
        near = cot.at[where, pl.ds(0, width)]
        copies.append(pltpu.make_async_copy(cots[j], near, sems.at[EXP_FF + j]))
        near = cot.at[where, pl.ds(width, LANES)]
        low = hids[j].at[:, pl.ds(wide + LANES, LANES)]
        copies.append(pltpu.make_async_copy(low, near, sems.at[2 * EXP_FF + j]))
    copies.append(pltpu.make_async_copy(rights, block.at[pl.ds(width, LANES)], sems.at[3 * EXP_FF]))
    expert = row // (parts // EXP_FF)
    for m in range(parts):
        owner = jnp.bitwise_xor(row, m)
        where = pl.ds(pl.multiple_of(owner * depth, depth), depth)
        inner = inners[m] if m else inners[0].at[expert]
        last = lasts[m] if m else lasts[0].at[expert]
        near = block.at[where, pl.ds(0, 2 * units)]
        copies.append(pltpu.make_async_copy(inner, near, sems.at[3 * EXP_FF + 1 + m]))
        near = block.at[where, pl.ds(2 * units, units)]
        copies.append(pltpu.make_async_copy(last, near, sems.at[3 * EXP_FF + 1 + parts + m]))
    for copy in copies:
        copy.start()
    for copy in copies:
        copy.wait()
    gate_scale = hid[:, wide : wide + 1].astype(F32) + hid[:, wide + 1 : wide + 2].astype(F32)
    product[...] = jnp.zeros_like(product)

    def forward(start, size):
        here = pl.ds(start, size)
        up_here = pl.ds(units + start, size)
        down_here = pl.ds(2 * units + start, size)
        gate = jnp.dot(hid[:, :wide], block[:, here], preferred_element_type=F32)
        up = jnp.dot(hid[:, :wide], block[:, up_here], preferred_element_type=F32)
        grad = jnp.dot(cot[...], block[:, down_here], preferred_element_type=F32)
        sig = 1.0 / (1.0 + jnp.exp(-gate))
        mixed = (gate * sig * up).astype(BF16)
        act[:, down_here] = mixed
        product[...] += jnp.sum(mixed.astype(F32) * grad, axis=1, keepdims=True)
        grad = grad * gate_scale
        act[:, here] = (grad * up * sig * (1.0 + gate * (1.0 - sig))).astype(BF16)
        act[:, up_here] = (grad * gate * sig).astype(BF16)

    step = 2 * LANES
    full = units // step

    @pl.loop(0, full)
    def _(i):
        forward(pl.multiple_of(i * step, step), step)

    if units % step:
        forward(full * step, units % step)

    def backward(start, size):
        here = pl.ds(start, size)
        result = lax.dot_general(
            act[:, : 2 * units], block[here, : 2 * units], (((1,), (1,)), ((), ())),
            preferred_element_type=F32,
        ).astype(BF16)
        for j in range(EXP_FF):
            grads[j][:, here] = result[j * CAP_FF : (j + 1) * CAP_FF]
        result = lax.dot_general(
            act[:, 2 * units :], block[here, 2 * units :], (((1,), (1,)), ((), ())),
            preferred_element_type=F32,
        )
        result = (result * gate_scale).astype(BF16)
        for j in range(EXP_FF):
            downs[j][:, here] = result[j * CAP_FF : (j + 1) * CAP_FF]

    full_rows = wide // step

    @pl.loop(0, full_rows)
    def _(i):
        backward(pl.multiple_of(i * step, step), step)

    if wide % step:
        backward(full_rows * step, wide % step)
    total = product[...]
    high = total.astype(BF16)
    low = (total - high.astype(F32)).astype(BF16)
    lane = lax.broadcasted_iota(jnp.int32, (EXP_FF * CAP_FF, LANES), 1)
    packed = jnp.where(lane == 0, high.astype(F32), jnp.where(lane == 1, low.astype(F32), 0.0)).astype(BF16)
    for j in range(EXP_FF):
        grads[j][:, wide:] = packed[j * CAP_FF : (j + 1) * CAP_FF]
    ext = hid[:, width:wide]
    low_ext = (cot[:, width:].astype(F32) * gate_scale).astype(BF16)
    for n, low_rows in enumerate((ext, ext, low_ext)):
        adapt[n][...] = lax.dot_general(
            low_rows,
            act[:, n * units : (n + 1) * units],
            (((0,), (0,)), ((), ())),
            preferred_element_type=F32,
        ).astype(BF16)


def feed_forward(hids, cots, inners, lasts, rights):
    parts = len(inners)
    depth, units = lasts[1].shape
    triple = 3 * units
    width = depth * parts
    rows = EXP_FF * CAP_FF
    hbm = pl.BlockSpec(memory_space=pl.ANY)
    vmem = pl.BlockSpec(memory_space=pltpu.VMEM)
    wide = width + LANES
    return pl.pallas_call(
        functools.partial(ffn_kernel, parts, depth, width, units),
        out_shape=[jax.ShapeDtypeStruct((CAP_FF, wide + LANES), BF16)] * EXP_FF
        + [jax.ShapeDtypeStruct((CAP_FF, wide), BF16)] * EXP_FF
        + [jax.ShapeDtypeStruct((LANES, units), BF16)] * 3,
        in_specs=[hbm] * (2 * EXP_FF + 2 * parts + 1),
        out_specs=[vmem] * (2 * EXP_FF + 3),
        scratch_shapes=[
            pltpu.VMEM((rows, wide + LANES), BF16),
            pltpu.VMEM((rows, wide), BF16),
            pltpu.VMEM((wide, triple), BF16),
            pltpu.VMEM((rows, triple), BF16),
            pltpu.VMEM((rows, 1), F32),
            pltpu.SemaphoreType.DMA((3 * EXP_FF + 1 + 2 * parts,)),
        ],
        compiler_params=pltpu.CompilerParams(vmem_limit_bytes=62 * 2**20),
    )(*hids, *cots, *inners, *lasts, rights)


def on_device(
    inputs,
    cotangent,
    lengths,
    adapter_pick,
    attn_route,
    ffn_route,
    norm_one,
    norm_two,
    router_attn,
    router_ffn,
    kv_weight,
    query_weight,
    out_weight,
    inner_weight,
    down_weight,
    query_left,
    query_right,
    kv_left,
    kv_right,
    out_left,
    out_right,
    inner_left,
    inner_right,
    down_left,
    down_right,
):
    count = inputs.shape[0]
    rows_axis = lax.axis_size("row")
    replicas = rows_axis // EXP_FF
    units = inner_weight.shape[3]
    adapter = adapter_pick[0]
    cosine, sine = tables(count, HEAD_DIM)
    turns = (
        jnp.concatenate([cosine, cosine], axis=1),
        jnp.concatenate([-sine, sine], axis=1),
    )

    cols = lax.axis_size("col")
    padding = -units % LANES

    def padded(value):
        if not padding:
            return value
        return jnp.pad(value, [(0, 0)] * (value.ndim - 1) + [(0, padding)])

    down_flat = padded(down_weight)

    rights = jnp.concatenate(
        [
            query_right[adapter],
            kv_right[adapter][:, 0],
            kv_right[adapter][:, 1],
            out_right[adapter],
        ]
    )
    lefts_own = [
        value.swapaxes(1, 2)
        for value in (query_left, kv_left, out_left, inner_left, down_left)
    ]
    (
        inner_flat,
        kv_full,
        query_full,
        out_full,
        *cot_rows,
        hidden_one,
        lefts,
        stat_attn,
        low_in,
        keys,
        values,
        queries,
        attended,
        probability,
        attended_rows,
        low_rows,
        out_rows,
        picks_attn,
        picks_ffn,
        ranks,
        gate_rows,
        picks,
    ) = front(
        [
            lengths,
            adapter_pick,
            attn_route,
            ffn_route,
            cotangent,
            norm_one[None, :],
            router_attn.T,
            *turns,
            rights,
        ],
        lefts_own,
        inputs,
        [kv_weight, query_weight, out_weight],
        padded(inner_weight),
        rows_axis,
        cols,
        replicas,
    )
    picks = picks[:, 0, 0].astype(jnp.int32)
    right_inner_all = inner_right.reshape(ADAPT * RANK, 2, units)
    right_down_all = down_right.reshape(ADAPT * RANK, units)
    ffn_right = jnp.concatenate(
        [padded(right_inner_all[:, 0]), padded(right_inner_all[:, 1]), padded(right_down_all)],
        axis=1,
    )

    *outs, hidden_two, middle, stat_ffn, totals_attn = middle_forward(
        adapter_pick,
        norm_two[None, :],
        router_ffn.T,
        stat_attn,
        low_rows,
        low_in,
        [out_rows, picks_attn, picks_ffn, lefts, inputs],
        [inner_flat, down_flat],
        rows_axis,
        cols,
        replicas,
    )
    inners = [inner_flat, *outs[: rows_axis - 1]]
    lasts = [down_flat, *outs[rows_axis - 1 : 2 * rows_axis - 2]]
    hidden_in = outs[2 * rows_axis - 2 :]
    results = feed_forward(hidden_in, cot_rows, inners, lasts, ffn_right)
    grad_middle, grad_full, totals, branch_ffn, low_down_part = middle_back(
        results[:EXP_FF],
        results[EXP_FF : 2 * EXP_FF],
        adapter_pick,
        norm_two[None, :],
        router_ffn.T,
        stat_ffn,
        [picks_ffn, lefts, hidden_two, middle, cotangent],
        cols,
        replicas,
    )
    rights_ffn = lax.optimization_barrier(lax.psum(lax.optimization_barrier((*results[2 * EXP_FF :], totals))[:3], "row"))
    rights_ffn = [
        value[:, :units].reshape(ADAPT, RANK, units).astype(F32) for value in rights_ffn
    ]

    output, grad_inputs, *grads = tail(
        [
            picks,
            norm_one[None, :],
            router_attn.T,
            stat_attn,
            *turns,
            rights,
            ranks,
            gate_rows,
            totals_attn,
            totals,
            low_down_part,
        ],
        [
            grad_full,
            picks_attn,
            attended_rows,
            queries,
            keys,
            values,
            probability,
            attended,
            lefts,
            hidden_one,
            hidden_two,
            grad_middle,
            middle,
            cotangent,
            inputs,
        ],
        branch_ffn,
        [out_full, query_full, kv_full],
        rows_axis,
        cols,
    )
    lefts_back = [grad.swapaxes(1, 2) for grad in grads[:5]]
    rights_back = grads[5:]
    return (
        output,
        grad_inputs,
        lefts_back[0],
        rights_back[0],
        lefts_back[1],
        jnp.stack(rights_back[1:3], axis=2),
        lefts_back[2],
        rights_back[3],
        lefts_back[3],
        jnp.stack(rights_ffn[:2], axis=2),
        lefts_back[4],
        rights_ffn[2],
    )


def solution(mesh):
    placed = (
        P("row", "col"),
        P("row", "col"),
        P("row"),
        P("row"),
        P("row", None),
        P("row", None),
        P(),
        P(),
        P(),
        P(),
        P(None, "row", "col"),
        P(None, "row", "col"),
        P(None, "row", "col"),
        P(None, "row", None, "col"),
        P(None, "row", "col"),
        P(None, "row", None),
        P(None, None, "col"),
        P(None, "row", None),
        P(None, None, None, "col"),
        P(None, "row", None),
        P(None, None, "col"),
        P(None, "row", None),
        P(None, None, None, "col"),
        P(None, "row", None),
        P(None, None, "col"),
    )
    return jax.shard_map(
        on_device,
        mesh=mesh,
        in_specs=placed,
        out_specs=(
            P("row", "col"),
            P("row", "col"),
            P(None, "row", None),
            P(None, None, "col"),
            P(None, "row", None),
            P(None, None, None, "col"),
            P(None, "row", None),
            P(None, None, "col"),
            P(None, "row", None),
            P(None, None, None, "col"),
            P(None, "row", None),
            P(None, None, "col"),
        ),
        check_vma=False,
    )
```

```python
import functools

import jax
import jax.numpy as jnp
from jax import lax
from jax.experimental import pallas as pl
from jax.experimental.pallas import tpu as pltpu
from jax.sharding import PartitionSpec as P

HEAD_DIM = 128
EXP_ATT = 8
EXP_FF = 4
TOPK = 2
ADAPT = 8
RANK = 16
CAP_ATT = 80
CAP_FF = 160
EPSILON = 1e-06
ROPE_BASE = 10000.0
HIGHEST = lax.Precision.HIGHEST
F32 = jnp.float32
BF16 = jnp.bfloat16
LANES = 128


def tables(count, head_width):
    position = jnp.arange(count).astype(F32)
    frequency = ROPE_BASE ** (-jnp.arange(head_width // 2).astype(F32) * 2.0 / head_width)
    angle = position[:, None] * frequency[None, :]
    return (jnp.cos(angle), jnp.sin(angle))


def opposite(axis, offset):
    index = jnp.bitwise_xor(lax.axis_index(axis), offset)
    if axis == "row":
        return (index, lax.axis_index("col"))
    return (lax.axis_index("row"), index)


def greet(partners):
    barrier = pltpu.get_barrier_semaphore()
    for partner in partners:
        pl.semaphore_signal(
            barrier, inc=1, device_id=partner, device_id_type=pl.DeviceIdType.MESH
        )
    pl.semaphore_wait(barrier, len(partners))


def split(value):
    high = value.astype(BF16).astype(F32)
    return high, value - high


def pack(columns, lanes):
    lane = lax.broadcasted_iota(jnp.int32, (columns[0].shape[0], LANES), 1)
    result = jnp.zeros((columns[0].shape[0], LANES), F32)
    for column, n in zip(columns, lanes):
        result = jnp.where(lane == n, column, result)
    return result


def route_term(stat, grads, router, start, size):
    gates = [stat[:, k : k + 1] for k in range(TOPK)]
    mean = gates[0] * grads[0] + gates[1] * grads[1]
    product = 0.0
    term = 0.0
    weights = [gates[k] * (grads[k] - mean) for k in range(TOPK)]
    for k in range(TOPK):
        product += weights[k] * stat[:, 2 + k : 3 + k]
    for e in range(router.shape[0]):
        weight = 0.0
        for k in range(TOPK):
            weight += jnp.where(stat[:, 5 + k : 6 + k] == float(e), weights[k], 0.0)
        term += weight * router[e : e + 1, pl.ds(start, size)].astype(F32)
    return term, product


def fetch(sources, targets, sems):
    copies = []
    for n, (source, target) in enumerate(zip(sources, targets)):
        copies.append(pltpu.make_async_copy(source, target, sems.at[n]))
        copies[-1].start()
    return copies


def remote(source, target, send, recv, n, device):
    copy = pltpu.make_async_remote_copy(
        src_ref=source,
        dst_ref=target,
        send_sem=send.at[n],
        recv_sem=recv.at[n],
        device_id=device,
        device_id_type=pl.DeviceIdType.MESH,
    )
    copy.start()
    return copy


def dispatch_matrices(route, flip, experts, capacity):
    route = [column.astype(jnp.int32) for column in route]
    count = route[0].shape[0]
    lane = lax.broadcasted_iota(jnp.int32, (count, LANES), 1)
    chosen = [(route[k] == lane).astype(F32) for k in range(TOPK)]
    place = lax.broadcasted_iota(jnp.int32, (count, count), 0)
    other = lax.broadcasted_iota(jnp.int32, (count, count), 1)
    before = (other < place).astype(F32).astype(BF16)
    earlier = jnp.dot(
        before, (chosen[0] + chosen[1]).astype(BF16), preferred_element_type=F32
    )
    rows = lax.broadcasted_iota(jnp.int32, (count, experts * capacity), 1)
    results = []
    for k in range(TOPK):
        position = jnp.sum(earlier * chosen[k], axis=1, keepdims=True).astype(jnp.int32)
        mine = jnp.bitwise_xor(route[k], flip) * capacity + position
        results.append((rows == mine).astype(F32).astype(BF16))
    return results


def turn(value, cosine, sine):
    half = HEAD_DIM // 2
    heads = []
    for h in range(value.shape[1] // HEAD_DIM):
        head = value[:, h * HEAD_DIM : (h + 1) * HEAD_DIM]
        heads.append(head * cosine + pltpu.roll(head, half, axis=1) * sine)
    return jnp.concatenate(heads, axis=1)


def scores_of(stat_route, logits, experts):
    chosen = []
    for k in range(TOPK):
        score = 0.0
        for e in range(experts):
            score += jnp.where(stat_route[k] == float(e), logits[:, e : e + 1], 0.0)
        chosen.append(score)
    top = jnp.maximum(chosen[0], chosen[1])
    powers = [jnp.exp(score - top) for score in chosen]
    return chosen, [power / (powers[0] + powers[1]) for power in powers]


def front_kernel(parts, cols, replicas, *refs):
    lengths, pick, routes_attn, routes_ffn, cot, norm, router, cosine, sine = refs[:9]
    query_right, kv_right, out_right = refs[9:12]
    left_refs = refs[12:17]
    tokens = refs[17]
    blocks = refs[18:21]
    pairs, pairs_right = refs[21:23]
    outs = refs[23:]
    flat, flat_right, rights = outs[:3]
    outs = outs[3:]
    wholes = outs[:3]
    cot_wholes = outs[3 : 3 + EXP_FF]
    (
        hidden,
        lefts,
        stat,
        low_in,
        keys,
        values,
        queries,
        attended,
        probability,
        att_rows,
        low_rows,
        out_rows,
        picks_attn,
        picks_ffn,
        ranks,
        gate_rows,
        picks,
    ) = outs[3 + EXP_FF : 20 + EXP_FF]
    (
        x_all,
        own_rows,
        landed,
        hidden_rows,
        buffer,
        query_rows,
        pick_out,
        lefts_out,
        pair_in,
        pair_out,
        send,
        recv,
        local,
        load,
    ) = outs[20 + EXP_FF :]
    row = lax.axis_index("row")
    col = lax.axis_index("col")
    depth = blocks[0].shape[1]
    count, wide = tokens.shape
    width = hidden.shape[1]
    head_width = keys.shape[1]
    heads = head_width // HEAD_DIM
    across = [None] + [opposite("row", m) for m in range(1, parts)]
    along = [opposite("col", i) for i in range(1, cols)]
    greet(across[1:] + along)
    started, kept = [], []
    received = set()
    here = pl.ds(pl.multiple_of(col * wide, wide), wide)
    own = pl.ds(pl.multiple_of(row * depth, depth), depth)

    def send_to(source, target, device):
        copy = remote(source, target, send, recv, len(started), device)
        started.append(copy)
        return copy

    def arrive(copy):
        copy.wait_recv()
        received.add(id(copy))

    def keep(source, target):
        copy = pltpu.make_async_copy(source, target, local.at[len(kept)])
        copy.start()
        kept.append(copy)
        return copy

    pair = 2
    chunks = [
        (a, start) for a in range(3) for start in range(0, blocks[a].shape[0], pair)
    ]

    def place(n, offset, item=None):
        array, start = chunks[n]
        owner = jnp.bitwise_xor(row, offset)
        owner_rows = pl.ds(pl.multiple_of(owner * depth, depth), depth)
        if item is None:
            return wholes[array].at[pl.ds(start, pair), owner_rows]
        return wholes[array].at[start + item, owner_rows]

    first, direct, relayed, beside = {}, {}, {}, {}

    def push_own(n):
        if n >= len(chunks):
            return
        array, start = chunks[n]
        source = blocks[array].at[pl.ds(start, pair)]
        if parts == 8:
            first[n] = [send_to(source, place(n, 0), across[m]) for m in (2, 4)]
            beside[n] = [send_to(source, place(n, 0), across[1])]
        else:
            direct[n] = [send_to(source, place(n, 0), across[m]) for m in range(1, parts)]

    def relay(n):
        if parts == 8:
            for copy in first[n]:
                arrive(copy)
            relayed[n] = [
                send_to(place(n, 2, 0), place(n, 2, 0), across[4]),
                send_to(place(n, 4, 1), place(n, 4, 1), across[2]),
            ]
            for offset in (2, 4):
                beside[n].append(send_to(place(n, offset), place(n, offset), across[1]))

    def finish(n):
        if parts == 8:
            for copy in relayed[n]:
                arrive(copy)
            beside[n].append(send_to(place(n, 6), place(n, 6), across[1]))
            for copy in beside[n]:
                arrive(copy)
        else:
            for copy in direct[n]:
                arrive(copy)

    token_copies = [send_to(tokens, x_all.at[:, here], device) for device in along]
    token_kept = keep(tokens, x_all.at[:, here])
    block_kept = [keep(blocks[a], wholes[a].at[:, own]) for a in range(3)]
    pick_out[...] = jnp.full(pick_out.shape, 1.0, F32) * pick[0].astype(F32)
    picks[0] = pick_out[...]
    pick_copies = [
        send_to(pick_out, picks.at[m], across[m]) for m in range(1, parts)
    ]
    window, behind = 9, 5
    for n in range(window):
        push_own(n)

    table = jnp.concatenate(
        [
            routes_attn[...].astype(F32),
            routes_ffn[...].astype(F32),
            jnp.zeros((8 - 2 * TOPK, count), F32),
        ]
    )
    same = lax.broadcasted_iota(jnp.int32, (8, LANES), 0) == lax.broadcasted_iota(
        jnp.int32, (8, LANES), 1
    )
    table = lax.dot_general(
        table.astype(BF16),
        same.astype(F32).astype(BF16),
        (((0,), (0,)), ((), ())),
        preferred_element_type=F32,
    )
    route_attn = [table[:, k : k + 1] for k in range(TOPK)]
    route_ffn = [table[:, TOPK + k : TOPK + k + 1] for k in range(TOPK)]
    chosen_adapter = pick[0]
    rights[:RANK] = query_right[chosen_adapter]
    pair_right = kv_right[chosen_adapter].reshape(RANK, 2 * head_width)
    rights[RANK : 2 * RANK] = pair_right[:, :head_width]
    rights[2 * RANK : 3 * RANK] = pair_right[:, head_width:]
    rights[3 * RANK :] = out_right[chosen_adapter]

    position = lax.broadcasted_iota(jnp.int32, (count, 1), 0)
    valid = position < lengths[0]
    matrices = dispatch_matrices(route_ffn, row // replicas, EXP_FF, CAP_FF)
    for k in range(TOPK):
        picks_ffn[k] = matrices[k]
    masked = jnp.where(valid, cot[...].astype(F32), 0.0).astype(BF16)

    def rows_of(matrix, value):
        return lax.dot_general(
            matrix, value, (((0,), (0,)), ((), ())), preferred_element_type=F32
        )

    def times(left, right):
        return lax.dot_general(
            left, right, (((1,), (1,)), ((), ())), preferred_element_type=F32
        )

    dispatched = rows_of(matrices[0] + matrices[1], masked).astype(BF16)
    for j in range(EXP_FF):
        own_rows[j] = dispatched[j * CAP_FF : (j + 1) * CAP_FF]
    traded = [
        send_to(own_rows.at[j], landed.at[j - 1], across[j * replicas])
        for j in range(1, EXP_FF)
    ]
    attn = dispatch_matrices(route_attn, 0, EXP_ATT, CAP_ATT)
    for k in range(TOPK):
        picks_attn[k] = attn[k]
    attn_any = attn[0] + attn[1]
    picks_attn[TOPK] = attn_any

    left_copies = []
    for m in range(parts):
        if m:
            arrive(pick_copies[m - 1])
        theirs = picks[m, 0:1, 0:1]
        for p in range(5):
            value = jnp.zeros((RANK, depth), F32)
            for a in range(ADAPT):
                value += jnp.where(theirs == float(a), left_refs[p][a].astype(F32), 0.0)
            lefts_out[m, p * RANK : (p + 1) * RANK] = value.astype(BF16)
        if m:
            left_copies.append(send_to(lefts_out.at[m], lefts.at[:, own], across[m]))
        else:
            lefts[:, own] = lefts_out[0]
    for j in range(EXP_FF):
        if j:
            arrive(traded[j - 1])
            source = landed.at[j - 1]
        else:
            source = own_rows.at[0]
        keep(source, cot_wholes[j].at[:, here])
        for device in along:
            send_to(source, cot_wholes[j].at[:, here], device)
    relay(0)
    push_own(window)

    for copy in token_copies:
        arrive(copy)
    token_kept.wait()
    square = jnp.zeros((count, 1), F32)
    for q in range(cols):
        value = x_all[:, q * wide : (q + 1) * wide].astype(F32)
        square += jnp.sum(value * value, axis=1, keepdims=True)
    scale = lax.rsqrt(square * (1.0 / width) + EPSILON)
    for q in range(cols):
        span = slice(q * wide, (q + 1) * wide)
        value = x_all[:, span].astype(F32)
        hidden[:, span] = (value * scale * norm[:, span]).astype(BF16)
    for copy in left_copies:
        arrive(copy)
    relay(1)
    push_own(window + 1)
    logits = times(hidden[...], router[...])
    chosen, gates = scores_of(route_attn, logits, EXP_ATT)
    columns = [*gates, *chosen, scale, *route_attn, valid.astype(F32), *route_ffn]
    stat[...] = pack(columns, range(10))
    rank_both = times(hidden[...], lefts[: 2 * RANK])
    ranks[...] = rank_both
    rank_query = rank_both[:, :RANK].astype(BF16)
    rank_kv = rank_both[:, RANK:].astype(BF16)
    low_down = times(masked, lefts[4 * RANK : 5 * RANK, here])
    low_in[...] = jnp.concatenate(
        [
            jnp.zeros((count, 2 * RANK), F32),
            low_down,
            jnp.zeros((count, LANES - 3 * RANK), F32),
        ],
        axis=1,
    )
    gate_wide = 0.0
    for k in range(TOPK):
        columns = pack([*split(gates[k])], range(2)).astype(BF16)
        gate_wide += rows_of(attn[k], columns)
    gate_row = gate_wide[:, 0:1] + gate_wide[:, 1:2]
    gate_rows[...] = gate_row
    rank_rows = rows_of(attn_any, rank_query).astype(BF16)
    for q in range(cols):
        span = slice(q * wide, (q + 1) * wide)
        hidden_rows[:, span] = rows_of(attn_any, hidden[:, span]).astype(BF16)

    def attend():
        value = query_rows[...]
        high = value.astype(BF16)
        low = (value - high.astype(F32)).astype(BF16)
        for k in range(TOPK):
            query = jnp.dot(attn[k], high, preferred_element_type=F32) + jnp.dot(
                attn[k], low, preferred_element_type=F32
            )
            queries[k] = turn(query, cosine[...], sine[...]).astype(BF16)
        other = lax.broadcasted_iota(jnp.int32, (count, count), 1)
        place_row = lax.broadcasted_iota(jnp.int32, (count, count), 0)
        allowed = (other <= place_row) & (other < lengths[0])
        for h in range(heads):
            span = slice(h * HEAD_DIM, (h + 1) * HEAD_DIM)
            for k in range(TOPK):
                scores = times(queries[k, :, span], keys[:, span]) * HEAD_DIM ** (-0.5)
                scores = jnp.where(allowed, scores, -1e30)
                power = jnp.exp(scores - jnp.max(scores, axis=1, keepdims=True))
                probs = power / jnp.sum(power, axis=1, keepdims=True)
                probability[h, k] = probs
                attended[k, :, span] = jnp.dot(
                    probs.astype(BF16), values[:, span], preferred_element_type=F32
                ).astype(BF16)
        rows = rows_of(attn[0], attended[0]) + rows_of(attn[1], attended[1])
        att_rows[...] = rows.astype(BF16)
        low = times(att_rows[...], rights[3 * RANK :]) * gate_row
        low_rows[...] = jnp.concatenate(
            [
                jnp.zeros((low.shape[0], RANK), F32),
                low,
                jnp.zeros((low.shape[0], LANES - 2 * RANK), F32),
            ],
            axis=1,
        ).astype(BF16)

    def compute(n):
        array, start = chunks[n]
        weight = buffer.at[n % 2]
        if array == 0:
            key = jnp.dot(hidden[...], weight[0], preferred_element_type=F32) + jnp.dot(
                rank_kv, rights[RANK : 2 * RANK], preferred_element_type=F32
            )
            keys[...] = turn(key, cosine[...], sine[...]).astype(BF16)
            value = jnp.dot(hidden[...], weight[1], preferred_element_type=F32) + jnp.dot(
                rank_kv, rights[2 * RANK : 3 * RANK], preferred_element_type=F32
            )
            values[...] = value.astype(BF16)
            return
        for item in range(pair):
            e = start + item
            span = slice(e * CAP_ATT, (e + 1) * CAP_ATT)
            if array == 1:
                query_rows[span] = jnp.dot(
                    hidden_rows[span], weight[item], preferred_element_type=F32
                ) + jnp.dot(rank_rows[span], rights[:RANK], preferred_element_type=F32)
            else:
                out_rows[span] = (times(att_rows[span], weight[item]) * gate_row[span]).astype(
                    BF16
                )
        if array == 1 and start + pair == EXP_ATT:
            attend()

    def flatten(e):
        copy = pltpu.make_async_copy(pairs.at[e], pair_in, load.at[2])
        copy.start()
        copy.wait()
        step = 64

        @pl.loop(0, pair_in.shape[0] // step)
        def _(i):
            span = pl.ds(pl.multiple_of(i * step, step), step)
            pair_out[span] = pair_in[span].reshape(step, pair_out.shape[1])

        copy = pltpu.make_async_copy(pair_out, flat.at[e], load.at[3])
        copy.start()
        copy.wait()

    near = pair_in.at[pl.ds(0, pairs_right.shape[0])]
    copy = pltpu.make_async_copy(pairs_right, near, load.at[2])
    copy.start()
    copy.wait()
    step = 64
    pair_rows = pairs_right.shape[0]

    @pl.loop(0, pair_rows // step)
    def _(i):
        span = pl.ds(pl.multiple_of(i * step, step), step)
        pair_out[span] = pair_in[span].reshape(step, pair_out.shape[1])

    copy = pltpu.make_async_copy(pair_out.at[pl.ds(0, pair_rows)], flat_right, load.at[3])
    copy.start()
    copy.wait()
    loads = {}
    total = len(chunks)
    for n in range(2, total + behind + 1):
        if n < total:
            relay(n)
            push_own(n + window)
        if n - 2 < EXP_FF:
            flatten(n - 2)
        for m in range(n - behind + 1) if n == 2 else [n - behind]:
            if 0 <= m < total:
                if m == 0:
                    for copy in block_kept:
                        copy.wait()
                finish(m)
                loads[m] = pltpu.make_async_copy(
                    place_whole(wholes, chunks[m], pair), buffer.at[m % 2], load.at[m % 2]
                )
                loads[m].start()
            if 0 <= m - 1 < total:
                loads[m - 1].wait()
                compute(m - 1)
    for copy in started:
        if id(copy) not in received:
            copy.wait_recv()
    for copy in started:
        copy.wait_send()
    for copy in kept[1 + len(block_kept) :]:
        copy.wait()


def place_whole(wholes, chunk, pair):
    array, start = chunk
    return wholes[array].at[pl.ds(start, pair)]


def front(smalls, lefts, tokens, blocks, pairs, pairs_right, parts, cols, replicas):
    hbm = pl.BlockSpec(memory_space=pl.ANY)
    vmem = pl.BlockSpec(memory_space=pltpu.VMEM)
    smem = pl.BlockSpec(memory_space=pltpu.SMEM)
    count, wide = tokens.shape
    width = wide * cols
    depth, head_width = blocks[0].shape[1:]
    heads = head_width // HEAD_DIM
    rows = EXP_ATT * CAP_ATT
    rows_ffn = EXP_FF * CAP_FF
    shape = jax.ShapeDtypeStruct
    flat = (pairs.shape[0], pairs.shape[1], 2 * pairs.shape[3])
    n_chunks = sum(block.shape[0] for block in blocks) // 2
    per_chunk = 8 if parts == 8 else parts - 1
    remotes = (
        n_chunks * per_chunk + (cols - 1) * (1 + EXP_FF) + EXP_FF - 1 + 2 * (parts - 1)
    )
    return pl.pallas_call(
        functools.partial(front_kernel, parts, cols, replicas),
        out_shape=[
            shape(flat, BF16),
            shape((pairs_right.shape[0], flat[2]), BF16),
            shape((4 * RANK, head_width), BF16),
        ]
        + [shape((b.shape[0], width, head_width), BF16) for b in blocks]
        + [shape((CAP_FF, width), BF16)] * EXP_FF
        + [
            shape((count, width), BF16),
            shape((5 * RANK, width), BF16),
            shape((count, LANES), F32),
            shape((count, LANES), F32),
            shape((count, head_width), BF16),
            shape((count, head_width), BF16),
            shape((TOPK, count, head_width), BF16),
            shape((TOPK, count, head_width), BF16),
            shape((heads, TOPK, count, count), F32),
            shape((rows, head_width), BF16),
            shape((rows, LANES), BF16),
            shape((rows, width), BF16),
            shape((TOPK + 1, count, rows), BF16),
            shape((TOPK, count, rows_ffn), BF16),
            shape((count, 2 * RANK), F32),
            shape((rows, 1), F32),
            shape((parts, 8, LANES), F32),
        ],
        in_specs=[smem] * 2 + [vmem] * 15 + [hbm] * 6,
        out_specs=[hbm, hbm, vmem] + [hbm] * (3 + EXP_FF) + [vmem] * 17,
        scratch_shapes=[
            pltpu.VMEM((count, width), BF16),
            pltpu.VMEM((EXP_FF, CAP_FF, wide), BF16),
            pltpu.VMEM((EXP_FF - 1, CAP_FF, wide), BF16),
            pltpu.VMEM((rows, width), BF16),
            pltpu.VMEM((2, 2, width, head_width), BF16),
            pltpu.VMEM((rows, head_width), F32),
            pltpu.VMEM((8, LANES), F32),
            pltpu.VMEM((parts, 5 * RANK, depth), BF16),
            pltpu.VMEM(pairs.shape[1:], BF16),
            pltpu.VMEM(flat[1:], BF16),
            pltpu.SemaphoreType.DMA((remotes,)),
            pltpu.SemaphoreType.DMA((remotes,)),
            pltpu.SemaphoreType.DMA((4 + EXP_FF,)),
            pltpu.SemaphoreType.DMA((4,)),
        ],
        compiler_params=pltpu.CompilerParams(
            collective_id=1, has_side_effects=True, vmem_limit_bytes=62 * 2**20
        ),
    )(*smalls, *lefts, tokens, *blocks, pairs, pairs_right)


def middle_back_kernel(cols, replicas, *refs):
    blocks, downs = refs[:EXP_FF], refs[EXP_FF : 2 * EXP_FF]
    adapter, norm, router, stat = refs[2 * EXP_FF : 2 * EXP_FF + 4]
    sources = refs[2 * EXP_FF + 4 : 2 * EXP_FF + 9]
    grad_middle, grad_whole, totals, branch, low_down = refs[2 * EXP_FF + 9 : 2 * EXP_FF + 14]
    scratch = refs[2 * EXP_FF + 14 :]
    picks_ffn, lefts, hidden, middle, cot = scratch[:5]
    rows, down_rows, exact_part, parts, extra, parts_in, extra_in, low, send, recv, local = (
        scratch[5:]
    )
    col = lax.axis_index("col")
    count, wide = middle.shape
    width = hidden.shape[1]
    across = [opposite("row", j * replicas) for j in range(1, EXP_FF)]
    along = [opposite("col", i) for i in range(1, cols)]
    greet(across + along)
    near = fetch(
        [*blocks, downs[0], *sources],
        [
            *(rows.at[pl.ds(j * CAP_FF, CAP_FF)] for j in range(EXP_FF)),
            down_rows.at[pl.ds(0, CAP_FF)],
            *scratch[:5],
        ],
        local,
    )
    base = 0
    down_copies = [
        remote(
            downs[j],
            down_rows.at[pl.ds(j * CAP_FF, CAP_FF)],
            send,
            recv,
            base + j - 1,
            across[j - 1],
        )
        for j in range(1, EXP_FF)
    ]
    for copy in near:
        copy.wait()
    picks = [picks_ffn[0], picks_ffn[1]]
    any_pick = picks[0] + picks[1]

    def back(pick, source, start, size):
        return jnp.dot(pick, source[:, start : start + size], preferred_element_type=F32)

    sub = lax.broadcasted_iota(jnp.int32, (LANES, LANES), 0)
    lane = lax.broadcasted_iota(jnp.int32, (LANES, LANES), 1)
    mine = lax.broadcasted_iota(jnp.int32, (count, LANES), 1) // RANK == adapter[0]
    place_rank = (lane == RANK + sub % RANK).astype(F32).astype(BF16)

    def own_rank(value):
        value = jnp.where(mine, value, 0.0).astype(BF16)
        return jnp.dot(value, place_rank, preferred_element_type=F32)

    gate_grads = []
    for k in range(TOPK):
        pair = back(picks[k], rows, width + LANES, LANES)
        gate_grads.append(pair[:, 0:1] + pair[:, 1:2])
    rank = own_rank(back(any_pick, rows, width, LANES))
    rank_low = rank[:, RANK : 2 * RANK].astype(BF16)
    product = jnp.zeros((count, 1), F32)
    for q in range(cols):
        here = slice(q * wide, (q + 1) * wide)
        part = back(any_pick, rows, q * wide, wide) + jnp.dot(
            rank_low, lefts[3 * RANK : 4 * RANK, here], preferred_element_type=F32
        )
        product += jnp.sum(part * hidden[:, here].astype(F32), axis=1, keepdims=True)
        exact_part[q] = part
        parts[q] = part.astype(BF16)
    columns = [*split(gate_grads[0]), *split(gate_grads[1]), *split(product)]
    small = pack(columns, range(6)) + rank
    extra[...] = small.astype(BF16)
    base += EXP_FF - 1
    arrivals = []
    for i in range(1, cols):
        target = jnp.bitwise_xor(col, i)
        n = base + 2 * (i - 1)
        arrivals.append(remote(extra, extra_in.at[i - 1], send, recv, n + 1, along[i - 1]))
        arrivals.append(
            remote(parts.at[target], parts_in.at[i - 1], send, recv, n, along[i - 1])
        )
    for copy in arrivals:
        copy.wait_recv()
    grad = exact_part[col]
    total = small
    for i in range(cols - 1):
        grad += parts_in[i].astype(F32)
        total += extra_in[i].astype(F32)
    totals[...] = total
    gate_grads = [total[:, 0:1] + total[:, 1:2], total[:, 2:3] + total[:, 3:4]]
    first = pl.multiple_of(col * wide, wide)
    term, more = route_term(stat, gate_grads, router, first, wide)
    inner = total[:, 4:5] + total[:, 5:6] + more
    scaled = (grad + term) * norm[:, pl.ds(first, wide)]
    factor = stat[:, 4:5]
    valid = stat[:, 7:8]
    result = (
        cot[...].astype(F32) * valid
        + factor * scaled
        - middle[...] * (factor * factor * inner * (1.0 / width))
    )
    grad_middle[...] = result
    low[...] = result.astype(BF16)
    here = pl.ds(first, wide)
    kept = pltpu.make_async_copy(low, grad_whole.at[:, here], local.at[10])
    kept.start()
    base += 2 * (cols - 1)
    last = [
        remote(low, grad_whole.at[:, here], send, recv, base + i, along[i])
        for i in range(cols - 1)
    ]
    for copy in down_copies:
        copy.wait_recv()
    rank = own_rank(back(any_pick, down_rows, width, LANES))
    rank_low = rank[:, RANK : 2 * RANK].astype(BF16)
    low_down[...] = rank
    for q in range(cols):
        here = slice(q * wide, (q + 1) * wide)
        part = back(any_pick, down_rows, q * wide, wide) + jnp.dot(
            rank_low, lefts[4 * RANK : 5 * RANK, here], preferred_element_type=F32
        )
        branch[:, here] = part.astype(BF16)
    for copy in last:
        copy.wait_recv()
    for copy in down_copies + arrivals + last:
        copy.wait_send()
    kept.wait()


def middle_back(blocks, downs, adapter, norm, router, stat, sources, cols, replicas):
    hbm = pl.BlockSpec(memory_space=pl.ANY)
    vmem = pl.BlockSpec(memory_space=pltpu.VMEM)
    smem = pl.BlockSpec(memory_space=pltpu.SMEM)
    count, wide = sources[-1].shape
    total = EXP_FF - 1 + 3 * (cols - 1)
    rows = EXP_FF * CAP_FF
    return pl.pallas_call(
        functools.partial(middle_back_kernel, cols, replicas),
        out_shape=[
            jax.ShapeDtypeStruct((count, wide), F32),
            jax.ShapeDtypeStruct((count, wide * cols), BF16),
            jax.ShapeDtypeStruct((count, LANES), F32),
            jax.ShapeDtypeStruct((count, wide * cols), BF16),
            jax.ShapeDtypeStruct((count, LANES), F32),
        ],
        in_specs=[hbm] * (2 * EXP_FF) + [smem, vmem, vmem, vmem] + [hbm] * 5,
        out_specs=[vmem, hbm, vmem, vmem, vmem],
        scratch_shapes=[pltpu.VMEM(source.shape, source.dtype) for source in sources]
        + [
            pltpu.VMEM((rows, blocks[0].shape[1]), BF16),
            pltpu.VMEM((rows, downs[0].shape[1]), BF16),
            pltpu.VMEM((cols, count, wide), F32),
            pltpu.VMEM((cols, count, wide), BF16),
            pltpu.VMEM((count, LANES), BF16),
            pltpu.VMEM((cols - 1, count, wide), BF16),
            pltpu.VMEM((cols - 1, count, LANES), BF16),
            pltpu.VMEM((count, wide), BF16),
            pltpu.SemaphoreType.DMA((total,)),
            pltpu.SemaphoreType.DMA((total,)),
            pltpu.SemaphoreType.DMA((11,)),
        ],
        compiler_params=pltpu.CompilerParams(
            collective_id=4, has_side_effects=True, vmem_limit_bytes=62 * 2**20
        ),
    )(*blocks, *downs, adapter, norm, router, stat, *sources)


def tail_kernel(parts_axis, cols, *refs):
    (
        adapters,
        norm,
        router,
        stat,
        cosine,
        sine,
        rights,
        ranks,
        gate_rows,
        totals_attn,
        totals_ffn,
        low_down,
    ) = refs[:12]
    sources = refs[12:27]
    branch, out_whole, query_whole, kv_whole = refs[27:31]
    output, grad_inputs = refs[31:33]
    left_outs = refs[33:38]
    right_outs = refs[38:42]
    (
        grad_whole,
        picks,
        att_rows,
        queries,
        keys,
        values,
        probability,
        attended,
        lefts_whole,
        hidden_one,
        hidden_two,
        grad_middle,
        middle,
        cot,
        tokens,
    ) = refs[42:57]
    (
        cot_own,
        cot_whole,
        branch_in,
        rows,
        grads,
        buffer,
        query_grads,
        key_grad,
        value_grad,
        part,
        parts,
        extra,
        parts_in,
        extra_in,
        right_parts,
        rights_in,
        lefts,
        lefts_in,
        send,
        recv,
        local,
        load,
    ) = refs[57:]
    row = lax.axis_index("row")
    col = lax.axis_index("col")
    count, wide = tokens.shape
    width = hidden_one.shape[1]
    depth = width // parts_axis
    head_width = keys.shape[1]
    heads = head_width // HEAD_DIM
    along = [opposite("col", i) for i in range(1, cols)]
    across = [opposite("row", m) for m in range(1, parts_axis)]
    greet(across + along)
    started = []

    def send_to(source, target, device):
        copy = remote(source, target, send, recv, len(started), device)
        started.append(copy)
        return copy

    pair = 2
    chunks = [
        (whole, start)
        for whole in (out_whole, query_whole, kv_whole)
        for start in range(0, whole.shape[0], pair)
    ]
    loads = []
    for n, (whole, start) in enumerate(chunks):
        loads.append(
            pltpu.make_async_copy(whole.at[pl.ds(start, pair)], buffer.at[n % 2], load.at[n % 2])
        )
    near = fetch(sources, refs[42:57], local)
    loads[0].start()
    loads[1].start()
    first = pl.multiple_of(col * wide, wide)
    here = pl.ds(first, wide)
    valid = stat[:, 7:8]
    branch_copies = []
    for i in range(1, cols):
        target = jnp.bitwise_xor(col, i)
        theirs = pl.ds(pl.multiple_of(target * wide, wide), wide)
        branch_copies.append(send_to(branch.at[:, theirs], branch_in.at[i - 1], along[i - 1]))
    mine = pltpu.make_async_copy(branch.at[:, here], branch_in.at[cols - 1], local.at[15])
    mine.start()
    for copy in near:
        copy.wait()
    cot_own[...] = (cot[...].astype(F32) * valid).astype(BF16)
    cot_whole[:, here] = cot_own[...]
    cot_copies = [send_to(cot_own, cot_whole.at[:, here], device) for device in along]

    def rows_of(matrix, value):
        return lax.dot_general(
            matrix, value, (((0,), (0,)), ((), ())), preferred_element_type=F32
        )

    def times(left, right):
        return lax.dot_general(
            left, right, (((1,), (1,)), ((), ())), preferred_element_type=F32
        )

    def dot(left, right):
        return jnp.dot(left, right, preferred_element_type=F32)

    any_pick = picks[TOPK]
    low_grad = times(grad_whole[...], lefts_whole[2 * RANK : 3 * RANK])
    low_rows = rows_of(any_pick, low_grad.astype(BF16)).astype(BF16)
    for q in range(cols):
        span = slice(q * wide, (q + 1) * wide)
        rows[:, span] = rows_of(any_pick, grad_whole[:, span]).astype(BF16)
    number = 0

    def next_weights():
        nonlocal number
        loads[number].wait()
        return buffer.at[number % 2]

    def done_weights():
        nonlocal number
        if number + 2 < len(chunks):
            loads[number + 2].start()
        number += 1

    for start in range(0, EXP_ATT, pair):
        weight = next_weights()
        for item in range(pair):
            span = slice((start + item) * CAP_ATT, (start + item + 1) * CAP_ATT)
            grads[span] = dot(rows[span], weight[item]) + dot(low_rows[span], rights[3 * RANK :])
        done_weights()
    value = grads[...]
    gate_grad = jnp.sum(att_rows[...].astype(F32) * value, axis=1, keepdims=True)
    gate_pack = pack([*split(gate_grad)], range(2)).astype(BF16)
    gate_grads = []
    gated = (value * gate_rows[...]).astype(BF16)
    right_out = jnp.zeros((RANK, head_width), F32)
    for k in range(TOPK):
        both = dot(picks[k], gate_pack)
        gate_grads.append(both[:, 0:1] + both[:, 1:2])
        query_grads[k] = dot(picks[k], gated).astype(BF16)
        right_out += rows_of((stat[:, k : k + 1] * low_grad).astype(BF16), attended[k])
    scaling = HEAD_DIM ** (-0.5)
    query_sum = []
    for h in range(heads):
        span = slice(h * HEAD_DIM, (h + 1) * HEAD_DIM)
        key_total, value_total, sum_head = 0.0, 0.0, 0.0
        for k in range(TOPK):
            grad_att = query_grads[k, :, span]
            probs = probability[h, k]
            grad_prob = times(grad_att, values[:, span])
            centre = jnp.sum(probs * grad_prob, axis=1, keepdims=True)
            grad_score = (probs * (grad_prob - centre)).astype(BF16)
            value_total += rows_of(probs.astype(BF16), grad_att)
            key_total += rows_of(grad_score, queries[k, :, span])
            grad_query = dot(grad_score, keys[:, span]) * scaling
            turned = turn(grad_query, cosine[...], -sine[...]).astype(BF16)
            query_grads[k, :, span] = turned
            sum_head += turned.astype(F32)
        key_grad[:, span] = turn(key_total * scaling, cosine[...], -sine[...]).astype(BF16)
        value_grad[:, span] = value_total.astype(BF16)
        query_sum.append(sum_head.astype(BF16))
    query_sum = jnp.concatenate(query_sum, axis=1)
    rank_query = ranks[:, :RANK].astype(BF16)
    rank_kv = ranks[:, RANK:].astype(BF16)
    right_values = [
        rows_of(rank_query, query_sum),
        rows_of(rank_kv, key_grad[...]),
        rows_of(rank_kv, value_grad[...]),
        right_out,
    ]
    for p in range(4):
        right_parts[:, p * head_width : (p + 1) * head_width] = right_values[p].astype(BF16)
    right_copies = [
        send_to(right_parts, rights_in.at[m], across[m]) for m in range(parts_axis - 1)
    ]
    grad_rank_query = times(query_sum, rights[:RANK])
    grad_rank_kv = times(key_grad[...], rights[RANK : 2 * RANK]) + times(
        value_grad[...], rights[2 * RANK : 3 * RANK]
    )
    query_rows = (rows_of(picks[0], query_grads[0]) + rows_of(picks[1], query_grads[1])).astype(
        BF16
    )
    for start in range(0, EXP_ATT, pair):
        weight = next_weights()
        for item in range(pair):
            span = slice((start + item) * CAP_ATT, (start + item + 1) * CAP_ATT)
            rows[span] = times(query_rows[span], weight[item]).astype(BF16)
        done_weights()
    weight = next_weights()
    low = jnp.concatenate([grad_rank_query, grad_rank_kv], axis=1).astype(BF16)
    product = jnp.zeros((count, 1), F32)
    for q in range(cols):
        span = slice(q * wide, (q + 1) * wide)
        value = (
            dot(any_pick, rows[:, span])
            + times(key_grad[...], weight[0, span])
            + times(value_grad[...], weight[1, span])
            + dot(low, lefts_whole[: 2 * RANK, span])
        )
        product += jnp.sum(value * hidden_one[:, span].astype(F32), axis=1, keepdims=True)
        part[q] = value
        parts[q] = value.astype(BF16)
    columns = [*split(gate_grads[0]), *split(gate_grads[1]), *split(product)]
    small = pack(columns, range(6)) + jnp.concatenate(
        [
            jnp.zeros((count, RANK), F32),
            grad_rank_query,
            grad_rank_kv,
            low_down[:, RANK : 2 * RANK],
            jnp.zeros((count, LANES - 4 * RANK), F32),
        ],
        axis=1,
    )
    extra[...] = small.astype(BF16)
    extra_copies, part_copies = [], []
    for i in range(1, cols):
        target = jnp.bitwise_xor(col, i)
        extra_copies.append(send_to(extra, extra_in.at[i - 1], along[i - 1]))
        part_copies.append(send_to(parts.at[target], parts_in.at[i - 1], along[i - 1]))
    mine.wait()
    for copy in branch_copies:
        copy.wait_recv()
    result = middle[...]
    for i in range(cols):
        result += branch_in[i].astype(F32)
    output[...] = (result * valid).astype(BF16)
    for copy in cot_copies:
        copy.wait_recv()

    def outer(left, right):
        return rows_of(left, right).astype(BF16)

    whole = outer(totals_attn[...].astype(BF16), grad_whole[...])
    for m in range(parts_axis):
        lefts[m, 2 * RANK : 3 * RANK] = whole[RANK : 2 * RANK, m * depth : (m + 1) * depth]
    whole = outer(totals_ffn[...].astype(BF16), hidden_two[...])
    for m in range(parts_axis):
        lefts[m, 3 * RANK : 4 * RANK] = whole[RANK : 2 * RANK, m * depth : (m + 1) * depth]
    chosen_by = [
        [jnp.where(adapters[m] == a, 1.0, 0.0).astype(F32) for a in range(ADAPT)]
        for m in range(parts_axis)
    ]

    def share(values, target):
        for a in range(ADAPT):
            result = chosen_by[0][a] * values[0]
            for m in range(1, parts_axis):
                result += chosen_by[m][a] * values[m]
            target[a] = result

    for copy in right_copies:
        copy.wait_recv()
    for p in range(4):
        span = slice(p * head_width, (p + 1) * head_width)
        share(
            [right_parts[:, span].astype(F32)]
            + [rights_in[m, :, span].astype(F32) for m in range(parts_axis - 1)],
            right_outs[p],
        )
    total = small
    for i in range(cols - 1):
        extra_copies[i].wait_recv()
        total += extra_in[i].astype(F32)
    low_totals = total.astype(BF16)
    whole = outer(low_totals, hidden_one[...])
    for m in range(parts_axis):
        lefts[m, : 2 * RANK] = whole[RANK : 3 * RANK, m * depth : (m + 1) * depth]
    whole = outer(low_totals, cot_whole[...])
    for m in range(parts_axis):
        lefts[m, 4 * RANK :] = whole[3 * RANK : 4 * RANK, m * depth : (m + 1) * depth]
    left_copies = [
        send_to(lefts.at[jnp.bitwise_xor(row, m)], lefts_in.at[m - 1], across[m - 1])
        for m in range(1, parts_axis)
    ]
    gate_totals = [total[:, 0:1] + total[:, 1:2], total[:, 2:3] + total[:, 3:4]]
    term, more = route_term(stat, gate_totals, router, first, wide)
    inner = total[:, 4:5] + total[:, 5:6] + more
    grad = part[col] + term
    for i in range(cols - 1):
        part_copies[i].wait_recv()
        grad += parts_in[i].astype(F32)
    factor = stat[:, 4:5]
    grad_inputs[...] = (
        grad_middle[...]
        + factor * (grad * norm[:, here])
        - tokens[...].astype(F32) * (factor * factor * inner * (1.0 / width))
    )
    for copy in left_copies:
        copy.wait_recv()
    for p in range(5):
        span = slice(p * RANK, (p + 1) * RANK)
        share(
            [lefts[row, span].astype(F32)]
            + [lefts_in[m, span].astype(F32) for m in range(parts_axis - 1)],
            left_outs[p],
        )
    for copy in started:
        copy.wait_send()


def tail(smalls, sources, branch, wholes, parts_axis, cols):
    hbm = pl.BlockSpec(memory_space=pl.ANY)
    vmem = pl.BlockSpec(memory_space=pltpu.VMEM)
    smem = pl.BlockSpec(memory_space=pltpu.SMEM)
    count, wide = sources[-1].shape
    width = wide * cols
    depth = width // parts_axis
    head_width = wholes[0].shape[2]
    rows = EXP_ATT * CAP_ATT
    shape = jax.ShapeDtypeStruct
    total = 4 * (cols - 1) + 2 * (parts_axis - 1)
    return pl.pallas_call(
        functools.partial(tail_kernel, parts_axis, cols),
        out_shape=[shape((count, wide), BF16), shape((count, wide), F32)]
        + [shape((ADAPT, RANK, depth), F32)] * 5
        + [shape((ADAPT, RANK, head_width), F32)] * 4,
        in_specs=[smem] + [vmem] * 11 + [hbm] * 19,
        out_specs=[vmem] * 11,
        scratch_shapes=[pltpu.VMEM(source.shape, source.dtype) for source in sources]
        + [
            pltpu.VMEM((count, wide), BF16),
            pltpu.VMEM((count, width), BF16),
            pltpu.VMEM((cols, count, wide), BF16),
            pltpu.VMEM((rows, width), BF16),
            pltpu.VMEM((rows, head_width), F32),
            pltpu.VMEM((2, 2, width, head_width), BF16),
            pltpu.VMEM((TOPK, count, head_width), BF16),
            pltpu.VMEM((count, head_width), BF16),
            pltpu.VMEM((count, head_width), BF16),
            pltpu.VMEM((cols, count, wide), F32),
            pltpu.VMEM((cols, count, wide), BF16),
            pltpu.VMEM((count, LANES), BF16),
            pltpu.VMEM((cols - 1, count, wide), BF16),
            pltpu.VMEM((cols - 1, count, LANES), BF16),
            pltpu.VMEM((RANK, 4 * head_width), BF16),
            pltpu.VMEM((parts_axis - 1, RANK, 4 * head_width), BF16),
            pltpu.VMEM((parts_axis, 5 * RANK, depth), BF16),
            pltpu.VMEM((parts_axis - 1, 5 * RANK, depth), BF16),
            pltpu.SemaphoreType.DMA((total,)),
            pltpu.SemaphoreType.DMA((total,)),
            pltpu.SemaphoreType.DMA((16,)),
            pltpu.SemaphoreType.DMA((2,)),
        ],
        compiler_params=pltpu.CompilerParams(
            collective_id=5, has_side_effects=True, vmem_limit_bytes=62 * 2**20
        ),
    )(*smalls, *sources, branch, *wholes)


def middle_kernel(parts_axis, cols, replicas, *refs):
    adapter, norm, router, route, low_rows, low_in = refs[:6]
    sources = refs[6:11]
    weights = refs[11:13]
    outs = refs[13:]
    extra_chunks = parts_axis - 1
    chunks = [(None,) + tuple(outs[n * extra_chunks : (n + 1) * extra_chunks]) for n in (0, 1)]
    outs = outs[2 * extra_chunks :]
    hids = outs[:EXP_FF]
    hidden_out, middle, stat, totals = outs[EXP_FF : EXP_FF + 4]
    scratch = outs[EXP_FF + 4 :]
    out_rows, picks_attn, picks_ffn, lefts, tokens = scratch[:5]
    (
        exact_part,
        parts,
        extra,
        parts_in,
        extra_in,
        square,
        square_in,
        low,
        hidden,
        message,
        send,
        recv,
        local,
    ) = scratch[5:]
    col = lax.axis_index("col")
    count, wide = tokens.shape
    width = hidden.shape[1]
    across = [opposite("row", j * replicas) for j in range(1, EXP_FF)]
    beside = [opposite("row", i) for i in range(1, replicas)]
    along = [opposite("col", i) for i in range(1, cols)]
    greet(across + beside + along)
    near = fetch(sources, scratch[:5], local)
    used = [0]
    started = []

    def send_to(source, target, device):
        copy = remote(source, target, send, recv, used[0], device)
        used[0] += 1
        started.append(copy)
        return copy

    expert = lax.axis_index("row") // replicas
    piece_copies = [
        [
            send_to(weights[n].at[jnp.bitwise_xor(expert, j)], chunks[n][j * replicas], across[j - 1])
            for n in (0, 1)
        ]
        for j in range(1, EXP_FF)
    ]
    sibling_copies = [
        send_to(weights[n].at[expert], chunks[n][i], beside[i - 1])
        for i in range(1, replicas)
        for n in (0, 1)
    ]
    for copy in near:
        copy.wait()

    def back(source):
        return jnp.dot(picks_attn[TOPK], source, preferred_element_type=F32)

    def rows_of(matrix, value):
        return lax.dot_general(
            matrix, value, (((0,), (0,)), ((), ())), preferred_element_type=F32
        )

    sub = lax.broadcasted_iota(jnp.int32, (LANES, LANES), 0)
    lane = lax.broadcasted_iota(jnp.int32, (LANES, LANES), 1)
    lanes = lax.broadcasted_iota(jnp.int32, (count, LANES), 1)
    low_out = back(low_rows[...])
    small = low_in[...] + low_out
    low_out = low_out[:, RANK : 2 * RANK].astype(BF16)
    for q in range(cols):
        here = slice(q * wide, (q + 1) * wide)
        part = back(out_rows[:, here]) + jnp.dot(
            low_out, lefts[2 * RANK : 3 * RANK, here], preferred_element_type=F32
        )
        exact_part[q] = part
        parts[q] = part.astype(BF16)
    extra[...] = small.astype(BF16)
    part_copies = []
    extra_copies = []
    for i in range(1, cols):
        target = jnp.bitwise_xor(col, i)
        part_copies.append(send_to(parts.at[target], parts_in.at[i - 1], along[i - 1]))
        extra_copies.append(send_to(extra, extra_in.at[i - 1], along[i - 1]))
    value = tokens[...].astype(F32) + exact_part[col]
    total = small
    for i in range(cols - 1):
        part_copies[i].wait_recv()
        value += parts_in[i].astype(F32)
    middle[...] = value
    square[...] = lax.dot_general(
        jnp.ones((8, wide), F32),
        value * value,
        (((1,), (1,)), ((), ())),
        precision=HIGHEST,
        preferred_element_type=F32,
    )
    square_copies = [
        send_to(square, square_in.at[i], along[i]) for i in range(cols - 1)
    ]
    for i in range(cols - 1):
        extra_copies[i].wait_recv()
        total += extra_in[i].astype(F32)
    totals[...] = total
    squares = square[...]
    for i in range(cols - 1):
        square_copies[i].wait_recv()
        squares += square_in[i]
    squares = lax.dot_general(
        squares,
        jnp.full((8, LANES), 0.125, F32),
        (((0,), (0,)), ((), ())),
        precision=HIGHEST,
        preferred_element_type=F32,
    )
    scale = lax.rsqrt(squares[:, 0:1] * (1.0 / width) + EPSILON)
    first = pl.multiple_of(col * wide, wide)
    here = pl.ds(first, wide)
    low[...] = (value * scale * norm[:, here]).astype(BF16)
    hidden[:, here] = low[...]
    hidden_copies = [send_to(low, hidden.at[:, here], along[i]) for i in range(cols - 1)]
    mine = lanes // RANK == adapter[0]

    def own_adapter(value, start):
        spread = (sub - start == lane % RANK).astype(F32).astype(BF16)
        value = jnp.dot(value.astype(BF16), spread, preferred_element_type=F32)
        return jnp.where(mine, value, 0.0).astype(BF16)

    picks = [picks_ffn[0], picks_ffn[1]]
    any_pick = picks[0] + picks[1]
    message[:, width + 2 * LANES :] = rows_of(any_pick, own_adapter(total, 2 * RANK)).astype(BF16)
    for copy in hidden_copies:
        copy.wait_recv()
    kept = pltpu.make_async_copy(hidden, hidden_out, local.at[6])
    kept.start()

    def times(right):
        return lax.dot_general(
            hidden[...], right, (((1,), (1,)), ((), ())), preferred_element_type=F32
        )

    logits = times(router[...])
    routes = [route[:, 8 + k : 9 + k] for k in range(TOPK)]
    chosen, gates = scores_of(routes, logits, EXP_FF)
    stat[...] = pack(
        [*gates, *chosen, scale, *routes, route[:, 7:8]], range(8)
    )
    gate_rows = 0.0
    for k in range(TOPK):
        columns = pack([*split(gates[k])], range(2)).astype(BF16)
        gate_rows += rows_of(picks[k], columns)
    message[:, width + LANES : width + 2 * LANES] = gate_rows.astype(BF16)
    rank = times(lefts[3 * RANK : 4 * RANK])
    rank = jnp.concatenate([rank, jnp.zeros((count, LANES - RANK), F32)], axis=1)
    message[:, width : width + LANES] = rows_of(any_pick, own_adapter(rank, 0)).astype(BF16)
    for q in range(cols):
        span = slice(q * wide, (q + 1) * wide)
        message[:, span] = rows_of(any_pick, hidden[:, span]).astype(BF16)
    traded = [
        send_to(message.at[pl.ds(j * CAP_FF, CAP_FF)], hids[j], across[j - 1])
        for j in range(EXP_FF - 1, 0, -1)
    ]
    own = pltpu.make_async_copy(message.at[pl.ds(0, CAP_FF)], hids[0], local.at[7])
    own.start()
    for j in range(1, EXP_FF):
        for n in (0, 1):
            piece_copies[j - 1][n].wait_recv()
            for i in range(1, replicas):
                m = j * replicas
                sibling_copies.append(send_to(chunks[n][m], chunks[n][m + i], beside[i - 1]))
    for copy in traded + sibling_copies:
        copy.wait_recv()
    for copy in started:
        copy.wait_send()
    kept.wait()
    own.wait()


def middle_forward(adapter, norm, router, route, low_rows, low_in, sources, weights, parts_axis, cols, replicas):
    hbm = pl.BlockSpec(memory_space=pl.ANY)
    vmem = pl.BlockSpec(memory_space=pltpu.VMEM)
    smem = pl.BlockSpec(memory_space=pltpu.SMEM)
    count, wide = sources[-1].shape
    width = wide * cols
    rows = EXP_FF * CAP_FF
    full = width + 3 * LANES
    total = 2 * (parts_axis - 1) + 4 * (cols - 1) + EXP_FF - 1
    return pl.pallas_call(
        functools.partial(middle_kernel, parts_axis, cols, replicas),
        out_shape=[jax.ShapeDtypeStruct(weights[0].shape[1:], BF16)] * (parts_axis - 1)
        + [jax.ShapeDtypeStruct(weights[1].shape[1:], BF16)] * (parts_axis - 1)
        + [jax.ShapeDtypeStruct((CAP_FF, full), BF16)] * EXP_FF
        + [
            jax.ShapeDtypeStruct((count, width), BF16),
            jax.ShapeDtypeStruct((count, wide), F32),
            jax.ShapeDtypeStruct((count, LANES), F32),
            jax.ShapeDtypeStruct((count, LANES), F32),
        ],
        in_specs=[smem] + [vmem] * 5 + [hbm] * 7,
        out_specs=[hbm] * (2 * parts_axis - 1 + EXP_FF) + [vmem] * 3,
        scratch_shapes=[pltpu.VMEM(source.shape, source.dtype) for source in sources]
        + [
            pltpu.VMEM((cols, count, wide), F32),
            pltpu.VMEM((cols, count, wide), BF16),
            pltpu.VMEM((count, LANES), BF16),
            pltpu.VMEM((cols - 1, count, wide), BF16),
            pltpu.VMEM((cols - 1, count, LANES), BF16),
            pltpu.VMEM((8, count), F32),
            pltpu.VMEM((cols - 1, 8, count), F32),
            pltpu.VMEM((count, wide), BF16),
            pltpu.VMEM((count, width), BF16),
            pltpu.VMEM((rows, full), BF16),
            pltpu.SemaphoreType.DMA((total,)),
            pltpu.SemaphoreType.DMA((total,)),
            pltpu.SemaphoreType.DMA((8,)),
        ],
        compiler_params=pltpu.CompilerParams(
            collective_id=3, has_side_effects=True, vmem_limit_bytes=62 * 2**20
        ),
    )(adapter, norm, router, route, low_rows, low_in, *sources, *weights)


def ffn_kernel(parts, depth, width, units, *refs):
    hids = refs[:EXP_FF]
    cots = refs[EXP_FF : 2 * EXP_FF]
    inners = refs[2 * EXP_FF : 2 * EXP_FF + parts]
    lasts = refs[2 * EXP_FF + parts : 2 * EXP_FF + 2 * parts]
    rights = refs[2 * EXP_FF + 2 * parts : 2 * EXP_FF + 2 * parts + 2]
    outs = refs[2 * EXP_FF + 2 * parts + 2 :]
    grads = outs[:EXP_FF]
    downs = outs[EXP_FF : 2 * EXP_FF]
    adapt = outs[2 * EXP_FF : 2 * EXP_FF + 3]
    hid, cot, block, act, product, leaving, sems, send, recv = outs[2 * EXP_FF + 3 :]
    replicas = parts // EXP_FF
    across = [opposite("row", j * replicas) for j in range(1, EXP_FF)]
    greet(across)
    row = lax.axis_index("row")
    wide = width + LANES
    copies = []
    for j in range(EXP_FF):
        where = pl.ds(j * CAP_FF, CAP_FF)
        near = hids[j].at[:, pl.ds(0, wide + LANES)]
        copies.append(pltpu.make_async_copy(near, hid.at[where], sems.at[j]))
        near = cot.at[where, pl.ds(0, width)]
        copies.append(pltpu.make_async_copy(cots[j], near, sems.at[EXP_FF + j]))
        near = cot.at[where, pl.ds(width, LANES)]
        low = hids[j].at[:, pl.ds(wide + LANES, LANES)]
        copies.append(pltpu.make_async_copy(low, near, sems.at[2 * EXP_FF + j]))
    for n, (start, size) in enumerate(((0, 2 * units), (2 * units, units))):
        near = block.at[pl.ds(width, LANES), pl.ds(start, size)]
        copies.append(pltpu.make_async_copy(rights[n], near, sems.at[3 * EXP_FF + n]))
    expert = row // replicas
    for m in range(parts):
        owner = jnp.bitwise_xor(row, m)
        where = pl.ds(pl.multiple_of(owner * depth, depth), depth)
        inner = inners[m] if m else inners[0].at[expert]
        last = lasts[m] if m else lasts[0].at[expert]
        near = block.at[where, pl.ds(0, 2 * units)]
        copies.append(pltpu.make_async_copy(inner, near, sems.at[3 * EXP_FF + 2 + m]))
        near = block.at[where, pl.ds(2 * units, units)]
        copies.append(pltpu.make_async_copy(last, near, sems.at[3 * EXP_FF + 2 + parts + m]))
    for copy in copies:
        copy.start()
    for copy in copies:
        copy.wait()
    gate_scale = hid[:, wide : wide + 1].astype(F32) + hid[:, wide + 1 : wide + 2].astype(F32)
    product[...] = jnp.zeros_like(product)

    def forward(start, size):
        here = pl.ds(start, size)
        up_here = pl.ds(units + start, size)
        down_here = pl.ds(2 * units + start, size)
        gate = jnp.dot(hid[:, :wide], block[:, here], preferred_element_type=F32)
        up = jnp.dot(hid[:, :wide], block[:, up_here], preferred_element_type=F32)
        grad = jnp.dot(cot[...], block[:, down_here], preferred_element_type=F32)
        sig = 1.0 / (1.0 + jnp.exp(-gate))
        mixed = (gate * sig * up).astype(BF16)
        act[:, down_here] = mixed
        product[...] += jnp.sum(mixed.astype(F32) * grad, axis=1, keepdims=True)
        grad = grad * gate_scale
        act[:, here] = (grad * up * sig * (1.0 + gate * (1.0 - sig))).astype(BF16)
        act[:, up_here] = (grad * gate * sig).astype(BF16)

    step = 2 * LANES
    full = units // step

    @pl.loop(0, full)
    def _(i):
        forward(pl.multiple_of(i * step, step), step)

    if units % step:
        forward(full * step, units % step)

    total = product[...]
    high = total.astype(BF16)
    low = (total - high.astype(F32)).astype(BF16)
    lane = lax.broadcasted_iota(jnp.int32, (EXP_FF * CAP_FF, LANES), 1)
    packed = jnp.where(
        lane == 0, high.astype(F32), jnp.where(lane == 1, low.astype(F32), 0.0)
    ).astype(BF16)
    traded = []
    spans = [(start, 4 * LANES) for start in range(0, width, 4 * LANES)] + [(width, LANES)]
    for start, size in spans:
        here = pl.ds(start, size)
        result = lax.dot_general(
            act[:, : 2 * units],
            block[here, : 2 * units],
            (((1,), (1,)), ((), ())),
            preferred_element_type=F32,
        ).astype(BF16)
        sent = here
        if start == width:
            result = jnp.concatenate([result, packed], axis=1)
            sent = pl.ds(start, 2 * LANES)
        grads[0][:, sent] = result[:CAP_FF]
        for j in range(1, EXP_FF):
            leaving[j - 1, :, sent] = result[j * CAP_FF : (j + 1) * CAP_FF]
            traded.append(
                remote(
                    leaving.at[j - 1, :, sent],
                    grads[j].at[:, sent],
                    send,
                    recv,
                    len(traded),
                    across[j - 1],
                )
            )

    def backward(start, size):
        here = pl.ds(start, size)
        result = lax.dot_general(
            act[:, 2 * units :],
            block[here, 2 * units :],
            (((1,), (1,)), ((), ())),
            preferred_element_type=F32,
        )
        result = (result * gate_scale).astype(BF16)
        for j in range(EXP_FF):
            downs[j][:, here] = result[j * CAP_FF : (j + 1) * CAP_FF]

    full_rows = wide // step

    @pl.loop(0, full_rows)
    def _(i):
        backward(pl.multiple_of(i * step, step), step)

    if wide % step:
        backward(full_rows * step, wide % step)
    ext = hid[:, width:wide]
    low_ext = (cot[:, width:].astype(F32) * gate_scale).astype(BF16)
    for n, low_rows in enumerate((ext, ext, low_ext)):
        adapt[n][...] = lax.dot_general(
            low_rows,
            act[:, n * units : (n + 1) * units],
            (((0,), (0,)), ((), ())),
            preferred_element_type=F32,
        ).astype(BF16)
    for copy in traded:
        copy.wait()


def feed_forward(hids, cots, inners, lasts, rights):
    parts = len(inners)
    depth, units = lasts[1].shape
    triple = 3 * units
    width = depth * parts
    remotes = (EXP_FF - 1) * (width // (4 * LANES) + 1)
    rows = EXP_FF * CAP_FF
    hbm = pl.BlockSpec(memory_space=pl.ANY)
    vmem = pl.BlockSpec(memory_space=pltpu.VMEM)
    wide = width + LANES
    return pl.pallas_call(
        functools.partial(ffn_kernel, parts, depth, width, units),
        out_shape=[jax.ShapeDtypeStruct((CAP_FF, wide + LANES), BF16)] * EXP_FF
        + [jax.ShapeDtypeStruct((CAP_FF, wide), BF16)] * EXP_FF
        + [jax.ShapeDtypeStruct((LANES, units), BF16)] * 3,
        in_specs=[hbm] * (2 * EXP_FF + 2 * parts + 2),
        out_specs=[vmem] + [hbm] * (EXP_FF - 1) + [vmem] * (EXP_FF + 3),
        scratch_shapes=[
            pltpu.VMEM((rows, wide + LANES), BF16),
            pltpu.VMEM((rows, wide), BF16),
            pltpu.VMEM((wide, triple), BF16),
            pltpu.VMEM((rows, triple), BF16),
            pltpu.VMEM((rows, 1), F32),
            pltpu.VMEM((EXP_FF - 1, CAP_FF, wide + LANES), BF16),
            pltpu.SemaphoreType.DMA((3 * EXP_FF + 2 + 2 * parts,)),
            pltpu.SemaphoreType.DMA((remotes,)),
            pltpu.SemaphoreType.DMA((remotes,)),
        ],
        compiler_params=pltpu.CompilerParams(
            collective_id=2, has_side_effects=True, vmem_limit_bytes=62 * 2**20
        ),
    )(*hids, *cots, *inners, *lasts, *rights)


def on_device(
    inputs,
    cotangent,
    lengths,
    adapter_pick,
    attn_route,
    ffn_route,
    norm_one,
    norm_two,
    router_attn,
    router_ffn,
    kv_weight,
    query_weight,
    out_weight,
    inner_weight,
    down_weight,
    query_left,
    query_right,
    kv_left,
    kv_right,
    out_left,
    out_right,
    inner_left,
    inner_right,
    down_left,
    down_right,
):
    count = inputs.shape[0]
    rows_axis = lax.axis_size("row")
    replicas = rows_axis // EXP_FF
    units = inner_weight.shape[3]
    cosine, sine = tables(count, HEAD_DIM)
    turns = (
        jnp.concatenate([cosine, cosine], axis=1),
        jnp.concatenate([-sine, sine], axis=1),
    )

    cols = lax.axis_size("col")
    padding = -units % LANES

    def padded(value):
        if not padding:
            return value
        return jnp.pad(value, [(0, 0)] * (value.ndim - 1) + [(0, padding)])

    down_flat = padded(down_weight)

    lefts_own = [
        value.swapaxes(1, 2)
        for value in (query_left, kv_left, out_left, inner_left, down_left)
    ]
    (
        inner_flat,
        inner_right_flat,
        rights,
        kv_full,
        query_full,
        out_full,
        *cot_rows,
        hidden_one,
        lefts,
        stat_attn,
        low_in,
        keys,
        values,
        queries,
        attended,
        probability,
        attended_rows,
        low_rows,
        out_rows,
        picks_attn,
        picks_ffn,
        ranks,
        gate_rows,
        picks,
    ) = front(
        [
            lengths,
            adapter_pick,
            attn_route.T,
            ffn_route.T,
            cotangent,
            norm_one[None, :],
            router_attn.T,
            *turns,
            query_right,
            kv_right,
            out_right,
        ],
        lefts_own,
        inputs,
        [kv_weight, query_weight, out_weight],
        padded(inner_weight),
        padded(inner_right).reshape(ADAPT * RANK, 2, units + padding),
        rows_axis,
        cols,
        replicas,
    )
    picks = picks[:, 0, 0].astype(jnp.int32)
    ffn_right = [inner_right_flat, padded(down_right).reshape(ADAPT * RANK, units + padding)]

    *outs, hidden_two, middle, stat_ffn, totals_attn = middle_forward(
        adapter_pick,
        norm_two[None, :],
        router_ffn.T,
        stat_attn,
        low_rows,
        low_in,
        [out_rows, picks_attn, picks_ffn, lefts, inputs],
        [inner_flat, down_flat],
        rows_axis,
        cols,
        replicas,
    )
    inners = [inner_flat, *outs[: rows_axis - 1]]
    lasts = [down_flat, *outs[rows_axis - 1 : 2 * rows_axis - 2]]
    hidden_in = outs[2 * rows_axis - 2 :]
    results = feed_forward(hidden_in, cot_rows, inners, lasts, ffn_right)
    grad_middle, grad_full, totals, branch_ffn, low_down_part = middle_back(
        results[:EXP_FF],
        results[EXP_FF : 2 * EXP_FF],
        adapter_pick,
        norm_two[None, :],
        router_ffn.T,
        stat_ffn,
        [picks_ffn, lefts, hidden_two, middle, cotangent],
        cols,
        replicas,
    )
    rights_ffn = lax.optimization_barrier((*results[2 * EXP_FF :], totals))[:3]
    rights_ffn = lax.optimization_barrier(lax.psum(rights_ffn, "row"))
    rights_ffn = [
        value[:, :units].reshape(ADAPT, RANK, units).astype(F32) for value in rights_ffn
    ]

    output, grad_inputs, *grads = tail(
        [
            picks,
            norm_one[None, :],
            router_attn.T,
            stat_attn,
            *turns,
            rights,
            ranks,
            gate_rows,
            totals_attn,
            totals,
            low_down_part,
        ],
        [
            grad_full,
            picks_attn,
            attended_rows,
            queries,
            keys,
            values,
            probability,
            attended,
            lefts,
            hidden_one,
            hidden_two,
            grad_middle,
            middle,
            cotangent,
            inputs,
        ],
        branch_ffn,
        [out_full, query_full, kv_full],
        rows_axis,
        cols,
    )
    lefts_back = [grad.swapaxes(1, 2) for grad in grads[:5]]
    rights_back = grads[5:]
    return (
        output,
        grad_inputs,
        lefts_back[0],
        rights_back[0],
        lefts_back[1],
        jnp.stack(rights_back[1:3], axis=2),
        lefts_back[2],
        rights_back[3],
        lefts_back[3],
        jnp.stack(rights_ffn[:2], axis=2),
        lefts_back[4],
        rights_ffn[2],
    )


def solution(mesh):
    placed = (
        P("row", "col"),
        P("row", "col"),
        P("row"),
        P("row"),
        P("row", None),
        P("row", None),
        P(),
        P(),
        P(),
        P(),
        P(None, "row", "col"),
        P(None, "row", "col"),
        P(None, "row", "col"),
        P(None, "row", None, "col"),
        P(None, "row", "col"),
        P(None, "row", None),
        P(None, None, "col"),
        P(None, "row", None),
        P(None, None, None, "col"),
        P(None, "row", None),
        P(None, None, "col"),
        P(None, "row", None),
        P(None, None, None, "col"),
        P(None, "row", None),
        P(None, None, "col"),
    )
    return jax.shard_map(
        on_device,
        mesh=mesh,
        in_specs=placed,
        out_specs=(
            P("row", "col"),
            P("row", "col"),
            P(None, "row", None),
            P(None, None, "col"),
            P(None, "row", None),
            P(None, None, None, "col"),
            P(None, "row", None),
            P(None, None, "col"),
            P(None, "row", None),
            P(None, None, None, "col"),
            P(None, "row", None),
            P(None, None, "col"),
        ),
        check_vma=False,
    )
```

```python
import functools

import jax
import jax.numpy as jnp
from jax import lax
from jax.experimental import pallas as pl
from jax.experimental.pallas import tpu as pltpu
from jax.sharding import PartitionSpec as P

HEAD_DIM = 128
EXP_ATT = 8
EXP_FF = 4
TOPK = 2
ADAPT = 8
RANK = 16
CAP_ATT = 80
CAP_FF = 160
EPSILON = 1e-06
ROPE_BASE = 10000.0
HIGHEST = lax.Precision.HIGHEST
F32 = jnp.float32
BF16 = jnp.bfloat16
LANES = 128
EARLY = 2


def tables(count, head_width):
    position = jnp.arange(count).astype(F32)
    frequency = ROPE_BASE ** (-jnp.arange(head_width // 2).astype(F32) * 2.0 / head_width)
    angle = position[:, None] * frequency[None, :]
    return (jnp.cos(angle), jnp.sin(angle))


def opposite(axis, offset):
    index = jnp.bitwise_xor(lax.axis_index(axis), offset)
    if axis == "row":
        return (index, lax.axis_index("col"))
    return (lax.axis_index("row"), index)


def greet(partners):
    barrier = pltpu.get_barrier_semaphore()
    for partner in partners:
        pl.semaphore_signal(
            barrier, inc=1, device_id=partner, device_id_type=pl.DeviceIdType.MESH
        )
    pl.semaphore_wait(barrier, len(partners))


def split(value):
    high = value.astype(BF16).astype(F32)
    return high, value - high


def pack(columns, lanes):
    lane = lax.broadcasted_iota(jnp.int32, (columns[0].shape[0], LANES), 1)
    result = jnp.zeros((columns[0].shape[0], LANES), F32)
    for column, n in zip(columns, lanes):
        result = jnp.where(lane == n, column, result)
    return result


def route_term(stat, grads, router, start, size):
    gates = [stat[:, k : k + 1] for k in range(TOPK)]
    mean = gates[0] * grads[0] + gates[1] * grads[1]
    product = 0.0
    term = 0.0
    weights = [gates[k] * (grads[k] - mean) for k in range(TOPK)]
    for k in range(TOPK):
        product += weights[k] * stat[:, 2 + k : 3 + k]
    for e in range(router.shape[0]):
        weight = 0.0
        for k in range(TOPK):
            weight += jnp.where(stat[:, 5 + k : 6 + k] == float(e), weights[k], 0.0)
        term += weight * router[e : e + 1, pl.ds(start, size)].astype(F32)
    return term, product


def fetch(sources, targets, sems):
    copies = []
    for n, (source, target) in enumerate(zip(sources, targets)):
        copies.append(pltpu.make_async_copy(source, target, sems.at[n]))
        copies[-1].start()
    return copies


def remote(source, target, send, recv, n, device):
    copy = pltpu.make_async_remote_copy(
        src_ref=source,
        dst_ref=target,
        send_sem=send.at[n],
        recv_sem=recv.at[n],
        device_id=device,
        device_id_type=pl.DeviceIdType.MESH,
    )
    copy.start()
    return copy


def dispatch_matrices(route, flip, experts, capacity):
    route = [column.astype(jnp.int32) for column in route]
    count = route[0].shape[0]
    lane = lax.broadcasted_iota(jnp.int32, (count, LANES), 1)
    chosen = [(route[k] == lane).astype(F32) for k in range(TOPK)]
    place = lax.broadcasted_iota(jnp.int32, (count, count), 0)
    other = lax.broadcasted_iota(jnp.int32, (count, count), 1)
    before = (other < place).astype(F32).astype(BF16)
    earlier = jnp.dot(
        before, (chosen[0] + chosen[1]).astype(BF16), preferred_element_type=F32
    )
    rows = lax.broadcasted_iota(jnp.int32, (count, experts * capacity), 1)
    results = []
    for k in range(TOPK):
        position = jnp.sum(earlier * chosen[k], axis=1, keepdims=True).astype(jnp.int32)
        mine = jnp.bitwise_xor(route[k], flip) * capacity + position
        results.append((rows == mine).astype(F32).astype(BF16))
    return results


def turn(value, cosine, sine):
    half = HEAD_DIM // 2
    heads = []
    for h in range(value.shape[1] // HEAD_DIM):
        head = value[:, h * HEAD_DIM : (h + 1) * HEAD_DIM]
        heads.append(head * cosine + pltpu.roll(head, half, axis=1) * sine)
    return jnp.concatenate(heads, axis=1)


def scores_of(stat_route, logits, experts):
    chosen = []
    for k in range(TOPK):
        score = 0.0
        for e in range(experts):
            score += jnp.where(stat_route[k] == float(e), logits[:, e : e + 1], 0.0)
        chosen.append(score)
    top = jnp.maximum(chosen[0], chosen[1])
    powers = [jnp.exp(score - top) for score in chosen]
    return chosen, [power / (powers[0] + powers[1]) for power in powers]


def front_kernel(parts, cols, replicas, *refs):
    lengths, pick, routes_attn, routes_ffn, cot, norm, router, cosine, sine = refs[:9]
    query_right, kv_right, out_right = refs[9:12]
    left_refs = refs[12:17]
    tokens = refs[17]
    blocks = refs[18:21]
    pairs, pairs_right, downs = refs[21:24]
    outs = refs[24:]
    flat, flat_right, rights = outs[:3]
    early = outs[3 : 3 + EARLY]
    outs = outs[3 + EARLY :]
    wholes = outs[:3]
    cot_wholes = outs[3 : 3 + EXP_FF]
    (
        hidden,
        lefts,
        stat,
        low_in,
        keys,
        values,
        queries,
        attended,
        probability,
        att_rows,
        low_rows,
        out_rows,
        picks_attn,
        picks_ffn,
        ranks,
        gate_rows,
        picks,
    ) = outs[3 + EXP_FF : 20 + EXP_FF]
    (
        x_all,
        own_rows,
        landed,
        hidden_rows,
        buffer,
        query_rows,
        pick_out,
        lefts_out,
        pair_in,
        pair_out,
        send,
        recv,
        local,
        load,
    ) = outs[20 + EXP_FF :]
    row = lax.axis_index("row")
    col = lax.axis_index("col")
    depth = blocks[0].shape[1]
    count, wide = tokens.shape
    width = hidden.shape[1]
    head_width = keys.shape[1]
    heads = head_width // HEAD_DIM
    across = [None] + [opposite("row", m) for m in range(1, parts)]
    along = [opposite("col", i) for i in range(1, cols)]
    greet(across[1:] + along)
    started, kept = [], []
    received = set()
    here = pl.ds(pl.multiple_of(col * wide, wide), wide)
    own = pl.ds(pl.multiple_of(row * depth, depth), depth)

    def send_to(source, target, device):
        copy = remote(source, target, send, recv, len(started), device)
        started.append(copy)
        return copy

    def arrive(copy):
        copy.wait_recv()
        received.add(id(copy))

    def keep(source, target):
        copy = pltpu.make_async_copy(source, target, local.at[len(kept)])
        copy.start()
        kept.append(copy)
        return copy

    pair = 2
    chunks = [
        (a, start) for a in range(3) for start in range(0, blocks[a].shape[0], pair)
    ]

    def place(n, offset, item=None):
        array, start = chunks[n]
        owner = jnp.bitwise_xor(row, offset)
        owner_rows = pl.ds(pl.multiple_of(owner * depth, depth), depth)
        if item is None:
            return wholes[array].at[pl.ds(start, pair), owner_rows]
        return wholes[array].at[start + item, owner_rows]

    first, direct, relayed, beside = {}, {}, {}, {}

    def push_own(n):
        if n >= len(chunks):
            return
        array, start = chunks[n]
        source = blocks[array].at[pl.ds(start, pair)]
        if parts == 8:
            first[n] = [send_to(source, place(n, 0), across[m]) for m in (2, 4)]
            beside[n] = [send_to(source, place(n, 0), across[1])]
        else:
            direct[n] = [send_to(source, place(n, 0), across[m]) for m in range(1, parts)]

    def relay(n):
        if parts == 8:
            for copy in first[n]:
                arrive(copy)
            relayed[n] = [
                send_to(place(n, 2, 0), place(n, 2, 0), across[4]),
                send_to(place(n, 4, 1), place(n, 4, 1), across[2]),
            ]
            for offset in (2, 4):
                beside[n].append(send_to(place(n, offset), place(n, offset), across[1]))

    def finish(n):
        if parts == 8:
            for copy in relayed[n]:
                arrive(copy)
            beside[n].append(send_to(place(n, 6), place(n, 6), across[1]))
            for copy in beside[n]:
                arrive(copy)
        else:
            for copy in direct[n]:
                arrive(copy)

    token_copies = [send_to(tokens, x_all.at[:, here], device) for device in along]
    token_kept = keep(tokens, x_all.at[:, here])
    block_kept = [keep(blocks[a], wholes[a].at[:, own]) for a in range(3)]
    pick_out[...] = jnp.full(pick_out.shape, 1.0, F32) * pick[0].astype(F32)
    picks[0] = pick_out[...]
    pick_copies = [
        send_to(pick_out, picks.at[m], across[m]) for m in range(1, parts)
    ]
    window, behind = 9, 5
    for n in range(window):
        push_own(n)

    table = jnp.concatenate(
        [
            routes_attn[...].astype(F32),
            routes_ffn[...].astype(F32),
            jnp.zeros((8 - 2 * TOPK, count), F32),
        ]
    )
    same = lax.broadcasted_iota(jnp.int32, (8, LANES), 0) == lax.broadcasted_iota(
        jnp.int32, (8, LANES), 1
    )
    table = lax.dot_general(
        table.astype(BF16),
        same.astype(F32).astype(BF16),
        (((0,), (0,)), ((), ())),
        preferred_element_type=F32,
    )
    route_attn = [table[:, k : k + 1] for k in range(TOPK)]
    route_ffn = [table[:, TOPK + k : TOPK + k + 1] for k in range(TOPK)]
    chosen_adapter = pick[0]
    rights[:RANK] = query_right[chosen_adapter]
    pair_right = kv_right[chosen_adapter].reshape(RANK, 2 * head_width)
    rights[RANK : 2 * RANK] = pair_right[:, :head_width]
    rights[2 * RANK : 3 * RANK] = pair_right[:, head_width:]
    rights[3 * RANK :] = out_right[chosen_adapter]

    position = lax.broadcasted_iota(jnp.int32, (count, 1), 0)
    valid = position < lengths[0]
    matrices = dispatch_matrices(route_ffn, row // replicas, EXP_FF, CAP_FF)
    for k in range(TOPK):
        picks_ffn[k] = matrices[k]
    masked = jnp.where(valid, cot[...].astype(F32), 0.0).astype(BF16)

    def rows_of(matrix, value):
        return lax.dot_general(
            matrix, value, (((0,), (0,)), ((), ())), preferred_element_type=F32
        )

    def times(left, right):
        return lax.dot_general(
            left, right, (((1,), (1,)), ((), ())), preferred_element_type=F32
        )

    dispatched = rows_of(matrices[0] + matrices[1], masked).astype(BF16)
    for j in range(EXP_FF):
        own_rows[j] = dispatched[j * CAP_FF : (j + 1) * CAP_FF]
    traded = [
        send_to(own_rows.at[j], landed.at[j - 1], across[j * replicas])
        for j in range(1, EXP_FF)
    ]
    attn = dispatch_matrices(route_attn, 0, EXP_ATT, CAP_ATT)
    for k in range(TOPK):
        picks_attn[k] = attn[k]
    attn_any = attn[0] + attn[1]
    picks_attn[TOPK] = attn_any

    left_copies = []
    for m in range(parts):
        if m:
            arrive(pick_copies[m - 1])
        theirs = picks[m, 0:1, 0:1]
        for p in range(5):
            value = jnp.zeros((RANK, depth), F32)
            for a in range(ADAPT):
                value += jnp.where(theirs == float(a), left_refs[p][a].astype(F32), 0.0)
            lefts_out[m, p * RANK : (p + 1) * RANK] = value.astype(BF16)
        if m:
            left_copies.append(send_to(lefts_out.at[m], lefts.at[:, own], across[m]))
        else:
            lefts[:, own] = lefts_out[0]
    for j in range(EXP_FF):
        if j:
            arrive(traded[j - 1])
            source = landed.at[j - 1]
        else:
            source = own_rows.at[0]
        keep(source, cot_wholes[j].at[:, here])
        for device in along:
            send_to(source, cot_wholes[j].at[:, here], device)
    relay(0)
    push_own(window)

    for copy in token_copies:
        arrive(copy)
    token_kept.wait()
    square = jnp.zeros((count, 1), F32)
    for q in range(cols):
        value = x_all[:, q * wide : (q + 1) * wide].astype(F32)
        square += jnp.sum(value * value, axis=1, keepdims=True)
    scale = lax.rsqrt(square * (1.0 / width) + EPSILON)
    for q in range(cols):
        span = slice(q * wide, (q + 1) * wide)
        value = x_all[:, span].astype(F32)
        hidden[:, span] = (value * scale * norm[:, span]).astype(BF16)
    for copy in left_copies:
        arrive(copy)
    relay(1)
    push_own(window + 1)
    logits = times(hidden[...], router[...])
    chosen, gates = scores_of(route_attn, logits, EXP_ATT)
    columns = [*gates, *chosen, scale, *route_attn, valid.astype(F32), *route_ffn]
    stat[...] = pack(columns, range(10))
    rank_both = times(hidden[...], lefts[: 2 * RANK])
    ranks[...] = rank_both
    rank_query = rank_both[:, :RANK].astype(BF16)
    rank_kv = rank_both[:, RANK:].astype(BF16)
    low_down = times(masked, lefts[4 * RANK : 5 * RANK, here])
    low_in[...] = jnp.concatenate(
        [
            jnp.zeros((count, 2 * RANK), F32),
            low_down,
            jnp.zeros((count, LANES - 3 * RANK), F32),
        ],
        axis=1,
    )
    gate_wide = 0.0
    for k in range(TOPK):
        columns = pack([*split(gates[k])], range(2)).astype(BF16)
        gate_wide += rows_of(attn[k], columns)
    gate_row = gate_wide[:, 0:1] + gate_wide[:, 1:2]
    gate_rows[...] = gate_row
    rank_rows = rows_of(attn_any, rank_query).astype(BF16)
    for q in range(cols):
        span = slice(q * wide, (q + 1) * wide)
        hidden_rows[:, span] = rows_of(attn_any, hidden[:, span]).astype(BF16)

    def attend():
        value = query_rows[...]
        high = value.astype(BF16)
        low = (value - high.astype(F32)).astype(BF16)
        for k in range(TOPK):
            query = jnp.dot(attn[k], high, preferred_element_type=F32) + jnp.dot(
                attn[k], low, preferred_element_type=F32
            )
            queries[k] = turn(query, cosine[...], sine[...]).astype(BF16)
        other = lax.broadcasted_iota(jnp.int32, (count, count), 1)
        place_row = lax.broadcasted_iota(jnp.int32, (count, count), 0)
        allowed = (other <= place_row) & (other < lengths[0])
        for h in range(heads):
            span = slice(h * HEAD_DIM, (h + 1) * HEAD_DIM)
            for k in range(TOPK):
                scores = times(queries[k, :, span], keys[:, span]) * HEAD_DIM ** (-0.5)
                scores = jnp.where(allowed, scores, -1e30)
                power = jnp.exp(scores - jnp.max(scores, axis=1, keepdims=True))
                probs = power / jnp.sum(power, axis=1, keepdims=True)
                probability[h, k] = probs
                attended[k, :, span] = jnp.dot(
                    probs.astype(BF16), values[:, span], preferred_element_type=F32
                ).astype(BF16)
        rows = rows_of(attn[0], attended[0]) + rows_of(attn[1], attended[1])
        att_rows[...] = rows.astype(BF16)
        low = times(att_rows[...], rights[3 * RANK :]) * gate_row
        low_rows[...] = jnp.concatenate(
            [
                jnp.zeros((low.shape[0], RANK), F32),
                low,
                jnp.zeros((low.shape[0], LANES - 2 * RANK), F32),
            ],
            axis=1,
        ).astype(BF16)

    def compute(n):
        array, start = chunks[n]
        weight = buffer.at[n % 2]
        if array == 0:
            key = jnp.dot(hidden[...], weight[0], preferred_element_type=F32) + jnp.dot(
                rank_kv, rights[RANK : 2 * RANK], preferred_element_type=F32
            )
            keys[...] = turn(key, cosine[...], sine[...]).astype(BF16)
            value = jnp.dot(hidden[...], weight[1], preferred_element_type=F32) + jnp.dot(
                rank_kv, rights[2 * RANK : 3 * RANK], preferred_element_type=F32
            )
            values[...] = value.astype(BF16)
            return
        for item in range(pair):
            e = start + item
            span = slice(e * CAP_ATT, (e + 1) * CAP_ATT)
            if array == 1:
                query_rows[span] = jnp.dot(
                    hidden_rows[span], weight[item], preferred_element_type=F32
                ) + jnp.dot(rank_rows[span], rights[:RANK], preferred_element_type=F32)
            else:
                out_rows[span] = (times(att_rows[span], weight[item]) * gate_row[span]).astype(
                    BF16
                )
        if array == 1 and start + pair == EXP_ATT:
            attend()

    def flatten(e):
        copy = pltpu.make_async_copy(pairs.at[e], pair_in, load.at[2])
        copy.start()
        copy.wait()
        step = 64

        @pl.loop(0, pair_in.shape[0] // step)
        def _(i):
            span = pl.ds(pl.multiple_of(i * step, step), step)
            pair_out[span] = pair_in[span].reshape(step, pair_out.shape[1])

        copy = pltpu.make_async_copy(pair_out, flat.at[e], load.at[3])
        copy.start()
        copy.wait()

    near = pair_in.at[pl.ds(0, pairs_right.shape[0])]
    copy = pltpu.make_async_copy(pairs_right, near, load.at[2])
    copy.start()
    copy.wait()
    step = 64
    pair_rows = pairs_right.shape[0]

    @pl.loop(0, pair_rows // step)
    def _(i):
        span = pl.ds(pl.multiple_of(i * step, step), step)
        pair_out[span] = pair_in[span].reshape(step, pair_out.shape[1])

    copy = pltpu.make_async_copy(pair_out.at[pl.ds(0, pair_rows)], flat_right, load.at[3])
    copy.start()
    copy.wait()
    loads = {}
    total = len(chunks)
    for n in range(2, total + behind + 1):
        if n < total:
            relay(n)
            push_own(n + window)
        if n - 2 < EXP_FF:
            flatten(n - 2)
        if n == total - 1:
            for j in range(1, EARLY + 1):
                which = jnp.bitwise_xor(row // replicas, j)
                send_to(downs.at[which], early[j - 1], across[j * replicas])
        for m in range(n - behind + 1) if n == 2 else [n - behind]:
            if 0 <= m < total:
                if m == 0:
                    for copy in block_kept:
                        copy.wait()
                finish(m)
                loads[m] = pltpu.make_async_copy(
                    place_whole(wholes, chunks[m], pair), buffer.at[m % 2], load.at[m % 2]
                )
                loads[m].start()
            if 0 <= m - 1 < total:
                loads[m - 1].wait()
                compute(m - 1)
    for copy in started:
        if id(copy) not in received:
            copy.wait_recv()
    for copy in started:
        copy.wait_send()
    for copy in kept[1 + len(block_kept) :]:
        copy.wait()


def place_whole(wholes, chunk, pair):
    array, start = chunk
    return wholes[array].at[pl.ds(start, pair)]


def front(smalls, lefts, tokens, blocks, pairs, pairs_right, downs, parts, cols, replicas):
    hbm = pl.BlockSpec(memory_space=pl.ANY)
    vmem = pl.BlockSpec(memory_space=pltpu.VMEM)
    smem = pl.BlockSpec(memory_space=pltpu.SMEM)
    count, wide = tokens.shape
    width = wide * cols
    depth, head_width = blocks[0].shape[1:]
    heads = head_width // HEAD_DIM
    rows = EXP_ATT * CAP_ATT
    rows_ffn = EXP_FF * CAP_FF
    shape = jax.ShapeDtypeStruct
    flat = (pairs.shape[0], pairs.shape[1], 2 * pairs.shape[3])
    n_chunks = sum(block.shape[0] for block in blocks) // 2
    per_chunk = 8 if parts == 8 else parts - 1
    remotes = (
        n_chunks * per_chunk + (cols - 1) * (1 + EXP_FF) + EXP_FF - 1 + 2 * (parts - 1) + EARLY
    )
    return pl.pallas_call(
        functools.partial(front_kernel, parts, cols, replicas),
        out_shape=[
            shape(flat, BF16),
            shape((pairs_right.shape[0], flat[2]), BF16),
            shape((4 * RANK, head_width), BF16),
        ]
        + [shape(downs.shape[1:], BF16)] * EARLY
        + [shape((b.shape[0], width, head_width), BF16) for b in blocks]
        + [shape((CAP_FF, width), BF16)] * EXP_FF
        + [
            shape((count, width), BF16),
            shape((5 * RANK, width), BF16),
            shape((count, LANES), F32),
            shape((count, LANES), F32),
            shape((count, head_width), BF16),
            shape((count, head_width), BF16),
            shape((TOPK, count, head_width), BF16),
            shape((TOPK, count, head_width), BF16),
            shape((heads, TOPK, count, count), F32),
            shape((rows, head_width), BF16),
            shape((rows, LANES), BF16),
            shape((rows, width), BF16),
            shape((TOPK + 1, count, rows), BF16),
            shape((TOPK, count, rows_ffn), BF16),
            shape((count, 2 * RANK), F32),
            shape((rows, 1), F32),
            shape((parts, 8, LANES), F32),
        ],
        in_specs=[smem] * 2 + [vmem] * 15 + [hbm] * 7,
        out_specs=[hbm, hbm, vmem] + [hbm] * (EARLY + 3 + EXP_FF) + [vmem] * 17,
        scratch_shapes=[
            pltpu.VMEM((count, width), BF16),
            pltpu.VMEM((EXP_FF, CAP_FF, wide), BF16),
            pltpu.VMEM((EXP_FF - 1, CAP_FF, wide), BF16),
            pltpu.VMEM((rows, width), BF16),
            pltpu.VMEM((2, 2, width, head_width), BF16),
            pltpu.VMEM((rows, head_width), F32),
            pltpu.VMEM((8, LANES), F32),
            pltpu.VMEM((parts, 5 * RANK, depth), BF16),
            pltpu.VMEM(pairs.shape[1:], BF16),
            pltpu.VMEM(flat[1:], BF16),
            pltpu.SemaphoreType.DMA((remotes,)),
            pltpu.SemaphoreType.DMA((remotes,)),
            pltpu.SemaphoreType.DMA((4 + EXP_FF,)),
            pltpu.SemaphoreType.DMA((4,)),
        ],
        compiler_params=pltpu.CompilerParams(
            collective_id=1, has_side_effects=True, vmem_limit_bytes=62 * 2**20
        ),
    )(*smalls, *lefts, tokens, *blocks, pairs, pairs_right, downs)


def middle_back_kernel(cols, replicas, *refs):
    blocks, downs = refs[:EXP_FF], refs[EXP_FF : 2 * EXP_FF]
    adapter, norm, router, stat = refs[2 * EXP_FF : 2 * EXP_FF + 4]
    sources = refs[2 * EXP_FF + 4 : 2 * EXP_FF + 9]
    grad_middle, grad_whole, totals, branch, low_down = refs[2 * EXP_FF + 9 : 2 * EXP_FF + 14]
    scratch = refs[2 * EXP_FF + 14 :]
    picks_ffn, lefts, hidden, middle, cot = scratch[:5]
    rows, down_rows, exact_part, parts, extra, parts_in, extra_in, low, send, recv, local = (
        scratch[5:]
    )
    col = lax.axis_index("col")
    count, wide = middle.shape
    width = hidden.shape[1]
    across = [opposite("row", j * replicas) for j in range(1, EXP_FF)]
    along = [opposite("col", i) for i in range(1, cols)]
    greet(across + along)
    near = fetch(
        [*blocks, downs[0], *sources],
        [
            *(rows.at[pl.ds(j * CAP_FF, CAP_FF)] for j in range(EXP_FF)),
            down_rows.at[pl.ds(0, CAP_FF)],
            *scratch[:5],
        ],
        local,
    )
    base = 0
    down_copies = [
        remote(
            downs[j],
            down_rows.at[pl.ds(j * CAP_FF, CAP_FF)],
            send,
            recv,
            base + j - 1,
            across[j - 1],
        )
        for j in range(1, EXP_FF)
    ]
    for copy in near:
        copy.wait()
    picks = [picks_ffn[0], picks_ffn[1]]
    any_pick = picks[0] + picks[1]

    def back(pick, source, start, size):
        return jnp.dot(pick, source[:, start : start + size], preferred_element_type=F32)

    sub = lax.broadcasted_iota(jnp.int32, (LANES, LANES), 0)
    lane = lax.broadcasted_iota(jnp.int32, (LANES, LANES), 1)
    mine = lax.broadcasted_iota(jnp.int32, (count, LANES), 1) // RANK == adapter[0]
    place_rank = (lane == RANK + sub % RANK).astype(F32).astype(BF16)

    def own_rank(value):
        value = jnp.where(mine, value, 0.0).astype(BF16)
        return jnp.dot(value, place_rank, preferred_element_type=F32)

    gate_grads = []
    for k in range(TOPK):
        pair = back(picks[k], rows, width + LANES, LANES)
        gate_grads.append(pair[:, 0:1] + pair[:, 1:2])
    rank = own_rank(back(any_pick, rows, width, LANES))
    rank_low = rank[:, RANK : 2 * RANK].astype(BF16)
    product = jnp.zeros((count, 1), F32)
    for q in range(cols):
        here = slice(q * wide, (q + 1) * wide)
        part = back(any_pick, rows, q * wide, wide) + jnp.dot(
            rank_low, lefts[3 * RANK : 4 * RANK, here], preferred_element_type=F32
        )
        product += jnp.sum(part * hidden[:, here].astype(F32), axis=1, keepdims=True)
        exact_part[q] = part
        parts[q] = part.astype(BF16)
    columns = [*split(gate_grads[0]), *split(gate_grads[1]), *split(product)]
    small = pack(columns, range(6)) + rank
    extra[...] = small.astype(BF16)
    base += EXP_FF - 1
    arrivals = []
    for i in range(1, cols):
        target = jnp.bitwise_xor(col, i)
        n = base + 2 * (i - 1)
        arrivals.append(remote(extra, extra_in.at[i - 1], send, recv, n + 1, along[i - 1]))
        arrivals.append(
            remote(parts.at[target], parts_in.at[i - 1], send, recv, n, along[i - 1])
        )
    for copy in arrivals:
        copy.wait_recv()
    grad = exact_part[col]
    total = small
    for i in range(cols - 1):
        grad += parts_in[i].astype(F32)
        total += extra_in[i].astype(F32)
    totals[...] = total
    gate_grads = [total[:, 0:1] + total[:, 1:2], total[:, 2:3] + total[:, 3:4]]
    first = pl.multiple_of(col * wide, wide)
    term, more = route_term(stat, gate_grads, router, first, wide)
    inner = total[:, 4:5] + total[:, 5:6] + more
    scaled = (grad + term) * norm[:, pl.ds(first, wide)]
    factor = stat[:, 4:5]
    valid = stat[:, 7:8]
    result = (
        cot[...].astype(F32) * valid
        + factor * scaled
        - middle[...] * (factor * factor * inner * (1.0 / width))
    )
    grad_middle[...] = result
    low[...] = result.astype(BF16)
    here = pl.ds(first, wide)
    kept = pltpu.make_async_copy(low, grad_whole.at[:, here], local.at[10])
    kept.start()
    base += 2 * (cols - 1)
    last = [
        remote(low, grad_whole.at[:, here], send, recv, base + i, along[i])
        for i in range(cols - 1)
    ]
    for copy in down_copies:
        copy.wait_recv()
    rank = own_rank(back(any_pick, down_rows, width, LANES))
    rank_low = rank[:, RANK : 2 * RANK].astype(BF16)
    low_down[...] = rank
    for q in range(cols):
        here = slice(q * wide, (q + 1) * wide)
        part = back(any_pick, down_rows, q * wide, wide) + jnp.dot(
            rank_low, lefts[4 * RANK : 5 * RANK, here], preferred_element_type=F32
        )
        branch[:, here] = part.astype(BF16)
    for copy in last:
        copy.wait_recv()
    for copy in down_copies + arrivals + last:
        copy.wait_send()
    kept.wait()


def middle_back(blocks, downs, adapter, norm, router, stat, sources, cols, replicas):
    hbm = pl.BlockSpec(memory_space=pl.ANY)
    vmem = pl.BlockSpec(memory_space=pltpu.VMEM)
    smem = pl.BlockSpec(memory_space=pltpu.SMEM)
    count, wide = sources[-1].shape
    total = EXP_FF - 1 + 3 * (cols - 1)
    rows = EXP_FF * CAP_FF
    return pl.pallas_call(
        functools.partial(middle_back_kernel, cols, replicas),
        out_shape=[
            jax.ShapeDtypeStruct((count, wide), F32),
            jax.ShapeDtypeStruct((count, wide * cols), BF16),
            jax.ShapeDtypeStruct((count, LANES), F32),
            jax.ShapeDtypeStruct((count, wide * cols), BF16),
            jax.ShapeDtypeStruct((count, LANES), F32),
        ],
        in_specs=[hbm] * (2 * EXP_FF) + [smem, vmem, vmem, vmem] + [hbm] * 5,
        out_specs=[vmem, hbm, vmem, vmem, vmem],
        scratch_shapes=[pltpu.VMEM(source.shape, source.dtype) for source in sources]
        + [
            pltpu.VMEM((rows, blocks[0].shape[1]), BF16),
            pltpu.VMEM((rows, downs[0].shape[1]), BF16),
            pltpu.VMEM((cols, count, wide), F32),
            pltpu.VMEM((cols, count, wide), BF16),
            pltpu.VMEM((count, LANES), BF16),
            pltpu.VMEM((cols - 1, count, wide), BF16),
            pltpu.VMEM((cols - 1, count, LANES), BF16),
            pltpu.VMEM((count, wide), BF16),
            pltpu.SemaphoreType.DMA((total,)),
            pltpu.SemaphoreType.DMA((total,)),
            pltpu.SemaphoreType.DMA((11,)),
        ],
        compiler_params=pltpu.CompilerParams(
            collective_id=4, has_side_effects=True, vmem_limit_bytes=62 * 2**20
        ),
    )(*blocks, *downs, adapter, norm, router, stat, *sources)


def tail_kernel(parts_axis, cols, *refs):
    (
        adapters,
        norm,
        router,
        stat,
        cosine,
        sine,
        rights,
        ranks,
        gate_rows,
        totals_attn,
        totals_ffn,
        low_down,
    ) = refs[:12]
    sources = refs[12:27]
    branch, out_whole, query_whole, kv_whole = refs[27:31]
    output, grad_inputs = refs[31:33]
    left_outs = refs[33:38]
    right_outs = refs[38:42]
    (
        grad_whole,
        picks,
        att_rows,
        queries,
        keys,
        values,
        probability,
        attended,
        lefts_whole,
        hidden_one,
        hidden_two,
        grad_middle,
        middle,
        cot,
        tokens,
    ) = refs[42:57]
    (
        cot_own,
        cot_whole,
        branch_in,
        rows,
        grads,
        buffer,
        query_grads,
        key_grad,
        value_grad,
        part,
        parts,
        extra,
        parts_in,
        extra_in,
        right_parts,
        rights_in,
        lefts,
        lefts_in,
        send,
        recv,
        local,
        load,
    ) = refs[57:]
    row = lax.axis_index("row")
    col = lax.axis_index("col")
    count, wide = tokens.shape
    width = hidden_one.shape[1]
    depth = width // parts_axis
    head_width = keys.shape[1]
    heads = head_width // HEAD_DIM
    along = [opposite("col", i) for i in range(1, cols)]
    across = [opposite("row", m) for m in range(1, parts_axis)]
    greet(across + along)
    started = []

    def send_to(source, target, device):
        copy = remote(source, target, send, recv, len(started), device)
        started.append(copy)
        return copy

    pair = 2
    chunks = [
        (whole, start)
        for whole in (out_whole, query_whole, kv_whole)
        for start in range(0, whole.shape[0], pair)
    ]
    loads = []
    for n, (whole, start) in enumerate(chunks):
        loads.append(
            pltpu.make_async_copy(whole.at[pl.ds(start, pair)], buffer.at[n % 2], load.at[n % 2])
        )
    near = fetch(sources, refs[42:57], local)
    loads[0].start()
    loads[1].start()
    first = pl.multiple_of(col * wide, wide)
    here = pl.ds(first, wide)
    valid = stat[:, 7:8]
    branch_copies = []
    for i in range(1, cols):
        target = jnp.bitwise_xor(col, i)
        theirs = pl.ds(pl.multiple_of(target * wide, wide), wide)
        branch_copies.append(send_to(branch.at[:, theirs], branch_in.at[i - 1], along[i - 1]))
    mine = pltpu.make_async_copy(branch.at[:, here], branch_in.at[cols - 1], local.at[15])
    mine.start()
    for copy in near:
        copy.wait()
    cot_own[...] = (cot[...].astype(F32) * valid).astype(BF16)
    cot_whole[:, here] = cot_own[...]
    cot_copies = [send_to(cot_own, cot_whole.at[:, here], device) for device in along]

    def rows_of(matrix, value):
        return lax.dot_general(
            matrix, value, (((0,), (0,)), ((), ())), preferred_element_type=F32
        )

    def times(left, right):
        return lax.dot_general(
            left, right, (((1,), (1,)), ((), ())), preferred_element_type=F32
        )

    def dot(left, right):
        return jnp.dot(left, right, preferred_element_type=F32)

    any_pick = picks[TOPK]
    low_grad = times(grad_whole[...], lefts_whole[2 * RANK : 3 * RANK])
    low_rows = rows_of(any_pick, low_grad.astype(BF16)).astype(BF16)
    for q in range(cols):
        span = slice(q * wide, (q + 1) * wide)
        rows[:, span] = rows_of(any_pick, grad_whole[:, span]).astype(BF16)
    number = 0

    def next_weights():
        nonlocal number
        loads[number].wait()
        return buffer.at[number % 2]

    def done_weights():
        nonlocal number
        if number + 2 < len(chunks):
            loads[number + 2].start()
        number += 1

    for start in range(0, EXP_ATT, pair):
        weight = next_weights()
        for item in range(pair):
            span = slice((start + item) * CAP_ATT, (start + item + 1) * CAP_ATT)
            grads[span] = dot(rows[span], weight[item]) + dot(low_rows[span], rights[3 * RANK :])
        done_weights()
    value = grads[...]
    gate_grad = jnp.sum(att_rows[...].astype(F32) * value, axis=1, keepdims=True)
    gate_pack = pack([*split(gate_grad)], range(2)).astype(BF16)
    gate_grads = []
    gated = (value * gate_rows[...]).astype(BF16)
    right_out = jnp.zeros((RANK, head_width), F32)
    for k in range(TOPK):
        both = dot(picks[k], gate_pack)
        gate_grads.append(both[:, 0:1] + both[:, 1:2])
        query_grads[k] = dot(picks[k], gated).astype(BF16)
        right_out += rows_of((stat[:, k : k + 1] * low_grad).astype(BF16), attended[k])
    scaling = HEAD_DIM ** (-0.5)
    query_sum = []
    for h in range(heads):
        span = slice(h * HEAD_DIM, (h + 1) * HEAD_DIM)
        key_total, value_total, sum_head = 0.0, 0.0, 0.0
        for k in range(TOPK):
            grad_att = query_grads[k, :, span]
            probs = probability[h, k]
            grad_prob = times(grad_att, values[:, span])
            centre = jnp.sum(probs * grad_prob, axis=1, keepdims=True)
            grad_score = (probs * (grad_prob - centre)).astype(BF16)
            value_total += rows_of(probs.astype(BF16), grad_att)
            key_total += rows_of(grad_score, queries[k, :, span])
            grad_query = dot(grad_score, keys[:, span]) * scaling
            turned = turn(grad_query, cosine[...], -sine[...]).astype(BF16)
            query_grads[k, :, span] = turned
            sum_head += turned.astype(F32)
        key_grad[:, span] = turn(key_total * scaling, cosine[...], -sine[...]).astype(BF16)
        value_grad[:, span] = value_total.astype(BF16)
        query_sum.append(sum_head.astype(BF16))
    query_sum = jnp.concatenate(query_sum, axis=1)
    rank_query = ranks[:, :RANK].astype(BF16)
    rank_kv = ranks[:, RANK:].astype(BF16)
    right_values = [
        rows_of(rank_query, query_sum),
        rows_of(rank_kv, key_grad[...]),
        rows_of(rank_kv, value_grad[...]),
        right_out,
    ]
    for p in range(4):
        right_parts[:, p * head_width : (p + 1) * head_width] = right_values[p].astype(BF16)
    right_copies = [
        send_to(right_parts, rights_in.at[m], across[m]) for m in range(parts_axis - 1)
    ]
    grad_rank_query = times(query_sum, rights[:RANK])
    grad_rank_kv = times(key_grad[...], rights[RANK : 2 * RANK]) + times(
        value_grad[...], rights[2 * RANK : 3 * RANK]
    )
    query_rows = (rows_of(picks[0], query_grads[0]) + rows_of(picks[1], query_grads[1])).astype(
        BF16
    )
    for start in range(0, EXP_ATT, pair):
        weight = next_weights()
        for item in range(pair):
            span = slice((start + item) * CAP_ATT, (start + item + 1) * CAP_ATT)
            rows[span] = times(query_rows[span], weight[item]).astype(BF16)
        done_weights()
    weight = next_weights()
    low = jnp.concatenate([grad_rank_query, grad_rank_kv], axis=1).astype(BF16)
    product = jnp.zeros((count, 1), F32)
    for q in range(cols):
        span = slice(q * wide, (q + 1) * wide)
        value = (
            dot(any_pick, rows[:, span])
            + times(key_grad[...], weight[0, span])
            + times(value_grad[...], weight[1, span])
            + dot(low, lefts_whole[: 2 * RANK, span])
        )
        product += jnp.sum(value * hidden_one[:, span].astype(F32), axis=1, keepdims=True)
        part[q] = value
        parts[q] = value.astype(BF16)
    columns = [*split(gate_grads[0]), *split(gate_grads[1]), *split(product)]
    small = pack(columns, range(6)) + jnp.concatenate(
        [
            jnp.zeros((count, RANK), F32),
            grad_rank_query,
            grad_rank_kv,
            low_down[:, RANK : 2 * RANK],
            jnp.zeros((count, LANES - 4 * RANK), F32),
        ],
        axis=1,
    )
    extra[...] = small.astype(BF16)
    extra_copies, part_copies = [], []
    for i in range(1, cols):
        target = jnp.bitwise_xor(col, i)
        extra_copies.append(send_to(extra, extra_in.at[i - 1], along[i - 1]))
        part_copies.append(send_to(parts.at[target], parts_in.at[i - 1], along[i - 1]))
    mine.wait()
    for copy in branch_copies:
        copy.wait_recv()
    result = middle[...]
    for i in range(cols):
        result += branch_in[i].astype(F32)
    output[...] = (result * valid).astype(BF16)
    for copy in cot_copies:
        copy.wait_recv()

    def outer(left, right):
        return rows_of(left, right).astype(BF16)

    whole = outer(totals_attn[...].astype(BF16), grad_whole[...])
    for m in range(parts_axis):
        lefts[m, 2 * RANK : 3 * RANK] = whole[RANK : 2 * RANK, m * depth : (m + 1) * depth]
    whole = outer(totals_ffn[...].astype(BF16), hidden_two[...])
    for m in range(parts_axis):
        lefts[m, 3 * RANK : 4 * RANK] = whole[RANK : 2 * RANK, m * depth : (m + 1) * depth]
    chosen_by = [
        [jnp.where(adapters[m] == a, 1.0, 0.0).astype(F32) for a in range(ADAPT)]
        for m in range(parts_axis)
    ]

    def share(values, target):
        for a in range(ADAPT):
            result = chosen_by[0][a] * values[0]
            for m in range(1, parts_axis):
                result += chosen_by[m][a] * values[m]
            target[a] = result

    for copy in right_copies:
        copy.wait_recv()
    for p in range(4):
        span = slice(p * head_width, (p + 1) * head_width)
        share(
            [right_parts[:, span].astype(F32)]
            + [rights_in[m, :, span].astype(F32) for m in range(parts_axis - 1)],
            right_outs[p],
        )
    total = small
    for i in range(cols - 1):
        extra_copies[i].wait_recv()
        total += extra_in[i].astype(F32)
    low_totals = total.astype(BF16)
    whole = outer(low_totals, hidden_one[...])
    for m in range(parts_axis):
        lefts[m, : 2 * RANK] = whole[RANK : 3 * RANK, m * depth : (m + 1) * depth]
    whole = outer(low_totals, cot_whole[...])
    for m in range(parts_axis):
        lefts[m, 4 * RANK :] = whole[3 * RANK : 4 * RANK, m * depth : (m + 1) * depth]
    left_copies = [
        send_to(lefts.at[jnp.bitwise_xor(row, m)], lefts_in.at[m - 1], across[m - 1])
        for m in range(1, parts_axis)
    ]
    gate_totals = [total[:, 0:1] + total[:, 1:2], total[:, 2:3] + total[:, 3:4]]
    term, more = route_term(stat, gate_totals, router, first, wide)
    inner = total[:, 4:5] + total[:, 5:6] + more
    grad = part[col] + term
    for i in range(cols - 1):
        part_copies[i].wait_recv()
        grad += parts_in[i].astype(F32)
    factor = stat[:, 4:5]
    grad_inputs[...] = (
        grad_middle[...]
        + factor * (grad * norm[:, here])
        - tokens[...].astype(F32) * (factor * factor * inner * (1.0 / width))
    )
    for copy in left_copies:
        copy.wait_recv()
    for p in range(5):
        span = slice(p * RANK, (p + 1) * RANK)
        share(
            [lefts[row, span].astype(F32)]
            + [lefts_in[m, span].astype(F32) for m in range(parts_axis - 1)],
            left_outs[p],
        )
    for copy in started:
        copy.wait_send()


def tail(smalls, sources, branch, wholes, parts_axis, cols):
    hbm = pl.BlockSpec(memory_space=pl.ANY)
    vmem = pl.BlockSpec(memory_space=pltpu.VMEM)
    smem = pl.BlockSpec(memory_space=pltpu.SMEM)
    count, wide = sources[-1].shape
    width = wide * cols
    depth = width // parts_axis
    head_width = wholes[0].shape[2]
    rows = EXP_ATT * CAP_ATT
    shape = jax.ShapeDtypeStruct
    total = 4 * (cols - 1) + 2 * (parts_axis - 1)
    return pl.pallas_call(
        functools.partial(tail_kernel, parts_axis, cols),
        out_shape=[shape((count, wide), BF16), shape((count, wide), F32)]
        + [shape((ADAPT, RANK, depth), F32)] * 5
        + [shape((ADAPT, RANK, head_width), F32)] * 4,
        in_specs=[smem] + [vmem] * 11 + [hbm] * 19,
        out_specs=[vmem] * 11,
        scratch_shapes=[pltpu.VMEM(source.shape, source.dtype) for source in sources]
        + [
            pltpu.VMEM((count, wide), BF16),
            pltpu.VMEM((count, width), BF16),
            pltpu.VMEM((cols, count, wide), BF16),
            pltpu.VMEM((rows, width), BF16),
            pltpu.VMEM((rows, head_width), F32),
            pltpu.VMEM((2, 2, width, head_width), BF16),
            pltpu.VMEM((TOPK, count, head_width), BF16),
            pltpu.VMEM((count, head_width), BF16),
            pltpu.VMEM((count, head_width), BF16),
            pltpu.VMEM((cols, count, wide), F32),
            pltpu.VMEM((cols, count, wide), BF16),
            pltpu.VMEM((count, LANES), BF16),
            pltpu.VMEM((cols - 1, count, wide), BF16),
            pltpu.VMEM((cols - 1, count, LANES), BF16),
            pltpu.VMEM((RANK, 4 * head_width), BF16),
            pltpu.VMEM((parts_axis - 1, RANK, 4 * head_width), BF16),
            pltpu.VMEM((parts_axis, 5 * RANK, depth), BF16),
            pltpu.VMEM((parts_axis - 1, 5 * RANK, depth), BF16),
            pltpu.SemaphoreType.DMA((total,)),
            pltpu.SemaphoreType.DMA((total,)),
            pltpu.SemaphoreType.DMA((16,)),
            pltpu.SemaphoreType.DMA((2,)),
        ],
        compiler_params=pltpu.CompilerParams(
            collective_id=5, has_side_effects=True, vmem_limit_bytes=62 * 2**20
        ),
    )(*smalls, *sources, branch, *wholes)


def middle_kernel(parts_axis, cols, replicas, *refs):
    adapter, norm, router, route, low_rows, low_in = refs[:6]
    sources = refs[6:11]
    weights = refs[11:13]
    early = refs[13 : 13 + EARLY]
    outs = refs[13 + EARLY :]
    chunks = [[None, *outs[: parts_axis - 1]], [None]]
    outs = outs[parts_axis - 1 :]
    for m in range(1, parts_axis):
        if m % replicas == 0 and m <= EARLY * replicas:
            chunks[1].append(early[m // replicas - 1])
        else:
            chunks[1].append(outs[0])
            outs = outs[1:]
    hids = outs[:EXP_FF]
    hidden_out, middle, stat, totals = outs[EXP_FF : EXP_FF + 4]
    scratch = outs[EXP_FF + 4 :]
    out_rows, picks_attn, picks_ffn, lefts, tokens = scratch[:5]
    (
        exact_part,
        parts,
        extra,
        parts_in,
        extra_in,
        square,
        square_in,
        low,
        hidden,
        message,
        send,
        recv,
        local,
    ) = scratch[5:]
    col = lax.axis_index("col")
    count, wide = tokens.shape
    width = hidden.shape[1]
    across = [opposite("row", j * replicas) for j in range(1, EXP_FF)]
    beside = [opposite("row", i) for i in range(1, replicas)]
    along = [opposite("col", i) for i in range(1, cols)]
    greet(across + beside + along)
    near = fetch(sources, scratch[:5], local)
    used = [0]
    started = []

    def send_to(source, target, device):
        copy = remote(source, target, send, recv, used[0], device)
        used[0] += 1
        started.append(copy)
        return copy

    expert = lax.axis_index("row") // replicas
    piece_copies = [
        [
            send_to(weights[n].at[jnp.bitwise_xor(expert, j)], chunks[n][j * replicas], across[j - 1])
            for n in ((0,) if j <= EARLY else (0, 1))
        ]
        for j in range(1, EXP_FF)
    ]
    sibling_copies = [
        send_to(weights[n].at[expert], chunks[n][i], beside[i - 1])
        for i in range(1, replicas)
        for n in (0, 1)
    ]
    for j in range(1, EARLY + 1):
        for i in range(1, replicas):
            m = j * replicas
            sibling_copies.append(send_to(chunks[1][m], chunks[1][m + i], beside[i - 1]))
    for copy in near:
        copy.wait()

    def back(source):
        return jnp.dot(picks_attn[TOPK], source, preferred_element_type=F32)

    def rows_of(matrix, value):
        return lax.dot_general(
            matrix, value, (((0,), (0,)), ((), ())), preferred_element_type=F32
        )

    sub = lax.broadcasted_iota(jnp.int32, (LANES, LANES), 0)
    lane = lax.broadcasted_iota(jnp.int32, (LANES, LANES), 1)
    lanes = lax.broadcasted_iota(jnp.int32, (count, LANES), 1)
    low_out = back(low_rows[...])
    small = low_in[...] + low_out
    low_out = low_out[:, RANK : 2 * RANK].astype(BF16)
    for q in range(cols):
        here = slice(q * wide, (q + 1) * wide)
        part = back(out_rows[:, here]) + jnp.dot(
            low_out, lefts[2 * RANK : 3 * RANK, here], preferred_element_type=F32
        )
        exact_part[q] = part
        parts[q] = part.astype(BF16)
    extra[...] = small.astype(BF16)
    part_copies = []
    extra_copies = []
    for i in range(1, cols):
        target = jnp.bitwise_xor(col, i)
        part_copies.append(send_to(parts.at[target], parts_in.at[i - 1], along[i - 1]))
        extra_copies.append(send_to(extra, extra_in.at[i - 1], along[i - 1]))
    value = tokens[...].astype(F32) + exact_part[col]
    total = small
    for i in range(cols - 1):
        part_copies[i].wait_recv()
        value += parts_in[i].astype(F32)
    middle[...] = value
    square[...] = lax.dot_general(
        jnp.ones((8, wide), F32),
        value * value,
        (((1,), (1,)), ((), ())),
        precision=HIGHEST,
        preferred_element_type=F32,
    )
    square_copies = [
        send_to(square, square_in.at[i], along[i]) for i in range(cols - 1)
    ]
    for i in range(cols - 1):
        extra_copies[i].wait_recv()
        total += extra_in[i].astype(F32)
    totals[...] = total
    squares = square[...]
    for i in range(cols - 1):
        square_copies[i].wait_recv()
        squares += square_in[i]
    squares = lax.dot_general(
        squares,
        jnp.full((8, LANES), 0.125, F32),
        (((0,), (0,)), ((), ())),
        precision=HIGHEST,
        preferred_element_type=F32,
    )
    scale = lax.rsqrt(squares[:, 0:1] * (1.0 / width) + EPSILON)
    first = pl.multiple_of(col * wide, wide)
    here = pl.ds(first, wide)
    low[...] = (value * scale * norm[:, here]).astype(BF16)
    hidden[:, here] = low[...]
    hidden_copies = [send_to(low, hidden.at[:, here], along[i]) for i in range(cols - 1)]
    mine = lanes // RANK == adapter[0]

    def own_adapter(value, start):
        spread = (sub - start == lane % RANK).astype(F32).astype(BF16)
        value = jnp.dot(value.astype(BF16), spread, preferred_element_type=F32)
        return jnp.where(mine, value, 0.0).astype(BF16)

    picks = [picks_ffn[0], picks_ffn[1]]
    any_pick = picks[0] + picks[1]
    message[:, width + 2 * LANES :] = rows_of(any_pick, own_adapter(total, 2 * RANK)).astype(BF16)
    for copy in hidden_copies:
        copy.wait_recv()
    kept = pltpu.make_async_copy(hidden, hidden_out, local.at[6])
    kept.start()

    def times(right):
        return lax.dot_general(
            hidden[...], right, (((1,), (1,)), ((), ())), preferred_element_type=F32
        )

    logits = times(router[...])
    routes = [route[:, 8 + k : 9 + k] for k in range(TOPK)]
    chosen, gates = scores_of(routes, logits, EXP_FF)
    stat[...] = pack(
        [*gates, *chosen, scale, *routes, route[:, 7:8]], range(8)
    )
    gate_rows = 0.0
    for k in range(TOPK):
        columns = pack([*split(gates[k])], range(2)).astype(BF16)
        gate_rows += rows_of(picks[k], columns)
    message[:, width + LANES : width + 2 * LANES] = gate_rows.astype(BF16)
    rank = times(lefts[3 * RANK : 4 * RANK])
    rank = jnp.concatenate([rank, jnp.zeros((count, LANES - RANK), F32)], axis=1)
    message[:, width : width + LANES] = rows_of(any_pick, own_adapter(rank, 0)).astype(BF16)
    for q in range(cols):
        span = slice(q * wide, (q + 1) * wide)
        message[:, span] = rows_of(any_pick, hidden[:, span]).astype(BF16)
    traded = [
        send_to(message.at[pl.ds(j * CAP_FF, CAP_FF)], hids[j], across[j - 1])
        for j in range(EXP_FF - 1, 0, -1)
    ]
    own = pltpu.make_async_copy(message.at[pl.ds(0, CAP_FF)], hids[0], local.at[7])
    own.start()
    for j in range(1, EXP_FF):
        for n in range(len(piece_copies[j - 1])):
            piece_copies[j - 1][n].wait_recv()
            for i in range(1, replicas):
                m = j * replicas
                sibling_copies.append(send_to(chunks[n][m], chunks[n][m + i], beside[i - 1]))
    for copy in traded + sibling_copies:
        copy.wait_recv()
    for copy in started:
        copy.wait_send()
    kept.wait()
    own.wait()


def middle_forward(adapter, norm, router, route, low_rows, low_in, sources, weights, early, parts_axis, cols, replicas):
    hbm = pl.BlockSpec(memory_space=pl.ANY)
    vmem = pl.BlockSpec(memory_space=pltpu.VMEM)
    smem = pl.BlockSpec(memory_space=pltpu.SMEM)
    count, wide = sources[-1].shape
    width = wide * cols
    rows = EXP_FF * CAP_FF
    full = width + 3 * LANES
    total = 2 * (parts_axis - 1) + 4 * (cols - 1) + EXP_FF - 1
    return pl.pallas_call(
        functools.partial(middle_kernel, parts_axis, cols, replicas),
        out_shape=[jax.ShapeDtypeStruct(weights[0].shape[1:], BF16)] * (parts_axis - 1)
        + [jax.ShapeDtypeStruct(weights[1].shape[1:], BF16)] * (parts_axis - 1 - EARLY)
        + [jax.ShapeDtypeStruct((CAP_FF, full), BF16)] * EXP_FF
        + [
            jax.ShapeDtypeStruct((count, width), BF16),
            jax.ShapeDtypeStruct((count, wide), F32),
            jax.ShapeDtypeStruct((count, LANES), F32),
            jax.ShapeDtypeStruct((count, LANES), F32),
        ],
        in_specs=[smem] + [vmem] * 5 + [hbm] * (7 + EARLY),
        out_specs=[hbm] * (2 * parts_axis - 1 - EARLY + EXP_FF) + [vmem] * 3,
        scratch_shapes=[pltpu.VMEM(source.shape, source.dtype) for source in sources]
        + [
            pltpu.VMEM((cols, count, wide), F32),
            pltpu.VMEM((cols, count, wide), BF16),
            pltpu.VMEM((count, LANES), BF16),
            pltpu.VMEM((cols - 1, count, wide), BF16),
            pltpu.VMEM((cols - 1, count, LANES), BF16),
            pltpu.VMEM((8, count), F32),
            pltpu.VMEM((cols - 1, 8, count), F32),
            pltpu.VMEM((count, wide), BF16),
            pltpu.VMEM((count, width), BF16),
            pltpu.VMEM((rows, full), BF16),
            pltpu.SemaphoreType.DMA((total,)),
            pltpu.SemaphoreType.DMA((total,)),
            pltpu.SemaphoreType.DMA((8,)),
        ],
        compiler_params=pltpu.CompilerParams(
            collective_id=3, has_side_effects=True, vmem_limit_bytes=62 * 2**20
        ),
    )(adapter, norm, router, route, low_rows, low_in, *sources, *weights, *early)


def ffn_kernel(parts, depth, width, units, *refs):
    hids = refs[:EXP_FF]
    cots = refs[EXP_FF : 2 * EXP_FF]
    inners = refs[2 * EXP_FF : 2 * EXP_FF + parts]
    lasts = refs[2 * EXP_FF + parts : 2 * EXP_FF + 2 * parts]
    rights = refs[2 * EXP_FF + 2 * parts : 2 * EXP_FF + 2 * parts + 2]
    outs = refs[2 * EXP_FF + 2 * parts + 2 :]
    grads = outs[:EXP_FF]
    downs = outs[EXP_FF : 2 * EXP_FF]
    adapt = outs[2 * EXP_FF : 2 * EXP_FF + 3]
    hid, cot, block, act, product, leaving, sems, send, recv = outs[2 * EXP_FF + 3 :]
    replicas = parts // EXP_FF
    across = [opposite("row", j * replicas) for j in range(1, EXP_FF)]
    greet(across)
    row = lax.axis_index("row")
    wide = width + LANES
    copies = []
    for j in range(EXP_FF):
        where = pl.ds(j * CAP_FF, CAP_FF)
        near = hids[j].at[:, pl.ds(0, wide + LANES)]
        copies.append(pltpu.make_async_copy(near, hid.at[where], sems.at[j]))
        near = cot.at[where, pl.ds(0, width)]
        copies.append(pltpu.make_async_copy(cots[j], near, sems.at[EXP_FF + j]))
        near = cot.at[where, pl.ds(width, LANES)]
        low = hids[j].at[:, pl.ds(wide + LANES, LANES)]
        copies.append(pltpu.make_async_copy(low, near, sems.at[2 * EXP_FF + j]))
    for n, (start, size) in enumerate(((0, 2 * units), (2 * units, units))):
        near = block.at[pl.ds(width, LANES), pl.ds(start, size)]
        copies.append(pltpu.make_async_copy(rights[n], near, sems.at[3 * EXP_FF + n]))
    expert = row // replicas
    for m in range(parts):
        owner = jnp.bitwise_xor(row, m)
        where = pl.ds(pl.multiple_of(owner * depth, depth), depth)
        inner = inners[m] if m else inners[0].at[expert]
        last = lasts[m] if m else lasts[0].at[expert]
        near = block.at[where, pl.ds(0, 2 * units)]
        copies.append(pltpu.make_async_copy(inner, near, sems.at[3 * EXP_FF + 2 + m]))
        near = block.at[where, pl.ds(2 * units, units)]
        copies.append(pltpu.make_async_copy(last, near, sems.at[3 * EXP_FF + 2 + parts + m]))
    for copy in copies:
        copy.start()
    for copy in copies:
        copy.wait()
    gate_scale = hid[:, wide : wide + 1].astype(F32) + hid[:, wide + 1 : wide + 2].astype(F32)
    product[...] = jnp.zeros_like(product)

    def forward(start, size):
        here = pl.ds(start, size)
        up_here = pl.ds(units + start, size)
        down_here = pl.ds(2 * units + start, size)
        gate = jnp.dot(hid[:, :wide], block[:, here], preferred_element_type=F32)
        up = jnp.dot(hid[:, :wide], block[:, up_here], preferred_element_type=F32)
        grad = jnp.dot(cot[...], block[:, down_here], preferred_element_type=F32)
        sig = 1.0 / (1.0 + jnp.exp(-gate))
        mixed = (gate * sig * up).astype(BF16)
        act[:, down_here] = mixed
        product[...] += jnp.sum(mixed.astype(F32) * grad, axis=1, keepdims=True)
        grad = grad * gate_scale
        act[:, here] = (grad * up * sig * (1.0 + gate * (1.0 - sig))).astype(BF16)
        act[:, up_here] = (grad * gate * sig).astype(BF16)

    step = 2 * LANES
    full = units // step

    @pl.loop(0, full)
    def _(i):
        forward(pl.multiple_of(i * step, step), step)

    if units % step:
        forward(full * step, units % step)

    total = product[...]
    high = total.astype(BF16)
    low = (total - high.astype(F32)).astype(BF16)
    lane = lax.broadcasted_iota(jnp.int32, (EXP_FF * CAP_FF, LANES), 1)
    packed = jnp.where(
        lane == 0, high.astype(F32), jnp.where(lane == 1, low.astype(F32), 0.0)
    ).astype(BF16)
    traded = []
    spans = [(start, 4 * LANES) for start in range(0, width, 4 * LANES)] + [(width, LANES)]
    for start, size in spans:
        here = pl.ds(start, size)
        result = lax.dot_general(
            act[:, : 2 * units],
            block[here, : 2 * units],
            (((1,), (1,)), ((), ())),
            preferred_element_type=F32,
        ).astype(BF16)
        sent = here
        if start == width:
            result = jnp.concatenate([result, packed], axis=1)
            sent = pl.ds(start, 2 * LANES)
        grads[0][:, sent] = result[:CAP_FF]
        for j in range(1, EXP_FF):
            leaving[j - 1, :, sent] = result[j * CAP_FF : (j + 1) * CAP_FF]
            traded.append(
                remote(
                    leaving.at[j - 1, :, sent],
                    grads[j].at[:, sent],
                    send,
                    recv,
                    len(traded),
                    across[j - 1],
                )
            )

    def backward(start, size):
        here = pl.ds(start, size)
        result = lax.dot_general(
            act[:, 2 * units :],
            block[here, 2 * units :],
            (((1,), (1,)), ((), ())),
            preferred_element_type=F32,
        )
        result = (result * gate_scale).astype(BF16)
        for j in range(EXP_FF):
            downs[j][:, here] = result[j * CAP_FF : (j + 1) * CAP_FF]

    full_rows = wide // step

    @pl.loop(0, full_rows)
    def _(i):
        backward(pl.multiple_of(i * step, step), step)

    if wide % step:
        backward(full_rows * step, wide % step)
    ext = hid[:, width:wide]
    low_ext = (cot[:, width:].astype(F32) * gate_scale).astype(BF16)
    for n, low_rows in enumerate((ext, ext, low_ext)):
        adapt[n][...] = lax.dot_general(
            low_rows,
            act[:, n * units : (n + 1) * units],
            (((0,), (0,)), ((), ())),
            preferred_element_type=F32,
        ).astype(BF16)
    for copy in traded:
        copy.wait()


def feed_forward(hids, cots, inners, lasts, rights):
    parts = len(inners)
    depth, units = lasts[1].shape
    triple = 3 * units
    width = depth * parts
    remotes = (EXP_FF - 1) * (width // (4 * LANES) + 1)
    rows = EXP_FF * CAP_FF
    hbm = pl.BlockSpec(memory_space=pl.ANY)
    vmem = pl.BlockSpec(memory_space=pltpu.VMEM)
    wide = width + LANES
    return pl.pallas_call(
        functools.partial(ffn_kernel, parts, depth, width, units),
        out_shape=[jax.ShapeDtypeStruct((CAP_FF, wide + LANES), BF16)] * EXP_FF
        + [jax.ShapeDtypeStruct((CAP_FF, wide), BF16)] * EXP_FF
        + [jax.ShapeDtypeStruct((LANES, units), BF16)] * 3,
        in_specs=[hbm] * (2 * EXP_FF + 2 * parts + 2),
        out_specs=[vmem] + [hbm] * (EXP_FF - 1) + [vmem] * (EXP_FF + 3),
        scratch_shapes=[
            pltpu.VMEM((rows, wide + LANES), BF16),
            pltpu.VMEM((rows, wide), BF16),
            pltpu.VMEM((wide, triple), BF16),
            pltpu.VMEM((rows, triple), BF16),
            pltpu.VMEM((rows, 1), F32),
            pltpu.VMEM((EXP_FF - 1, CAP_FF, wide + LANES), BF16),
            pltpu.SemaphoreType.DMA((3 * EXP_FF + 2 + 2 * parts,)),
            pltpu.SemaphoreType.DMA((remotes,)),
            pltpu.SemaphoreType.DMA((remotes,)),
        ],
        compiler_params=pltpu.CompilerParams(
            collective_id=2, has_side_effects=True, vmem_limit_bytes=62 * 2**20
        ),
    )(*hids, *cots, *inners, *lasts, *rights)


def on_device(
    inputs,
    cotangent,
    lengths,
    adapter_pick,
    attn_route,
    ffn_route,
    norm_one,
    norm_two,
    router_attn,
    router_ffn,
    kv_weight,
    query_weight,
    out_weight,
    inner_weight,
    down_weight,
    query_left,
    query_right,
    kv_left,
    kv_right,
    out_left,
    out_right,
    inner_left,
    inner_right,
    down_left,
    down_right,
):
    count = inputs.shape[0]
    rows_axis = lax.axis_size("row")
    replicas = rows_axis // EXP_FF
    units = inner_weight.shape[3]
    cosine, sine = tables(count, HEAD_DIM)
    turns = (
        jnp.concatenate([cosine, cosine], axis=1),
        jnp.concatenate([-sine, sine], axis=1),
    )

    cols = lax.axis_size("col")
    padding = -units % LANES

    def padded(value):
        if not padding:
            return value
        return jnp.pad(value, [(0, 0)] * (value.ndim - 1) + [(0, padding)])

    down_flat = padded(down_weight)

    lefts_own = [
        value.swapaxes(1, 2)
        for value in (query_left, kv_left, out_left, inner_left, down_left)
    ]
    (
        inner_flat,
        inner_right_flat,
        rights,
        *outs,
    ) = front(
        [
            lengths,
            adapter_pick,
            attn_route.T,
            ffn_route.T,
            cotangent,
            norm_one[None, :],
            router_attn.T,
            *turns,
            query_right,
            kv_right,
            out_right,
        ],
        lefts_own,
        inputs,
        [kv_weight, query_weight, out_weight],
        padded(inner_weight),
        padded(inner_right).reshape(ADAPT * RANK, 2, units + padding),
        down_flat,
        rows_axis,
        cols,
        replicas,
    )
    early = outs[:EARLY]
    (
        kv_full,
        query_full,
        out_full,
        *cot_rows,
        hidden_one,
        lefts,
        stat_attn,
        low_in,
        keys,
        values,
        queries,
        attended,
        probability,
        attended_rows,
        low_rows,
        out_rows,
        picks_attn,
        picks_ffn,
        ranks,
        gate_rows,
        picks,
    ) = outs[EARLY:]
    picks = picks[:, 0, 0].astype(jnp.int32)
    ffn_right = [inner_right_flat, padded(down_right).reshape(ADAPT * RANK, units + padding)]

    *outs, hidden_two, middle, stat_ffn, totals_attn = middle_forward(
        adapter_pick,
        norm_two[None, :],
        router_ffn.T,
        stat_attn,
        low_rows,
        low_in,
        [out_rows, picks_attn, picks_ffn, lefts, inputs],
        [inner_flat, down_flat],
        early,
        rows_axis,
        cols,
        replicas,
    )
    inners = [inner_flat, *outs[: rows_axis - 1]]
    outs = outs[rows_axis - 1 :]
    lasts = [down_flat]
    for m in range(1, rows_axis):
        if m % replicas == 0 and m <= EARLY * replicas:
            lasts.append(early[m // replicas - 1])
        else:
            lasts.append(outs[0])
            outs = outs[1:]
    hidden_in = outs
    results = feed_forward(hidden_in, cot_rows, inners, lasts, ffn_right)
    grad_middle, grad_full, totals, branch_ffn, low_down_part = middle_back(
        results[:EXP_FF],
        results[EXP_FF : 2 * EXP_FF],
        adapter_pick,
        norm_two[None, :],
        router_ffn.T,
        stat_ffn,
        [picks_ffn, lefts, hidden_two, middle, cotangent],
        cols,
        replicas,
    )
    rights_ffn = lax.optimization_barrier((*results[2 * EXP_FF :], totals))[:3]
    rights_ffn = lax.optimization_barrier(lax.psum(rights_ffn, "row"))
    rights_ffn = [
        value[:, :units].reshape(ADAPT, RANK, units).astype(F32) for value in rights_ffn
    ]

    output, grad_inputs, *grads = tail(
        [
            picks,
            norm_one[None, :],
            router_attn.T,
            stat_attn,
            *turns,
            rights,
            ranks,
            gate_rows,
            totals_attn,
            totals,
            low_down_part,
        ],
        [
            grad_full,
            picks_attn,
            attended_rows,
            queries,
            keys,
            values,
            probability,
            attended,
            lefts,
            hidden_one,
            hidden_two,
            grad_middle,
            middle,
            cotangent,
            inputs,
        ],
        branch_ffn,
        [out_full, query_full, kv_full],
        rows_axis,
        cols,
    )
    lefts_back = [grad.swapaxes(1, 2) for grad in grads[:5]]
    rights_back = grads[5:]
    return (
        output,
        grad_inputs,
        lefts_back[0],
        rights_back[0],
        lefts_back[1],
        jnp.stack(rights_back[1:3], axis=2),
        lefts_back[2],
        rights_back[3],
        lefts_back[3],
        jnp.stack(rights_ffn[:2], axis=2),
        lefts_back[4],
        rights_ffn[2],
    )


def solution(mesh):
    placed = (
        P("row", "col"),
        P("row", "col"),
        P("row"),
        P("row"),
        P("row", None),
        P("row", None),
        P(),
        P(),
        P(),
        P(),
        P(None, "row", "col"),
        P(None, "row", "col"),
        P(None, "row", "col"),
        P(None, "row", None, "col"),
        P(None, "row", "col"),
        P(None, "row", None),
        P(None, None, "col"),
        P(None, "row", None),
        P(None, None, None, "col"),
        P(None, "row", None),
        P(None, None, "col"),
        P(None, "row", None),
        P(None, None, None, "col"),
        P(None, "row", None),
        P(None, None, "col"),
    )
    return jax.shard_map(
        on_device,
        mesh=mesh,
        in_specs=placed,
        out_specs=(
            P("row", "col"),
            P("row", "col"),
            P(None, "row", None),
            P(None, None, "col"),
            P(None, "row", None),
            P(None, None, None, "col"),
            P(None, "row", None),
            P(None, None, "col"),
            P(None, "row", None),
            P(None, None, None, "col"),
            P(None, "row", None),
            P(None, None, "col"),
        ),
        check_vma=False,
    )
```

```python
import functools

import jax
import jax.numpy as jnp
from jax import lax
from jax.experimental import pallas as pl
from jax.experimental.pallas import tpu as pltpu
from jax.sharding import PartitionSpec as P

HEAD_DIM = 128
EXP_ATT = 8
EXP_FF = 4
TOPK = 2
ADAPT = 8
RANK = 16
CAP_ATT = 80
CAP_FF = 160
EPSILON = 1e-06
ROPE_BASE = 10000.0
HIGHEST = lax.Precision.HIGHEST
F32 = jnp.float32
BF16 = jnp.bfloat16
LANES = 128
EARLY = 2


def tables(count, head_width):
    position = jnp.arange(count).astype(F32)
    frequency = ROPE_BASE ** (-jnp.arange(head_width // 2).astype(F32) * 2.0 / head_width)
    angle = position[:, None] * frequency[None, :]
    return (jnp.cos(angle), jnp.sin(angle))


def opposite(axis, offset):
    index = jnp.bitwise_xor(lax.axis_index(axis), offset)
    if axis == "row":
        return (index, lax.axis_index("col"))
    return (lax.axis_index("row"), index)


def greet(partners):
    barrier = pltpu.get_barrier_semaphore()
    for partner in partners:
        pl.semaphore_signal(
            barrier, inc=1, device_id=partner, device_id_type=pl.DeviceIdType.MESH
        )
    pl.semaphore_wait(barrier, len(partners))


def split(value):
    high = value.astype(BF16).astype(F32)
    return high, value - high


def pack(columns, lanes):
    lane = lax.broadcasted_iota(jnp.int32, (columns[0].shape[0], LANES), 1)
    result = jnp.zeros((columns[0].shape[0], LANES), F32)
    for column, n in zip(columns, lanes):
        result = jnp.where(lane == n, column, result)
    return result


def route_term(stat, grads, router, start, size):
    gates = [stat[:, k : k + 1] for k in range(TOPK)]
    mean = gates[0] * grads[0] + gates[1] * grads[1]
    product = 0.0
    term = 0.0
    weights = [gates[k] * (grads[k] - mean) for k in range(TOPK)]
    for k in range(TOPK):
        product += weights[k] * stat[:, 2 + k : 3 + k]
    for e in range(router.shape[0]):
        weight = 0.0
        for k in range(TOPK):
            weight += jnp.where(stat[:, 5 + k : 6 + k] == float(e), weights[k], 0.0)
        term += weight * router[e : e + 1, pl.ds(start, size)].astype(F32)
    return term, product


def fetch(sources, targets, sems):
    copies = []
    for n, (source, target) in enumerate(zip(sources, targets)):
        copies.append(pltpu.make_async_copy(source, target, sems.at[n]))
        copies[-1].start()
    return copies


def remote(source, target, send, recv, n, device):
    copy = pltpu.make_async_remote_copy(
        src_ref=source,
        dst_ref=target,
        send_sem=send.at[n],
        recv_sem=recv.at[n],
        device_id=device,
        device_id_type=pl.DeviceIdType.MESH,
    )
    copy.start()
    return copy


def dispatch_matrices(route, flip, experts, capacity):
    route = [column.astype(jnp.int32) for column in route]
    count = route[0].shape[0]
    lane = lax.broadcasted_iota(jnp.int32, (count, LANES), 1)
    chosen = [(route[k] == lane).astype(F32) for k in range(TOPK)]
    place = lax.broadcasted_iota(jnp.int32, (count, count), 0)
    other = lax.broadcasted_iota(jnp.int32, (count, count), 1)
    before = (other < place).astype(F32).astype(BF16)
    earlier = jnp.dot(
        before, (chosen[0] + chosen[1]).astype(BF16), preferred_element_type=F32
    )
    rows = lax.broadcasted_iota(jnp.int32, (count, experts * capacity), 1)
    results = []
    for k in range(TOPK):
        position = jnp.sum(earlier * chosen[k], axis=1, keepdims=True).astype(jnp.int32)
        mine = jnp.bitwise_xor(route[k], flip) * capacity + position
        results.append((rows == mine).astype(F32).astype(BF16))
    return results


def turn(value, cosine, sine):
    half = HEAD_DIM // 2
    heads = []
    for h in range(value.shape[1] // HEAD_DIM):
        head = value[:, h * HEAD_DIM : (h + 1) * HEAD_DIM]
        heads.append(head * cosine + pltpu.roll(head, half, axis=1) * sine)
    return jnp.concatenate(heads, axis=1)


def scores_of(stat_route, logits, experts):
    chosen = []
    for k in range(TOPK):
        score = 0.0
        for e in range(experts):
            score += jnp.where(stat_route[k] == float(e), logits[:, e : e + 1], 0.0)
        chosen.append(score)
    top = jnp.maximum(chosen[0], chosen[1])
    powers = [jnp.exp(score - top) for score in chosen]
    return chosen, [power / (powers[0] + powers[1]) for power in powers]


def front_kernel(parts, cols, replicas, *refs):
    lengths, pick, routes_attn, routes_ffn, cot, norm, router, cosine, sine = refs[:9]
    query_right, kv_right, out_right = refs[9:12]
    left_refs = refs[12:17]
    tokens = refs[17]
    blocks = refs[18:21]
    pairs, pairs_right, downs = refs[21:24]
    outs = refs[24:]
    flat, flat_right, rights = outs[:3]
    early = outs[3 : 3 + EARLY]
    outs = outs[3 + EARLY :]
    wholes = outs[:3]
    cot_wholes = outs[3 : 3 + EXP_FF]
    (
        hidden,
        lefts,
        stat,
        low_in,
        keys,
        values,
        queries,
        attended,
        probability,
        att_rows,
        low_rows,
        out_rows,
        picks_attn,
        picks_ffn,
        ranks,
        gate_rows,
        picks,
    ) = outs[3 + EXP_FF : 20 + EXP_FF]
    (
        x_all,
        own_rows,
        landed,
        hidden_rows,
        buffer,
        query_rows,
        pick_out,
        lefts_out,
        pair_in,
        pair_out,
        send,
        recv,
        local,
        load,
    ) = outs[20 + EXP_FF :]
    row = lax.axis_index("row")
    col = lax.axis_index("col")
    depth = blocks[0].shape[1]
    count, wide = tokens.shape
    width = hidden.shape[1]
    head_width = keys.shape[1]
    heads = head_width // HEAD_DIM
    across = [None] + [opposite("row", m) for m in range(1, parts)]
    along = [opposite("col", i) for i in range(1, cols)]
    greet(across[1:] + along)
    started, kept = [], []
    received = set()
    here = pl.ds(pl.multiple_of(col * wide, wide), wide)
    own = pl.ds(pl.multiple_of(row * depth, depth), depth)

    def send_to(source, target, device):
        copy = remote(source, target, send, recv, len(started), device)
        started.append(copy)
        return copy

    def arrive(copy):
        copy.wait_recv()
        received.add(id(copy))

    def keep(source, target):
        copy = pltpu.make_async_copy(source, target, local.at[len(kept)])
        copy.start()
        kept.append(copy)
        return copy

    pair = 2
    chunks = [
        (a, start) for a in range(3) for start in range(0, blocks[a].shape[0], pair)
    ]

    def place(n, offset, item=None):
        array, start = chunks[n]
        owner = jnp.bitwise_xor(row, offset)
        owner_rows = pl.ds(pl.multiple_of(owner * depth, depth), depth)
        if item is None:
            return wholes[array].at[pl.ds(start, pair), owner_rows]
        return wholes[array].at[start + item, owner_rows]

    first, direct, relayed, beside = {}, {}, {}, {}

    def push_own(n):
        if n >= len(chunks):
            return
        array, start = chunks[n]
        source = blocks[array].at[pl.ds(start, pair)]
        if parts == 8:
            first[n] = [send_to(source, place(n, 0), across[m]) for m in (2, 4)]
            beside[n] = [send_to(source, place(n, 0), across[1])]
        else:
            direct[n] = [send_to(source, place(n, 0), across[m]) for m in range(1, parts)]

    def relay(n):
        if parts == 8:
            for copy in first[n]:
                arrive(copy)
            relayed[n] = [
                send_to(place(n, 2, 0), place(n, 2, 0), across[4]),
                send_to(place(n, 4, 1), place(n, 4, 1), across[2]),
            ]
            for offset in (2, 4):
                beside[n].append(send_to(place(n, offset), place(n, offset), across[1]))

    def finish(n):
        if parts == 8:
            for copy in relayed[n]:
                arrive(copy)
            beside[n].append(send_to(place(n, 6), place(n, 6), across[1]))
            for copy in beside[n]:
                arrive(copy)
        else:
            for copy in direct[n]:
                arrive(copy)

    token_copies = [send_to(tokens, x_all.at[:, here], device) for device in along]
    token_kept = keep(tokens, x_all.at[:, here])
    block_kept = [keep(blocks[a], wholes[a].at[:, own]) for a in range(3)]
    pick_out[...] = jnp.full(pick_out.shape, 1.0, F32) * pick[0].astype(F32)
    picks[0] = pick_out[...]
    pick_copies = [
        send_to(pick_out, picks.at[m], across[m]) for m in range(1, parts)
    ]
    window, behind = 9, 5
    for n in range(window):
        push_own(n)

    table = jnp.concatenate(
        [
            routes_attn[...].astype(F32),
            routes_ffn[...].astype(F32),
            jnp.zeros((8 - 2 * TOPK, count), F32),
        ]
    )
    same = lax.broadcasted_iota(jnp.int32, (8, LANES), 0) == lax.broadcasted_iota(
        jnp.int32, (8, LANES), 1
    )
    table = lax.dot_general(
        table.astype(BF16),
        same.astype(F32).astype(BF16),
        (((0,), (0,)), ((), ())),
        preferred_element_type=F32,
    )
    route_attn = [table[:, k : k + 1] for k in range(TOPK)]
    route_ffn = [table[:, TOPK + k : TOPK + k + 1] for k in range(TOPK)]
    chosen_adapter = pick[0]
    rights[:RANK] = query_right[chosen_adapter]
    pair_right = kv_right[chosen_adapter].reshape(RANK, 2 * head_width)
    rights[RANK : 2 * RANK] = pair_right[:, :head_width]
    rights[2 * RANK : 3 * RANK] = pair_right[:, head_width:]
    rights[3 * RANK :] = out_right[chosen_adapter]

    position = lax.broadcasted_iota(jnp.int32, (count, 1), 0)
    valid = position < lengths[0]
    matrices = dispatch_matrices(route_ffn, row // replicas, EXP_FF, CAP_FF)
    for k in range(TOPK):
        picks_ffn[k] = matrices[k]
    masked = jnp.where(valid, cot[...].astype(F32), 0.0).astype(BF16)

    def rows_of(matrix, value):
        return lax.dot_general(
            matrix, value, (((0,), (0,)), ((), ())), preferred_element_type=F32
        )

    def times(left, right):
        return lax.dot_general(
            left, right, (((1,), (1,)), ((), ())), preferred_element_type=F32
        )

    dispatched = rows_of(matrices[0] + matrices[1], masked).astype(BF16)
    for j in range(EXP_FF):
        own_rows[j] = dispatched[j * CAP_FF : (j + 1) * CAP_FF]
    traded = [
        send_to(own_rows.at[j], landed.at[j - 1], across[j * replicas])
        for j in range(1, EXP_FF)
    ]
    attn = dispatch_matrices(route_attn, 0, EXP_ATT, CAP_ATT)
    for k in range(TOPK):
        picks_attn[k] = attn[k]
    attn_any = attn[0] + attn[1]
    picks_attn[TOPK] = attn_any

    left_copies = []
    for m in range(parts):
        if m:
            arrive(pick_copies[m - 1])
        theirs = picks[m, 0:1, 0:1]
        for p in range(5):
            value = jnp.zeros((RANK, depth), F32)
            for a in range(ADAPT):
                value += jnp.where(theirs == float(a), left_refs[p][a].astype(F32), 0.0)
            lefts_out[m, p * RANK : (p + 1) * RANK] = value.astype(BF16)
        if m:
            left_copies.append(send_to(lefts_out.at[m], lefts.at[:, own], across[m]))
        else:
            lefts[:, own] = lefts_out[0]
    for j in range(EXP_FF):
        if j:
            arrive(traded[j - 1])
            source = landed.at[j - 1]
        else:
            source = own_rows.at[0]
        keep(source, cot_wholes[j].at[:, here])
        for device in along:
            send_to(source, cot_wholes[j].at[:, here], device)
    relay(0)
    push_own(window)

    for copy in token_copies:
        arrive(copy)
    token_kept.wait()
    square = jnp.zeros((count, 1), F32)
    for q in range(cols):
        value = x_all[:, q * wide : (q + 1) * wide].astype(F32)
        square += jnp.sum(value * value, axis=1, keepdims=True)
    scale = lax.rsqrt(square * (1.0 / width) + EPSILON)
    for q in range(cols):
        span = slice(q * wide, (q + 1) * wide)
        value = x_all[:, span].astype(F32)
        hidden[:, span] = (value * scale * norm[:, span]).astype(BF16)
    for copy in left_copies:
        arrive(copy)
    relay(1)
    push_own(window + 1)
    logits = times(hidden[...], router[...])
    chosen, gates = scores_of(route_attn, logits, EXP_ATT)
    columns = [*gates, *chosen, scale, *route_attn, valid.astype(F32), *route_ffn]
    stat[...] = pack(columns, range(10))
    rank_both = times(hidden[...], lefts[: 2 * RANK])
    ranks[...] = rank_both
    rank_query = rank_both[:, :RANK].astype(BF16)
    rank_kv = rank_both[:, RANK:].astype(BF16)
    low_down = times(masked, lefts[4 * RANK : 5 * RANK, here])
    low_in[...] = jnp.concatenate(
        [
            jnp.zeros((count, 2 * RANK), F32),
            low_down,
            jnp.zeros((count, LANES - 3 * RANK), F32),
        ],
        axis=1,
    )
    gate_wide = 0.0
    for k in range(TOPK):
        columns = pack([*split(gates[k])], range(2)).astype(BF16)
        gate_wide += rows_of(attn[k], columns)
    gate_row = gate_wide[:, 0:1] + gate_wide[:, 1:2]
    gate_rows[...] = gate_row
    rank_rows = rows_of(attn_any, rank_query).astype(BF16)
    for q in range(cols):
        span = slice(q * wide, (q + 1) * wide)
        hidden_rows[:, span] = rows_of(attn_any, hidden[:, span]).astype(BF16)

    def attend():
        value = query_rows[...]
        high = value.astype(BF16)
        low = (value - high.astype(F32)).astype(BF16)
        for k in range(TOPK):
            query = jnp.dot(attn[k], high, preferred_element_type=F32) + jnp.dot(
                attn[k], low, preferred_element_type=F32
            )
            queries[k] = turn(query, cosine[...], sine[...]).astype(BF16)
        other = lax.broadcasted_iota(jnp.int32, (count, count), 1)
        place_row = lax.broadcasted_iota(jnp.int32, (count, count), 0)
        allowed = (other <= place_row) & (other < lengths[0])
        for h in range(heads):
            span = slice(h * HEAD_DIM, (h + 1) * HEAD_DIM)
            for k in range(TOPK):
                scores = times(queries[k, :, span], keys[:, span]) * HEAD_DIM ** (-0.5)
                scores = jnp.where(allowed, scores, -1e30)
                power = jnp.exp(scores - jnp.max(scores, axis=1, keepdims=True))
                probs = power / jnp.sum(power, axis=1, keepdims=True)
                probability[h, k] = probs
                attended[k, :, span] = jnp.dot(
                    probs.astype(BF16), values[:, span], preferred_element_type=F32
                ).astype(BF16)
        rows = rows_of(attn[0], attended[0]) + rows_of(attn[1], attended[1])
        att_rows[...] = rows.astype(BF16)
        low = times(att_rows[...], rights[3 * RANK :]) * gate_row
        low_rows[...] = jnp.concatenate(
            [
                jnp.zeros((low.shape[0], RANK), F32),
                low,
                jnp.zeros((low.shape[0], LANES - 2 * RANK), F32),
            ],
            axis=1,
        ).astype(BF16)

    def compute(n):
        array, start = chunks[n]
        weight = buffer.at[n % 2]
        if array == 0:
            key = jnp.dot(hidden[...], weight[0], preferred_element_type=F32) + jnp.dot(
                rank_kv, rights[RANK : 2 * RANK], preferred_element_type=F32
            )
            keys[...] = turn(key, cosine[...], sine[...]).astype(BF16)
            value = jnp.dot(hidden[...], weight[1], preferred_element_type=F32) + jnp.dot(
                rank_kv, rights[2 * RANK : 3 * RANK], preferred_element_type=F32
            )
            values[...] = value.astype(BF16)
            return
        for item in range(pair):
            e = start + item
            span = slice(e * CAP_ATT, (e + 1) * CAP_ATT)
            if array == 1:
                query_rows[span] = jnp.dot(
                    hidden_rows[span], weight[item], preferred_element_type=F32
                ) + jnp.dot(rank_rows[span], rights[:RANK], preferred_element_type=F32)
            else:
                out_rows[span] = (times(att_rows[span], weight[item]) * gate_row[span]).astype(
                    BF16
                )
        if array == 1 and start + pair == EXP_ATT:
            attend()

    def flatten(e):
        copy = pltpu.make_async_copy(pairs.at[e], pair_in, load.at[2])
        copy.start()
        copy.wait()
        step = 64

        @pl.loop(0, pair_in.shape[0] // step)
        def _(i):
            span = pl.ds(pl.multiple_of(i * step, step), step)
            pair_out[span] = pair_in[span].reshape(step, pair_out.shape[1])

        copy = pltpu.make_async_copy(pair_out, flat.at[e], load.at[3])
        copy.start()
        copy.wait()

    near = pair_in.at[pl.ds(0, pairs_right.shape[0])]
    copy = pltpu.make_async_copy(pairs_right, near, load.at[2])
    copy.start()
    copy.wait()
    step = 64
    pair_rows = pairs_right.shape[0]

    @pl.loop(0, pair_rows // step)
    def _(i):
        span = pl.ds(pl.multiple_of(i * step, step), step)
        pair_out[span] = pair_in[span].reshape(step, pair_out.shape[1])

    copy = pltpu.make_async_copy(pair_out.at[pl.ds(0, pair_rows)], flat_right, load.at[3])
    copy.start()
    copy.wait()
    loads = {}
    total = len(chunks)
    for n in range(2, total + behind + 1):
        if n < total:
            relay(n)
            push_own(n + window)
        if n - 2 < EXP_FF:
            flatten(n - 2)
        if n == total - 1:
            for j in range(1, EARLY + 1):
                which = jnp.bitwise_xor(row // replicas, j)
                send_to(downs.at[which], early[j - 1], across[j * replicas])
        for m in range(n - behind + 1) if n == 2 else [n - behind]:
            if 0 <= m < total:
                if m == 0:
                    for copy in block_kept:
                        copy.wait()
                finish(m)
                loads[m] = pltpu.make_async_copy(
                    place_whole(wholes, chunks[m], pair), buffer.at[m % 2], load.at[m % 2]
                )
                loads[m].start()
            if 0 <= m - 1 < total:
                loads[m - 1].wait()
                compute(m - 1)
    for copy in started:
        if id(copy) not in received:
            copy.wait_recv()
    for copy in started:
        copy.wait_send()
    for copy in kept[1 + len(block_kept) :]:
        copy.wait()


def place_whole(wholes, chunk, pair):
    array, start = chunk
    return wholes[array].at[pl.ds(start, pair)]


def front(smalls, lefts, tokens, blocks, pairs, pairs_right, downs, parts, cols, replicas):
    hbm = pl.BlockSpec(memory_space=pl.ANY)
    vmem = pl.BlockSpec(memory_space=pltpu.VMEM)
    smem = pl.BlockSpec(memory_space=pltpu.SMEM)
    count, wide = tokens.shape
    width = wide * cols
    depth, head_width = blocks[0].shape[1:]
    heads = head_width // HEAD_DIM
    rows = EXP_ATT * CAP_ATT
    rows_ffn = EXP_FF * CAP_FF
    shape = jax.ShapeDtypeStruct
    flat = (pairs.shape[0], pairs.shape[1], 2 * pairs.shape[3])
    n_chunks = sum(block.shape[0] for block in blocks) // 2
    per_chunk = 8 if parts == 8 else parts - 1
    remotes = (
        n_chunks * per_chunk + (cols - 1) * (1 + EXP_FF) + EXP_FF - 1 + 2 * (parts - 1) + EARLY
    )
    return pl.pallas_call(
        functools.partial(front_kernel, parts, cols, replicas),
        out_shape=[
            shape(flat, BF16),
            shape((pairs_right.shape[0], flat[2]), BF16),
            shape((4 * RANK, head_width), BF16),
        ]
        + [shape(downs.shape[1:], BF16)] * EARLY
        + [shape((b.shape[0], width, head_width), BF16) for b in blocks]
        + [shape((CAP_FF, width), BF16)] * EXP_FF
        + [
            shape((count, width), BF16),
            shape((5 * RANK, width), BF16),
            shape((count, LANES), F32),
            shape((count, LANES), F32),
            shape((count, head_width), BF16),
            shape((count, head_width), BF16),
            shape((TOPK, count, head_width), BF16),
            shape((TOPK, count, head_width), BF16),
            shape((heads, TOPK, count, count), F32),
            shape((rows, head_width), BF16),
            shape((rows, LANES), BF16),
            shape((rows, width), BF16),
            shape((TOPK + 1, count, rows), BF16),
            shape((TOPK, count, rows_ffn), BF16),
            shape((count, 2 * RANK), F32),
            shape((rows, 1), F32),
            shape((parts, 8, LANES), F32),
        ],
        in_specs=[smem] * 2 + [vmem] * 15 + [hbm] * 7,
        out_specs=[hbm, hbm, vmem] + [hbm] * (EARLY + 3 + EXP_FF) + [vmem] * 17,
        scratch_shapes=[
            pltpu.VMEM((count, width), BF16),
            pltpu.VMEM((EXP_FF, CAP_FF, wide), BF16),
            pltpu.VMEM((EXP_FF - 1, CAP_FF, wide), BF16),
            pltpu.VMEM((rows, width), BF16),
            pltpu.VMEM((2, 2, width, head_width), BF16),
            pltpu.VMEM((rows, head_width), F32),
            pltpu.VMEM((8, LANES), F32),
            pltpu.VMEM((parts, 5 * RANK, depth), BF16),
            pltpu.VMEM(pairs.shape[1:], BF16),
            pltpu.VMEM(flat[1:], BF16),
            pltpu.SemaphoreType.DMA((remotes,)),
            pltpu.SemaphoreType.DMA((remotes,)),
            pltpu.SemaphoreType.DMA((4 + EXP_FF,)),
            pltpu.SemaphoreType.DMA((4,)),
        ],
        compiler_params=pltpu.CompilerParams(
            collective_id=1, has_side_effects=True, vmem_limit_bytes=62 * 2**20
        ),
    )(*smalls, *lefts, tokens, *blocks, pairs, pairs_right, downs)


def middle_back_kernel(cols, replicas, *refs):
    blocks, downs = refs[:EXP_FF], refs[EXP_FF : 2 * EXP_FF]
    adapter, norm, router, stat = refs[2 * EXP_FF : 2 * EXP_FF + 4]
    sources = refs[2 * EXP_FF + 4 : 2 * EXP_FF + 9]
    grad_middle, grad_whole, totals, branch, low_down = refs[2 * EXP_FF + 9 : 2 * EXP_FF + 14]
    scratch = refs[2 * EXP_FF + 14 :]
    picks_ffn, lefts, hidden, middle, cot = scratch[:5]
    rows, down_rows, exact_part, parts, extra, parts_in, extra_in, low, send, recv, local = (
        scratch[5:]
    )
    col = lax.axis_index("col")
    count, wide = middle.shape
    width = hidden.shape[1]
    across = [opposite("row", j * replicas) for j in range(1, EXP_FF)]
    along = [opposite("col", i) for i in range(1, cols)]
    greet(across + along)
    near = fetch(
        [*blocks, downs[0], *sources],
        [
            *(rows.at[pl.ds(j * CAP_FF, CAP_FF)] for j in range(EXP_FF)),
            down_rows.at[pl.ds(0, CAP_FF)],
            *scratch[:5],
        ],
        local,
    )
    base = 0
    down_copies = [
        remote(
            downs[j],
            down_rows.at[pl.ds(j * CAP_FF, CAP_FF)],
            send,
            recv,
            base + j - 1,
            across[j - 1],
        )
        for j in range(1, EXP_FF)
    ]
    for copy in near:
        copy.wait()
    picks = [picks_ffn[0], picks_ffn[1]]
    any_pick = picks[0] + picks[1]

    def back(pick, source, start, size):
        return jnp.dot(pick, source[:, start : start + size], preferred_element_type=F32)

    sub = lax.broadcasted_iota(jnp.int32, (LANES, LANES), 0)
    lane = lax.broadcasted_iota(jnp.int32, (LANES, LANES), 1)
    mine = lax.broadcasted_iota(jnp.int32, (count, LANES), 1) // RANK == adapter[0]
    place_rank = (lane == RANK + sub % RANK).astype(F32).astype(BF16)

    def own_rank(value):
        value = jnp.where(mine, value, 0.0).astype(BF16)
        return jnp.dot(value, place_rank, preferred_element_type=F32)

    gate_grads = []
    for k in range(TOPK):
        pair = back(picks[k], rows, width + LANES, LANES)
        gate_grads.append(pair[:, 0:1] + pair[:, 1:2])
    rank = own_rank(back(any_pick, rows, width, LANES))
    rank_low = rank[:, RANK : 2 * RANK].astype(BF16)
    product = jnp.zeros((count, 1), F32)
    for q in range(cols):
        here = slice(q * wide, (q + 1) * wide)
        part = back(any_pick, rows, q * wide, wide) + jnp.dot(
            rank_low, lefts[3 * RANK : 4 * RANK, here], preferred_element_type=F32
        )
        product += jnp.sum(part * hidden[:, here].astype(F32), axis=1, keepdims=True)
        exact_part[q] = part
        parts[q] = part.astype(BF16)
    columns = [*split(gate_grads[0]), *split(gate_grads[1]), *split(product)]
    small = pack(columns, range(6)) + rank
    extra[...] = small.astype(BF16)
    base += EXP_FF - 1
    arrivals = []
    for i in range(1, cols):
        target = jnp.bitwise_xor(col, i)
        n = base + 2 * (i - 1)
        arrivals.append(remote(extra, extra_in.at[i - 1], send, recv, n + 1, along[i - 1]))
        arrivals.append(
            remote(parts.at[target], parts_in.at[i - 1], send, recv, n, along[i - 1])
        )
    for copy in arrivals:
        copy.wait_recv()
    grad = exact_part[col]
    total = small
    for i in range(cols - 1):
        grad += parts_in[i].astype(F32)
        total += extra_in[i].astype(F32)
    totals[...] = total
    gate_grads = [total[:, 0:1] + total[:, 1:2], total[:, 2:3] + total[:, 3:4]]
    first = pl.multiple_of(col * wide, wide)
    term, more = route_term(stat, gate_grads, router, first, wide)
    inner = total[:, 4:5] + total[:, 5:6] + more
    scaled = (grad + term) * norm[:, pl.ds(first, wide)]
    factor = stat[:, 4:5]
    valid = stat[:, 7:8]
    result = (
        cot[...].astype(F32) * valid
        + factor * scaled
        - middle[...] * (factor * factor * inner * (1.0 / width))
    )
    grad_middle[...] = result
    low[...] = result.astype(BF16)
    here = pl.ds(first, wide)
    kept = pltpu.make_async_copy(low, grad_whole.at[:, here], local.at[10])
    kept.start()
    base += 2 * (cols - 1)
    last = [
        remote(low, grad_whole.at[:, here], send, recv, base + i, along[i])
        for i in range(cols - 1)
    ]
    for copy in down_copies:
        copy.wait_recv()
    rank = own_rank(back(any_pick, down_rows, width, LANES))
    rank_low = rank[:, RANK : 2 * RANK].astype(BF16)
    low_down[...] = rank
    for q in range(cols):
        here = slice(q * wide, (q + 1) * wide)
        part = back(any_pick, down_rows, q * wide, wide) + jnp.dot(
            rank_low, lefts[4 * RANK : 5 * RANK, here], preferred_element_type=F32
        )
        branch[:, here] = part.astype(BF16)
    for copy in last:
        copy.wait_recv()
    for copy in down_copies + arrivals + last:
        copy.wait_send()
    kept.wait()


def middle_back(blocks, downs, adapter, norm, router, stat, sources, cols, replicas):
    hbm = pl.BlockSpec(memory_space=pl.ANY)
    vmem = pl.BlockSpec(memory_space=pltpu.VMEM)
    smem = pl.BlockSpec(memory_space=pltpu.SMEM)
    count, wide = sources[-1].shape
    total = EXP_FF - 1 + 3 * (cols - 1)
    rows = EXP_FF * CAP_FF
    return pl.pallas_call(
        functools.partial(middle_back_kernel, cols, replicas),
        out_shape=[
            jax.ShapeDtypeStruct((count, wide), F32),
            jax.ShapeDtypeStruct((count, wide * cols), BF16),
            jax.ShapeDtypeStruct((count, LANES), F32),
            jax.ShapeDtypeStruct((count, wide * cols), BF16),
            jax.ShapeDtypeStruct((count, LANES), F32),
        ],
        in_specs=[hbm] * (2 * EXP_FF) + [smem, vmem, vmem, vmem] + [hbm] * 5,
        out_specs=[vmem, hbm, vmem, vmem, vmem],
        scratch_shapes=[pltpu.VMEM(source.shape, source.dtype) for source in sources]
        + [
            pltpu.VMEM((rows, blocks[0].shape[1]), BF16),
            pltpu.VMEM((rows, downs[0].shape[1]), BF16),
            pltpu.VMEM((cols, count, wide), F32),
            pltpu.VMEM((cols, count, wide), BF16),
            pltpu.VMEM((count, LANES), BF16),
            pltpu.VMEM((cols - 1, count, wide), BF16),
            pltpu.VMEM((cols - 1, count, LANES), BF16),
            pltpu.VMEM((count, wide), BF16),
            pltpu.SemaphoreType.DMA((total,)),
            pltpu.SemaphoreType.DMA((total,)),
            pltpu.SemaphoreType.DMA((11,)),
        ],
        compiler_params=pltpu.CompilerParams(
            collective_id=4, has_side_effects=True, vmem_limit_bytes=62 * 2**20
        ),
    )(*blocks, *downs, adapter, norm, router, stat, *sources)


def tail_kernel(parts_axis, cols, *refs):
    (
        adapters,
        norm,
        router,
        stat,
        cosine,
        sine,
        rights,
        ranks,
        gate_rows,
        totals_attn,
        totals_ffn,
        low_down,
    ) = refs[:12]
    sources = refs[12:27]
    branch, out_whole, query_whole, kv_whole = refs[27:31]
    output, grad_inputs = refs[31:33]
    left_outs = refs[33:38]
    right_outs = refs[38:42]
    (
        grad_whole,
        picks,
        att_rows,
        queries,
        keys,
        values,
        probability,
        attended,
        lefts_whole,
        hidden_one,
        hidden_two,
        grad_middle,
        middle,
        cot,
        tokens,
    ) = refs[42:57]
    (
        cot_own,
        cot_whole,
        branch_in,
        rows,
        grads,
        buffer,
        query_grads,
        key_grad,
        value_grad,
        part,
        parts,
        extra,
        parts_in,
        extra_in,
        right_parts,
        rights_in,
        lefts,
        lefts_in,
        send,
        recv,
        local,
        load,
    ) = refs[57:]
    row = lax.axis_index("row")
    col = lax.axis_index("col")
    count, wide = tokens.shape
    width = hidden_one.shape[1]
    depth = width // parts_axis
    head_width = keys.shape[1]
    heads = head_width // HEAD_DIM
    along = [opposite("col", i) for i in range(1, cols)]
    across = [opposite("row", m) for m in range(1, parts_axis)]
    greet(across + along)
    started = []

    def send_to(source, target, device):
        copy = remote(source, target, send, recv, len(started), device)
        started.append(copy)
        return copy

    pair = 2
    chunks = [
        (whole, start)
        for whole in (out_whole, query_whole, kv_whole)
        for start in range(0, whole.shape[0], pair)
    ]
    loads = []
    for n, (whole, start) in enumerate(chunks):
        loads.append(
            pltpu.make_async_copy(whole.at[pl.ds(start, pair)], buffer.at[n % 2], load.at[n % 2])
        )
    near = fetch(sources, refs[42:57], local)
    loads[0].start()
    loads[1].start()
    first = pl.multiple_of(col * wide, wide)
    here = pl.ds(first, wide)
    valid = stat[:, 7:8]
    branch_copies = []
    for i in range(1, cols):
        target = jnp.bitwise_xor(col, i)
        theirs = pl.ds(pl.multiple_of(target * wide, wide), wide)
        branch_copies.append(send_to(branch.at[:, theirs], branch_in.at[i - 1], along[i - 1]))
    mine = pltpu.make_async_copy(branch.at[:, here], branch_in.at[cols - 1], local.at[15])
    mine.start()
    for copy in near:
        copy.wait()
    cot_own[...] = (cot[...].astype(F32) * valid).astype(BF16)
    cot_whole[:, here] = cot_own[...]
    cot_copies = [send_to(cot_own, cot_whole.at[:, here], device) for device in along]

    def rows_of(matrix, value):
        return lax.dot_general(
            matrix, value, (((0,), (0,)), ((), ())), preferred_element_type=F32
        )

    def times(left, right):
        return lax.dot_general(
            left, right, (((1,), (1,)), ((), ())), preferred_element_type=F32
        )

    def dot(left, right):
        return jnp.dot(left, right, preferred_element_type=F32)

    any_pick = picks[TOPK]
    low_grad = times(grad_whole[...], lefts_whole[2 * RANK : 3 * RANK])
    low_rows = rows_of(any_pick, low_grad.astype(BF16)).astype(BF16)
    for q in range(cols):
        span = slice(q * wide, (q + 1) * wide)
        rows[:, span] = rows_of(any_pick, grad_whole[:, span]).astype(BF16)
    number = 0

    def next_weights():
        nonlocal number
        loads[number].wait()
        return buffer.at[number % 2]

    def done_weights():
        nonlocal number
        if number + 2 < len(chunks):
            loads[number + 2].start()
        number += 1

    for start in range(0, EXP_ATT, pair):
        weight = next_weights()
        for item in range(pair):
            span = slice((start + item) * CAP_ATT, (start + item + 1) * CAP_ATT)
            grads[span] = dot(rows[span], weight[item]) + dot(low_rows[span], rights[3 * RANK :])
        done_weights()
    value = grads[...]
    gate_grad = jnp.sum(att_rows[...].astype(F32) * value, axis=1, keepdims=True)
    gate_pack = pack([*split(gate_grad)], range(2)).astype(BF16)
    gate_grads = []
    gated = (value * gate_rows[...]).astype(BF16)
    right_out = jnp.zeros((RANK, head_width), F32)
    for k in range(TOPK):
        both = dot(picks[k], gate_pack)
        gate_grads.append(both[:, 0:1] + both[:, 1:2])
        query_grads[k] = dot(picks[k], gated).astype(BF16)
        right_out += rows_of((stat[:, k : k + 1] * low_grad).astype(BF16), attended[k])
    scaling = HEAD_DIM ** (-0.5)
    query_sum = []
    for h in range(heads):
        span = slice(h * HEAD_DIM, (h + 1) * HEAD_DIM)
        key_total, value_total, sum_head = 0.0, 0.0, 0.0
        for k in range(TOPK):
            grad_att = query_grads[k, :, span]
            probs = probability[h, k]
            grad_prob = times(grad_att, values[:, span])
            centre = jnp.sum(probs * grad_prob, axis=1, keepdims=True)
            grad_score = (probs * (grad_prob - centre)).astype(BF16)
            value_total += rows_of(probs.astype(BF16), grad_att)
            key_total += rows_of(grad_score, queries[k, :, span])
            grad_query = dot(grad_score, keys[:, span]) * scaling
            turned = turn(grad_query, cosine[...], -sine[...]).astype(BF16)
            query_grads[k, :, span] = turned
            sum_head += turned.astype(F32)
        key_grad[:, span] = turn(key_total * scaling, cosine[...], -sine[...]).astype(BF16)
        value_grad[:, span] = value_total.astype(BF16)
        query_sum.append(sum_head.astype(BF16))
    query_sum = jnp.concatenate(query_sum, axis=1)
    rank_query = ranks[:, :RANK].astype(BF16)
    rank_kv = ranks[:, RANK:].astype(BF16)
    right_values = [
        rows_of(rank_query, query_sum),
        rows_of(rank_kv, key_grad[...]),
        rows_of(rank_kv, value_grad[...]),
        right_out,
    ]
    for p in range(4):
        right_parts[:, p * head_width : (p + 1) * head_width] = right_values[p].astype(BF16)
    right_copies = [
        send_to(right_parts, rights_in.at[m], across[m]) for m in range(parts_axis - 1)
    ]
    grad_rank_query = times(query_sum, rights[:RANK])
    grad_rank_kv = times(key_grad[...], rights[RANK : 2 * RANK]) + times(
        value_grad[...], rights[2 * RANK : 3 * RANK]
    )
    query_rows = (rows_of(picks[0], query_grads[0]) + rows_of(picks[1], query_grads[1])).astype(
        BF16
    )
    for start in range(0, EXP_ATT, pair):
        weight = next_weights()
        for item in range(pair):
            span = slice((start + item) * CAP_ATT, (start + item + 1) * CAP_ATT)
            rows[span] = times(query_rows[span], weight[item]).astype(BF16)
        done_weights()
    weight = next_weights()
    low = jnp.concatenate([grad_rank_query, grad_rank_kv], axis=1).astype(BF16)
    product = jnp.zeros((count, 1), F32)
    for q in range(cols):
        span = slice(q * wide, (q + 1) * wide)
        value = (
            dot(any_pick, rows[:, span])
            + times(key_grad[...], weight[0, span])
            + times(value_grad[...], weight[1, span])
            + dot(low, lefts_whole[: 2 * RANK, span])
        )
        product += jnp.sum(value * hidden_one[:, span].astype(F32), axis=1, keepdims=True)
        part[q] = value
        parts[q] = value.astype(BF16)
    columns = [*split(gate_grads[0]), *split(gate_grads[1]), *split(product)]
    small = pack(columns, range(6)) + jnp.concatenate(
        [
            jnp.zeros((count, RANK), F32),
            grad_rank_query,
            grad_rank_kv,
            low_down[:, RANK : 2 * RANK],
            jnp.zeros((count, LANES - 4 * RANK), F32),
        ],
        axis=1,
    )
    extra[...] = small.astype(BF16)
    extra_copies, part_copies = [], []
    for i in range(1, cols):
        target = jnp.bitwise_xor(col, i)
        extra_copies.append(send_to(extra, extra_in.at[i - 1], along[i - 1]))
        part_copies.append(send_to(parts.at[target], parts_in.at[i - 1], along[i - 1]))
    mine.wait()
    for copy in branch_copies:
        copy.wait_recv()
    result = middle[...]
    for i in range(cols):
        result += branch_in[i].astype(F32)
    output[...] = (result * valid).astype(BF16)
    for copy in cot_copies:
        copy.wait_recv()

    def outer(left, right):
        return rows_of(left, right).astype(BF16)

    whole = outer(totals_attn[...].astype(BF16), grad_whole[...])
    for m in range(parts_axis):
        lefts[m, 2 * RANK : 3 * RANK] = whole[RANK : 2 * RANK, m * depth : (m + 1) * depth]
    whole = outer(totals_ffn[...].astype(BF16), hidden_two[...])
    for m in range(parts_axis):
        lefts[m, 3 * RANK : 4 * RANK] = whole[RANK : 2 * RANK, m * depth : (m + 1) * depth]
    chosen_by = [
        [jnp.where(adapters[m] == a, 1.0, 0.0).astype(F32) for a in range(ADAPT)]
        for m in range(parts_axis)
    ]

    def share(values, target):
        for a in range(ADAPT):
            result = chosen_by[0][a] * values[0]
            for m in range(1, parts_axis):
                result += chosen_by[m][a] * values[m]
            target[a] = result

    for copy in right_copies:
        copy.wait_recv()
    for p in range(4):
        span = slice(p * head_width, (p + 1) * head_width)
        share(
            [right_parts[:, span].astype(F32)]
            + [rights_in[m, :, span].astype(F32) for m in range(parts_axis - 1)],
            right_outs[p],
        )
    total = small
    for i in range(cols - 1):
        extra_copies[i].wait_recv()
        total += extra_in[i].astype(F32)
    low_totals = total.astype(BF16)
    whole = outer(low_totals, hidden_one[...])
    for m in range(parts_axis):
        lefts[m, : 2 * RANK] = whole[RANK : 3 * RANK, m * depth : (m + 1) * depth]
    whole = outer(low_totals, cot_whole[...])
    for m in range(parts_axis):
        lefts[m, 4 * RANK :] = whole[3 * RANK : 4 * RANK, m * depth : (m + 1) * depth]
    left_copies = [
        send_to(lefts.at[jnp.bitwise_xor(row, m)], lefts_in.at[m - 1], across[m - 1])
        for m in range(1, parts_axis)
    ]
    gate_totals = [total[:, 0:1] + total[:, 1:2], total[:, 2:3] + total[:, 3:4]]
    term, more = route_term(stat, gate_totals, router, first, wide)
    inner = total[:, 4:5] + total[:, 5:6] + more
    grad = part[col] + term
    for i in range(cols - 1):
        part_copies[i].wait_recv()
        grad += parts_in[i].astype(F32)
    factor = stat[:, 4:5]
    grad_inputs[...] = (
        grad_middle[...]
        + factor * (grad * norm[:, here])
        - tokens[...].astype(F32) * (factor * factor * inner * (1.0 / width))
    )
    for copy in left_copies:
        copy.wait_recv()
    for p in range(5):
        span = slice(p * RANK, (p + 1) * RANK)
        share(
            [lefts[row, span].astype(F32)]
            + [lefts_in[m, span].astype(F32) for m in range(parts_axis - 1)],
            left_outs[p],
        )
    for copy in started:
        copy.wait_send()


def tail(smalls, sources, branch, wholes, parts_axis, cols):
    hbm = pl.BlockSpec(memory_space=pl.ANY)
    vmem = pl.BlockSpec(memory_space=pltpu.VMEM)
    smem = pl.BlockSpec(memory_space=pltpu.SMEM)
    count, wide = sources[-1].shape
    width = wide * cols
    depth = width // parts_axis
    head_width = wholes[0].shape[2]
    rows = EXP_ATT * CAP_ATT
    shape = jax.ShapeDtypeStruct
    total = 4 * (cols - 1) + 2 * (parts_axis - 1)
    return pl.pallas_call(
        functools.partial(tail_kernel, parts_axis, cols),
        out_shape=[shape((count, wide), BF16), shape((count, wide), F32)]
        + [shape((ADAPT, RANK, depth), F32)] * 5
        + [shape((ADAPT, RANK, head_width), F32)] * 4,
        in_specs=[smem] + [vmem] * 11 + [hbm] * 19,
        out_specs=[vmem] * 11,
        scratch_shapes=[pltpu.VMEM(source.shape, source.dtype) for source in sources]
        + [
            pltpu.VMEM((count, wide), BF16),
            pltpu.VMEM((count, width), BF16),
            pltpu.VMEM((cols, count, wide), BF16),
            pltpu.VMEM((rows, width), BF16),
            pltpu.VMEM((rows, head_width), F32),
            pltpu.VMEM((2, 2, width, head_width), BF16),
            pltpu.VMEM((TOPK, count, head_width), BF16),
            pltpu.VMEM((count, head_width), BF16),
            pltpu.VMEM((count, head_width), BF16),
            pltpu.VMEM((cols, count, wide), F32),
            pltpu.VMEM((cols, count, wide), BF16),
            pltpu.VMEM((count, LANES), BF16),
            pltpu.VMEM((cols - 1, count, wide), BF16),
            pltpu.VMEM((cols - 1, count, LANES), BF16),
            pltpu.VMEM((RANK, 4 * head_width), BF16),
            pltpu.VMEM((parts_axis - 1, RANK, 4 * head_width), BF16),
            pltpu.VMEM((parts_axis, 5 * RANK, depth), BF16),
            pltpu.VMEM((parts_axis - 1, 5 * RANK, depth), BF16),
            pltpu.SemaphoreType.DMA((total,)),
            pltpu.SemaphoreType.DMA((total,)),
            pltpu.SemaphoreType.DMA((16,)),
            pltpu.SemaphoreType.DMA((2,)),
        ],
        compiler_params=pltpu.CompilerParams(
            collective_id=5, has_side_effects=True, vmem_limit_bytes=62 * 2**20
        ),
    )(*smalls, *sources, branch, *wholes)


def middle_kernel(parts_axis, cols, replicas, *refs):
    adapter, norm, router, route, low_rows, low_in = refs[:6]
    sources = refs[6:11]
    weights = refs[11:13]
    early = refs[13 : 13 + EARLY]
    outs = refs[13 + EARLY :]
    chunks = [[None, *outs[: parts_axis - 1]], [None]]
    outs = outs[parts_axis - 1 :]
    for m in range(1, parts_axis):
        if m % replicas == 0 and m <= EARLY * replicas:
            chunks[1].append(early[m // replicas - 1])
        else:
            chunks[1].append(outs[0])
            outs = outs[1:]
    hids = outs[:EXP_FF]
    hidden_out, middle, stat, totals = outs[EXP_FF : EXP_FF + 4]
    scratch = outs[EXP_FF + 4 :]
    out_rows, picks_attn, picks_ffn, lefts, tokens = scratch[:5]
    (
        exact_part,
        parts,
        extra,
        parts_in,
        extra_in,
        square,
        square_in,
        low,
        hidden,
        message,
        send,
        recv,
        local,
    ) = scratch[5:]
    col = lax.axis_index("col")
    count, wide = tokens.shape
    width = hidden.shape[1]
    across = [opposite("row", j * replicas) for j in range(1, EXP_FF)]
    beside = [opposite("row", i) for i in range(1, replicas)]
    along = [opposite("col", i) for i in range(1, cols)]
    greet(across + beside + along)
    near = fetch(sources, scratch[:5], local)
    used = [0]
    started = []

    def send_to(source, target, device):
        copy = remote(source, target, send, recv, used[0], device)
        used[0] += 1
        started.append(copy)
        return copy

    expert = lax.axis_index("row") // replicas
    piece_copies = [
        [
            send_to(weights[n].at[jnp.bitwise_xor(expert, j)], chunks[n][j * replicas], across[j - 1])
            for n in ((0,) if j <= EARLY else (0, 1))
        ]
        for j in range(1, EXP_FF)
    ]
    sibling_copies = [
        send_to(weights[n].at[expert], chunks[n][i], beside[i - 1])
        for i in range(1, replicas)
        for n in (0, 1)
    ]
    for j in range(1, EARLY + 1):
        for i in range(1, replicas):
            m = j * replicas
            sibling_copies.append(send_to(chunks[1][m], chunks[1][m + i], beside[i - 1]))
    for copy in near:
        copy.wait()

    def back(source):
        return jnp.dot(picks_attn[TOPK], source, preferred_element_type=F32)

    def rows_of(matrix, value):
        return lax.dot_general(
            matrix, value, (((0,), (0,)), ((), ())), preferred_element_type=F32
        )

    sub = lax.broadcasted_iota(jnp.int32, (LANES, LANES), 0)
    lane = lax.broadcasted_iota(jnp.int32, (LANES, LANES), 1)
    lanes = lax.broadcasted_iota(jnp.int32, (count, LANES), 1)
    low_out = back(low_rows[...])
    small = low_in[...] + low_out
    low_out = low_out[:, RANK : 2 * RANK].astype(BF16)
    for q in range(cols):
        here = slice(q * wide, (q + 1) * wide)
        part = back(out_rows[:, here]) + jnp.dot(
            low_out, lefts[2 * RANK : 3 * RANK, here], preferred_element_type=F32
        )
        exact_part[q] = part
        parts[q] = part.astype(BF16)
    extra[...] = small.astype(BF16)
    part_copies = []
    extra_copies = []
    for i in range(1, cols):
        target = jnp.bitwise_xor(col, i)
        part_copies.append(send_to(parts.at[target], parts_in.at[i - 1], along[i - 1]))
        extra_copies.append(send_to(extra, extra_in.at[i - 1], along[i - 1]))
    value = tokens[...].astype(F32) + exact_part[col]
    total = small
    for i in range(cols - 1):
        part_copies[i].wait_recv()
        value += parts_in[i].astype(F32)
    middle[...] = value
    square[...] = lax.dot_general(
        jnp.ones((8, wide), F32),
        value * value,
        (((1,), (1,)), ((), ())),
        precision=HIGHEST,
        preferred_element_type=F32,
    )
    square_copies = [
        send_to(square, square_in.at[i], along[i]) for i in range(cols - 1)
    ]
    for i in range(cols - 1):
        extra_copies[i].wait_recv()
        total += extra_in[i].astype(F32)
    totals[...] = total
    squares = square[...]
    for i in range(cols - 1):
        square_copies[i].wait_recv()
        squares += square_in[i]
    squares = lax.dot_general(
        squares,
        jnp.full((8, LANES), 0.125, F32),
        (((0,), (0,)), ((), ())),
        precision=HIGHEST,
        preferred_element_type=F32,
    )
    scale = lax.rsqrt(squares[:, 0:1] * (1.0 / width) + EPSILON)
    first = pl.multiple_of(col * wide, wide)
    here = pl.ds(first, wide)
    low[...] = (value * scale * norm[:, here]).astype(BF16)
    hidden[:, here] = low[...]
    hidden_copies = [send_to(low, hidden.at[:, here], along[i]) for i in range(cols - 1)]
    mine = lanes // RANK == adapter[0]

    def own_adapter(value, start):
        spread = (sub - start == lane % RANK).astype(F32).astype(BF16)
        value = jnp.dot(value.astype(BF16), spread, preferred_element_type=F32)
        return jnp.where(mine, value, 0.0).astype(BF16)

    picks = [picks_ffn[0], picks_ffn[1]]
    any_pick = picks[0] + picks[1]
    message[:, width + 2 * LANES :] = rows_of(any_pick, own_adapter(total, 2 * RANK)).astype(BF16)
    for copy in hidden_copies:
        copy.wait_recv()
    kept = pltpu.make_async_copy(hidden, hidden_out, local.at[6])
    kept.start()

    def times(right):
        return lax.dot_general(
            hidden[...], right, (((1,), (1,)), ((), ())), preferred_element_type=F32
        )

    logits = times(router[...])
    routes = [route[:, 8 + k : 9 + k] for k in range(TOPK)]
    chosen, gates = scores_of(routes, logits, EXP_FF)
    stat[...] = pack(
        [*gates, *chosen, scale, *routes, route[:, 7:8]], range(8)
    )
    gate_rows = 0.0
    for k in range(TOPK):
        columns = pack([*split(gates[k])], range(2)).astype(BF16)
        gate_rows += rows_of(picks[k], columns)
    message[:, width + LANES : width + 2 * LANES] = gate_rows.astype(BF16)
    rank = times(lefts[3 * RANK : 4 * RANK])
    rank = jnp.concatenate([rank, jnp.zeros((count, LANES - RANK), F32)], axis=1)
    message[:, width : width + LANES] = rows_of(any_pick, own_adapter(rank, 0)).astype(BF16)
    for q in range(cols):
        span = slice(q * wide, (q + 1) * wide)
        message[:, span] = rows_of(any_pick, hidden[:, span]).astype(BF16)
    traded = [
        send_to(message.at[pl.ds(j * CAP_FF, CAP_FF)], hids[j], across[j - 1])
        for j in range(EXP_FF - 1, 0, -1)
    ]
    own = pltpu.make_async_copy(message.at[pl.ds(0, CAP_FF)], hids[0], local.at[7])
    own.start()
    for j in range(1, EXP_FF):
        for n in range(len(piece_copies[j - 1])):
            piece_copies[j - 1][n].wait_recv()
            for i in range(1, replicas):
                m = j * replicas
                sibling_copies.append(send_to(chunks[n][m], chunks[n][m + i], beside[i - 1]))
    for copy in traded + sibling_copies:
        copy.wait_recv()
    for copy in started:
        copy.wait_send()
    kept.wait()
    own.wait()


def middle_forward(adapter, norm, router, route, low_rows, low_in, sources, weights, early, parts_axis, cols, replicas):
    hbm = pl.BlockSpec(memory_space=pl.ANY)
    vmem = pl.BlockSpec(memory_space=pltpu.VMEM)
    smem = pl.BlockSpec(memory_space=pltpu.SMEM)
    count, wide = sources[-1].shape
    width = wide * cols
    rows = EXP_FF * CAP_FF
    full = width + 3 * LANES
    total = 2 * (parts_axis - 1) + 4 * (cols - 1) + EXP_FF - 1
    return pl.pallas_call(
        functools.partial(middle_kernel, parts_axis, cols, replicas),
        out_shape=[jax.ShapeDtypeStruct(weights[0].shape[1:], BF16)] * (parts_axis - 1)
        + [jax.ShapeDtypeStruct(weights[1].shape[1:], BF16)] * (parts_axis - 1 - EARLY)
        + [jax.ShapeDtypeStruct((CAP_FF, full), BF16)] * EXP_FF
        + [
            jax.ShapeDtypeStruct((count, width), BF16),
            jax.ShapeDtypeStruct((count, wide), F32),
            jax.ShapeDtypeStruct((count, LANES), F32),
            jax.ShapeDtypeStruct((count, LANES), F32),
        ],
        in_specs=[smem] + [vmem] * 5 + [hbm] * (7 + EARLY),
        out_specs=[hbm] * (2 * parts_axis - 1 - EARLY + EXP_FF) + [vmem] * 3,
        scratch_shapes=[pltpu.VMEM(source.shape, source.dtype) for source in sources]
        + [
            pltpu.VMEM((cols, count, wide), F32),
            pltpu.VMEM((cols, count, wide), BF16),
            pltpu.VMEM((count, LANES), BF16),
            pltpu.VMEM((cols - 1, count, wide), BF16),
            pltpu.VMEM((cols - 1, count, LANES), BF16),
            pltpu.VMEM((8, count), F32),
            pltpu.VMEM((cols - 1, 8, count), F32),
            pltpu.VMEM((count, wide), BF16),
            pltpu.VMEM((count, width), BF16),
            pltpu.VMEM((rows, full), BF16),
            pltpu.SemaphoreType.DMA((total,)),
            pltpu.SemaphoreType.DMA((total,)),
            pltpu.SemaphoreType.DMA((8,)),
        ],
        compiler_params=pltpu.CompilerParams(
            collective_id=3, has_side_effects=True, vmem_limit_bytes=62 * 2**20
        ),
    )(adapter, norm, router, route, low_rows, low_in, *sources, *weights, *early)


def ffn_kernel(parts, depth, width, units, *refs):
    hids = refs[:EXP_FF]
    cots = refs[EXP_FF : 2 * EXP_FF]
    inners = refs[2 * EXP_FF : 2 * EXP_FF + parts]
    lasts = refs[2 * EXP_FF + parts : 2 * EXP_FF + 2 * parts]
    rights = refs[2 * EXP_FF + 2 * parts : 2 * EXP_FF + 2 * parts + 2]
    outs = refs[2 * EXP_FF + 2 * parts + 2 :]
    grads = outs[:EXP_FF]
    downs = outs[EXP_FF : 2 * EXP_FF]
    adapt = outs[2 * EXP_FF : 2 * EXP_FF + 3]
    hid, cot, block, act, product, leaving, sems, send, recv = outs[2 * EXP_FF + 3 :]
    replicas = parts // EXP_FF
    across = [opposite("row", j * replicas) for j in range(1, EXP_FF)]
    greet(across)
    row = lax.axis_index("row")
    wide = width + LANES
    copies = []
    for j in range(EXP_FF):
        where = pl.ds(j * CAP_FF, CAP_FF)
        near = hids[j].at[:, pl.ds(0, wide + LANES)]
        copies.append(pltpu.make_async_copy(near, hid.at[where], sems.at[j]))
        near = cot.at[where, pl.ds(0, width)]
        copies.append(pltpu.make_async_copy(cots[j], near, sems.at[EXP_FF + j]))
        near = cot.at[where, pl.ds(width, LANES)]
        low = hids[j].at[:, pl.ds(wide + LANES, LANES)]
        copies.append(pltpu.make_async_copy(low, near, sems.at[2 * EXP_FF + j]))
    for n, (start, size) in enumerate(((0, 2 * units), (2 * units, units))):
        near = block.at[pl.ds(width, LANES), pl.ds(start, size)]
        copies.append(pltpu.make_async_copy(rights[n], near, sems.at[3 * EXP_FF + n]))
    expert = row // replicas
    step = 2 * LANES
    full = units // step
    early_tiles = full // 2 + 1
    early = early_tiles * step
    second = []
    for m in range(parts):
        owner = jnp.bitwise_xor(row, m)
        where = pl.ds(pl.multiple_of(owner * depth, depth), depth)
        inner = inners[m] if m else inners[0].at[expert]
        last = lasts[m] if m else lasts[0].at[expert]
        for n, (source, start) in enumerate(((inner, 0), (inner, units), (last, 0))):
            for late, (begin, size) in enumerate(((0, early), (early, units - early))):
                if size:
                    near = block.at[where, pl.ds(n * units + begin, size)]
                    near_sem = sems.at[3 * EXP_FF + 2 + 6 * m + 3 * late + n]
                    far = source.at[:, pl.ds(start + begin, size)]
                    copy = pltpu.make_async_copy(far, near, near_sem)
                    (second if late else copies).append(copy)
    for copy in copies + second:
        copy.start()
    for copy in copies:
        copy.wait()
    gate_scale = hid[:, wide : wide + 1].astype(F32) + hid[:, wide + 1 : wide + 2].astype(F32)
    product[...] = jnp.zeros_like(product)

    def forward(start, size):
        here = pl.ds(start, size)
        up_here = pl.ds(units + start, size)
        down_here = pl.ds(2 * units + start, size)
        gate = jnp.dot(hid[:, :wide], block[:, here], preferred_element_type=F32)
        up = jnp.dot(hid[:, :wide], block[:, up_here], preferred_element_type=F32)
        grad = jnp.dot(cot[...], block[:, down_here], preferred_element_type=F32)
        sig = 1.0 / (1.0 + jnp.exp(-gate))
        mixed = (gate * sig * up).astype(BF16)
        act[:, down_here] = mixed
        product[...] += jnp.sum(mixed.astype(F32) * grad, axis=1, keepdims=True)
        grad = grad * gate_scale
        act[:, here] = (grad * up * sig * (1.0 + gate * (1.0 - sig))).astype(BF16)
        act[:, up_here] = (grad * gate * sig).astype(BF16)

    @pl.loop(0, early_tiles)
    def _(i):
        forward(pl.multiple_of(i * step, step), step)

    for copy in second:
        copy.wait()

    @pl.loop(early_tiles, full)
    def _(i):
        forward(pl.multiple_of(i * step, step), step)

    if units % step:
        forward(full * step, units % step)

    total = product[...]
    high = total.astype(BF16)
    low = (total - high.astype(F32)).astype(BF16)
    lane = lax.broadcasted_iota(jnp.int32, (EXP_FF * CAP_FF, LANES), 1)
    packed = jnp.where(
        lane == 0, high.astype(F32), jnp.where(lane == 1, low.astype(F32), 0.0)
    ).astype(BF16)
    traded = []
    spans = [(start, 4 * LANES) for start in range(0, width, 4 * LANES)] + [(width, LANES)]
    for start, size in spans:
        here = pl.ds(start, size)
        result = lax.dot_general(
            act[:, : 2 * units],
            block[here, : 2 * units],
            (((1,), (1,)), ((), ())),
            preferred_element_type=F32,
        ).astype(BF16)
        sent = here
        if start == width:
            result = jnp.concatenate([result, packed], axis=1)
            sent = pl.ds(start, 2 * LANES)
        grads[0][:, sent] = result[:CAP_FF]
        for j in range(1, EXP_FF):
            leaving[j - 1, :, sent] = result[j * CAP_FF : (j + 1) * CAP_FF]
            traded.append(
                remote(
                    leaving.at[j - 1, :, sent],
                    grads[j].at[:, sent],
                    send,
                    recv,
                    len(traded),
                    across[j - 1],
                )
            )

    def backward(start, size):
        here = pl.ds(start, size)
        result = lax.dot_general(
            act[:, 2 * units :],
            block[here, 2 * units :],
            (((1,), (1,)), ((), ())),
            preferred_element_type=F32,
        )
        result = (result * gate_scale).astype(BF16)
        for j in range(EXP_FF):
            downs[j][:, here] = result[j * CAP_FF : (j + 1) * CAP_FF]

    full_rows = wide // step

    @pl.loop(0, full_rows)
    def _(i):
        backward(pl.multiple_of(i * step, step), step)

    if wide % step:
        backward(full_rows * step, wide % step)
    ext = hid[:, width:wide]
    low_ext = (cot[:, width:].astype(F32) * gate_scale).astype(BF16)
    for n, low_rows in enumerate((ext, ext, low_ext)):
        adapt[n][...] = lax.dot_general(
            low_rows,
            act[:, n * units : (n + 1) * units],
            (((0,), (0,)), ((), ())),
            preferred_element_type=F32,
        ).astype(BF16)
    for copy in traded:
        copy.wait()


def feed_forward(hids, cots, inners, lasts, rights):
    parts = len(inners)
    depth, units = lasts[1].shape
    triple = 3 * units
    width = depth * parts
    remotes = (EXP_FF - 1) * (width // (4 * LANES) + 1)
    rows = EXP_FF * CAP_FF
    hbm = pl.BlockSpec(memory_space=pl.ANY)
    vmem = pl.BlockSpec(memory_space=pltpu.VMEM)
    wide = width + LANES
    return pl.pallas_call(
        functools.partial(ffn_kernel, parts, depth, width, units),
        out_shape=[jax.ShapeDtypeStruct((CAP_FF, wide + LANES), BF16)] * EXP_FF
        + [jax.ShapeDtypeStruct((CAP_FF, wide), BF16)] * EXP_FF
        + [jax.ShapeDtypeStruct((LANES, units), BF16)] * 3,
        in_specs=[hbm] * (2 * EXP_FF + 2 * parts + 2),
        out_specs=[vmem] + [hbm] * (EXP_FF - 1) + [vmem] * (EXP_FF + 3),
        scratch_shapes=[
            pltpu.VMEM((rows, wide + LANES), BF16),
            pltpu.VMEM((rows, wide), BF16),
            pltpu.VMEM((wide, triple), BF16),
            pltpu.VMEM((rows, triple), BF16),
            pltpu.VMEM((rows, 1), F32),
            pltpu.VMEM((EXP_FF - 1, CAP_FF, wide + LANES), BF16),
            pltpu.SemaphoreType.DMA((3 * EXP_FF + 2 + 6 * parts,)),
            pltpu.SemaphoreType.DMA((remotes,)),
            pltpu.SemaphoreType.DMA((remotes,)),
        ],
        compiler_params=pltpu.CompilerParams(
            collective_id=2, has_side_effects=True, vmem_limit_bytes=62 * 2**20
        ),
    )(*hids, *cots, *inners, *lasts, *rights)


def on_device(
    inputs,
    cotangent,
    lengths,
    adapter_pick,
    attn_route,
    ffn_route,
    norm_one,
    norm_two,
    router_attn,
    router_ffn,
    kv_weight,
    query_weight,
    out_weight,
    inner_weight,
    down_weight,
    query_left,
    query_right,
    kv_left,
    kv_right,
    out_left,
    out_right,
    inner_left,
    inner_right,
    down_left,
    down_right,
):
    count = inputs.shape[0]
    rows_axis = lax.axis_size("row")
    replicas = rows_axis // EXP_FF
    units = inner_weight.shape[3]
    cosine, sine = tables(count, HEAD_DIM)
    turns = (
        jnp.concatenate([cosine, cosine], axis=1),
        jnp.concatenate([-sine, sine], axis=1),
    )

    cols = lax.axis_size("col")
    padding = -units % LANES

    def padded(value):
        if not padding:
            return value
        return jnp.pad(value, [(0, 0)] * (value.ndim - 1) + [(0, padding)])

    down_flat = padded(down_weight)

    lefts_own = [
        value.swapaxes(1, 2)
        for value in (query_left, kv_left, out_left, inner_left, down_left)
    ]
    (
        inner_flat,
        inner_right_flat,
        rights,
        *outs,
    ) = front(
        [
            lengths,
            adapter_pick,
            attn_route.T,
            ffn_route.T,
            cotangent,
            norm_one[None, :],
            router_attn.T,
            *turns,
            query_right,
            kv_right,
            out_right,
        ],
        lefts_own,
        inputs,
        [kv_weight, query_weight, out_weight],
        padded(inner_weight),
        padded(inner_right).reshape(ADAPT * RANK, 2, units + padding),
        down_flat,
        rows_axis,
        cols,
        replicas,
    )
    early = outs[:EARLY]
    (
        kv_full,
        query_full,
        out_full,
        *cot_rows,
        hidden_one,
        lefts,
        stat_attn,
        low_in,
        keys,
        values,
        queries,
        attended,
        probability,
        attended_rows,
        low_rows,
        out_rows,
        picks_attn,
        picks_ffn,
        ranks,
        gate_rows,
        picks,
    ) = outs[EARLY:]
    picks = picks[:, 0, 0].astype(jnp.int32)
    ffn_right = [inner_right_flat, padded(down_right).reshape(ADAPT * RANK, units + padding)]

    *outs, hidden_two, middle, stat_ffn, totals_attn = middle_forward(
        adapter_pick,
        norm_two[None, :],
        router_ffn.T,
        stat_attn,
        low_rows,
        low_in,
        [out_rows, picks_attn, picks_ffn, lefts, inputs],
        [inner_flat, down_flat],
        early,
        rows_axis,
        cols,
        replicas,
    )
    inners = [inner_flat, *outs[: rows_axis - 1]]
    outs = outs[rows_axis - 1 :]
    lasts = [down_flat]
    for m in range(1, rows_axis):
        if m % replicas == 0 and m <= EARLY * replicas:
            lasts.append(early[m // replicas - 1])
        else:
            lasts.append(outs[0])
            outs = outs[1:]
    hidden_in = outs
    results = feed_forward(hidden_in, cot_rows, inners, lasts, ffn_right)
    grad_middle, grad_full, totals, branch_ffn, low_down_part = middle_back(
        results[:EXP_FF],
        results[EXP_FF : 2 * EXP_FF],
        adapter_pick,
        norm_two[None, :],
        router_ffn.T,
        stat_ffn,
        [picks_ffn, lefts, hidden_two, middle, cotangent],
        cols,
        replicas,
    )
    rights_ffn = lax.optimization_barrier((*results[2 * EXP_FF :], totals))[:3]
    rights_ffn = lax.optimization_barrier(lax.psum(rights_ffn, "row"))
    rights_ffn = [
        value[:, :units].reshape(ADAPT, RANK, units).astype(F32) for value in rights_ffn
    ]

    output, grad_inputs, *grads = tail(
        [
            picks,
            norm_one[None, :],
            router_attn.T,
            stat_attn,
            *turns,
            rights,
            ranks,
            gate_rows,
            totals_attn,
            totals,
            low_down_part,
        ],
        [
            grad_full,
            picks_attn,
            attended_rows,
            queries,
            keys,
            values,
            probability,
            attended,
            lefts,
            hidden_one,
            hidden_two,
            grad_middle,
            middle,
            cotangent,
            inputs,
        ],
        branch_ffn,
        [out_full, query_full, kv_full],
        rows_axis,
        cols,
    )
    lefts_back = [grad.swapaxes(1, 2) for grad in grads[:5]]
    rights_back = grads[5:]
    return (
        output,
        grad_inputs,
        lefts_back[0],
        rights_back[0],
        lefts_back[1],
        jnp.stack(rights_back[1:3], axis=2),
        lefts_back[2],
        rights_back[3],
        lefts_back[3],
        jnp.stack(rights_ffn[:2], axis=2),
        lefts_back[4],
        rights_ffn[2],
    )


def solution(mesh):
    placed = (
        P("row", "col"),
        P("row", "col"),
        P("row"),
        P("row"),
        P("row", None),
        P("row", None),
        P(),
        P(),
        P(),
        P(),
        P(None, "row", "col"),
        P(None, "row", "col"),
        P(None, "row", "col"),
        P(None, "row", None, "col"),
        P(None, "row", "col"),
        P(None, "row", None),
        P(None, None, "col"),
        P(None, "row", None),
        P(None, None, None, "col"),
        P(None, "row", None),
        P(None, None, "col"),
        P(None, "row", None),
        P(None, None, None, "col"),
        P(None, "row", None),
        P(None, None, "col"),
    )
    return jax.shard_map(
        on_device,
        mesh=mesh,
        in_specs=placed,
        out_specs=(
            P("row", "col"),
            P("row", "col"),
            P(None, "row", None),
            P(None, None, "col"),
            P(None, "row", None),
            P(None, None, None, "col"),
            P(None, "row", None),
            P(None, None, "col"),
            P(None, "row", None),
            P(None, None, None, "col"),
            P(None, "row", None),
            P(None, None, "col"),
        ),
        check_vma=False,
    )
```
